32 devices in a mesh: grp: 2 (over x), chan: 16 (over z, y, core).
Axes of the slice: x: 2, y: 2, z: 4, core: 2. Of those that a mesh axis runs over, the one named last changes fastest.
Arguments:
- spectra: bfloat16 [1024, 2, 4, 4096], P(None, None, None, ('grp', 'chan')), parts along dimension 3, may hold values from -6 to 6
- quality: int32 [32, 4], P(('grp', 'chan')), parts along dimension 0, may hold values 0 or 1
Outputs:
- near_corr: bfloat16 [32, 9, 128, 128], P(('grp', 'chan')), parts along dimension 0
- far_corr: bfloat16 [32, 9, 128, 128], P(('grp', 'chan')), parts along dimension 0
The draws below stay inside these ranges and needn't reach their ends.
There are 2 independent parts, one for each index of `grp`. The reference program is written for one: setup_inputs(seed, part) draws one part's arguments, and reference() takes and returns one part's arrays. A program takes and returns all parts, laid end to end along the dimension named above; each array names one. Nothing has to cross between parts.
All inputs are finite; a program needn't handle non-finite values. No bound on the sum of `quality` on one device may be relied on, other than what follows from the above.
Results may differ from the reference program's by a relative error of at most 0.012.
Values may be sent and summed in bfloat16 or wider, within the bound.
No kernel may reach another device: no remote copies, remote signals or barrier semaphores. Data moves between devices by JAX's collectives and lax.ppermute only.
A program may use at most 64 MiB of HBM per device.

```python
import math
import jax
import jax.numpy as jnp
from jax import lax

F = 1024
W = 4
CH = 128
HL = 4
NBLK = 16
CHANNELS = 2048


def set_ends(values, stream_key, low, high):
    spot = [jax.random.randint(jax.random.fold_in(stream_key, axis), (), 0, length) for axis, length in enumerate(values.shape)]
    main_axis = values.shape.index(max(values.shape))
    beside = spot[:main_axis] + [(spot[main_axis] + 1) % values.shape[main_axis]] + spot[main_axis + 1:]
    return values.at[tuple(spot)].set(low).at[tuple(beside)].set(high)


def block_scale(key, extent, pieces, least, high):
    gain, own = 1.0, jax.random.fold_in(key, 6)
    for dim, blocks in pieces:
        steps = jnp.exp(jax.random.uniform(jax.random.fold_in(own, dim), (blocks,), jnp.float32, least / len(pieces), high / len(pieces)))
        gain = gain * jnp.repeat(steps, extent[dim] // blocks).reshape([-1 if axis == dim else 1 for axis in range(len(extent))])
    return gain


def bell_draw(own_key, shape, spread, reach, split=(), kind=jnp.bfloat16):
    loudness = block_scale(own_key, shape, split, -0.22, 0.18) if split else 1.0
    drawn = jax.random.normal(own_key, shape, jnp.float32) * spread * loudness
    return jnp.minimum(jnp.maximum(drawn, -reach), reach).astype(kind)


def setup_inputs(seed: int = 0, part: int = 0) -> dict:
    streams_of = jax.random.split(jax.random.key(seed), 3)
    own_keys = jax.random.split(jax.random.fold_in(streams_of[2], part), 3)
    spectra = bell_draw(own_keys[0], (F, 2, W, CHANNELS), 1.0, 6.0, ((3, 16),))
    quality = set_ends((jax.random.randint(own_keys[1], (NBLK, W), 0, 4) < 3).astype(jnp.int32), jax.random.fold_in(own_keys[1], 1), 0, 1)
    return dict(spectra=spectra, quality=quality)


def lag_table(freq_count, window_count):
    lag_values = jnp.arange(2 * HL + 1, dtype=jnp.float32) - HL
    freq_values = jnp.arange(freq_count, dtype=jnp.float32)
    phases = jnp.pi / freq_count * lag_values[:, None] * freq_values[None, :]
    factor = 1.0 / math.sqrt(window_count * freq_count)
    return jnp.stack([jnp.cos(phases) * factor, -jnp.sin(phases) * factor], axis=1).astype(jnp.bfloat16)

def cross_lag_ref(first_spec, second_spec, weights, lag_coeffs):
    freq_count = first_spec.shape[0]
    channel_count = first_spec.shape[3]
    block_len = min(128, freq_count)
    first_wide = first_spec.astype(jnp.float32)
    masked = second_spec.astype(jnp.float32) * weights.astype(jnp.float32)[None, None, :, None]
    coeff_wide = lag_coeffs.astype(jnp.float32)
    accum = jnp.zeros((lag_coeffs.shape[0], channel_count, channel_count), jnp.float32)
    for offset in range(0, freq_count, block_len):
        first_blk = first_wide[offset:offset + block_len]
        second_blk = masked[offset:offset + block_len]
        cos_part = coeff_wide[:, 0, offset:offset + block_len][:, :, None, None]
        sin_part = coeff_wide[:, 1, offset:offset + block_len][:, :, None, None]
        real_in = first_blk[None, :, 0]
        imag_in = first_blk[None, :, 1]
        left_real = cos_part * real_in + sin_part * imag_in
        left_imag = cos_part * imag_in - sin_part * real_in
        left = lax.optimization_barrier(jnp.stack([left_real, left_imag], axis=2).astype(jnp.bfloat16)).astype(jnp.float32)
        accum = accum + jnp.einsum('lfcwi,fcwj->lij', left, second_blk)
    return accum

def reference(spectra, quality):
    block_total = quality.shape[0]
    coeffs = lag_table(F, W)
    shaped = spectra.reshape(F, 2, W, block_total, CH)

    def one_block(index):
        neighbour_idx = ((index + 1) % block_total).astype(jnp.int32)
        opposite_idx = ((index + block_total // 2) % block_total).astype(jnp.int32)
        own_spec = lax.dynamic_index_in_dim(shaped, index, 3, keepdims=False)
        near_spec = lax.dynamic_index_in_dim(shaped, neighbour_idx, 3, keepdims=False)
        far_spec = lax.dynamic_index_in_dim(shaped, opposite_idx, 3, keepdims=False)
        own_flags = lax.dynamic_index_in_dim(quality, index, 0, keepdims=False)
        near_flags = lax.dynamic_index_in_dim(quality, neighbour_idx, 0, keepdims=False)
        far_flags = lax.dynamic_index_in_dim(quality, opposite_idx, 0, keepdims=False)
        near_out = cross_lag_ref(own_spec, near_spec, own_flags * near_flags, coeffs)
        far_out = cross_lag_ref(own_spec, far_spec, own_flags * far_flags, coeffs)
        return (near_out.astype(jnp.bfloat16), far_out.astype(jnp.bfloat16))
    near_all, far_all = lax.map(one_block, jnp.arange(block_total, dtype=jnp.int32))
    return (near_all, far_all)
```

```python
import functools
import math

import jax
import jax.numpy as jnp
from jax import lax
from jax.experimental import pallas as pl
from jax.experimental.pallas import tpu as pltpu
from jax.sharding import PartitionSpec as P

HL = 4
LAGS = 2 * HL + 1
STEP = 1024
PARTS = 4


def goes_down(pair, half):
    return pair == 0 or pair == half - 1 or (pair % 2 == 1 and pair != 1)


def lag_rows(freq_count, window_count):
    per_bin = 2 * window_count
    row = jnp.arange(freq_count * per_bin, dtype=jnp.int32)
    freq_values = (row // per_bin).astype(jnp.float32)
    sign = jnp.where(row % per_bin < window_count, 1.0, -1.0)
    lag_values = jnp.arange(HL + 1, dtype=jnp.float32)
    phases = jnp.pi / freq_count * lag_values[:, None] * freq_values[None, :]
    factor = 1.0 / math.sqrt(window_count * freq_count)
    cos_part = jnp.cos(phases) * factor
    sin_part = -jnp.sin(phases[1:]) * factor * sign[None, :]
    return jnp.concatenate([cos_part, sin_part], axis=0).astype(jnp.bfloat16)


def turn_kernel(x_ref, plain_ref, swapped_ref):
    x = x_ref[...].astype(jnp.float32)
    rows, cols = x.shape
    swapped = pltpu.roll(x.reshape(rows // 8, 8, cols), 4, 1).reshape(rows, cols)
    plain_ref[...] = x.T.astype(jnp.bfloat16)
    swapped_ref[...] = swapped.T.astype(jnp.bfloat16)


def turn(x):
    rows, cols = x.shape
    out = jax.ShapeDtypeStruct((cols, rows), jnp.bfloat16)
    return pl.pallas_call(
        turn_kernel,
        grid=(rows // STEP,),
        in_specs=[pl.BlockSpec((STEP, cols), lambda s: (s, 0))],
        out_specs=[pl.BlockSpec((cols, STEP), lambda s: (0, s))] * 2,
        out_shape=[out, out],
        compiler_params=pltpu.CompilerParams(vmem_limit_bytes=32 * 1024 * 1024),
        cost_estimate=pl.CostEstimate(flops=0, bytes_accessed=6 * rows * cols, transcendentals=0),
        name="turn",
    )(x)


def corr_kernel(first, last, mirrored, flag_ref, plain_ref, swapped_ref, coeff_ref, partner_ref, weight_ref, *rest):
    acc_in = None if first else rest[0]
    outs = rest if first else rest[1:]
    scratch = outs[-1]
    outs = outs[:-1]
    if last:
        acc = outs[-1]
        outs = outs[:-1]
    else:
        acc = outs[0]
    step = pl.program_id(0)
    cols = partner_ref.shape[1]

    @pl.when(step == 0)
    def _():
        if first:
            acc[...] = jnp.zeros_like(acc)
        else:
            acc[...] = acc_in[...]

    for k in range(HL + 1):
        scratch[k * cols:(k + 1) * cols, :] = plain_ref[...] * coeff_ref[k:k + 1, :]
    for k in range(HL + 1, LAGS):
        scratch[k * cols:(k + 1) * cols, :] = swapped_ref[...] * coeff_ref[k:k + 1, :]
    rows = partner_ref.shape[0]
    weights = jnp.broadcast_to(weight_ref[...][None], (rows // 16, 16, cols)).reshape(rows, cols)
    acc[...] += jnp.dot(scratch[...], partner_ref[...] * weights, preferred_element_type=jnp.float32)

    if last:
        @pl.when(step == pl.num_programs(0) - 1)
        def _():
            def result(lag):
                k = abs(lag - HL)
                even = acc[k * cols:(k + 1) * cols, :]
                if k == 0:
                    return even
                odd = acc[(HL + k) * cols:(HL + k + 1) * cols, :]
                return even + odd if lag > HL else even - odd

            if mirrored == "both":
                for lag in range(LAGS):
                    value = result(lag)
                    outs[0][lag] = value.astype(jnp.bfloat16)
                    outs[1][LAGS - 1 - lag] = value.T.astype(jnp.bfloat16)
            elif mirrored == "no":
                for lag in range(LAGS):
                    outs[0][lag] = result(lag).astype(jnp.bfloat16)
            else:
                @pl.when(flag_ref[0] == 0)
                def _():
                    for lag in range(LAGS):
                        outs[0][lag] = result(lag).astype(jnp.bfloat16)

                @pl.when(flag_ref[0] != 0)
                def _():
                    for lag in range(LAGS):
                        outs[0][LAGS - 1 - lag] = result(lag).T.astype(jnp.bfloat16)


def corr(turned, coeffs, partner, start, weights, flag, acc, last, mirrored, name):
    plain, swapped = turned
    cols = plain.shape[0]
    rows = partner.shape[0]
    first = acc is None
    skip = start // STEP
    acc_shape = jax.ShapeDtypeStruct((LAGS * cols, cols), jnp.float32)
    acc_spec = pl.BlockSpec((LAGS * cols, cols), lambda s: (0, 0))
    res_shape = jax.ShapeDtypeStruct((LAGS, cols, cols), jnp.bfloat16)
    res_spec = pl.BlockSpec((LAGS, cols, cols), lambda s: (0, 0, 0))
    in_specs = [
        pl.BlockSpec(memory_space=pltpu.SMEM),
        pl.BlockSpec((cols, STEP), lambda s: (0, s + skip)),
        pl.BlockSpec((cols, STEP), lambda s: (0, s + skip)),
        pl.BlockSpec((LAGS, STEP), lambda s: (0, s + skip)),
        pl.BlockSpec((STEP, cols), lambda s: (s, 0)),
        pl.BlockSpec((16, cols), lambda s: (0, 0)),
    ]
    args = [flag, plain, swapped, coeffs, partner, weights]
    if not first:
        in_specs.append(acc_spec)
        args.append(acc)
    scratch = [pltpu.VMEM((LAGS * cols, STEP), jnp.bfloat16)]
    if last:
        count = 2 if mirrored == "both" else 1
        out_shape, out_specs = [res_shape] * count, [res_spec] * count
        scratch = [pltpu.VMEM((LAGS * cols, cols), jnp.float32)] + scratch
    else:
        out_shape, out_specs = [acc_shape], [acc_spec]
    return pl.pallas_call(
        functools.partial(corr_kernel, first, last, mirrored),
        grid=(rows // STEP,),
        in_specs=in_specs,
        out_specs=out_specs,
        out_shape=out_shape,
        scratch_shapes=scratch,
        compiler_params=pltpu.CompilerParams(vmem_limit_bytes=32 * 1024 * 1024),
        cost_estimate=pl.CostEstimate(
            flops=2 * LAGS * cols * cols * rows, bytes_accessed=6 * rows * cols, transcendentals=0
        ),
        name=name,
    )(*args)


def row_weights(own_flags, partner_flags, cols):
    both = (own_flags * partner_flags).astype(jnp.bfloat16)
    return jnp.broadcast_to(jnp.tile(both, 16 // both.shape[0])[:, None], (16, cols))


def local(spectra, quality):
    count = lax.axis_size("chan")
    half = count // 2
    me = lax.axis_index("chan")
    freq_count, _, window_count, cols = spectra.shape
    block = spectra.reshape(-1, cols)
    rows = block.shape[0]

    down = [goes_down(p, half) for p in range(half)]
    far_pairs = [(p + half, p) if d else (p, p + half) for p, d in enumerate(down)]
    back_pairs = [(p, p + half) if d else (p + half, p) for p, d in enumerate(down)]
    near_pairs = [(d + 1, d) for d in range(count - 1) if d != half - 1]
    swap_pairs = [(0, half - 1), (half - 1, 0)]
    side_pairs = [(0, half - 1), (half - 1, count - 1)]

    piece = rows // PARTS
    far_in = [lax.ppermute(block[s * piece:(s + 1) * piece], "chan", far_pairs) for s in range(PARTS)]
    near_in = lax.ppermute(block, "chan", near_pairs)
    swap_in = lax.ppermute(block, "chan", swap_pairs)

    flags = lax.all_gather(quality[0], "chan")
    near_at = lax.rem(me + 1, count)
    far_at = lax.rem(me + half, count)
    swap_at = jnp.where(me == 0, half - 1, 0)

    def flags_of(at):
        return lax.dynamic_index_in_dim(flags, at, 0, keepdims=False)

    near_w = row_weights(quality[0], flags_of(near_at), cols)
    far_w = row_weights(quality[0], flags_of(far_at), cols)
    side_w = row_weights(flags_of(swap_at), flags_of(far_at), cols)

    coeffs = lag_rows(freq_count, window_count)
    turned = turn(block)
    swap_turned = turn(swap_in)
    flag = (me == half - 1).astype(jnp.int32).reshape(1)

    near_own, = corr(turned, coeffs, near_in, 0, near_w, flag, None, True, "no", "near_corr")
    far_acc = side_acc = None
    for s in range(PARTS - 1):
        far_acc, = corr(turned, coeffs, far_in[s], s * piece, far_w, flag, far_acc, False, "no", "far_part")
        side_acc, = corr(swap_turned, coeffs, far_in[s], s * piece, side_w, flag, side_acc, False, "no", "side_part")
    at = (PARTS - 1) * piece
    far_own, far_mirror = corr(turned, coeffs, far_in[-1], at, far_w, flag, far_acc, True, "both", "far_last")
    side_own, = corr(swap_turned, coeffs, far_in[-1], at, side_w, flag, side_acc, True, "flag", "side_last")

    far_back = lax.ppermute(far_mirror, "chan", back_pairs)
    side_back = lax.ppermute(side_own, "chan", side_pairs)

    is_down = jnp.asarray(down)[lax.rem(me, half)]
    hosts = is_down == (me < half)
    far = jnp.where(hosts, far_own, far_back)
    near = jnp.where((me == half - 1) | (me == count - 1), side_back, near_own)
    return near[None], far[None]


def solution(mesh):
    return jax.shard_map(
        local,
        mesh=mesh,
        in_specs=(P(None, None, None, ("grp", "chan")), P(("grp", "chan"), None)),
        out_specs=(P(("grp", "chan"), None, None, None), P(("grp", "chan"), None, None, None)),
        check_vma=False,
    )
```

```python
import functools
import math

import jax
import jax.numpy as jnp
from jax import lax
from jax.experimental import pallas as pl
from jax.experimental.pallas import tpu as pltpu
from jax.sharding import PartitionSpec as P

HL = 4
LAGS = 2 * HL + 1
STEP = 1024
PIECES = (2, 6, 8)


def goes_down(pair, half):
    return pair == 0 or pair == half - 1 or (pair % 2 == 1 and pair != 1)


def lag_rows(freq_count, window_count):
    per_bin = 2 * window_count
    row = jnp.arange(freq_count * per_bin, dtype=jnp.int32)
    freq_values = (row // per_bin).astype(jnp.float32)
    sign = jnp.where(row % per_bin < window_count, 1.0, -1.0)
    lag_values = jnp.arange(HL + 1, dtype=jnp.float32)
    phases = jnp.pi / freq_count * lag_values[:, None] * freq_values[None, :]
    factor = 1.0 / math.sqrt(window_count * freq_count)
    cos_part = jnp.cos(phases) * factor
    sin_part = -jnp.sin(phases[1:]) * factor * sign[None, :]
    return jnp.concatenate([cos_part, sin_part], axis=0).astype(jnp.bfloat16)


def mask_kernel(x_ref, weight_ref, masked_ref):
    rows, cols = x_ref.shape
    weights = jnp.broadcast_to(weight_ref[...][None], (rows // 16, 16, cols)).reshape(rows, cols)
    masked_ref[...] = x_ref[...] * weights


def mask(x, weights, start, rows, name):
    cols = x.shape[1]
    skip = start // STEP
    return pl.pallas_call(
        mask_kernel,
        grid=(rows // STEP,),
        in_specs=[
            pl.BlockSpec((STEP, cols), lambda s: (s + skip, 0)),
            pl.BlockSpec((16, cols), lambda s: (0, 0)),
        ],
        out_specs=pl.BlockSpec((STEP, cols), lambda s: (s, 0)),
        out_shape=jax.ShapeDtypeStruct((rows, cols), jnp.bfloat16),
        compiler_params=pltpu.CompilerParams(vmem_limit_bytes=32 * 1024 * 1024),
        cost_estimate=pl.CostEstimate(flops=rows * cols, bytes_accessed=4 * rows * cols, transcendentals=0),
        name=name,
    )(x, weights)


def turn_kernel(x_ref, plain_ref, swapped_ref):
    x = x_ref[...].astype(jnp.float32)
    rows, cols = x.shape
    swapped = pltpu.roll(x.reshape(rows // 8, 8, cols), 4, 1).reshape(rows, cols)
    plain_ref[...] = x.T.astype(jnp.bfloat16)
    swapped_ref[...] = swapped.T.astype(jnp.bfloat16)


def turn(x, name):
    rows, cols = x.shape
    out = jax.ShapeDtypeStruct((cols, rows), jnp.bfloat16)
    return pl.pallas_call(
        turn_kernel,
        grid=(rows // STEP,),
        in_specs=[pl.BlockSpec((STEP, cols), lambda s: (s, 0))],
        out_specs=[pl.BlockSpec((cols, STEP), lambda s: (0, s))] * 2,
        out_shape=[out, out],
        compiler_params=pltpu.CompilerParams(vmem_limit_bytes=32 * 1024 * 1024),
        cost_estimate=pl.CostEstimate(flops=0, bytes_accessed=6 * rows * cols, transcendentals=0),
        name=name,
    )(x)


def corr_kernel(first, last, mirrored, flag_ref, plain_ref, swapped_ref, coeff_ref, partner_ref, *rest):
    acc_in = None if first else rest[0]
    outs = rest if first else rest[1:]
    scratch = outs[-1]
    outs = outs[:-1]
    if last:
        acc = outs[-1]
        outs = outs[:-1]
    else:
        acc = outs[0]
    step = pl.program_id(0)
    cols = partner_ref.shape[1]

    @pl.when(step == 0)
    def _():
        if first:
            acc[...] = jnp.zeros_like(acc)
        else:
            acc[...] = acc_in[...]

    for k in range(HL + 1):
        scratch[k * cols:(k + 1) * cols, :] = plain_ref[...] * coeff_ref[k:k + 1, :]
    for k in range(HL + 1, LAGS):
        scratch[k * cols:(k + 1) * cols, :] = swapped_ref[...] * coeff_ref[k:k + 1, :]
    acc[...] += jnp.dot(scratch[...], partner_ref[...], preferred_element_type=jnp.float32)

    if last:
        @pl.when(step == pl.num_programs(0) - 1)
        def _():
            def result(lag):
                k = abs(lag - HL)
                even = acc[k * cols:(k + 1) * cols, :]
                if k == 0:
                    return even
                odd = acc[(HL + k) * cols:(HL + k + 1) * cols, :]
                return even + odd if lag > HL else even - odd

            if mirrored == "both":
                for lag in range(LAGS):
                    value = result(lag)
                    outs[0][lag] = value.astype(jnp.bfloat16)
                    outs[1][LAGS - 1 - lag] = value.T.astype(jnp.bfloat16)
            elif mirrored == "no":
                for lag in range(LAGS):
                    outs[0][lag] = result(lag).astype(jnp.bfloat16)
            else:
                @pl.when(flag_ref[0] == 0)
                def _():
                    for lag in range(LAGS):
                        outs[0][lag] = result(lag).astype(jnp.bfloat16)

                @pl.when(flag_ref[0] != 0)
                def _():
                    for lag in range(LAGS):
                        outs[0][LAGS - 1 - lag] = result(lag).T.astype(jnp.bfloat16)


def corr(turned, coeffs, partner, start, flag, acc, last, mirrored, name):
    plain, swapped = turned
    cols = plain.shape[0]
    rows = partner.shape[0]
    first = acc is None
    skip = start // STEP
    acc_shape = jax.ShapeDtypeStruct((LAGS * cols, cols), jnp.float32)
    acc_spec = pl.BlockSpec((LAGS * cols, cols), lambda s: (0, 0))
    res_shape = jax.ShapeDtypeStruct((LAGS, cols, cols), jnp.bfloat16)
    res_spec = pl.BlockSpec((LAGS, cols, cols), lambda s: (0, 0, 0))
    in_specs = [
        pl.BlockSpec(memory_space=pltpu.SMEM),
        pl.BlockSpec((cols, STEP), lambda s: (0, s + skip)),
        pl.BlockSpec((cols, STEP), lambda s: (0, s + skip)),
        pl.BlockSpec((LAGS, STEP), lambda s: (0, s + skip)),
        pl.BlockSpec((STEP, cols), lambda s: (s, 0)),
    ]
    args = [flag, plain, swapped, coeffs, partner]
    if not first:
        in_specs.append(acc_spec)
        args.append(acc)
    scratch = [pltpu.VMEM((LAGS * cols, STEP), jnp.bfloat16)]
    if last:
        count = 2 if mirrored == "both" else 1
        out_shape, out_specs = [res_shape] * count, [res_spec] * count
        scratch = [pltpu.VMEM((LAGS * cols, cols), jnp.float32)] + scratch
    else:
        out_shape, out_specs = [acc_shape], [acc_spec]
    return pl.pallas_call(
        functools.partial(corr_kernel, first, last, mirrored),
        grid=(rows // STEP,),
        in_specs=in_specs,
        out_specs=out_specs,
        out_shape=out_shape,
        scratch_shapes=scratch,
        compiler_params=pltpu.CompilerParams(vmem_limit_bytes=32 * 1024 * 1024),
        cost_estimate=pl.CostEstimate(
            flops=2 * LAGS * cols * cols * rows, bytes_accessed=6 * rows * cols, transcendentals=0
        ),
        name=name,
    )(*args)


def local(spectra, quality):
    count = lax.axis_size("chan")
    half = count // 2
    me = lax.axis_index("chan")
    freq_count, _, window_count, cols = spectra.shape
    block = spectra.reshape(-1, cols)
    rows = block.shape[0]
    weights = jnp.tile(quality[0].astype(jnp.bfloat16), 16 // window_count)
    weights = jnp.broadcast_to(weights[:, None], (16, cols))

    down = [goes_down(p, half) for p in range(half)]
    far_pairs = [(p + half, p) if d else (p, p + half) for p, d in enumerate(down)]
    far_pairs += [(0, 1), (half - 1, half - 2)]
    near_pairs = [(d + 1, d) for d in range(1, count - 1) if d not in (half - 2, half - 1)]
    near_pairs += [(0, half - 1), (half - 1, 0)]
    back_pairs = [(p, p + half) if d else (p + half, p) for p, d in enumerate(down)]
    back_pairs += [(1, 0)]
    side_pairs = [(0, half - 1), (half - 1, count - 1)]

    ends = [rows * e // 8 for e in PIECES]
    starts = [0] + ends[:-1]
    pieces = [mask(block, weights, a, b - a, f"mask_{s}") for s, (a, b) in enumerate(zip(starts, ends))]
    far_in = [lax.ppermute(piece, "chan", far_pairs) for piece in pieces]
    block, weights, _ = lax.optimization_barrier((block, weights, pieces))
    masked = mask(block, weights, 0, rows, "mask_all")
    near_in = lax.ppermute(masked, "chan", near_pairs)

    coeffs = lag_rows(freq_count, window_count)
    turned = turn(masked, "turn_own")
    flag = (me == half - 1).astype(jnp.int32).reshape(1)
    near_own, = corr(turned, coeffs, near_in, 0, flag, None, True, "no", "near_corr")
    side_turned = turn(near_in, "turn_near")

    far_acc = side_acc = None
    for s in range(len(pieces) - 1):
        far_acc, = corr(turned, coeffs, far_in[s], starts[s], flag, far_acc, False, "no", f"far_{s}")
        side_acc, = corr(side_turned, coeffs, far_in[s], starts[s], flag, side_acc, False, "no", f"side_{s}")
    far_acc, side_acc, near_own, last_in = lax.optimization_barrier((far_acc, side_acc, near_own, far_in[-1]))
    far_own, far_mirror = corr(turned, coeffs, last_in, starts[-1], flag, far_acc, True, "both", "far_last")
    far_back = lax.ppermute(far_mirror, "chan", back_pairs)
    side_own, = corr(side_turned, coeffs, last_in, starts[-1], flag, side_acc, True, "flag", "side_last")
    side_back = lax.ppermute(side_own, "chan", side_pairs)

    hosts = jnp.asarray(down)[lax.rem(me, half)] == (me < half)
    far = jnp.where(hosts, far_own, far_back)
    near = jnp.where((me == half - 1) | (me == count - 1), side_back, near_own)
    near = jnp.where(me == 0, far_back, jnp.where(me == half - 2, far_own, near))
    return near[None], far[None]


def solution(mesh):
    return jax.shard_map(
        local,
        mesh=mesh,
        in_specs=(P(None, None, None, ("grp", "chan")), P(("grp", "chan"), None)),
        out_specs=(P(("grp", "chan"), None, None, None), P(("grp", "chan"), None, None, None)),
        check_vma=False,
    )
```

```python
import functools
import math

import jax
import jax.numpy as jnp
from jax import lax
from jax.experimental import pallas as pl
from jax.experimental.pallas import tpu as pltpu
from jax.sharding import PartitionSpec as P

HL = 4
LAGS = 2 * HL + 1
STEP = 1024
TILE = 256
ENDS = (5, 8)
PARAMS = pltpu.CompilerParams(vmem_limit_bytes=32 * 1024 * 1024)


def goes_down(pair, half):
    return pair in (0, half - 1) or pair % 2 == 1 and pair != 1


def lag_rows(freq_count, window_count):
    per_bin = 2 * window_count
    row = jnp.arange(freq_count * per_bin, dtype=jnp.int32)
    freq_values = (row // per_bin).astype(jnp.float32)
    sign = jnp.where(row % per_bin < window_count, 1.0, -1.0)
    lag_values = jnp.arange(HL + 1, dtype=jnp.float32)
    phases = jnp.pi / freq_count * lag_values[:, None] * freq_values[None, :]
    factor = 1.0 / math.sqrt(window_count * freq_count)
    cos_part = jnp.cos(phases) * factor
    sin_part = -jnp.sin(phases[1:]) * factor * sign[None, :]
    return jnp.concatenate([cos_part, sin_part], axis=0).astype(jnp.bfloat16)


def mask_kernel(ends, flags_ref, x_ref, *piece_refs):
    rows, cols = x_ref.shape
    windows = flags_ref.shape[1]
    step = pl.program_id(0)
    window = lax.broadcasted_iota(jnp.int32, (16, cols), 0) % windows
    weights = jnp.zeros((16, cols), jnp.float32)
    for w in range(windows):
        weights = jnp.where(window == w, flags_ref[0, w].astype(jnp.float32), weights)
    weights = jnp.broadcast_to(weights.astype(jnp.bfloat16)[None], (rows // 16, 16, cols))
    masked = x_ref[...] * weights.reshape(rows, cols)
    begin = 0
    for end, piece_ref in zip(ends, piece_refs):
        @pl.when((step >= begin) & (step < end))
        def _():
            piece_ref[...] = masked
        begin = end


def mask(x, flags):
    rows, cols = x.shape
    steps = rows // STEP
    ends = [steps * e // 8 for e in ENDS]
    begins = [0] + ends[:-1]
    sizes = [e - b for b, e in zip(begins, ends)]

    def place(begin, size):
        return lambda s: (jnp.clip(s - begin, 0, size - 1), 0)

    return pl.pallas_call(
        functools.partial(mask_kernel, ends),
        grid=(steps,),
        in_specs=[pl.BlockSpec(memory_space=pltpu.SMEM), pl.BlockSpec((STEP, cols), lambda s: (s, 0))],
        out_specs=[pl.BlockSpec((STEP, cols), place(b, n)) for b, n in zip(begins, sizes)],
        out_shape=[jax.ShapeDtypeStruct((n * STEP, cols), jnp.bfloat16) for n in sizes],
        compiler_params=PARAMS,
        cost_estimate=pl.CostEstimate(flops=rows * cols, bytes_accessed=4 * rows * cols, transcendentals=0),
        name="mask",
    )(flags, x)


def turn_kernel(active_ref, x_ref, plain_ref, swapped_ref):
    @pl.when(active_ref[0] != 0)
    def _():
        rows, cols = x_ref.shape
        same = lax.broadcasted_iota(jnp.int32, (cols, cols), 0) == lax.broadcasted_iota(jnp.int32, (cols, cols), 1)
        eye = jnp.where(same, 1.0, 0.0).astype(jnp.bfloat16)
        source = lax.broadcasted_iota(jnp.int32, (TILE, TILE), 0)
        target = lax.broadcasted_iota(jnp.int32, (TILE, TILE), 1)
        exchange = jnp.where((source ^ 4) == target, 1.0, 0.0).astype(jnp.bfloat16)
        plain = lax.dot_general(eye, x_ref[...], (((1,), (1,)), ((), ())), preferred_element_type=jnp.float32)
        plain = plain.astype(jnp.bfloat16)
        plain_ref[...] = plain
        for t in range(0, rows, TILE):
            swapped = jnp.dot(plain[:, t:t + TILE], exchange, preferred_element_type=jnp.float32)
            swapped_ref[:, t:t + TILE] = swapped.astype(jnp.bfloat16)


def turn(x, active, name):
    rows, cols = x.shape
    out = jax.ShapeDtypeStruct((cols, rows), jnp.bfloat16)
    return pl.pallas_call(
        turn_kernel,
        grid_spec=pltpu.PrefetchScalarGridSpec(
            num_scalar_prefetch=1,
            grid=(rows // STEP,),
            in_specs=[pl.BlockSpec((STEP, cols), lambda s, on: (s * on[0], 0))],
            out_specs=[pl.BlockSpec((cols, STEP), lambda s, on: (0, s * on[0]))] * 2,
        ),
        out_shape=[out, out],
        compiler_params=PARAMS,
        cost_estimate=pl.CostEstimate(flops=0, bytes_accessed=6 * rows * cols, transcendentals=0),
        name=name,
    )(active, x)


def lag_result(acc, cols, lag):
    k = abs(lag - HL)
    even = acc[k * cols:(k + 1) * cols, :]
    if k == 0:
        return even.astype(jnp.bfloat16)
    odd = acc[(HL + k) * cols:(HL + k + 1) * cols, :]
    return (even + odd if lag > HL else even - odd).astype(jnp.bfloat16)


def corr_kernel(first, kind, active_ref, plain_ref, swapped_ref, coeff_ref, partner_ref, *rest):
    acc_in = None if first else rest[0]
    refs = list(rest if first else rest[1:])
    buffers = [refs.pop(), refs.pop()]
    acc = refs.pop()
    step = pl.program_id(0)
    cols = partner_ref.shape[1]

    @pl.when(active_ref[0] != 0)
    def _():
        @pl.when(step == 0)
        def _():
            if first:
                acc[...] = jnp.zeros_like(acc)
            else:
                acc[...] = acc_in[...]

        def build(t):
            at = slice(t * TILE, (t + 1) * TILE)
            for k in range(LAGS):
                part = plain_ref if k <= HL else swapped_ref
                buffers[t % 2][k * cols:(k + 1) * cols, :] = part[:, at] * coeff_ref[k:k + 1, at]

        build(0)
        for t in range(STEP // TILE):
            if (t + 1) * TILE < STEP:
                build(t + 1)
            acc[...] += jnp.dot(
                buffers[t % 2][...], partner_ref[t * TILE:(t + 1) * TILE, :], preferred_element_type=jnp.float32
            )

        if kind != "part":
            @pl.when(step == pl.num_programs(0) - 1)
            def _():
                def write(out, mirrored):
                    for lag in range(LAGS):
                        value = lag_result(acc, cols, lag)
                        if mirrored:
                            out[LAGS - 1 - lag] = value.T
                        else:
                            out[lag] = value

                if kind == "plain":
                    write(refs[0], False)
                elif kind == "both":
                    write(refs[1], True)
                    write(refs[0], False)
                else:
                    pl.when(active_ref[1] == 0)(lambda: write(refs[0], False))
                    pl.when(active_ref[1] != 0)(lambda: write(refs[0], True))


def corr(active, turned, coeffs, start, partner, acc, kind, name):
    plain, swapped = turned
    cols = plain.shape[0]
    rows = partner.shape[0]
    first = acc is None
    skip = start // STEP
    acc_shape = jax.ShapeDtypeStruct((LAGS * cols, cols), jnp.float32)
    acc_spec = pl.BlockSpec((LAGS * cols, cols), lambda s, on: (0, 0))
    res_shape = jax.ShapeDtypeStruct((LAGS, cols, cols), jnp.bfloat16)
    res_spec = pl.BlockSpec((LAGS, cols, cols), lambda s, on: (0, 0, 0))
    in_specs = [
        pl.BlockSpec((cols, STEP), lambda s, on: (0, s * on[0])),
        pl.BlockSpec((cols, STEP), lambda s, on: (0, s * on[0])),
        pl.BlockSpec((LAGS, STEP), lambda s, on: (0, s * on[0] + skip)),
        pl.BlockSpec((STEP, cols), lambda s, on: (s * on[0], 0)),
    ]
    args = [plain, swapped, coeffs, partner]
    if not first:
        in_specs.append(acc_spec)
        args.append(acc)
    scratch = [pltpu.VMEM((LAGS * cols, TILE), jnp.bfloat16)] * 2
    if kind == "part":
        out_shape, out_specs = [acc_shape], [acc_spec]
    else:
        results = 2 if kind == "both" else 1
        out_shape, out_specs = [res_shape] * results, [res_spec] * results
        scratch = [pltpu.VMEM((LAGS * cols, cols), jnp.float32)] + scratch
    return pl.pallas_call(
        functools.partial(corr_kernel, first, kind),
        grid_spec=pltpu.PrefetchScalarGridSpec(
            num_scalar_prefetch=1,
            grid=(rows // STEP,),
            in_specs=in_specs,
            out_specs=out_specs,
            scratch_shapes=scratch,
        ),
        out_shape=out_shape,
        compiler_params=PARAMS,
        cost_estimate=pl.CostEstimate(
            flops=2 * LAGS * cols * cols * rows, bytes_accessed=6 * rows * cols, transcendentals=0
        ),
        name=name,
    )(active, *args)


def local(spectra, quality):
    count = lax.axis_size("chan")
    half = count // 2
    me = lax.axis_index("chan")
    freq_count, _, window_count, cols = spectra.shape
    block = spectra.reshape(-1, cols)

    down = [goes_down(p, half) for p in range(half)]
    far_pairs = [(p + half, p) if d else (p, p + half) for p, d in enumerate(down)]
    far_pairs += [(0, 1), (half - 1, half - 2)]
    near_pairs = [(d + 1, d) for d in range(1, count - 1) if d not in (half - 2, half - 1)]
    near_pairs += [(0, half - 1), (half - 1, 0)]
    back_pairs = [(p, p + half) if d else (p + half, p) for p, d in enumerate(down)]
    back_pairs += [(1, 0)]
    side_pairs = [(0, half - 1), (half - 1, count - 1)]

    def among(devices):
        return functools.reduce(jnp.logical_or, [me == d for d in devices])

    def switch(on, other=False):
        return jnp.stack([jnp.asarray(on), jnp.asarray(other)]).astype(jnp.int32)

    hosts = among([p if d else p + half for p, d in enumerate(down)])
    far_on = switch(hosts | (me == 1) | (me == half - 2))
    near_on = switch(~among([0, half - 2, half - 1, count - 1]))
    side_on = switch((me == 0) | (me == half - 1), me == half - 1)
    always = switch(True)

    pieces = mask(block, quality)
    starts = [0] + [piece.shape[0] for piece in pieces[:-1]]
    far_in, near_in = [], []
    for piece in pieces:
        far_in.append(lax.ppermute(piece, "chan", far_pairs))
        near_in.append(lax.ppermute(piece, "chan", near_pairs))

    coeffs = lag_rows(freq_count, window_count)
    own = [turn(piece, always, f"turn_own_{s}") for s, piece in enumerate(pieces)]
    side = [turn(near_in[0], side_on, "turn_side_0")]

    near_acc, = corr(near_on, own[0], coeffs, 0, near_in[0], None, "part", "near_first")
    side_acc, = corr(side_on, side[0], coeffs, 0, far_in[0], None, "part", "side_first")
    far_acc, = corr(far_on, own[0], coeffs, 0, far_in[0], None, "part", "far_first")

    near_acc, side_acc, far_acc, far_last_in, near_last_in = lax.optimization_barrier(
        (near_acc, side_acc, far_acc, far_in[1], near_in[1])
    )
    far_own, far_mirror = corr(far_on, own[1], coeffs, starts[1], far_last_in, far_acc, "both", "far_last")
    far_back = lax.ppermute(far_mirror, "chan", back_pairs)
    far_own, near_last_in = lax.optimization_barrier((far_own, near_last_in))
    side.append(turn(near_last_in, side_on, "turn_side_1"))
    side_own, = corr(side_on, side[1], coeffs, starts[1], far_last_in, side_acc, "flag", "side_last")
    side_back = lax.ppermute(side_own, "chan", side_pairs)
    side_own, near_acc = lax.optimization_barrier((side_own, near_acc))
    near_own, = corr(near_on, own[1], coeffs, starts[1], near_last_in, near_acc, "plain", "near_last")

    far = jnp.where(hosts, far_own, far_back)
    near = jnp.where((me == half - 1) | (me == count - 1), side_back, near_own)
    near = jnp.where(me == 0, far_back, jnp.where(me == half - 2, far_own, near))
    return near[None], far[None]


def solution(mesh):
    return jax.shard_map(
        local,
        mesh=mesh,
        in_specs=(P(None, None, None, ("grp", "chan")), P(("grp", "chan"), None)),
        out_specs=(P(("grp", "chan"), None, None, None), P(("grp", "chan"), None, None, None)),
        check_vma=False,
    )
```

```python
import functools
import math

import jax
import jax.numpy as jnp
from jax import lax
from jax.experimental import pallas as pl
from jax.experimental.pallas import tpu as pltpu
from jax.sharding import PartitionSpec as P

HL = 4
LAGS = 2 * HL + 1
STEP = 2048
TILE = 1024
PARAMS = pltpu.CompilerParams(vmem_limit_bytes=48 * 1024 * 1024)


def lag_rows(freq_count, window_count):
    per_bin = 2 * window_count
    row = jnp.arange(freq_count * per_bin, dtype=jnp.int32)
    freq_values = (row // per_bin).astype(jnp.float32)
    sign = jnp.where(row % per_bin < window_count, 1.0, -1.0)
    lag_values = jnp.arange(HL + 1, dtype=jnp.float32)
    phases = jnp.pi / freq_count * lag_values[:, None] * freq_values[None, :]
    factor = 1.0 / math.sqrt(window_count * freq_count)
    cos_part = jnp.cos(phases) * factor
    sin_part = -jnp.sin(phases[1:]) * factor * sign[None, :]
    return jnp.concatenate([cos_part, sin_part], axis=0).astype(jnp.bfloat16)


def mask_kernel(flags_ref, x_ref, masked_ref):
    rows, cols = x_ref.shape
    windows = flags_ref.shape[1]
    window = lax.broadcasted_iota(jnp.int32, (16, cols), 0) % windows
    weights = jnp.zeros((16, cols), jnp.float32)
    for w in range(windows):
        weights = jnp.where(window == w, flags_ref[0, w].astype(jnp.float32), weights)
    weights = jnp.broadcast_to(weights.astype(jnp.bfloat16)[None], (rows // 16, 16, cols))
    masked_ref[...] = x_ref[...] * weights.reshape(rows, cols)


def mask(x, flags):
    rows, cols = x.shape
    return pl.pallas_call(
        mask_kernel,
        grid=(rows // TILE,),
        in_specs=[pl.BlockSpec(memory_space=pltpu.SMEM), pl.BlockSpec((TILE, cols), lambda s: (s, 0))],
        out_specs=pl.BlockSpec((TILE, cols), lambda s: (s, 0)),
        out_shape=jax.ShapeDtypeStruct((rows, cols), jnp.bfloat16),
        compiler_params=PARAMS,
        cost_estimate=pl.CostEstimate(flops=rows * cols, bytes_accessed=4 * rows * cols, transcendentals=0),
        name="mask",
    )(flags, x)


def turn_kernel(active_ref, x_ref, plain_ref, swapped_ref):
    @pl.when(active_ref[0] != 0)
    def _():
        rows, cols = x_ref.shape
        same = lax.broadcasted_iota(jnp.int32, (cols, cols), 0) == lax.broadcasted_iota(jnp.int32, (cols, cols), 1)
        eye = jnp.where(same, 1.0, 0.0).astype(jnp.bfloat16)
        source = lax.broadcasted_iota(jnp.int32, (2 * cols, 2 * cols), 0)
        target = lax.broadcasted_iota(jnp.int32, (2 * cols, 2 * cols), 1)
        exchange = jnp.where((source ^ 4) == target, 1.0, 0.0).astype(jnp.bfloat16)
        plain = lax.dot_general(eye, x_ref[...], (((1,), (1,)), ((), ())), preferred_element_type=jnp.float32)
        plain = plain.astype(jnp.bfloat16)
        plain_ref[...] = plain
        for t in range(0, rows, 2 * cols):
            swapped = jnp.dot(plain[:, t:t + 2 * cols], exchange, preferred_element_type=jnp.float32)
            swapped_ref[:, t:t + 2 * cols] = swapped.astype(jnp.bfloat16)


def turn(x, active, name):
    rows, cols = x.shape
    out = jax.ShapeDtypeStruct((cols, rows), jnp.bfloat16)
    return pl.pallas_call(
        turn_kernel,
        grid_spec=pltpu.PrefetchScalarGridSpec(
            num_scalar_prefetch=1,
            grid=(rows // STEP,),
            in_specs=[pl.BlockSpec((STEP, cols), lambda s, on: (s * on[0], 0))],
            out_specs=[pl.BlockSpec((cols, STEP), lambda s, on: (0, s * on[0]))] * 2,
        ),
        out_shape=[out, out],
        compiler_params=PARAMS,
        cost_estimate=pl.CostEstimate(flops=0, bytes_accessed=6 * rows * cols, transcendentals=0),
        name=name,
    )(active, x)


def lag_result(acc, at, cols, lag):
    k = abs(lag - HL)
    even = acc[k * cols:(k + 1) * cols, at]
    if k == 0:
        return even.astype(jnp.bfloat16)
    odd = acc[(HL + k) * cols:(HL + k + 1) * cols, at]
    return (even + odd if lag > HL else even - odd).astype(jnp.bfloat16)


def corr_kernel(kinds, switch_ref, plain_ref, swapped_ref, coeff_ref, *rest):
    count = len(kinds)
    partner_refs = rest[:count]
    outs = list(rest[count:-3])
    acc, *buffers = rest[-3:]
    step = pl.program_id(0)
    cols = plain_ref.shape[0]

    @pl.when(switch_ref[0] != 0)
    def _():
        @pl.when(step == 0)
        def _():
            acc[...] = jnp.zeros_like(acc)

        def build(t):
            at = slice(t * TILE, (t + 1) * TILE)
            for k in range(LAGS):
                part = plain_ref if k <= HL else swapped_ref
                buffers[t % 2][k * cols:(k + 1) * cols, :] = part[:, at] * coeff_ref[k:k + 1, at]

        build(0)
        for t in range(STEP // TILE):
            if (t + 1) * TILE < STEP:
                build(t + 1)
            partner = [ref[t * TILE:(t + 1) * TILE, :] for ref in partner_refs]
            partner = partner[0] if count == 1 else jnp.concatenate(partner, axis=1)
            acc[...] += jnp.dot(buffers[t % 2][...], partner, preferred_element_type=jnp.float32)

        @pl.when(step == pl.num_programs(0) - 1)
        def _():
            def write(out, index, mirrored):
                for lag in range(LAGS):
                    value = lag_result(acc, slice(index * cols, (index + 1) * cols), cols, lag)
                    if mirrored:
                        out[LAGS - 1 - lag] = value.T
                    else:
                        out[lag] = value

            for index, kind in enumerate(kinds):
                out = outs.pop(0)
                if kind == "either":
                    pl.when(switch_ref[1] == 0)(functools.partial(write, out, index, False))
                    pl.when(switch_ref[1] != 0)(functools.partial(write, out, index, True))
                else:
                    write(out, index, False)
                if kind == "both":
                    write(outs.pop(0), index, True)


def corr(switch, turned, coeffs, partners, kinds, name):
    plain, swapped = turned
    cols, rows = plain.shape
    count = len(partners)
    res_shape = jax.ShapeDtypeStruct((LAGS, cols, cols), jnp.bfloat16)
    res_spec = pl.BlockSpec((LAGS, cols, cols), lambda s, on: (0, 0, 0))
    results = count + kinds.count("both")
    return pl.pallas_call(
        functools.partial(corr_kernel, kinds),
        grid_spec=pltpu.PrefetchScalarGridSpec(
            num_scalar_prefetch=1,
            grid=(rows // STEP,),
            in_specs=[
                pl.BlockSpec((cols, STEP), lambda s, on: (0, s * on[0])),
                pl.BlockSpec((cols, STEP), lambda s, on: (0, s * on[0])),
                pl.BlockSpec((LAGS, STEP), lambda s, on: (0, s * on[0])),
            ] + [pl.BlockSpec((STEP, cols), lambda s, on: (s * on[0], 0))] * count,
            out_specs=[res_spec] * results,
            scratch_shapes=[pltpu.VMEM((LAGS * cols, count * cols), jnp.float32)]
            + [pltpu.VMEM((LAGS * cols, TILE), jnp.bfloat16)] * 2,
        ),
        out_shape=[res_shape] * results,
        compiler_params=PARAMS,
        cost_estimate=pl.CostEstimate(
            flops=2 * count * LAGS * cols * cols * rows,
            bytes_accessed=2 * (2 + count) * rows * cols,
            transcendentals=0,
        ),
        name=name,
    )(switch, plain, swapped, coeffs, *partners)


def local(spectra, quality):
    count = lax.axis_size("chan")
    half = count // 2
    me = lax.axis_index("chan")
    freq_count, _, window_count, cols = spectra.shape
    block = spectra.reshape(-1, cols)

    first_far, second_far = [], []
    for p in range(half):
        if p in (0, half - 1):
            first_far.append((p + half, p))
        elif p % 2 == 0 and p >= half // 2:
            first_far.append((p, p + half))
        elif p in (1, 3):
            second_far.append((p, p + half))
        else:
            second_far.append((p + half, p))
    late_near = [(2, 1), (4, 3)]
    first_pairs = first_far + [(0, 1), (half - 1, half - 2)]
    second_pairs = second_far + late_near
    near_pairs = [(d + 1, d) for d in range(1, count - 1) if d not in (1, 3, half - 2, half - 1)]
    near_pairs += [(0, half - 1), (half - 1, 0)]
    first_back = [(t, s) for s, t in first_far] + [(1, 0)]
    second_back = [(t, s) for s, t in second_far]
    side_pairs = [(0, half - 1), (half - 1, count - 1)]

    def among(devices):
        return functools.reduce(jnp.logical_or, [me == d for d in devices])

    def switch(on, other=False):
        return jnp.stack([jnp.asarray(on), jnp.asarray(other)]).astype(jnp.int32)

    always = switch(True)
    second_on = switch(among([t for _, t in second_pairs]))
    side_on = switch(among([0, half - 1]), me == half - 1)

    masked = mask(block, quality)
    first_in = lax.ppermute(masked, "chan", first_pairs)
    near_in = lax.ppermute(masked, "chan", near_pairs)
    coeffs = lag_rows(freq_count, window_count)
    own = turn(masked, always, "turn_own")
    late, first_in, near_in, own, coeffs = lax.optimization_barrier((masked, first_in, near_in, own, coeffs))
    second_in = lax.ppermute(late, "chan", second_pairs)

    near, first, first_mirror = corr(always, own, coeffs, [near_in, first_in], ["plain", "both"], "near_first")
    first_returned = lax.ppermute(first_mirror, "chan", first_back)
    near, near_in = lax.optimization_barrier((near, near_in))
    side_turned = turn(near_in, side_on, "turn_side")
    side, = corr(side_on, side_turned, coeffs, [first_in], ["either"], "side")
    side_returned = lax.ppermute(side, "chan", side_pairs)

    side, second_in = lax.optimization_barrier((side, second_in))
    second, second_mirror = corr(second_on, own, coeffs, [second_in], ["both"], "second")
    second_returned = lax.ppermute(second_mirror, "chan", second_back)

    far = jnp.where(among([t for _, t in first_far]), first, second)
    far = jnp.where(among([s for s, _ in first_far]), first_returned, far)
    far = jnp.where(among([s for s, _ in second_far]), second_returned, far)
    near = jnp.where(among([t for _, t in late_near]), second, near)
    near = jnp.where(among([half - 1, count - 1]), side_returned, near)
    near = jnp.where(me == 0, first_returned, jnp.where(me == half - 2, first, near))
    return near[None], far[None]


def solution(mesh):
    return jax.shard_map(
        local,
        mesh=mesh,
        in_specs=(P(None, None, None, ("grp", "chan")), P(("grp", "chan"), None)),
        out_specs=(P(("grp", "chan"), None, None, None), P(("grp", "chan"), None, None, None)),
        check_vma=False,
    )
```

```python
import functools
import math

import jax
import jax.numpy as jnp
from jax import lax
from jax.experimental import pallas as pl
from jax.experimental.pallas import tpu as pltpu
from jax.sharding import PartitionSpec as P

HL = 4
LAGS = 2 * HL + 1
STEP = 1024
ENDS = (5, 8)
PARAMS = pltpu.CompilerParams(vmem_limit_bytes=63 * 1024 * 1024)


def lag_rows(freq_count, window_count):
    per_bin = 2 * window_count
    row = jnp.arange(freq_count * per_bin, dtype=jnp.int32)
    freq_values = (row // per_bin).astype(jnp.float32)
    sign = jnp.where(row % per_bin < window_count, 1.0, -1.0)
    lag_values = jnp.arange(HL + 1, dtype=jnp.float32)
    phases = jnp.pi / freq_count * lag_values[:, None] * freq_values[None, :]
    factor = 1.0 / math.sqrt(window_count * freq_count)
    cos_part = jnp.cos(phases) * factor
    sin_part = -jnp.sin(phases[1:]) * factor * sign[None, :]
    return jnp.concatenate([cos_part, sin_part], axis=0).astype(jnp.bfloat16)


def piece_specs(pieces, active):
    specs, begin = [], 0
    for piece in pieces:
        rows, cols = piece.shape
        count = rows // STEP

        def place(step, *switch, begin=begin, count=count):
            at = jnp.clip(step - begin, 0, count - 1)
            return (at * switch[0][0] if active else at, 0)

        specs.append(pl.BlockSpec((STEP, cols), place))
        begin += count
    return specs


def pick(refs, ends, step):
    value = refs[-1][...]
    for ref, end in reversed(list(zip(refs[:-1], ends))):
        value = jnp.where(step < end, ref[...], value)
    return value


def piece_ends(pieces):
    ends, end = [], 0
    for piece in pieces:
        end += piece.shape[0] // STEP
        ends.append(end)
    return ends


def mask_kernel(ends, flags_ref, x_ref, *piece_refs):
    rows, cols = x_ref.shape
    windows = flags_ref.shape[1]
    step = pl.program_id(0)
    window = lax.broadcasted_iota(jnp.int32, (16, cols), 0) % windows
    weights = jnp.zeros((16, cols), jnp.float32)
    for w in range(windows):
        weights = jnp.where(window == w, flags_ref[0, w].astype(jnp.float32), weights)
    weights = jnp.broadcast_to(weights.astype(jnp.bfloat16)[None], (rows // 16, 16, cols))
    masked = x_ref[...] * weights.reshape(rows, cols)
    begin = 0
    for end, piece_ref in zip(ends, piece_refs):
        @pl.when((step >= begin) & (step < end))
        def _():
            piece_ref[...] = masked
        begin = end


def mask(x, flags):
    rows, cols = x.shape
    ends = [rows * e // 8 for e in ENDS]
    shapes = [jax.ShapeDtypeStruct((e - b, cols), jnp.bfloat16) for b, e in zip([0] + ends, ends)]
    return pl.pallas_call(
        functools.partial(mask_kernel, piece_ends(shapes)),
        grid=(rows // STEP,),
        in_specs=[pl.BlockSpec(memory_space=pltpu.SMEM), pl.BlockSpec((STEP, cols), lambda s: (s, 0))],
        out_specs=piece_specs(shapes, False),
        out_shape=shapes,
        compiler_params=PARAMS,
        cost_estimate=pl.CostEstimate(flops=rows * cols, bytes_accessed=4 * rows * cols, transcendentals=0),
        name="mask",
    )(flags, x)


def turn_kernel(ends, switch_ref, *refs):
    plain_ref, swapped_ref = refs[-2:]

    @pl.when(switch_ref[0] != 0)
    def _():
        x = pick(refs[:-2], ends, pl.program_id(0))
        rows, cols = x.shape
        same = lax.broadcasted_iota(jnp.int32, (cols, cols), 0) == lax.broadcasted_iota(jnp.int32, (cols, cols), 1)
        eye = jnp.where(same, 1.0, 0.0).astype(jnp.bfloat16)
        source = lax.broadcasted_iota(jnp.int32, (2 * cols, 2 * cols), 0)
        target = lax.broadcasted_iota(jnp.int32, (2 * cols, 2 * cols), 1)
        exchange = jnp.where((source ^ 4) == target, 1.0, 0.0).astype(jnp.bfloat16)
        plain = lax.dot_general(eye, x, (((1,), (1,)), ((), ())), preferred_element_type=jnp.float32)
        plain = plain.astype(jnp.bfloat16)
        plain_ref[...] = plain
        for t in range(0, rows, 2 * cols):
            swapped = jnp.dot(plain[:, t:t + 2 * cols], exchange, preferred_element_type=jnp.float32)
            swapped_ref[:, t:t + 2 * cols] = swapped.astype(jnp.bfloat16)


def turn(pieces, switch, name, common=True):
    cols = pieces[0].shape[1]
    rows = sum(piece.shape[0] for piece in pieces)
    out = jax.ShapeDtypeStruct((cols, rows), jnp.bfloat16)
    return pl.pallas_call(
        functools.partial(turn_kernel, piece_ends(pieces)),
        grid_spec=pltpu.PrefetchScalarGridSpec(
            num_scalar_prefetch=1,
            grid=(rows // STEP,),
            in_specs=piece_specs(pieces, True),
            out_specs=[pl.BlockSpec((cols, STEP), lambda s, on: (0, s * on[0]))] * 2,
        ),
        out_shape=[out, out],
        compiler_params=PARAMS,
        cost_estimate=pl.CostEstimate(flops=0, bytes_accessed=6 * rows * cols if common else 0, transcendentals=0),
        name=name,
    )(switch, *pieces)


def lag_result(acc, at, cols, lag):
    k = abs(lag - HL)
    even = acc[k * cols:(k + 1) * cols, at]
    if k == 0:
        return even.astype(jnp.bfloat16)
    odd = acc[(HL + k) * cols:(HL + k + 1) * cols, at]
    return (even + odd if lag > HL else even - odd).astype(jnp.bfloat16)


def corr_kernel(ends, first, kinds, switch_ref, plain_ref, swapped_ref, coeff_ref, *rest):
    rest = list(rest)
    partner_refs = [[rest.pop(0) for _ in group] for group in ends]
    acc_in = None if first else rest.pop(0)
    scaled = rest.pop()
    acc = rest.pop()
    step = pl.program_id(0)
    cols = plain_ref.shape[0]

    @pl.when(switch_ref[0] != 0)
    def _():
        @pl.when(step == 0)
        def _():
            acc[...] = jnp.zeros_like(acc) if first else acc_in[...]

        for k in range(LAGS):
            part = plain_ref if k <= HL else swapped_ref
            scaled[k * cols:(k + 1) * cols, :] = part[...] * coeff_ref[k:k + 1, :]
        partner = [pick(refs, group, step) for refs, group in zip(partner_refs, ends)]
        partner = partner[0] if len(partner) == 1 else jnp.concatenate(partner, axis=1)
        acc[...] += jnp.dot(scaled[...], partner, preferred_element_type=jnp.float32)

        @pl.when(step == pl.num_programs(0) - 1)
        def _():
            def write(out, index, mirrored):
                for lag in range(LAGS):
                    value = lag_result(acc, slice(index * cols, (index + 1) * cols), cols, lag)
                    if mirrored:
                        out[LAGS - 1 - lag] = value.T
                    else:
                        out[lag] = value

            for index, kind in enumerate(kinds):
                out = rest.pop(0)
                if kind == "either":
                    pl.when(switch_ref[1] == 0)(functools.partial(write, out, index, False))
                    pl.when(switch_ref[1] != 0)(functools.partial(write, out, index, True))
                else:
                    write(out, index, False)
                if kind == "both":
                    write(rest.pop(0), index, True)


def corr(switch, turned, coeffs, partners, kinds, name, start=0, acc=None, common=True):
    plain, swapped = turned
    cols = plain.shape[0]
    rows = sum(piece.shape[0] for piece in partners[0])
    skip = start // STEP
    count = len(partners)
    total_shape = jax.ShapeDtypeStruct((LAGS * cols, count * cols), jnp.float32)
    total_spec = pl.BlockSpec(total_shape.shape, lambda s, on: (0, 0))
    in_specs = [
        pl.BlockSpec((cols, STEP), lambda s, on: (0, s * on[0] + skip)),
        pl.BlockSpec((cols, STEP), lambda s, on: (0, s * on[0] + skip)),
        pl.BlockSpec((LAGS, STEP), lambda s, on: (0, s * on[0] + skip)),
    ]
    args = [plain, swapped, coeffs]
    for pieces in partners:
        in_specs += piece_specs(pieces, True)
        args += pieces
    if acc is not None:
        in_specs.append(total_spec)
        args.append(acc)
    scratch = [pltpu.VMEM((LAGS * cols, STEP), jnp.bfloat16)]
    if kinds:
        results = count + kinds.count("both")
        out_shape = [jax.ShapeDtypeStruct((LAGS, cols, cols), jnp.bfloat16)] * results
        out_specs = [pl.BlockSpec((LAGS, cols, cols), lambda s, on: (0, 0, 0))] * results
        scratch = [pltpu.VMEM(total_shape.shape, jnp.float32)] + scratch
    else:
        out_shape, out_specs = [total_shape], [total_spec]
    return pl.pallas_call(
        functools.partial(corr_kernel, [piece_ends(pieces) for pieces in partners], acc is None, kinds or ()),
        grid_spec=pltpu.PrefetchScalarGridSpec(
            num_scalar_prefetch=1,
            grid=(rows // STEP,),
            in_specs=in_specs,
            out_specs=out_specs,
            scratch_shapes=scratch,
        ),
        out_shape=out_shape,
        compiler_params=PARAMS,
        cost_estimate=pl.CostEstimate(
            flops=2 * count * LAGS * cols * cols * rows if common else 0,
            bytes_accessed=2 * (2 + count) * rows * cols if common else 0,
            transcendentals=0,
        ),
        name=name,
    )(switch, *args)


def local(spectra, quality):
    count = lax.axis_size("chan")
    half = count // 2
    me = lax.axis_index("chan")
    freq_count, _, window_count, cols = spectra.shape
    block = spectra.reshape(-1, cols)

    first_far, second_far = [], []
    for p in range(half):
        if p in (0, half - 1):
            first_far.append((p + half, p))
        elif p % 2 == 0 and p >= half // 2:
            first_far.append((p, p + half))
        elif p in (1, 3):
            second_far.append((p, p + half))
        else:
            second_far.append((p + half, p))
    late_near = [(2, 1), (4, 3)]
    first_pairs = first_far + [(0, 1), (half - 1, half - 2)]
    second_pairs = second_far + late_near
    near_pairs = [(d + 1, d) for d in range(1, count - 1) if d not in (1, 3, half - 2, half - 1)]
    near_pairs += [(0, half - 1), (half - 1, 0)]
    first_back = [(t, s) for s, t in first_far] + [(1, 0)]
    second_back = [(t, s) for s, t in second_far]
    side_pairs = [(0, half - 1), (half - 1, count - 1)]

    def among(devices):
        return functools.reduce(jnp.logical_or, [me == d for d in devices])

    def switch(on, other=False):
        return jnp.stack([jnp.asarray(on), jnp.asarray(other)]).astype(jnp.int32)

    always = switch(True)
    second_on = switch(among([t for _, t in second_pairs]))
    side_on = switch(among([0, half - 1]), me == half - 1)

    large, small = mask(block, quality)
    first_large = lax.ppermute(large, "chan", first_pairs)
    near_small = lax.ppermute(small, "chan", near_pairs)
    near_large = lax.ppermute(large, "chan", near_pairs)
    first_small = lax.ppermute(small, "chan", first_pairs)
    coeffs = lag_rows(freq_count, window_count)
    own = turn([large, small], always, "turn_own")

    late_large, own, near_small = lax.optimization_barrier((large, own, near_small))
    second_large = lax.ppermute(late_large, "chan", second_pairs)
    first_in, near_in = [first_large, first_small], [near_large, near_small]
    near, first, first_mirror = corr(always, own, coeffs, [near_in, first_in], ["plain", "both"], "near_first")
    late_small, near = lax.optimization_barrier((small, near))
    second_small = lax.ppermute(late_small, "chan", second_pairs)
    first_returned = lax.ppermute(first_mirror, "chan", first_back)

    side_switch, near = lax.optimization_barrier((side_on, near))
    side_turned = turn(near_in, side_switch, "turn_side", common=False)
    side, = corr(side_switch, side_turned, coeffs, [first_in], ["either"], "side", common=False)
    side_returned = lax.ppermute(side, "chan", side_pairs)

    second_switch, side = lax.optimization_barrier((second_on, side))
    total, = corr(second_switch, own, coeffs, [[second_large]], None, "second_large")
    second, second_mirror = corr(
        second_switch, own, coeffs, [[second_small]], ["both"], "second_small", large.shape[0], total
    )
    second_returned = lax.ppermute(second_mirror, "chan", second_back)

    far = jnp.where(among([t for _, t in first_far]), first, second)
    far = jnp.where(among([s for s, _ in first_far]), first_returned, far)
    far = jnp.where(among([s for s, _ in second_far]), second_returned, far)
    near = jnp.where(among([t for _, t in late_near]), second, near)
    near = jnp.where(among([half - 1, count - 1]), side_returned, near)
    near = jnp.where(me == 0, first_returned, jnp.where(me == half - 2, first, near))
    return near[None], far[None]


def solution(mesh):
    return jax.shard_map(
        local,
        mesh=mesh,
        in_specs=(P(None, None, None, ("grp", "chan")), P(("grp", "chan"), None)),
        out_specs=(P(("grp", "chan"), None, None, None), P(("grp", "chan"), None, None, None)),
        check_vma=False,
    )
```

```python
import functools
import math

import jax
import jax.numpy as jnp
from jax import lax
from jax.experimental import pallas as pl
from jax.experimental.pallas import tpu as pltpu
from jax.sharding import PartitionSpec as P

HL = 4
LAGS = 2 * HL + 1
STEP = 1024
ENDS = (6, 8)
PARAMS = pltpu.CompilerParams(vmem_limit_bytes=16 * 1024 * 1024)


def lag_rows(freq_count, window_count):
    per_bin = 2 * window_count
    row = jnp.arange(freq_count * per_bin, dtype=jnp.int32)
    freq_values = (row // per_bin).astype(jnp.float32)
    sign = jnp.where(row % per_bin < window_count, 1.0, -1.0)
    lag_values = jnp.arange(HL + 1, dtype=jnp.float32)
    phases = jnp.pi / freq_count * lag_values[:, None] * freq_values[None, :]
    factor = 1.0 / math.sqrt(window_count * freq_count)
    cos_part = jnp.cos(phases) * factor
    sin_part = -jnp.sin(phases[1:]) * factor * sign[None, :]
    return jnp.concatenate([cos_part, sin_part], axis=0).astype(jnp.bfloat16)


def piece_specs(pieces, active):
    specs, begin = [], 0
    for piece in pieces:
        rows, cols = piece.shape
        count = rows // STEP

        def place(step, *switch, begin=begin, count=count):
            at = jnp.clip(step - begin, 0, count - 1)
            return (at * switch[0][0] if active else at, 0)

        specs.append(pl.BlockSpec((STEP, cols), place))
        begin += count
    return specs


def pick(refs, ends, step):
    value = refs[-1][...]
    for ref, end in reversed(list(zip(refs[:-1], ends))):
        value = jnp.where(step < end, ref[...], value)
    return value


def piece_ends(pieces):
    ends, end = [], 0
    for piece in pieces:
        end += piece.shape[0] // STEP
        ends.append(end)
    return ends


def mask_kernel(ends, flags_ref, x_ref, whole_ref, *piece_refs):
    rows, cols = x_ref.shape
    windows = flags_ref.shape[1]
    step = pl.program_id(0)
    window = lax.broadcasted_iota(jnp.int32, (16, cols), 0) % windows
    weights = jnp.zeros((16, cols), jnp.float32)
    for w in range(windows):
        weights = jnp.where(window == w, flags_ref[0, w].astype(jnp.float32), weights)
    weights = jnp.broadcast_to(weights.astype(jnp.bfloat16)[None], (rows // 16, 16, cols))
    masked = x_ref[...] * weights.reshape(rows, cols)
    whole_ref[...] = masked
    begin = 0
    for end, piece_ref in zip(ends, piece_refs):
        @pl.when((step >= begin) & (step < end))
        def _():
            piece_ref[...] = masked
        begin = end


def mask(x, flags):
    rows, cols = x.shape
    block_spec = pl.BlockSpec((STEP, cols), lambda s: (s, 0))
    ends = [rows * e // 8 for e in ENDS]
    shapes = [jax.ShapeDtypeStruct((e - b, cols), jnp.bfloat16) for b, e in zip([0] + ends, ends)]
    return pl.pallas_call(
        functools.partial(mask_kernel, piece_ends(shapes)),
        grid=(rows // STEP,),
        in_specs=[pl.BlockSpec(memory_space=pltpu.SMEM), block_spec],
        out_specs=[block_spec] + piece_specs(shapes, False),
        out_shape=[jax.ShapeDtypeStruct((rows, cols), jnp.bfloat16)] + shapes,
        compiler_params=PARAMS,
        cost_estimate=pl.CostEstimate(flops=rows * cols, bytes_accessed=4 * rows * cols, transcendentals=0),
        name="mask",
    )(flags, x)


def turn_kernel(ends, switch_ref, *refs):
    plain_ref, swapped_ref = refs[-2:]

    @pl.when(switch_ref[0] != 0)
    def _():
        x = pick(refs[:-2], ends, pl.program_id(0))
        rows, cols = x.shape
        same = lax.broadcasted_iota(jnp.int32, (cols, cols), 0) == lax.broadcasted_iota(jnp.int32, (cols, cols), 1)
        eye = jnp.where(same, 1.0, 0.0).astype(jnp.bfloat16)
        source = lax.broadcasted_iota(jnp.int32, (2 * cols, 2 * cols), 0)
        target = lax.broadcasted_iota(jnp.int32, (2 * cols, 2 * cols), 1)
        exchange = jnp.where((source ^ 4) == target, 1.0, 0.0).astype(jnp.bfloat16)
        plain = lax.dot_general(eye, x, (((1,), (1,)), ((), ())), preferred_element_type=jnp.float32)
        plain = plain.astype(jnp.bfloat16)
        plain_ref[...] = plain
        for t in range(0, rows, 2 * cols):
            swapped = jnp.dot(plain[:, t:t + 2 * cols], exchange, preferred_element_type=jnp.float32)
            swapped_ref[:, t:t + 2 * cols] = swapped.astype(jnp.bfloat16)


def turn(pieces, switch, name, common=True):
    cols = pieces[0].shape[1]
    rows = sum(piece.shape[0] for piece in pieces)
    out = jax.ShapeDtypeStruct((cols, rows), jnp.bfloat16)
    return pl.pallas_call(
        functools.partial(turn_kernel, piece_ends(pieces)),
        grid_spec=pltpu.PrefetchScalarGridSpec(
            num_scalar_prefetch=1,
            grid=(rows // STEP,),
            in_specs=piece_specs(pieces, True),
            out_specs=[pl.BlockSpec((cols, STEP), lambda s, on: (0, s * on[0]))] * 2,
        ),
        out_shape=[out, out],
        compiler_params=PARAMS,
        cost_estimate=pl.CostEstimate(flops=0, bytes_accessed=6 * rows * cols if common else 0, transcendentals=0),
        name=name,
    )(switch, *pieces)


def lag_result(acc, at, cols, lag):
    k = abs(lag - HL)
    even = acc[k * cols:(k + 1) * cols, at]
    if k == 0:
        return even.astype(jnp.bfloat16)
    odd = acc[(HL + k) * cols:(HL + k + 1) * cols, at]
    return (even + odd if lag > HL else even - odd).astype(jnp.bfloat16)


def corr_kernel(ends, first, kinds, switch_ref, plain_ref, swapped_ref, coeff_ref, *rest):
    rest = list(rest)
    partner_refs = [[rest.pop(0) for _ in group] for group in ends]
    acc_in = None if first else rest.pop(0)
    scaled = rest.pop()
    acc = rest.pop()
    step = pl.program_id(0)
    cols = plain_ref.shape[0]

    @pl.when(switch_ref[0] != 0)
    def _():
        @pl.when(step == 0)
        def _():
            acc[...] = jnp.zeros_like(acc) if first else acc_in[...]

        for k in range(LAGS):
            part = plain_ref if k <= HL else swapped_ref
            scaled[k * cols:(k + 1) * cols, :] = part[...] * coeff_ref[k:k + 1, :]
        partner = [pick(refs, group, step) for refs, group in zip(partner_refs, ends)]
        partner = partner[0] if len(partner) == 1 else jnp.concatenate(partner, axis=1)
        acc[...] += jnp.dot(scaled[...], partner, preferred_element_type=jnp.float32)

        @pl.when(step == pl.num_programs(0) - 1)
        def _():
            def write(out, index, mirrored):
                for lag in range(LAGS):
                    value = lag_result(acc, slice(index * cols, (index + 1) * cols), cols, lag)
                    if mirrored:
                        out[LAGS - 1 - lag] = value.T
                    else:
                        out[lag] = value

            for index, kind in enumerate(kinds):
                out = rest.pop(0)
                if kind == "either":
                    pl.when(switch_ref[1] == 0)(functools.partial(write, out, index, False))
                    pl.when(switch_ref[1] != 0)(functools.partial(write, out, index, True))
                else:
                    write(out, index, False)
                if kind == "both":
                    write(rest.pop(0), index, True)


def corr(switch, turned, coeffs, partners, kinds, name, start=0, acc=None, common=True):
    plain, swapped = turned
    cols = plain.shape[0]
    rows = sum(piece.shape[0] for piece in partners[0])
    skip = start // STEP
    count = len(partners)
    total_shape = jax.ShapeDtypeStruct((LAGS * cols, count * cols), jnp.float32)
    total_spec = pl.BlockSpec(total_shape.shape, lambda s, on: (0, 0))
    in_specs = [
        pl.BlockSpec((cols, STEP), lambda s, on: (0, s * on[0] + skip)),
        pl.BlockSpec((cols, STEP), lambda s, on: (0, s * on[0] + skip)),
        pl.BlockSpec((LAGS, STEP), lambda s, on: (0, s * on[0] + skip)),
    ]
    args = [plain, swapped, coeffs]
    for pieces in partners:
        in_specs += piece_specs(pieces, True)
        args += pieces
    if acc is not None:
        in_specs.append(total_spec)
        args.append(acc)
    scratch = [pltpu.VMEM((LAGS * cols, STEP), jnp.bfloat16)]
    if kinds:
        results = count + kinds.count("both")
        out_shape = [jax.ShapeDtypeStruct((LAGS, cols, cols), jnp.bfloat16)] * results
        out_specs = [pl.BlockSpec((LAGS, cols, cols), lambda s, on: (0, 0, 0))] * results
        scratch = [pltpu.VMEM(total_shape.shape, jnp.float32)] + scratch
    else:
        out_shape, out_specs = [total_shape], [total_spec]
    return pl.pallas_call(
        functools.partial(corr_kernel, [piece_ends(pieces) for pieces in partners], acc is None, kinds or ()),
        grid_spec=pltpu.PrefetchScalarGridSpec(
            num_scalar_prefetch=1,
            grid=(rows // STEP,),
            in_specs=in_specs,
            out_specs=out_specs,
            scratch_shapes=scratch,
        ),
        out_shape=out_shape,
        compiler_params=PARAMS,
        cost_estimate=pl.CostEstimate(
            flops=2 * count * LAGS * cols * cols * rows if common else 0,
            bytes_accessed=2 * (2 + count) * rows * cols if common else 0,
            transcendentals=0,
        ),
        name=name,
    )(switch, *args)


def local(spectra, quality):
    count = lax.axis_size("chan")
    half = count // 2
    me = lax.axis_index("chan")
    freq_count, _, window_count, cols = spectra.shape
    block = spectra.reshape(-1, cols)

    first_far, second_far = [], []
    for p in range(half):
        if p in (0, half - 1):
            first_far.append((p + half, p))
        elif p % 2 == 0 and p >= half // 2:
            first_far.append((p, p + half))
        elif p in (1, 3):
            second_far.append((p, p + half))
        else:
            second_far.append((p + half, p))
    late_near = [(2, 1), (4, 3)]
    first_pairs = first_far + [(0, 1), (half - 1, half - 2)]
    second_pairs = second_far + late_near
    near_pairs = [(d + 1, d) for d in range(1, count - 1) if d not in (1, 3, half - 2, half - 1)]
    near_pairs += [(0, half - 1), (half - 1, 0)]
    first_back = [(t, s) for s, t in first_far] + [(1, 0)]
    second_back = [(t, s) for s, t in second_far]
    side_pairs = [(0, half - 1), (half - 1, count - 1)]

    def among(devices):
        return functools.reduce(jnp.logical_or, [me == d for d in devices])

    def switch(on, other=False):
        return jnp.stack([jnp.asarray(on), jnp.asarray(other)]).astype(jnp.int32)

    always = switch(True)
    second_on = switch(among([t for _, t in second_pairs]))
    side_on = switch(among([0, half - 1]), me == half - 1)

    whole, large, small = mask(block, quality)
    first_in = lax.ppermute(whole, "chan", first_pairs)
    near_large = lax.ppermute(large, "chan", near_pairs)
    near_small = lax.ppermute(small, "chan", near_pairs)
    coeffs = lag_rows(freq_count, window_count)
    own = turn([whole], always, "turn_own")

    late_large, own, near_small = lax.optimization_barrier((large, own, near_small))
    second_large = lax.ppermute(late_large, "chan", second_pairs)
    near_in = [near_large, near_small]
    near, first, first_mirror = corr(always, own, coeffs, [near_in, [first_in]], ["plain", "both"], "near_first")
    late_small, near = lax.optimization_barrier((small, near))
    second_small = lax.ppermute(late_small, "chan", second_pairs)
    first_returned = lax.ppermute(first_mirror, "chan", first_back)

    side_switch, near = lax.optimization_barrier((side_on, near))
    side_turned = turn(near_in, side_switch, "turn_side", common=False)
    side, = corr(side_switch, side_turned, coeffs, [[first_in]], ["either"], "side", common=False)
    side_returned = lax.ppermute(side, "chan", side_pairs)

    second_switch, side, first_returned = lax.optimization_barrier((second_on, side, first_returned))
    total, = corr(second_switch, own, coeffs, [[second_large]], None, "second_large")
    second, second_mirror = corr(
        second_switch, own, coeffs, [[second_small]], ["both"], "second_small", large.shape[0], total
    )
    second_returned = lax.ppermute(second_mirror, "chan", second_back)

    far = jnp.where(among([t for _, t in first_far]), first, second)
    far = jnp.where(among([s for s, _ in first_far]), first_returned, far)
    far = jnp.where(among([s for s, _ in second_far]), second_returned, far)
    near = jnp.where(among([t for _, t in late_near]), second, near)
    near = jnp.where(among([half - 1, count - 1]), side_returned, near)
    near = jnp.where(me == 0, first_returned, jnp.where(me == half - 2, first, near))
    return near[None], far[None]


def solution(mesh):
    return jax.shard_map(
        local,
        mesh=mesh,
        in_specs=(P(None, None, None, ("grp", "chan")), P(("grp", "chan"), None)),
        out_specs=(P(("grp", "chan"), None, None, None), P(("grp", "chan"), None, None, None)),
        check_vma=False,
    )
```

```python
import functools
import math

import jax
import jax.numpy as jnp
from jax import lax
from jax.experimental import pallas as pl
from jax.experimental.pallas import tpu as pltpu
from jax.sharding import PartitionSpec as P

HL = 4
LAGS = 2 * HL + 1
STEP = 1024
PARAMS = pltpu.CompilerParams(vmem_limit_bytes=16 * 1024 * 1024)


def lag_rows(freq_count, window_count):
    per_bin = 2 * window_count
    row = jnp.arange(freq_count * per_bin, dtype=jnp.int32)
    freq_values = (row // per_bin).astype(jnp.float32)
    sign = jnp.where(row % per_bin < window_count, 1.0, -1.0)
    lag_values = jnp.arange(HL + 1, dtype=jnp.float32)
    phases = jnp.pi / freq_count * lag_values[:, None] * freq_values[None, :]
    factor = 1.0 / math.sqrt(window_count * freq_count)
    cos_part = jnp.cos(phases) * factor
    sin_part = -jnp.sin(phases[1:]) * factor * sign[None, :]
    return jnp.concatenate([cos_part, sin_part], axis=0).astype(jnp.bfloat16)


def split_kernel(x_ref, *half_refs):
    middle = pl.num_programs(0) // 2
    step = pl.program_id(0)

    @pl.when(step < middle)
    def _():
        half_refs[0][...] = x_ref[...]

    @pl.when(step >= middle)
    def _():
        half_refs[1][...] = x_ref[...]


def split(x):
    rows, cols = x.shape
    steps = rows // STEP
    half = jax.ShapeDtypeStruct((rows // 2, cols), x.dtype)
    return pl.pallas_call(
        split_kernel,
        grid=(steps,),
        in_specs=[pl.BlockSpec((STEP, cols), lambda s: (s, 0))],
        out_specs=[
            pl.BlockSpec((STEP, cols), lambda s: (jnp.minimum(s, steps // 2 - 1), 0)),
            pl.BlockSpec((STEP, cols), lambda s: (jnp.maximum(s - steps // 2, 0), 0)),
        ],
        out_shape=[half, half],
        compiler_params=PARAMS,
        cost_estimate=pl.CostEstimate(flops=0, bytes_accessed=4 * rows * cols, transcendentals=0),
        name="split",
    )(x)


def turn_kernel(active_ref, x_ref, plain_ref, swapped_ref):
    @pl.when(active_ref[0] != 0)
    def _():
        rows, cols = x_ref.shape
        same = lax.broadcasted_iota(jnp.int32, (cols, cols), 0) == lax.broadcasted_iota(jnp.int32, (cols, cols), 1)
        eye = jnp.where(same, 1.0, 0.0).astype(jnp.bfloat16)
        source = lax.broadcasted_iota(jnp.int32, (2 * cols, 2 * cols), 0)
        target = lax.broadcasted_iota(jnp.int32, (2 * cols, 2 * cols), 1)
        exchange = jnp.where((source ^ 4) == target, 1.0, 0.0).astype(jnp.bfloat16)
        plain = lax.dot_general(eye, x_ref[...], (((1,), (1,)), ((), ())), preferred_element_type=jnp.float32)
        plain = plain.astype(jnp.bfloat16)
        plain_ref[...] = plain
        for t in range(0, rows, 2 * cols):
            swapped = jnp.dot(plain[:, t:t + 2 * cols], exchange, preferred_element_type=jnp.float32)
            swapped_ref[:, t:t + 2 * cols] = swapped.astype(jnp.bfloat16)


def turn(x, switch, name, common=True):
    rows, cols = x.shape
    out = jax.ShapeDtypeStruct((cols, rows), jnp.bfloat16)
    return pl.pallas_call(
        turn_kernel,
        grid_spec=pltpu.PrefetchScalarGridSpec(
            num_scalar_prefetch=1,
            grid=(rows // STEP,),
            in_specs=[pl.BlockSpec((STEP, cols), lambda s, on: (s * on[0], 0))],
            out_specs=[pl.BlockSpec((cols, STEP), lambda s, on: (0, s * on[0]))] * 2,
        ),
        out_shape=[out, out],
        compiler_params=PARAMS,
        cost_estimate=pl.CostEstimate(flops=0, bytes_accessed=6 * rows * cols if common else 0, transcendentals=0),
        name=name,
    )(switch, x)


def lag_result(acc, at, cols, lag):
    k = abs(lag - HL)
    even = acc[k * cols:(k + 1) * cols, at]
    if k == 0:
        return even.astype(jnp.bfloat16)
    odd = acc[(HL + k) * cols:(HL + k + 1) * cols, at]
    return (even + odd if lag > HL else even - odd).astype(jnp.bfloat16)


def corr_kernel(windows, count, first, kinds, switch_ref, plain_ref, swapped_ref, coeff_ref, *rest):
    rest = list(rest)
    partner_refs = [rest.pop(0) for _ in range(count)]
    acc_in = None if first else rest.pop(0)
    scaled = rest.pop()
    acc = rest.pop()
    step = pl.program_id(0)
    cols, rows = plain_ref.shape

    @pl.when(switch_ref[0] != 0)
    def _():
        @pl.when(step == 0)
        def _():
            acc[...] = jnp.zeros_like(acc) if first else acc_in[...]

        for k in range(LAGS):
            part = plain_ref if k <= HL else swapped_ref
            scaled[k * cols:(k + 1) * cols, :] = part[...] * coeff_ref[k:k + 1, :]

        window = lax.broadcasted_iota(jnp.int32, (16, cols), 0) % windows
        partner = []
        for index, ref in enumerate(partner_refs):
            weights = jnp.zeros((16, cols), jnp.float32)
            for w in range(windows):
                weight = switch_ref[2 + index * windows + w].astype(jnp.float32)
                weights = jnp.where(window == w, weight, weights)
            weights = jnp.broadcast_to(weights.astype(jnp.bfloat16)[None], (rows // 16, 16, cols))
            partner.append(ref[...] * weights.reshape(rows, cols))
        partner = partner[0] if count == 1 else jnp.concatenate(partner, axis=1)
        acc[...] += jnp.dot(scaled[...], partner, preferred_element_type=jnp.float32)

        @pl.when(step == pl.num_programs(0) - 1)
        def _():
            def write(out, index, mirrored):
                for lag in range(LAGS):
                    value = lag_result(acc, slice(index * cols, (index + 1) * cols), cols, lag)
                    if mirrored:
                        out[LAGS - 1 - lag] = value.T
                    else:
                        out[lag] = value

            for index, kind in enumerate(kinds):
                out = rest.pop(0)
                if kind == "either":
                    pl.when(switch_ref[1] == 0)(functools.partial(write, out, index, False))
                    pl.when(switch_ref[1] != 0)(functools.partial(write, out, index, True))
                else:
                    write(out, index, False)
                if kind == "both":
                    write(rest.pop(0), index, True)


def corr(switch, turned, coeffs, partners, kinds, name, start=0, acc=None, common=True):
    plain, swapped = turned
    cols = plain.shape[0]
    rows = partners[0].shape[0]
    skip = start // STEP
    count = len(partners)
    windows = (switch.shape[0] - 2) // count
    total_shape = jax.ShapeDtypeStruct((LAGS * cols, count * cols), jnp.float32)
    total_spec = pl.BlockSpec(total_shape.shape, lambda s, on: (0, 0))
    in_specs = [
        pl.BlockSpec((cols, STEP), lambda s, on: (0, s * on[0] + skip)),
        pl.BlockSpec((cols, STEP), lambda s, on: (0, s * on[0] + skip)),
        pl.BlockSpec((LAGS, STEP), lambda s, on: (0, s * on[0] + skip)),
    ] + [pl.BlockSpec((STEP, cols), lambda s, on: (s * on[0], 0))] * count
    args = [plain, swapped, coeffs, *partners]
    if acc is not None:
        in_specs.append(total_spec)
        args.append(acc)
    scratch = [pltpu.VMEM((LAGS * cols, STEP), jnp.bfloat16)]
    if kinds:
        results = count + kinds.count("both")
        out_shape = [jax.ShapeDtypeStruct((LAGS, cols, cols), jnp.bfloat16)] * results
        out_specs = [pl.BlockSpec((LAGS, cols, cols), lambda s, on: (0, 0, 0))] * results
        scratch = [pltpu.VMEM(total_shape.shape, jnp.float32)] + scratch
    else:
        out_shape, out_specs = [total_shape], [total_spec]
    return pl.pallas_call(
        functools.partial(corr_kernel, windows, count, acc is None, kinds),
        grid_spec=pltpu.PrefetchScalarGridSpec(
            num_scalar_prefetch=1,
            grid=(rows // STEP,),
            in_specs=in_specs,
            out_specs=out_specs,
            scratch_shapes=scratch,
        ),
        out_shape=out_shape,
        compiler_params=PARAMS,
        cost_estimate=pl.CostEstimate(
            flops=2 * count * LAGS * cols * cols * rows if common else 0,
            bytes_accessed=2 * (2 + count) * rows * cols if common else 0,
            transcendentals=0,
        ),
        name=name,
    )(switch, *args)


def local(spectra, quality):
    count = lax.axis_size("chan")
    half = count // 2
    me = lax.axis_index("chan")
    freq_count, _, window_count, cols = spectra.shape
    block = spectra.reshape(-1, cols)

    first_far, second_far = [], []
    for p in range(half):
        if p in (0, half - 1):
            first_far.append((p + half, p))
        elif p % 2 == 0 and p >= half // 2:
            first_far.append((p, p + half))
        elif p in (1, 3):
            second_far.append((p, p + half))
        else:
            second_far.append((p + half, p))
    late_near = [(2, 1), (4, 3)]
    first_pairs = first_far + [(0, 1), (half - 1, half - 2)]
    second_pairs = second_far + late_near
    near_pairs = [(d + 1, d) for d in range(1, count - 1) if d not in (1, 3, half - 2, half - 1)]
    near_pairs += [(0, half - 1), (half - 1, 0)]
    first_back = [(t, s) for s, t in first_far] + [(1, 0)]
    second_back = [(t, s) for s, t in second_far]
    side_pairs = [(0, half - 1), (half - 1, count - 1)]

    def among(devices):
        return functools.reduce(jnp.logical_or, [me == d for d in devices])

    def switch(on, other, *weights):
        flags = jnp.stack([jnp.asarray(on), jnp.asarray(other)]).astype(jnp.int32)
        return jnp.concatenate([flags, *weights])

    first_in = lax.ppermute(block, "chan", first_pairs)
    near_in = lax.ppermute(block, "chan", near_pairs)
    first_flags = lax.ppermute(quality, "chan", first_pairs)[0]
    near_flags = lax.ppermute(quality, "chan", near_pairs)[0]
    second_flags = lax.ppermute(quality, "chan", second_pairs)[0]
    coeffs = lag_rows(freq_count, window_count)
    own = turn(block, switch(True, False), "turn_own")
    halves = split(block)

    late_half, own, coeffs, first_in, near_in = lax.optimization_barrier((halves[0], own, coeffs, first_in, near_in))
    second_in = [lax.ppermute(late_half, "chan", second_pairs)]
    flags = quality[0]
    both = switch(True, False, flags * near_flags, flags * first_flags)
    near, first, first_mirror = corr(both, own, coeffs, [near_in, first_in], ["plain", "both"], "near_first")
    late_half, near = lax.optimization_barrier((halves[1], near))
    second_in.append(lax.ppermute(late_half, "chan", second_pairs))
    first_returned = lax.ppermute(first_mirror, "chan", first_back)

    side_switch = switch(among([0, half - 1]), me == half - 1, near_flags * first_flags)
    side_switch, near = lax.optimization_barrier((side_switch, near))
    side_turned = turn(near_in, side_switch, "turn_side", common=False)
    side, = corr(side_switch, side_turned, coeffs, [first_in], ["either"], "side", common=False)
    side_returned = lax.ppermute(side, "chan", side_pairs)

    second_switch = switch(among([t for _, t in second_pairs]), False, flags * second_flags)
    second_switch, side, first_returned = lax.optimization_barrier((second_switch, side, first_returned))
    total, = corr(second_switch, own, coeffs, second_in[:1], (), "second_a")
    middle = halves[0].shape[0]
    second, second_mirror = corr(second_switch, own, coeffs, second_in[1:], ["both"], "second_b", middle, total)
    second_returned = lax.ppermute(second_mirror, "chan", second_back)

    far = jnp.where(among([t for _, t in first_far]), first, second)
    far = jnp.where(among([s for s, _ in first_far]), first_returned, far)
    far = jnp.where(among([s for s, _ in second_far]), second_returned, far)
    near = jnp.where(among([t for _, t in late_near]), second, near)
    near = jnp.where(among([half - 1, count - 1]), side_returned, near)
    near = jnp.where(me == 0, first_returned, jnp.where(me == half - 2, first, near))
    return near[None], far[None]


def solution(mesh):
    return jax.shard_map(
        local,
        mesh=mesh,
        in_specs=(P(None, None, None, ("grp", "chan")), P(("grp", "chan"), None)),
        out_specs=(P(("grp", "chan"), None, None, None), P(("grp", "chan"), None, None, None)),
        check_vma=False,
    )
```

```python
import functools
import math

import jax
import jax.numpy as jnp
from jax import lax
from jax.experimental import pallas as pl
from jax.experimental.pallas import tpu as pltpu
from jax.sharding import PartitionSpec as P

HL = 4
LAGS = 2 * HL + 1
STEP = 1024
PARTS = (5, 8)
PARAMS = pltpu.CompilerParams(vmem_limit_bytes=16 * 1024 * 1024)


def lag_rows(freq_count, window_count):
    per_bin = 2 * window_count
    row = jnp.arange(freq_count * per_bin, dtype=jnp.int32)
    freq_values = (row // per_bin).astype(jnp.float32)
    sign = jnp.where(row % per_bin < window_count, 1.0, -1.0)
    lag_values = jnp.arange(HL + 1, dtype=jnp.float32)
    phases = jnp.pi / freq_count * lag_values[:, None] * freq_values[None, :]
    factor = 1.0 / math.sqrt(window_count * freq_count)
    cos_part = jnp.cos(phases) * factor
    sin_part = -jnp.sin(phases[1:]) * factor * sign[None, :]
    return jnp.concatenate([cos_part, sin_part], axis=0).astype(jnp.bfloat16)


def split_kernel(middle, x_ref, first_ref, last_ref):
    step = pl.program_id(0)

    @pl.when(step < middle)
    def _():
        first_ref[...] = x_ref[...]

    @pl.when(step >= middle)
    def _():
        last_ref[...] = x_ref[...]


def split(x):
    rows, cols = x.shape
    steps = rows // STEP
    middle = steps * PARTS[0] // PARTS[1]
    return pl.pallas_call(
        functools.partial(split_kernel, middle),
        grid=(steps,),
        in_specs=[pl.BlockSpec((STEP, cols), lambda s: (s, 0))],
        out_specs=[
            pl.BlockSpec((STEP, cols), lambda s: (jnp.minimum(s, middle - 1), 0)),
            pl.BlockSpec((STEP, cols), lambda s: (jnp.maximum(s - middle, 0), 0)),
        ],
        out_shape=[jax.ShapeDtypeStruct((n * STEP, cols), x.dtype) for n in (middle, steps - middle)],
        compiler_params=PARAMS,
        cost_estimate=pl.CostEstimate(flops=0, bytes_accessed=4 * rows * cols, transcendentals=0),
        name="split",
    )(x)


def turn_kernel(active_ref, x_ref, plain_ref, swapped_ref):
    @pl.when(active_ref[0] != 0)
    def _():
        rows, cols = x_ref.shape
        same = lax.broadcasted_iota(jnp.int32, (cols, cols), 0) == lax.broadcasted_iota(jnp.int32, (cols, cols), 1)
        eye = jnp.where(same, 1.0, 0.0).astype(jnp.bfloat16)
        source = lax.broadcasted_iota(jnp.int32, (2 * cols, 2 * cols), 0)
        target = lax.broadcasted_iota(jnp.int32, (2 * cols, 2 * cols), 1)
        exchange = jnp.where((source ^ 4) == target, 1.0, 0.0).astype(jnp.bfloat16)
        plain = lax.dot_general(eye, x_ref[...], (((1,), (1,)), ((), ())), preferred_element_type=jnp.float32)
        plain = plain.astype(jnp.bfloat16)
        plain_ref[...] = plain
        for t in range(0, rows, 2 * cols):
            swapped = jnp.dot(plain[:, t:t + 2 * cols], exchange, preferred_element_type=jnp.float32)
            swapped_ref[:, t:t + 2 * cols] = swapped.astype(jnp.bfloat16)


def turn(x, switch, name, common=True):
    rows, cols = x.shape
    out = jax.ShapeDtypeStruct((cols, rows), jnp.bfloat16)
    return pl.pallas_call(
        turn_kernel,
        grid_spec=pltpu.PrefetchScalarGridSpec(
            num_scalar_prefetch=1,
            grid=(rows // STEP,),
            in_specs=[pl.BlockSpec((STEP, cols), lambda s, on: (s * on[0], 0))],
            out_specs=[pl.BlockSpec((cols, STEP), lambda s, on: (0, s * on[0]))] * 2,
        ),
        out_shape=[out, out],
        compiler_params=PARAMS,
        cost_estimate=pl.CostEstimate(flops=0, bytes_accessed=6 * rows * cols if common else 0, transcendentals=0),
        name=name,
    )(switch, x)


def write_lags(out, acc, at, cols, mirrored):
    for lag in range(LAGS):
        k = abs(lag - HL)
        value = acc[k * cols:(k + 1) * cols, at]
        if k:
            odd = acc[(HL + k) * cols:(HL + k + 1) * cols, at]
            value = value + odd if lag > HL else value - odd
        value = value.astype(jnp.bfloat16)
        if mirrored:
            out[LAGS - 1 - lag] = value.T
        else:
            out[lag] = value


def scale(scaled, plain, swapped, coeff_ref):
    cols = plain.shape[0]
    for k in range(LAGS):
        part = plain if k <= HL else swapped
        scaled[k * cols:(k + 1) * cols, :] = part * coeff_ref[k:k + 1, :]


def weigh(x, switch_ref, begin, windows):
    rows, cols = x.shape
    window = lax.broadcasted_iota(jnp.int32, (16, cols), 0) % windows
    weights = jnp.zeros((16, cols), jnp.float32)
    for w in range(windows):
        weights = jnp.where(window == w, switch_ref[begin + w].astype(jnp.float32), weights)
    weights = jnp.broadcast_to(weights.astype(jnp.bfloat16)[None], (rows // 16, 16, cols))
    return x * weights.reshape(rows, cols)


def first_kernel(windows, switch_ref, plain_ref, swapped_ref, plain_alt, swapped_alt, coeff_ref, near_ref, first_ref,
                 own_ref, near_out, far_out, back_out, acc, scaled):
    step = pl.program_id(0)
    cols = plain_ref.shape[0]
    near_mirrored, special = switch_ref[0], switch_ref[1]

    @pl.when(step == 0)
    def _():
        acc[...] = jnp.zeros_like(acc)

    @pl.when(special == 0)
    def _():
        scale(scaled, plain_ref[...], swapped_ref[...], coeff_ref)

    @pl.when(special != 0)
    def _():
        scale(scaled, plain_alt[...], swapped_alt[...], coeff_ref)

    near = weigh(near_ref[...], switch_ref, 2, windows)
    far = weigh(jnp.where(special != 0, own_ref[...], first_ref[...]), switch_ref, 2 + windows, windows)
    acc[...] += jnp.dot(scaled[...], jnp.concatenate([near, far], axis=1), preferred_element_type=jnp.float32)

    @pl.when(step == pl.num_programs(0) - 1)
    def _():
        near_at, far_at = slice(0, cols), slice(cols, 2 * cols)

        @pl.when(special == 0)
        def _():
            write_lags(back_out, acc, far_at, cols, True)
            write_lags(far_out, acc, far_at, cols, False)

        @pl.when(special != 0)
        def _():
            write_lags(back_out, acc, far_at, cols, False)
            write_lags(far_out, acc, far_at, cols, True)

        pl.when(near_mirrored == 0)(lambda: write_lags(near_out, acc, near_at, cols, False))
        pl.when(near_mirrored != 0)(lambda: write_lags(near_out, acc, near_at, cols, True))


def first_sums(switch, own, alt, coeffs, near_in, first_in, block):
    rows, cols = block.shape
    windows = (switch.shape[0] - 2) // 2
    result = jax.ShapeDtypeStruct((LAGS, cols, cols), jnp.bfloat16)
    left = pl.BlockSpec((cols, STEP), lambda s, on: (0, s * (1 - on[1])))
    left_alt = pl.BlockSpec((cols, STEP), lambda s, on: (0, s * on[1]))
    right = pl.BlockSpec((STEP, cols), lambda s, on: (s, 0))
    right_usual = pl.BlockSpec((STEP, cols), lambda s, on: (s * (1 - on[1]), 0))
    right_special = pl.BlockSpec((STEP, cols), lambda s, on: (s * on[1], 0))
    return pl.pallas_call(
        functools.partial(first_kernel, windows),
        grid_spec=pltpu.PrefetchScalarGridSpec(
            num_scalar_prefetch=1,
            grid=(rows // STEP,),
            in_specs=[left, left, left_alt, left_alt, pl.BlockSpec((LAGS, STEP), lambda s, on: (0, s)),
                      right, right_usual, right_special],
            out_specs=[pl.BlockSpec(result.shape, lambda s, on: (0, 0, 0))] * 3,
            scratch_shapes=[pltpu.VMEM((LAGS * cols, 2 * cols), jnp.float32),
                            pltpu.VMEM((LAGS * cols, STEP), jnp.bfloat16)],
        ),
        out_shape=[result] * 3,
        compiler_params=PARAMS,
        cost_estimate=pl.CostEstimate(
            flops=4 * LAGS * cols * cols * rows, bytes_accessed=8 * rows * cols, transcendentals=0
        ),
        name="first_sums",
    )(switch, *own, *alt, coeffs, near_in, first_in, block)


def second_kernel(windows, first, switch_ref, plain_ref, swapped_ref, coeff_ref, partner_ref, *rest):
    on, late_near = switch_ref[0], switch_ref[1]
    step = pl.program_id(0)
    cols = plain_ref.shape[0]
    if first:
        acc, scaled = rest
    else:
        acc_in, near_in, far_in, near_out, far_out, back_out, acc, scaled = rest

    @pl.when(on != 0)
    def _():
        @pl.when(step == 0)
        def _():
            acc[...] = jnp.zeros_like(acc) if first else acc_in[...]

        scale(scaled, plain_ref[...], swapped_ref[...], coeff_ref)
        partner = weigh(partner_ref[...], switch_ref, 2, windows)
        acc[...] += jnp.dot(scaled[...], partner, preferred_element_type=jnp.float32)

    if not first:
        @pl.when(step == pl.num_programs(0) - 1)
        def _():
            here = slice(0, cols)

            @pl.when((on != 0) & (late_near == 0))
            def _():
                write_lags(back_out, acc, here, cols, True)
                write_lags(far_out, acc, here, cols, False)

            @pl.when((on == 0) | (late_near != 0))
            def _():
                far_out[...] = far_in[...]

            pl.when(late_near != 0)(lambda: write_lags(near_out, acc, here, cols, False))

            @pl.when(late_near == 0)
            def _():
                near_out[...] = near_in[...]


def second_sums(switch, own, coeffs, partner, start, earlier=None):
    rows, cols = partner.shape
    windows = switch.shape[0] - 2
    skip = start // STEP
    total = jax.ShapeDtypeStruct((LAGS * cols, cols), jnp.float32)
    total_spec = pl.BlockSpec(total.shape, lambda s, on: (0, 0))
    result = jax.ShapeDtypeStruct((LAGS, cols, cols), jnp.bfloat16)
    result_spec = pl.BlockSpec(result.shape, lambda s, on: (0, 0, 0))
    left = pl.BlockSpec((cols, STEP), lambda s, on: (0, s * on[0] + skip))
    in_specs = [left, left, pl.BlockSpec((LAGS, STEP), lambda s, on: (0, s * on[0] + skip)),
                pl.BlockSpec((STEP, cols), lambda s, on: (s * on[0], 0))]
    scratch = [pltpu.VMEM((LAGS * cols, STEP), jnp.bfloat16)]
    if earlier is None:
        out_shape, out_specs, earlier = [total], [total_spec], []
    else:
        out_shape, out_specs = [result] * 3, [result_spec] * 3
        in_specs += [total_spec, result_spec, result_spec]
        scratch = [pltpu.VMEM(total.shape, jnp.float32)] + scratch
    return pl.pallas_call(
        functools.partial(second_kernel, windows, not earlier),
        grid_spec=pltpu.PrefetchScalarGridSpec(
            num_scalar_prefetch=1,
            grid=(rows // STEP,),
            in_specs=in_specs,
            out_specs=out_specs,
            scratch_shapes=scratch,
        ),
        out_shape=out_shape,
        compiler_params=PARAMS,
        cost_estimate=pl.CostEstimate(
            flops=2 * LAGS * cols * cols * rows, bytes_accessed=6 * rows * cols, transcendentals=0
        ),
        name="second_last" if earlier else "second_part",
    )(switch, *own, coeffs, partner, *earlier)


def local(spectra, quality):
    count = lax.axis_size("chan")
    half = count // 2
    me = lax.axis_index("chan")
    freq_count, _, window_count, cols = spectra.shape
    block = spectra.reshape(-1, cols)

    first_far, second_far = [], []
    for p in range(half):
        if p in (0, half - 1):
            first_far.append((p + half, p))
        elif p % 2 == 0 and p >= half // 2:
            first_far.append((p, p + half))
        elif p in (1, 3):
            second_far.append((p, p + half))
        else:
            second_far.append((p + half, p))
    late_near = [(2, 1), (4, 3)]
    first_pairs = first_far + [(0, 1), (half - 1, half - 2)]
    second_pairs = second_far + late_near
    near_pairs = [(d + 1, d) for d in range(1, count - 1) if d not in (1, 3, half - 2, half - 1)]
    near_pairs += [(0, half - 1), (half - 1, 0)]
    first_back = [(t, s) for s, t in first_far] + [(1, 0)]
    second_back = [(t, s) for s, t in second_far]
    side_pairs = [(0, half - 1), (half - 1, count - 1)]

    def among(devices):
        return functools.reduce(jnp.logical_or, [me == d for d in devices])

    def switch(on, other, *weights):
        flags = jnp.stack([jnp.asarray(on), jnp.asarray(other)]).astype(jnp.int32)
        return jnp.concatenate([flags, *weights])

    first_in = lax.ppermute(block, "chan", first_pairs)
    near_in = lax.ppermute(block, "chan", near_pairs)
    coeffs = lag_rows(freq_count, window_count)
    own = turn(block, switch(True, False), "turn_own")
    parts = split(block)
    sent_flags, own = lax.optimization_barrier((quality, own))
    first_flags = lax.ppermute(sent_flags, "chan", first_pairs)[0]
    near_flags = lax.ppermute(sent_flags, "chan", near_pairs)[0]
    second_flags = lax.ppermute(sent_flags, "chan", second_pairs)[0]
    special = among([0, half - 1])
    usual_flags = quality[0]
    left_flags = jnp.where(special, first_flags, usual_flags)
    first_switch = switch(me == 0, special, left_flags * near_flags, usual_flags * first_flags)
    second_switch = switch(
        among([t for _, t in second_pairs]), among([t for _, t in late_near]), usual_flags * second_flags
    )

    late_part, own, coeffs, first_in, near_in = lax.optimization_barrier((parts[0], own, coeffs, first_in, near_in))
    second_first = lax.ppermute(late_part, "chan", second_pairs)
    alt = turn(first_in, switch(special, False), "turn_first", common=False)
    near, far, back = first_sums(first_switch, own, alt, coeffs, near_in, first_in, block)
    late_part, near = lax.optimization_barrier((parts[1], near))
    second_last = lax.ppermute(late_part, "chan", second_pairs)
    first_returned = lax.ppermute(back, "chan", first_back)
    side_returned = lax.ppermute(near, "chan", side_pairs)

    second_switch, first_returned = lax.optimization_barrier((second_switch, first_returned))
    total, = second_sums(second_switch, own, coeffs, second_first, 0)
    near = jnp.where(among([half - 1, count - 1]), side_returned, near)
    near = jnp.where(me == 0, first_returned, jnp.where(me == half - 2, far, near))
    far = jnp.where(among([s for s, _ in first_far]), first_returned, far)
    near, far, back = second_sums(
        second_switch, own, coeffs, second_last, parts[0].shape[0], [total, near, far]
    )
    second_returned = lax.ppermute(back, "chan", second_back)
    far = jnp.where(among([s for s, _ in second_far]), second_returned, far)
    return near[None], far[None]


def solution(mesh):
    return jax.shard_map(
        local,
        mesh=mesh,
        in_specs=(P(None, None, None, ("grp", "chan")), P(("grp", "chan"), None)),
        out_specs=(P(("grp", "chan"), None, None, None), P(("grp", "chan"), None, None, None)),
        check_vma=False,
    )
```

```python
import functools
import math

import jax
import jax.numpy as jnp
from jax import lax
from jax.experimental import pallas as pl
from jax.experimental.pallas import tpu as pltpu
from jax.sharding import PartitionSpec as P

HL = 4
LAGS = 2 * HL + 1
STEP = 1024
PARTS = (5, 8)
PARAMS = pltpu.CompilerParams(vmem_limit_bytes=16 * 1024 * 1024)


def lag_rows(freq_count, window_count):
    per_bin = 2 * window_count
    row = jnp.arange(freq_count * per_bin, dtype=jnp.int32)
    freq_values = (row // per_bin).astype(jnp.float32)
    sign = jnp.where(row % per_bin < window_count, 1.0, -1.0)
    lag_values = jnp.arange(HL + 1, dtype=jnp.float32)
    phases = jnp.pi / freq_count * lag_values[:, None] * freq_values[None, :]
    factor = 1.0 / math.sqrt(window_count * freq_count)
    cos_part = jnp.cos(phases) * factor
    sin_part = -jnp.sin(phases[1:]) * factor * sign[None, :]
    return jnp.concatenate([cos_part, sin_part], axis=0).astype(jnp.bfloat16)


def split_kernel(middle, x_ref, first_ref, last_ref):
    step = pl.program_id(0)

    @pl.when(step < middle)
    def _():
        first_ref[...] = x_ref[...]

    @pl.when(step >= middle)
    def _():
        last_ref[...] = x_ref[...]


def split(x):
    rows, cols = x.shape
    steps = rows // STEP
    middle = steps * PARTS[0] // PARTS[1]
    return pl.pallas_call(
        functools.partial(split_kernel, middle),
        grid=(steps,),
        in_specs=[pl.BlockSpec((STEP, cols), lambda s: (s, 0))],
        out_specs=[
            pl.BlockSpec((STEP, cols), lambda s: (jnp.minimum(s, middle - 1), 0)),
            pl.BlockSpec((STEP, cols), lambda s: (jnp.maximum(s - middle, 0), 0)),
        ],
        out_shape=[jax.ShapeDtypeStruct((n * STEP, cols), x.dtype) for n in (middle, steps - middle)],
        compiler_params=PARAMS,
        cost_estimate=pl.CostEstimate(flops=0, bytes_accessed=4 * rows * cols, transcendentals=0),
        name="split",
    )(x)


def turn_kernel(active_ref, x_ref, plain_ref, swapped_ref):
    @pl.when(active_ref[0] != 0)
    def _():
        rows, cols = x_ref.shape
        same = lax.broadcasted_iota(jnp.int32, (cols, cols), 0) == lax.broadcasted_iota(jnp.int32, (cols, cols), 1)
        eye = jnp.where(same, 1.0, 0.0).astype(jnp.bfloat16)
        source = lax.broadcasted_iota(jnp.int32, (2 * cols, 2 * cols), 0)
        target = lax.broadcasted_iota(jnp.int32, (2 * cols, 2 * cols), 1)
        exchange = jnp.where((source ^ 4) == target, 1.0, 0.0).astype(jnp.bfloat16)
        plain = lax.dot_general(eye, x_ref[...], (((1,), (1,)), ((), ())), preferred_element_type=jnp.float32)
        plain = plain.astype(jnp.bfloat16)
        plain_ref[...] = plain
        for t in range(0, rows, 2 * cols):
            swapped = jnp.dot(plain[:, t:t + 2 * cols], exchange, preferred_element_type=jnp.float32)
            swapped_ref[:, t:t + 2 * cols] = swapped.astype(jnp.bfloat16)


def turn(x, switch, name, common=True):
    rows, cols = x.shape
    out = jax.ShapeDtypeStruct((cols, rows), jnp.bfloat16)
    return pl.pallas_call(
        turn_kernel,
        grid_spec=pltpu.PrefetchScalarGridSpec(
            num_scalar_prefetch=1,
            grid=(rows // STEP,),
            in_specs=[pl.BlockSpec((STEP, cols), lambda s, on: (s * on[0], 0))],
            out_specs=[pl.BlockSpec((cols, STEP), lambda s, on: (0, s * on[0]))] * 2,
        ),
        out_shape=[out, out],
        compiler_params=PARAMS,
        cost_estimate=pl.CostEstimate(flops=0, bytes_accessed=6 * rows * cols if common else 0, transcendentals=0),
        name=name,
    )(switch, x)


def write_lags(out, acc, at, cols, mirrored):
    for lag in range(LAGS):
        k = abs(lag - HL)
        value = acc[k * cols:(k + 1) * cols, at]
        if k:
            odd = acc[(HL + k) * cols:(HL + k + 1) * cols, at]
            value = value + odd if lag > HL else value - odd
        value = value.astype(jnp.bfloat16)
        if mirrored:
            out[LAGS - 1 - lag] = value.T
        else:
            out[lag] = value


def scale(scaled, plain, swapped, coeff_ref):
    cols = plain.shape[0]
    for k in range(LAGS):
        part = plain if k <= HL else swapped
        scaled[k * cols:(k + 1) * cols, :] = part * coeff_ref[k:k + 1, :]


def weigh(x, window_weights):
    rows, cols = x.shape
    window = lax.broadcasted_iota(jnp.int32, (16, cols), 0) % len(window_weights)
    weights = jnp.zeros((16, cols), jnp.float32)
    for w, weight in enumerate(window_weights):
        weights = jnp.where(window == w, weight.astype(jnp.float32), weights)
    weights = jnp.broadcast_to(weights.astype(jnp.bfloat16)[None], (rows // 16, 16, cols))
    return x * weights.reshape(rows, cols)


def first_kernel(windows, switch_ref, plain_ref, swapped_ref, plain_alt, swapped_alt, coeff_ref, near_ref, first_ref,
                 own_ref, near_out, far_out, back_out, acc, scaled):
    step = pl.program_id(0)
    cols = plain_ref.shape[0]
    near_mirrored, special = switch_ref[0], switch_ref[1]

    @pl.when(step == 0)
    def _():
        acc[...] = jnp.zeros_like(acc)

    plain = jnp.where(special != 0, plain_alt[...], plain_ref[...])
    swapped = jnp.where(special != 0, swapped_alt[...], swapped_ref[...])
    scale(scaled, plain, swapped, coeff_ref)
    flags = [[switch_ref[2 + part * windows + w] for w in range(windows)] for part in range(3)]
    near_weights = [jnp.where(special != 0, first, own) * near for own, near, first in zip(*flags)]
    near = weigh(near_ref[...], near_weights)
    far = weigh(jnp.where(special != 0, own_ref[...], first_ref[...]), [own * first for own, _, first in zip(*flags)])
    acc[...] += jnp.dot(scaled[...], jnp.concatenate([near, far], axis=1), preferred_element_type=jnp.float32)

    @pl.when(step == pl.num_programs(0) - 1)
    def _():
        near_at, far_at = slice(0, cols), slice(cols, 2 * cols)

        @pl.when(special == 0)
        def _():
            write_lags(back_out, acc, far_at, cols, True)
            write_lags(far_out, acc, far_at, cols, False)

        @pl.when(special != 0)
        def _():
            write_lags(back_out, acc, far_at, cols, False)
            write_lags(far_out, acc, far_at, cols, True)

        pl.when(near_mirrored == 0)(lambda: write_lags(near_out, acc, near_at, cols, False))
        pl.when(near_mirrored != 0)(lambda: write_lags(near_out, acc, near_at, cols, True))


def first_sums(switch, own, alt, coeffs, near_in, first_in, block):
    rows, cols = block.shape
    windows = (switch.shape[0] - 2) // 3
    result = jax.ShapeDtypeStruct((LAGS, cols, cols), jnp.bfloat16)
    left = pl.BlockSpec((cols, STEP), lambda s, on: (0, s * (1 - on[1])))
    left_alt = pl.BlockSpec((cols, STEP), lambda s, on: (0, s * on[1]))
    right = pl.BlockSpec((STEP, cols), lambda s, on: (s, 0))
    right_usual = pl.BlockSpec((STEP, cols), lambda s, on: (s * (1 - on[1]), 0))
    right_special = pl.BlockSpec((STEP, cols), lambda s, on: (s * on[1], 0))
    return pl.pallas_call(
        functools.partial(first_kernel, windows),
        grid_spec=pltpu.PrefetchScalarGridSpec(
            num_scalar_prefetch=1,
            grid=(rows // STEP,),
            in_specs=[left, left, left_alt, left_alt, pl.BlockSpec((LAGS, STEP), lambda s, on: (0, s)),
                      right, right_usual, right_special],
            out_specs=[pl.BlockSpec(result.shape, lambda s, on: (0, 0, 0))] * 3,
            scratch_shapes=[pltpu.VMEM((LAGS * cols, 2 * cols), jnp.float32),
                            pltpu.VMEM((LAGS * cols, STEP), jnp.bfloat16)],
        ),
        out_shape=[result] * 3,
        compiler_params=PARAMS,
        cost_estimate=pl.CostEstimate(
            flops=4 * LAGS * cols * cols * rows, bytes_accessed=8 * rows * cols, transcendentals=0
        ),
        name="first_sums",
    )(switch, *own, *alt, coeffs, near_in, first_in, block)


def second_kernel(windows, first, switch_ref, plain_ref, swapped_ref, coeff_ref, partner_ref, *rest):
    on, late_near = switch_ref[0], switch_ref[1]
    step = pl.program_id(0)
    cols = plain_ref.shape[0]
    if first:
        acc, scaled = rest
    else:
        acc_in, near_in, far_in, near_out, far_out, back_out, acc, scaled = rest

    @pl.when(on != 0)
    def _():
        @pl.when(step == 0)
        def _():
            acc[...] = jnp.zeros_like(acc) if first else acc_in[...]

        scale(scaled, plain_ref[...], swapped_ref[...], coeff_ref)
        partner = weigh(partner_ref[...], [switch_ref[2 + w] for w in range(windows)])
        acc[...] += jnp.dot(scaled[...], partner, preferred_element_type=jnp.float32)

    if not first:
        @pl.when(step == pl.num_programs(0) - 1)
        def _():
            here = slice(0, cols)

            @pl.when((on != 0) & (late_near == 0))
            def _():
                write_lags(back_out, acc, here, cols, True)
                write_lags(far_out, acc, here, cols, False)

            @pl.when((on == 0) | (late_near != 0))
            def _():
                far_out[...] = far_in[...]

            pl.when(late_near != 0)(lambda: write_lags(near_out, acc, here, cols, False))

            @pl.when(late_near == 0)
            def _():
                near_out[...] = near_in[...]


def second_sums(switch, own, coeffs, partner, start, earlier=None):
    rows, cols = partner.shape
    windows = switch.shape[0] - 2
    skip = start // STEP
    total = jax.ShapeDtypeStruct((LAGS * cols, cols), jnp.float32)
    total_spec = pl.BlockSpec(total.shape, lambda s, on: (0, 0))
    result = jax.ShapeDtypeStruct((LAGS, cols, cols), jnp.bfloat16)
    result_spec = pl.BlockSpec(result.shape, lambda s, on: (0, 0, 0))
    left = pl.BlockSpec((cols, STEP), lambda s, on: (0, s * on[0] + skip))
    in_specs = [left, left, pl.BlockSpec((LAGS, STEP), lambda s, on: (0, s * on[0] + skip)),
                pl.BlockSpec((STEP, cols), lambda s, on: (s * on[0], 0))]
    scratch = [pltpu.VMEM((LAGS * cols, STEP), jnp.bfloat16)]
    if earlier is None:
        out_shape, out_specs, earlier = [total], [total_spec], []
    else:
        out_shape, out_specs = [result] * 3, [result_spec] * 3
        in_specs += [total_spec, result_spec, result_spec]
        scratch = [pltpu.VMEM(total.shape, jnp.float32)] + scratch
    return pl.pallas_call(
        functools.partial(second_kernel, windows, not earlier),
        grid_spec=pltpu.PrefetchScalarGridSpec(
            num_scalar_prefetch=1,
            grid=(rows // STEP,),
            in_specs=in_specs,
            out_specs=out_specs,
            scratch_shapes=scratch,
        ),
        out_shape=out_shape,
        compiler_params=PARAMS,
        cost_estimate=pl.CostEstimate(
            flops=2 * LAGS * cols * cols * rows, bytes_accessed=6 * rows * cols, transcendentals=0
        ),
        name="second_last" if earlier else "second_part",
    )(switch, *own, coeffs, partner, *earlier)


def local(spectra, quality):
    count = lax.axis_size("chan")
    half = count // 2
    me = lax.axis_index("chan")
    freq_count, _, window_count, cols = spectra.shape
    block = spectra.reshape(-1, cols)

    first_far, second_far = [], []
    for p in range(half):
        if p in (0, half - 1):
            first_far.append((p + half, p))
        elif p % 2 == 0 and p >= half // 2:
            first_far.append((p, p + half))
        elif p in (1, 3):
            second_far.append((p, p + half))
        else:
            second_far.append((p + half, p))
    late_near = [(2, 1), (4, 3)]
    first_pairs = first_far + [(0, 1), (half - 1, half - 2)]
    second_pairs = second_far + late_near
    near_pairs = [(d + 1, d) for d in range(1, count - 1) if d not in (1, 3, half - 2, half - 1)]
    near_pairs += [(0, half - 1), (half - 1, 0)]
    first_back = [(t, s) for s, t in first_far] + [(1, 0)]
    second_back = [(t, s) for s, t in second_far]
    side_pairs = [(0, half - 1), (half - 1, count - 1)]

    def among(devices):
        return functools.reduce(jnp.logical_or, [me == d for d in devices])

    def switch(on, other, *weights):
        flags = jnp.stack([jnp.asarray(on), jnp.asarray(other)]).astype(jnp.int32)
        return jnp.concatenate([flags, *weights])

    first_in = lax.ppermute(block, "chan", first_pairs)
    near_in = lax.ppermute(block, "chan", near_pairs)
    coeffs = lag_rows(freq_count, window_count)
    own = turn(block, switch(True, False), "turn_own")
    parts = split(block)
    first_flags = lax.ppermute(quality, "chan", first_pairs)[0]
    near_flags = lax.ppermute(quality, "chan", near_pairs)[0]
    second_flags = lax.ppermute(quality, "chan", second_pairs)[0]
    special = among([0, half - 1])
    first_switch = switch(me == 0, special, quality[0], near_flags, first_flags)
    second_switch = switch(
        among([t for _, t in second_pairs]), among([t for _, t in late_near]), quality[0] * second_flags
    )

    late_part, own, coeffs, first_in, near_in = lax.optimization_barrier((parts[0], own, coeffs, first_in, near_in))
    second_first = lax.ppermute(late_part, "chan", second_pairs)
    alt = turn(first_in, switch(special, False), "turn_first", common=False)
    near, far, back = first_sums(first_switch, own, alt, coeffs, near_in, first_in, block)
    late_part, near = lax.optimization_barrier((parts[1], near))
    second_last = lax.ppermute(late_part, "chan", second_pairs)
    first_returned = lax.ppermute(back, "chan", first_back)
    side_returned = lax.ppermute(near, "chan", side_pairs)

    second_switch, first_returned = lax.optimization_barrier((second_switch, first_returned))
    total, = second_sums(second_switch, own, coeffs, second_first, 0)
    near = jnp.where(among([half - 1, count - 1]), side_returned, near)
    near = jnp.where(me == 0, first_returned, jnp.where(me == half - 2, far, near))
    far = jnp.where(among([s for s, _ in first_far]), first_returned, far)
    near, far, back = second_sums(
        second_switch, own, coeffs, second_last, parts[0].shape[0], [total, near, far]
    )
    second_returned = lax.ppermute(back, "chan", second_back)
    far = jnp.where(among([s for s, _ in second_far]), second_returned, far)
    return near[None], far[None]


def solution(mesh):
    return jax.shard_map(
        local,
        mesh=mesh,
        in_specs=(P(None, None, None, ("grp", "chan")), P(("grp", "chan"), None)),
        out_specs=(P(("grp", "chan"), None, None, None), P(("grp", "chan"), None, None, None)),
        check_vma=False,
    )
```

```python
import functools
import math

import jax
import jax.numpy as jnp
from jax import lax
from jax.experimental import pallas as pl
from jax.experimental.pallas import tpu as pltpu
from jax.sharding import PartitionSpec as P

HL = 4
LAGS = 2 * HL + 1
STEP = 1024
PARTS = (5, 8)
PARAMS = pltpu.CompilerParams(vmem_limit_bytes=48 * 1024 * 1024)


def lag_rows(freq_count, window_count):
    per_bin = 2 * window_count
    row = jnp.arange(freq_count * per_bin, dtype=jnp.int32)
    freq_values = (row // per_bin).astype(jnp.float32)
    sign = jnp.where(row % per_bin < window_count, 1.0, -1.0)
    lag_values = jnp.arange(HL + 1, dtype=jnp.float32)
    phases = jnp.pi / freq_count * lag_values[:, None] * freq_values[None, :]
    factor = 1.0 / math.sqrt(window_count * freq_count)
    cos_part = jnp.cos(phases) * factor
    sin_part = -jnp.sin(phases[1:]) * factor * sign[None, :]
    return jnp.concatenate([cos_part, sin_part], axis=0).astype(jnp.bfloat16)


def split_kernel(middle, x_ref, first_ref, last_ref):
    step = pl.program_id(0)

    @pl.when(step < middle)
    def _():
        first_ref[...] = x_ref[...]

    @pl.when(step >= middle)
    def _():
        last_ref[...] = x_ref[...]


def split(x):
    rows, cols = x.shape
    steps = rows // STEP
    middle = steps * PARTS[0] // PARTS[1]
    return pl.pallas_call(
        functools.partial(split_kernel, middle),
        grid=(steps,),
        in_specs=[pl.BlockSpec((STEP, cols), lambda s: (s, 0))],
        out_specs=[
            pl.BlockSpec((STEP, cols), lambda s: (jnp.minimum(s, middle - 1), 0)),
            pl.BlockSpec((STEP, cols), lambda s: (jnp.maximum(s - middle, 0), 0)),
        ],
        out_shape=[jax.ShapeDtypeStruct((n * STEP, cols), x.dtype) for n in (middle, steps - middle)],
        compiler_params=PARAMS,
        cost_estimate=pl.CostEstimate(flops=0, bytes_accessed=4 * rows * cols, transcendentals=0),
        name="split",
    )(x)


def left_kernel(switch_ref, x_ref, coeff_ref, left_ref):
    @pl.when(switch_ref[0] != 0)
    def _():
        rows, cols = x_ref.shape
        same = lax.broadcasted_iota(jnp.int32, (cols, cols), 0) == lax.broadcasted_iota(jnp.int32, (cols, cols), 1)
        eye = jnp.where(same, 1.0, 0.0).astype(jnp.bfloat16)
        source = lax.broadcasted_iota(jnp.int32, (2 * cols, 2 * cols), 0)
        target = lax.broadcasted_iota(jnp.int32, (2 * cols, 2 * cols), 1)
        exchange = jnp.where((source ^ 4) == target, 1.0, 0.0).astype(jnp.bfloat16)
        plain = lax.dot_general(eye, x_ref[...], (((1,), (1,)), ((), ())), preferred_element_type=jnp.float32)
        plain = plain.astype(jnp.bfloat16)
        for t in range(0, rows, 2 * cols):
            at = slice(t, t + 2 * cols)
            swapped = jnp.dot(plain[:, at], exchange, preferred_element_type=jnp.float32).astype(jnp.bfloat16)
            for k in range(LAGS):
                part = plain[:, at] if k <= HL else swapped
                left_ref[k * cols:(k + 1) * cols, at] = part * coeff_ref[k:k + 1, at]


def left_factors(x, coeffs, switch, name, common=True):
    rows, cols = x.shape
    return pl.pallas_call(
        left_kernel,
        grid_spec=pltpu.PrefetchScalarGridSpec(
            num_scalar_prefetch=1,
            grid=(rows // STEP,),
            in_specs=[pl.BlockSpec((STEP, cols), lambda s, on: (s * on[0], 0)),
                      pl.BlockSpec((LAGS, STEP), lambda s, on: (0, s * on[0]))],
            out_specs=pl.BlockSpec((LAGS * cols, STEP), lambda s, on: (0, s * on[0])),
        ),
        out_shape=jax.ShapeDtypeStruct((LAGS * cols, rows), jnp.bfloat16),
        compiler_params=PARAMS,
        cost_estimate=pl.CostEstimate(
            flops=0, bytes_accessed=2 * (LAGS + 1) * rows * cols if common else 0, transcendentals=0
        ),
        name=name,
    )(switch, x, coeffs)


def write_lags(out, acc, at, cols, mirrored):
    for lag in range(LAGS):
        k = abs(lag - HL)
        value = acc[k * cols:(k + 1) * cols, at]
        if k:
            odd = acc[(HL + k) * cols:(HL + k + 1) * cols, at]
            value = value + odd if lag > HL else value - odd
        value = value.astype(jnp.bfloat16)
        if mirrored:
            out[LAGS - 1 - lag] = value.T
        else:
            out[lag] = value


def weigh(x, window_weights):
    rows, cols = x.shape
    window = lax.broadcasted_iota(jnp.int32, (16, cols), 0) % len(window_weights)
    weights = jnp.zeros((16, cols), jnp.float32)
    for w, weight in enumerate(window_weights):
        weights = jnp.where(window == w, weight.astype(jnp.float32), weights)
    weights = jnp.broadcast_to(weights.astype(jnp.bfloat16)[None], (rows // 16, 16, cols))
    return x * weights.reshape(rows, cols)


def first_kernel(windows, switch_ref, left_ref, left_alt, near_ref, first_ref, own_ref, near_out, far_out, back_out, acc):
    step = pl.program_id(0)
    cols = near_ref.shape[1]
    near_mirrored, special = switch_ref[0], switch_ref[1]

    @pl.when(step == 0)
    def _():
        acc[...] = jnp.zeros_like(acc)

    flags = [[switch_ref[2 + part * windows + w] for w in range(windows)] for part in range(3)]
    near_weights = [jnp.where(special != 0, first, own) * near for own, near, first in zip(*flags)]
    near = weigh(near_ref[...], near_weights)
    far = weigh(jnp.where(special != 0, own_ref[...], first_ref[...]), [own * first for own, _, first in zip(*flags)])
    right = jnp.concatenate([near, far], axis=1)

    @pl.when(special == 0)
    def _():
        acc[...] += jnp.dot(left_ref[...], right, preferred_element_type=jnp.float32)

    @pl.when(special != 0)
    def _():
        acc[...] += jnp.dot(left_alt[...], right, preferred_element_type=jnp.float32)

    @pl.when(step == pl.num_programs(0) - 1)
    def _():
        near_at, far_at = slice(0, cols), slice(cols, 2 * cols)

        @pl.when(special == 0)
        def _():
            write_lags(back_out, acc, far_at, cols, True)
            write_lags(far_out, acc, far_at, cols, False)

        @pl.when(special != 0)
        def _():
            write_lags(back_out, acc, far_at, cols, False)
            write_lags(far_out, acc, far_at, cols, True)

        pl.when(near_mirrored == 0)(lambda: write_lags(near_out, acc, near_at, cols, False))
        pl.when(near_mirrored != 0)(lambda: write_lags(near_out, acc, near_at, cols, True))


def first_sums(switch, left, left_alt, near_in, first_in, block):
    rows, cols = block.shape
    windows = (switch.shape[0] - 2) // 3
    result = jax.ShapeDtypeStruct((LAGS, cols, cols), jnp.bfloat16)
    return pl.pallas_call(
        functools.partial(first_kernel, windows),
        grid_spec=pltpu.PrefetchScalarGridSpec(
            num_scalar_prefetch=1,
            grid=(rows // STEP,),
            in_specs=[
                pl.BlockSpec((LAGS * cols, STEP), lambda s, on: (0, s * (1 - on[1]))),
                pl.BlockSpec((LAGS * cols, STEP), lambda s, on: (0, s * on[1])),
                pl.BlockSpec((STEP, cols), lambda s, on: (s, 0)),
                pl.BlockSpec((STEP, cols), lambda s, on: (s * (1 - on[1]), 0)),
                pl.BlockSpec((STEP, cols), lambda s, on: (s * on[1], 0)),
            ],
            out_specs=[pl.BlockSpec(result.shape, lambda s, on: (0, 0, 0))] * 3,
            scratch_shapes=[pltpu.VMEM((LAGS * cols, 2 * cols), jnp.float32)],
        ),
        out_shape=[result] * 3,
        compiler_params=PARAMS,
        cost_estimate=pl.CostEstimate(
            flops=4 * LAGS * cols * cols * rows, bytes_accessed=2 * (LAGS + 2) * rows * cols, transcendentals=0
        ),
        name="first_sums",
    )(switch, left, left_alt, near_in, first_in, block)


def second_kernel(windows, first, switch_ref, left_ref, partner_ref, *rest):
    on, late_near = switch_ref[0], switch_ref[1]
    step = pl.program_id(0)
    cols = partner_ref.shape[1]
    if first:
        acc, = rest
    else:
        acc_in, near_in, far_in, back_in, near_out, far_out, back_out, acc = rest

    @pl.when(on != 0)
    def _():
        @pl.when(step == 0)
        def _():
            acc[...] = jnp.zeros_like(acc) if first else acc_in[...]

        partner = weigh(partner_ref[...], [switch_ref[2 + w] for w in range(windows)])
        acc[...] += jnp.dot(left_ref[...], partner, preferred_element_type=jnp.float32)

    if not first:
        @pl.when(step == pl.num_programs(0) - 1)
        def _():
            here = slice(0, cols)

            @pl.when((on != 0) & (late_near == 0))
            def _():
                write_lags(back_out, acc, here, cols, True)
                write_lags(far_out, acc, here, cols, False)

            @pl.when((on == 0) | (late_near != 0))
            def _():
                back_out[...] = back_in[...]
                far_out[...] = far_in[...]

            pl.when(late_near != 0)(lambda: write_lags(near_out, acc, here, cols, False))

            @pl.when(late_near == 0)
            def _():
                near_out[...] = near_in[...]


def second_sums(switch, left, partner, start, earlier=None):
    rows, cols = partner.shape
    windows = switch.shape[0] - 2
    skip = start // STEP
    total = jax.ShapeDtypeStruct((LAGS * cols, cols), jnp.float32)
    total_spec = pl.BlockSpec(total.shape, lambda s, on: (0, 0))
    result = jax.ShapeDtypeStruct((LAGS, cols, cols), jnp.bfloat16)
    result_spec = pl.BlockSpec(result.shape, lambda s, on: (0, 0, 0))
    in_specs = [pl.BlockSpec((LAGS * cols, STEP), lambda s, on: (0, s * on[0] + skip)),
                pl.BlockSpec((STEP, cols), lambda s, on: (s * on[0], 0))]
    scratch = []
    if earlier is None:
        out_shape, out_specs, earlier = [total], [total_spec], []
    else:
        out_shape, out_specs = [result] * 3, [result_spec] * 3
        in_specs += [total_spec] + [result_spec] * 3
        scratch = [pltpu.VMEM(total.shape, jnp.float32)]
    return pl.pallas_call(
        functools.partial(second_kernel, windows, not earlier),
        grid_spec=pltpu.PrefetchScalarGridSpec(
            num_scalar_prefetch=1,
            grid=(rows // STEP,),
            in_specs=in_specs,
            out_specs=out_specs,
            scratch_shapes=scratch,
        ),
        out_shape=out_shape,
        compiler_params=PARAMS,
        cost_estimate=pl.CostEstimate(
            flops=2 * LAGS * cols * cols * rows, bytes_accessed=2 * (LAGS + 1) * rows * cols, transcendentals=0
        ),
        name="second_last" if earlier else "second_part",
    )(switch, left, partner, *earlier)


def local(spectra, quality):
    count = lax.axis_size("chan")
    half = count // 2
    me = lax.axis_index("chan")
    freq_count, _, window_count, cols = spectra.shape
    block = spectra.reshape(-1, cols)

    first_far, second_far = [], []
    for p in range(half):
        if p in (0, half - 1):
            first_far.append((p + half, p))
        elif p % 2 == 0 and p >= half // 2:
            first_far.append((p, p + half))
        elif p in (1, 3):
            second_far.append((p, p + half))
        else:
            second_far.append((p + half, p))
    late_near = [(2, 1), (4, 3)]
    first_pairs = first_far + [(0, 1), (half - 1, half - 2)]
    second_pairs = second_far + late_near
    near_pairs = [(d + 1, d) for d in range(1, count - 1) if d not in (1, 3, half - 2, half - 1)]
    near_pairs += [(0, half - 1), (half - 1, 0)]
    first_back = [(t, s) for s, t in first_far]
    second_back = [(t, s) for s, t in second_far] + [(1, 0)]
    side_pairs = [(0, half - 1), (half - 1, count - 1)]

    def among(devices):
        return functools.reduce(jnp.logical_or, [me == d for d in devices])

    def switch(on, other, *weights):
        flags = jnp.stack([jnp.asarray(on), jnp.asarray(other)]).astype(jnp.int32)
        return jnp.concatenate([flags, *weights])

    first_in = lax.ppermute(block, "chan", first_pairs)
    near_in = lax.ppermute(block, "chan", near_pairs)
    coeffs = lag_rows(freq_count, window_count)
    left = left_factors(block, coeffs, switch(True, False), "left_own")
    parts = split(block)
    first_flags = lax.ppermute(quality, "chan", first_pairs)[0]
    near_flags = lax.ppermute(quality, "chan", near_pairs)[0]
    second_flags = lax.ppermute(quality, "chan", second_pairs)[0]
    special = among([0, half - 1])
    first_switch = switch(me == 0, special, quality[0], near_flags, first_flags)
    second_switch = switch(
        among([t for _, t in second_pairs]), among([t for _, t in late_near]), quality[0] * second_flags
    )

    late_part, left = lax.optimization_barrier((parts[0], left))
    second_first = lax.ppermute(late_part, "chan", second_pairs)
    left_alt = left_factors(first_in, coeffs, switch(special, False), "left_first", common=False)
    near, far, back = first_sums(first_switch, left, left_alt, near_in, first_in, block)
    late_part, near = lax.optimization_barrier((parts[1], near))
    second_last = lax.ppermute(late_part, "chan", second_pairs)
    first_returned = lax.ppermute(back, "chan", first_back)
    side_returned = lax.ppermute(near, "chan", side_pairs)

    second_switch, first_returned = lax.optimization_barrier((second_switch, first_returned))
    total, = second_sums(second_switch, left, second_first, 0)
    near = jnp.where(among([half - 1, count - 1]), side_returned, near)
    near = jnp.where(me == half - 2, far, near)
    far = jnp.where(among([s for s, _ in first_far]), first_returned, far)
    near, far, back = second_sums(
        second_switch, left, second_last, parts[0].shape[0], [total, near, far, back]
    )
    second_returned = lax.ppermute(back, "chan", second_back)
    near = jnp.where(me == 0, second_returned, near)
    far = jnp.where(among([s for s, _ in second_far]), second_returned, far)
    return near[None], far[None]


def solution(mesh):
    return jax.shard_map(
        local,
        mesh=mesh,
        in_specs=(P(None, None, None, ("grp", "chan")), P(("grp", "chan"), None)),
        out_specs=(P(("grp", "chan"), None, None, None), P(("grp", "chan"), None, None, None)),
        check_vma=False,
    )
```

```python
import functools
import math

import jax
import jax.numpy as jnp
from jax import lax
from jax.experimental import pallas as pl
from jax.experimental.pallas import tpu as pltpu
from jax.sharding import PartitionSpec as P

HL = 4
LAGS = 2 * HL + 1
STEP = 1024
PARTS = (3, 8)
PARAMS = pltpu.CompilerParams(vmem_limit_bytes=16 * 1024 * 1024)


def lag_rows(freq_count, window_count):
    per_bin = 2 * window_count
    row = jnp.arange(freq_count * per_bin, dtype=jnp.int32)
    freq_values = (row // per_bin).astype(jnp.float32)
    sign = jnp.where(row % per_bin < window_count, 1.0, -1.0)
    lag_values = jnp.arange(HL + 1, dtype=jnp.float32)
    phases = jnp.pi / freq_count * lag_values[:, None] * freq_values[None, :]
    factor = 1.0 / math.sqrt(window_count * freq_count)
    cos_part = jnp.cos(phases) * factor
    sin_part = -jnp.sin(phases[1:]) * factor * sign[None, :]
    return jnp.concatenate([cos_part, sin_part], axis=0).astype(jnp.bfloat16)


def split_kernel(middle, x_ref, first_ref, last_ref):
    step = pl.program_id(0)

    @pl.when(step < middle)
    def _():
        first_ref[...] = x_ref[...]

    @pl.when(step >= middle)
    def _():
        last_ref[...] = x_ref[...]


def split(x):
    rows, cols = x.shape
    steps = rows // STEP
    middle = steps * PARTS[0] // PARTS[1]
    return pl.pallas_call(
        functools.partial(split_kernel, middle),
        grid=(steps,),
        in_specs=[pl.BlockSpec((STEP, cols), lambda s: (s, 0))],
        out_specs=[
            pl.BlockSpec((STEP, cols), lambda s: (jnp.minimum(s, middle - 1), 0)),
            pl.BlockSpec((STEP, cols), lambda s: (jnp.maximum(s - middle, 0), 0)),
        ],
        out_shape=[jax.ShapeDtypeStruct((n * STEP, cols), x.dtype) for n in (middle, steps - middle)],
        compiler_params=PARAMS,
        cost_estimate=pl.CostEstimate(flops=0, bytes_accessed=4 * rows * cols, transcendentals=0),
        name="split",
    )(x)


def turn_kernel(active_ref, x_ref, plain_ref, swapped_ref):
    @pl.when(active_ref[0] != 0)
    def _():
        rows, cols = x_ref.shape
        same = lax.broadcasted_iota(jnp.int32, (cols, cols), 0) == lax.broadcasted_iota(jnp.int32, (cols, cols), 1)
        eye = jnp.where(same, 1.0, 0.0).astype(jnp.bfloat16)
        source = lax.broadcasted_iota(jnp.int32, (2 * cols, 2 * cols), 0)
        target = lax.broadcasted_iota(jnp.int32, (2 * cols, 2 * cols), 1)
        exchange = jnp.where((source ^ 4) == target, 1.0, 0.0).astype(jnp.bfloat16)
        plain = lax.dot_general(eye, x_ref[...], (((1,), (1,)), ((), ())), preferred_element_type=jnp.float32)
        plain = plain.astype(jnp.bfloat16)
        plain_ref[...] = plain
        for t in range(0, rows, 2 * cols):
            swapped = jnp.dot(plain[:, t:t + 2 * cols], exchange, preferred_element_type=jnp.float32)
            swapped_ref[:, t:t + 2 * cols] = swapped.astype(jnp.bfloat16)


def turn(x, switch, name, common=True):
    rows, cols = x.shape
    out = jax.ShapeDtypeStruct((cols, rows), jnp.bfloat16)
    return pl.pallas_call(
        turn_kernel,
        grid_spec=pltpu.PrefetchScalarGridSpec(
            num_scalar_prefetch=1,
            grid=(rows // STEP,),
            in_specs=[pl.BlockSpec((STEP, cols), lambda s, on: (s * on[0], 0))],
            out_specs=[pl.BlockSpec((cols, STEP), lambda s, on: (0, s * on[0]))] * 2,
        ),
        out_shape=[out, out],
        compiler_params=PARAMS,
        cost_estimate=pl.CostEstimate(flops=0, bytes_accessed=6 * rows * cols if common else 0, transcendentals=0),
        name=name,
    )(switch, x)


def write_lags(out, acc, at, cols, mirrored):
    for lag in range(LAGS):
        k = abs(lag - HL)
        value = acc[k * cols:(k + 1) * cols, at]
        if k:
            odd = acc[(HL + k) * cols:(HL + k + 1) * cols, at]
            value = value + odd if lag > HL else value - odd
        value = value.astype(jnp.bfloat16)
        if mirrored:
            out[LAGS - 1 - lag] = value.T
        else:
            out[lag] = value


def scale(scaled, plain, swapped, coeff_ref):
    cols = plain.shape[0]
    for k in range(LAGS):
        part = plain if k <= HL else swapped
        scaled[k * cols:(k + 1) * cols, :] = part * coeff_ref[k:k + 1, :]


def weigh(x, window_weights):
    rows, cols = x.shape
    window = lax.broadcasted_iota(jnp.int32, (16, cols), 0) % len(window_weights)
    weights = jnp.zeros((16, cols), jnp.float32)
    for w, weight in enumerate(window_weights):
        weights = jnp.where(window == w, weight.astype(jnp.float32), weights)
    weights = jnp.broadcast_to(weights.astype(jnp.bfloat16)[None], (rows // 16, 16, cols))
    return x * weights.reshape(rows, cols)


def first_kernel(windows, switch_ref, plain_ref, swapped_ref, plain_alt, swapped_alt, coeff_ref, near_ref, first_ref,
                 own_ref, near_out, far_out, back_out, acc, scaled):
    step = pl.program_id(0)
    cols = plain_ref.shape[0]
    near_mirrored, special = switch_ref[0], switch_ref[1]

    @pl.when(step == 0)
    def _():
        acc[...] = jnp.zeros_like(acc)

    plain = jnp.where(special != 0, plain_alt[...], plain_ref[...])
    swapped = jnp.where(special != 0, swapped_alt[...], swapped_ref[...])
    scale(scaled, plain, swapped, coeff_ref)
    flags = [[switch_ref[2 + part * windows + w] for w in range(windows)] for part in range(3)]
    near_weights = [jnp.where(special != 0, first, own) * near for own, near, first in zip(*flags)]
    near = weigh(near_ref[...], near_weights)
    far = weigh(jnp.where(special != 0, own_ref[...], first_ref[...]), [own * first for own, _, first in zip(*flags)])
    acc[...] += jnp.dot(scaled[...], jnp.concatenate([near, far], axis=1), preferred_element_type=jnp.float32)

    @pl.when(step == pl.num_programs(0) - 1)
    def _():
        near_at, far_at = slice(0, cols), slice(cols, 2 * cols)

        @pl.when(special == 0)
        def _():
            write_lags(back_out, acc, far_at, cols, True)
            write_lags(far_out, acc, far_at, cols, False)

        @pl.when(special != 0)
        def _():
            write_lags(back_out, acc, far_at, cols, False)
            write_lags(far_out, acc, far_at, cols, True)

        pl.when(near_mirrored == 0)(lambda: write_lags(near_out, acc, near_at, cols, False))
        pl.when(near_mirrored != 0)(lambda: write_lags(near_out, acc, near_at, cols, True))


def first_sums(switch, own, alt, coeffs, near_in, first_in, block):
    rows, cols = block.shape
    windows = (switch.shape[0] - 2) // 3
    result = jax.ShapeDtypeStruct((LAGS, cols, cols), jnp.bfloat16)
    left = pl.BlockSpec((cols, STEP), lambda s, on: (0, s * (1 - on[1])))
    left_alt = pl.BlockSpec((cols, STEP), lambda s, on: (0, s * on[1]))
    right = pl.BlockSpec((STEP, cols), lambda s, on: (s, 0))
    right_usual = pl.BlockSpec((STEP, cols), lambda s, on: (s * (1 - on[1]), 0))
    right_special = pl.BlockSpec((STEP, cols), lambda s, on: (s * on[1], 0))
    return pl.pallas_call(
        functools.partial(first_kernel, windows),
        grid_spec=pltpu.PrefetchScalarGridSpec(
            num_scalar_prefetch=1,
            grid=(rows // STEP,),
            in_specs=[left, left, left_alt, left_alt, pl.BlockSpec((LAGS, STEP), lambda s, on: (0, s)),
                      right, right_usual, right_special],
            out_specs=[pl.BlockSpec(result.shape, lambda s, on: (0, 0, 0))] * 3,
            scratch_shapes=[pltpu.VMEM((LAGS * cols, 2 * cols), jnp.float32),
                            pltpu.VMEM((LAGS * cols, STEP), jnp.bfloat16)],
        ),
        out_shape=[result] * 3,
        compiler_params=PARAMS,
        cost_estimate=pl.CostEstimate(
            flops=4 * LAGS * cols * cols * rows, bytes_accessed=8 * rows * cols, transcendentals=0
        ),
        name="first_sums",
    )(switch, *own, *alt, coeffs, near_in, first_in, block)


def second_kernel(windows, first, switch_ref, plain_ref, swapped_ref, coeff_ref, partner_ref, *rest):
    on, late_near = switch_ref[0], switch_ref[1]
    step = pl.program_id(0)
    cols = plain_ref.shape[0]
    if first:
        acc, scaled = rest
    else:
        acc_in, near_in, far_in, back_in, near_out, far_out, back_out, acc, scaled = rest

    @pl.when(on != 0)
    def _():
        @pl.when(step == 0)
        def _():
            acc[...] = jnp.zeros_like(acc) if first else acc_in[...]

        scale(scaled, plain_ref[...], swapped_ref[...], coeff_ref)
        partner = weigh(partner_ref[...], [switch_ref[2 + w] for w in range(windows)])
        acc[...] += jnp.dot(scaled[...], partner, preferred_element_type=jnp.float32)

    if not first:
        @pl.when(step == pl.num_programs(0) - 1)
        def _():
            here = slice(0, cols)

            @pl.when((on != 0) & (late_near == 0))
            def _():
                write_lags(back_out, acc, here, cols, True)
                write_lags(far_out, acc, here, cols, False)

            @pl.when((on == 0) | (late_near != 0))
            def _():
                back_out[...] = back_in[...]
                far_out[...] = far_in[...]

            pl.when(late_near != 0)(lambda: write_lags(near_out, acc, here, cols, False))

            @pl.when(late_near == 0)
            def _():
                near_out[...] = near_in[...]


def second_sums(switch, own, coeffs, partner, start, earlier=None):
    rows, cols = partner.shape
    windows = switch.shape[0] - 2
    skip = start // STEP
    total = jax.ShapeDtypeStruct((LAGS * cols, cols), jnp.float32)
    total_spec = pl.BlockSpec(total.shape, lambda s, on: (0, 0))
    result = jax.ShapeDtypeStruct((LAGS, cols, cols), jnp.bfloat16)
    result_spec = pl.BlockSpec(result.shape, lambda s, on: (0, 0, 0))
    left = pl.BlockSpec((cols, STEP), lambda s, on: (0, s * on[0] + skip))
    in_specs = [left, left, pl.BlockSpec((LAGS, STEP), lambda s, on: (0, s * on[0] + skip)),
                pl.BlockSpec((STEP, cols), lambda s, on: (s * on[0], 0))]
    scratch = [pltpu.VMEM((LAGS * cols, STEP), jnp.bfloat16)]
    if earlier is None:
        out_shape, out_specs, earlier = [total], [total_spec], []
    else:
        out_shape, out_specs = [result] * 3, [result_spec] * 3
        in_specs += [total_spec] + [result_spec] * 3
        scratch = [pltpu.VMEM(total.shape, jnp.float32)] + scratch
    return pl.pallas_call(
        functools.partial(second_kernel, windows, not earlier),
        grid_spec=pltpu.PrefetchScalarGridSpec(
            num_scalar_prefetch=1,
            grid=(rows // STEP,),
            in_specs=in_specs,
            out_specs=out_specs,
            scratch_shapes=scratch,
        ),
        out_shape=out_shape,
        compiler_params=PARAMS,
        cost_estimate=pl.CostEstimate(
            flops=2 * LAGS * cols * cols * rows, bytes_accessed=6 * rows * cols, transcendentals=0
        ),
        name="second_last" if earlier else "second_part",
    )(switch, *own, coeffs, partner, *earlier)


def local(spectra, quality):
    count = lax.axis_size("chan")
    half = count // 2
    me = lax.axis_index("chan")
    freq_count, _, window_count, cols = spectra.shape
    block = spectra.reshape(-1, cols)

    first_far, second_far = [], []
    for p in range(half):
        if p in (0, half - 1):
            first_far.append((p + half, p))
        elif p % 2 == 0 and p >= half // 2:
            first_far.append((p, p + half))
        elif p in (1, 3):
            second_far.append((p, p + half))
        else:
            second_far.append((p + half, p))
    late_near = [(2, 1), (4, 3)]
    first_pairs = first_far + [(0, 1), (half - 1, half - 2)]
    second_pairs = second_far + late_near
    near_pairs = [(d + 1, d) for d in range(1, count - 1) if d not in (1, 3, half - 2, half - 1)]
    near_pairs += [(0, half - 1), (half - 1, 0)]
    back_pairs = [(t, s) for s, t in first_far + second_far] + [(1, 0)]
    side_pairs = [(0, half - 1), (half - 1, count - 1)]

    def among(devices):
        return functools.reduce(jnp.logical_or, [me == d for d in devices])

    def switch(on, other, *weights):
        flags = jnp.stack([jnp.asarray(on), jnp.asarray(other)]).astype(jnp.int32)
        return jnp.concatenate([flags, *weights])

    near_in = lax.ppermute(block, "chan", near_pairs)
    first_in = lax.ppermute(block, "chan", first_pairs)
    coeffs = lag_rows(freq_count, window_count)
    own = turn(block, switch(True, False), "turn_own")
    parts = split(block)
    first_flags = lax.ppermute(quality, "chan", first_pairs)[0]
    near_flags = lax.ppermute(quality, "chan", near_pairs)[0]
    second_flags = lax.ppermute(quality, "chan", second_pairs)[0]
    special = among([0, half - 1])
    first_switch = switch(me == 0, special, quality[0], near_flags, first_flags)
    second_switch = switch(
        among([t for _, t in second_pairs]), among([t for _, t in late_near]), quality[0] * second_flags
    )

    near_in, parts, own, coeffs, first_in = lax.optimization_barrier((near_in, parts, own, coeffs, first_in))
    second_in = [lax.ppermute(part, "chan", second_pairs) for part in parts]
    alt = turn(first_in, switch(special, False), "turn_first", common=False)
    near, far, back = first_sums(first_switch, own, alt, coeffs, near_in, first_in, block)
    side_returned = lax.ppermute(near, "chan", side_pairs)
    second_switch, near = lax.optimization_barrier((second_switch, near))
    total, = second_sums(second_switch, own, coeffs, second_in[0], 0)

    near = jnp.where(among([half - 1, count - 1]), side_returned, near)
    near = jnp.where(me == half - 2, far, near)
    near, far, back = second_sums(
        second_switch, own, coeffs, second_in[1], parts[0].shape[0], [total, near, far, back]
    )
    returned = lax.ppermute(back, "chan", back_pairs)
    near = jnp.where(me == 0, returned, near)
    far = jnp.where(among([s for s, _ in first_far + second_far]), returned, far)
    return near[None], far[None]


def solution(mesh):
    return jax.shard_map(
        local,
        mesh=mesh,
        in_specs=(P(None, None, None, ("grp", "chan")), P(("grp", "chan"), None)),
        out_specs=(P(("grp", "chan"), None, None, None), P(("grp", "chan"), None, None, None)),
        check_vma=False,
    )
```

```python
import functools
import math

import jax
import jax.numpy as jnp
from jax import lax
from jax.experimental import pallas as pl
from jax.experimental.pallas import tpu as pltpu
from jax.sharding import PartitionSpec as P

HL = 4
LAGS = 2 * HL + 1
STEP = 1024
PARTS = (3, 8)
PARAMS = pltpu.CompilerParams(vmem_limit_bytes=16 * 1024 * 1024)


def lag_rows(freq_count, window_count):
    per_bin = 2 * window_count
    row = jnp.arange(freq_count * per_bin, dtype=jnp.int32)
    freq_values = (row // per_bin).astype(jnp.float32)
    sign = jnp.where(row % per_bin < window_count, 1.0, -1.0)
    lag_values = jnp.arange(HL + 1, dtype=jnp.float32)
    phases = jnp.pi / freq_count * lag_values[:, None] * freq_values[None, :]
    factor = 1.0 / math.sqrt(window_count * freq_count)
    cos_part = jnp.cos(phases) * factor
    sin_part = -jnp.sin(phases[1:]) * factor * sign[None, :]
    return jnp.concatenate([cos_part, sin_part], axis=0).astype(jnp.bfloat16)


def split_kernel(middle, windows, flags_ref, x_ref, first_ref, last_ref):
    step = pl.program_id(0)
    masked = weigh(x_ref[...], [flags_ref[w] for w in range(windows)])

    @pl.when(step < middle)
    def _():
        first_ref[...] = masked

    @pl.when(step >= middle)
    def _():
        last_ref[...] = masked


def split(flags, x):
    rows, cols = x.shape
    steps = rows // STEP
    middle = steps * PARTS[0] // PARTS[1]
    return pl.pallas_call(
        functools.partial(split_kernel, middle, flags.shape[0]),
        grid_spec=pltpu.PrefetchScalarGridSpec(
            num_scalar_prefetch=1,
            grid=(steps,),
            in_specs=[pl.BlockSpec((STEP, cols), lambda s, on: (s, 0))],
            out_specs=[
                pl.BlockSpec((STEP, cols), lambda s, on: (jnp.minimum(s, middle - 1), 0)),
                pl.BlockSpec((STEP, cols), lambda s, on: (jnp.maximum(s - middle, 0), 0)),
            ],
        ),
        out_shape=[jax.ShapeDtypeStruct((n * STEP, cols), x.dtype) for n in (middle, steps - middle)],
        compiler_params=PARAMS,
        cost_estimate=pl.CostEstimate(flops=rows * cols, bytes_accessed=4 * rows * cols, transcendentals=0),
        name="split",
    )(flags, x)


def turn_kernel(active_ref, x_ref, plain_ref, swapped_ref):
    @pl.when(active_ref[0] != 0)
    def _():
        rows, cols = x_ref.shape
        same = lax.broadcasted_iota(jnp.int32, (cols, cols), 0) == lax.broadcasted_iota(jnp.int32, (cols, cols), 1)
        eye = jnp.where(same, 1.0, 0.0).astype(jnp.bfloat16)
        source = lax.broadcasted_iota(jnp.int32, (2 * cols, 2 * cols), 0)
        target = lax.broadcasted_iota(jnp.int32, (2 * cols, 2 * cols), 1)
        exchange = jnp.where((source ^ 4) == target, 1.0, 0.0).astype(jnp.bfloat16)
        plain = lax.dot_general(eye, x_ref[...], (((1,), (1,)), ((), ())), preferred_element_type=jnp.float32)
        plain = plain.astype(jnp.bfloat16)
        plain_ref[...] = plain
        for t in range(0, rows, 2 * cols):
            swapped = jnp.dot(plain[:, t:t + 2 * cols], exchange, preferred_element_type=jnp.float32)
            swapped_ref[:, t:t + 2 * cols] = swapped.astype(jnp.bfloat16)


def turn(x, switch, name, common=True):
    rows, cols = x.shape
    out = jax.ShapeDtypeStruct((cols, rows), jnp.bfloat16)
    return pl.pallas_call(
        turn_kernel,
        grid_spec=pltpu.PrefetchScalarGridSpec(
            num_scalar_prefetch=1,
            grid=(rows // STEP,),
            in_specs=[pl.BlockSpec((STEP, cols), lambda s, on: (s * on[0], 0))],
            out_specs=[pl.BlockSpec((cols, STEP), lambda s, on: (0, s * on[0]))] * 2,
        ),
        out_shape=[out, out],
        compiler_params=PARAMS,
        cost_estimate=pl.CostEstimate(flops=0, bytes_accessed=6 * rows * cols if common else 0, transcendentals=0),
        name=name,
    )(switch, x)


def write_lags(out, acc, at, cols, mirrored):
    for lag in range(LAGS):
        k = abs(lag - HL)
        value = acc[k * cols:(k + 1) * cols, at]
        if k:
            odd = acc[(HL + k) * cols:(HL + k + 1) * cols, at]
            value = value + odd if lag > HL else value - odd
        value = value.astype(jnp.bfloat16)
        if mirrored:
            out[LAGS - 1 - lag] = value.T
        else:
            out[lag] = value


def scale(scaled, plain, swapped, coeff_ref):
    cols = plain.shape[0]
    for k in range(LAGS):
        part = plain if k <= HL else swapped
        scaled[k * cols:(k + 1) * cols, :] = part * coeff_ref[k:k + 1, :]


def weigh(x, window_weights):
    rows, cols = x.shape
    window = lax.broadcasted_iota(jnp.int32, (16, cols), 0) % len(window_weights)
    weights = jnp.zeros((16, cols), jnp.float32)
    for w, weight in enumerate(window_weights):
        weights = jnp.where(window == w, weight.astype(jnp.float32), weights)
    weights = jnp.broadcast_to(weights.astype(jnp.bfloat16)[None], (rows // 16, 16, cols))
    return x * weights.reshape(rows, cols)


def first_kernel(windows, switch_ref, plain_ref, swapped_ref, plain_alt, swapped_alt, coeff_ref, near_ref, near_alt,
                 first_ref, own_ref, near_out, far_out, back_out, acc, scaled):
    step = pl.program_id(0)
    cols = plain_ref.shape[0]
    near_mirrored, special, near_second = switch_ref[0], switch_ref[1], switch_ref[2]

    @pl.when(step == 0)
    def _():
        acc[...] = jnp.zeros_like(acc)

    plain = jnp.where(special != 0, plain_alt[...], plain_ref[...])
    swapped = jnp.where(special != 0, swapped_alt[...], swapped_ref[...])
    scale(scaled, plain, swapped, coeff_ref)
    flags = [[switch_ref[3 + part * windows + w] for w in range(windows)] for part in range(3)]
    near_weights = [jnp.where(special != 0, first, own) * near for own, near, first in zip(*flags)]
    near = weigh(jnp.where(near_second != 0, near_alt[...], near_ref[...]), near_weights)
    far = weigh(jnp.where(special != 0, own_ref[...], first_ref[...]), [own * first for own, _, first in zip(*flags)])
    acc[...] += jnp.dot(scaled[...], jnp.concatenate([near, far], axis=1), preferred_element_type=jnp.float32)

    @pl.when(step == pl.num_programs(0) - 1)
    def _():
        near_at, far_at = slice(0, cols), slice(cols, 2 * cols)

        @pl.when(special == 0)
        def _():
            write_lags(back_out, acc, far_at, cols, True)
            write_lags(far_out, acc, far_at, cols, False)

        @pl.when(special != 0)
        def _():
            write_lags(back_out, acc, far_at, cols, False)
            write_lags(far_out, acc, far_at, cols, True)

        pl.when(near_mirrored == 0)(lambda: write_lags(near_out, acc, near_at, cols, False))
        pl.when(near_mirrored != 0)(lambda: write_lags(near_out, acc, near_at, cols, True))


def first_sums(switch, own, alt, coeffs, near_in, near_alt, first_in, block):
    rows, cols = block.shape
    windows = (switch.shape[0] - 3) // 3
    result = jax.ShapeDtypeStruct((LAGS, cols, cols), jnp.bfloat16)
    left = pl.BlockSpec((cols, STEP), lambda s, on: (0, s * (1 - on[1])))
    left_alt = pl.BlockSpec((cols, STEP), lambda s, on: (0, s * on[1]))
    right_near = pl.BlockSpec((STEP, cols), lambda s, on: (s * (1 - on[2]), 0))
    right_near_alt = pl.BlockSpec((STEP, cols), lambda s, on: (s * on[2], 0))
    right_usual = pl.BlockSpec((STEP, cols), lambda s, on: (s * (1 - on[1]), 0))
    right_special = pl.BlockSpec((STEP, cols), lambda s, on: (s * on[1], 0))
    return pl.pallas_call(
        functools.partial(first_kernel, windows),
        grid_spec=pltpu.PrefetchScalarGridSpec(
            num_scalar_prefetch=1,
            grid=(rows // STEP,),
            in_specs=[left, left, left_alt, left_alt, pl.BlockSpec((LAGS, STEP), lambda s, on: (0, s)),
                      right_near, right_near_alt, right_usual, right_special],
            out_specs=[pl.BlockSpec(result.shape, lambda s, on: (0, 0, 0))] * 3,
            scratch_shapes=[pltpu.VMEM((LAGS * cols, 2 * cols), jnp.float32),
                            pltpu.VMEM((LAGS * cols, STEP), jnp.bfloat16)],
        ),
        out_shape=[result] * 3,
        compiler_params=PARAMS,
        cost_estimate=pl.CostEstimate(
            flops=4 * LAGS * cols * cols * rows, bytes_accessed=8 * rows * cols, transcendentals=0
        ),
        name="first_sums",
    )(switch, *own, *alt, coeffs, near_in, near_alt, first_in, block)


def second_kernel(windows, first, switch_ref, plain_ref, swapped_ref, coeff_ref, partner_ref, *rest):
    step = pl.program_id(0)
    cols = plain_ref.shape[0]
    if first:
        acc, scaled = rest
    else:
        acc_in, far_in, back_in, far_out, back_out, acc, scaled = rest

    @pl.when(switch_ref[0] != 0)
    def _():
        @pl.when(step == 0)
        def _():
            acc[...] = jnp.zeros_like(acc) if first else acc_in[...]

        scale(scaled, plain_ref[...], swapped_ref[...], coeff_ref)
        partner = weigh(partner_ref[...], [switch_ref[2 + w] for w in range(windows)])
        acc[...] += jnp.dot(scaled[...], partner, preferred_element_type=jnp.float32)

    if not first:
        @pl.when(step == pl.num_programs(0) - 1)
        def _():
            here = slice(0, cols)

            @pl.when(switch_ref[0] != 0)
            def _():
                write_lags(back_out, acc, here, cols, True)
                write_lags(far_out, acc, here, cols, False)

            @pl.when(switch_ref[0] == 0)
            def _():
                back_out[...] = back_in[...]
                far_out[...] = far_in[...]


def second_sums(switch, own, coeffs, partner, start, earlier=None):
    rows, cols = partner.shape
    skip = start // STEP
    total = jax.ShapeDtypeStruct((LAGS * cols, cols), jnp.float32)
    total_spec = pl.BlockSpec(total.shape, lambda s, on: (0, 0))
    result = jax.ShapeDtypeStruct((LAGS, cols, cols), jnp.bfloat16)
    result_spec = pl.BlockSpec(result.shape, lambda s, on: (0, 0, 0))
    left = pl.BlockSpec((cols, STEP), lambda s, on: (0, s * on[0] + skip))
    in_specs = [left, left, pl.BlockSpec((LAGS, STEP), lambda s, on: (0, s * on[0] + skip)),
                pl.BlockSpec((STEP, cols), lambda s, on: (s * on[0], 0))]
    scratch = [pltpu.VMEM((LAGS * cols, STEP), jnp.bfloat16)]
    if earlier is None:
        out_shape, out_specs, earlier = [total], [total_spec], []
    else:
        out_shape, out_specs = [result] * 2, [result_spec] * 2
        in_specs += [total_spec] + [result_spec] * 2
        scratch = [pltpu.VMEM(total.shape, jnp.float32)] + scratch
    return pl.pallas_call(
        functools.partial(second_kernel, switch.shape[0] - 2, not earlier),
        grid_spec=pltpu.PrefetchScalarGridSpec(
            num_scalar_prefetch=1,
            grid=(rows // STEP,),
            in_specs=in_specs,
            out_specs=out_specs,
            scratch_shapes=scratch,
        ),
        out_shape=out_shape,
        compiler_params=PARAMS,
        cost_estimate=pl.CostEstimate(
            flops=2 * LAGS * cols * cols * rows, bytes_accessed=6 * rows * cols, transcendentals=0
        ),
        name="second_last" if earlier else "second_part",
    )(switch, *own, coeffs, partner, *earlier)


def late_kernel(windows, middle, switch_ref, plain_ref, swapped_ref, coeff_ref, first_ref, last_ref, near_out, acc, scaled):
    step = pl.program_id(0)
    cols = plain_ref.shape[0]

    @pl.when(switch_ref[0] != 0)
    def _():
        @pl.when(step == 0)
        def _():
            acc[...] = jnp.zeros_like(acc)

        scale(scaled, plain_ref[...], swapped_ref[...], coeff_ref)
        partner = jnp.where(step < middle, first_ref[...], last_ref[...])
        partner = weigh(partner, [switch_ref[2 + w] for w in range(windows)])
        acc[...] += jnp.dot(scaled[...], partner, preferred_element_type=jnp.float32)
        pl.when(step == pl.num_programs(0) - 1)(lambda: write_lags(near_out, acc, slice(0, cols), cols, False))


def late_sums(switch, own, coeffs, parts):
    cols, rows = own[0].shape
    middle = parts[0].shape[0] // STEP
    left = pl.BlockSpec((cols, STEP), lambda s, on: (0, s * on[0]))
    result = jax.ShapeDtypeStruct((LAGS, cols, cols), jnp.bfloat16)
    return pl.pallas_call(
        functools.partial(late_kernel, switch.shape[0] - 2, middle),
        grid_spec=pltpu.PrefetchScalarGridSpec(
            num_scalar_prefetch=1,
            grid=(rows // STEP,),
            in_specs=[left, left, pl.BlockSpec((LAGS, STEP), lambda s, on: (0, s * on[0])),
                      pl.BlockSpec((STEP, cols), lambda s, on: (jnp.minimum(s, middle - 1) * on[0], 0)),
                      pl.BlockSpec((STEP, cols), lambda s, on: (jnp.maximum(s - middle, 0) * on[0], 0))],
            out_specs=pl.BlockSpec(result.shape, lambda s, on: (0, 0, 0)),
            scratch_shapes=[pltpu.VMEM((LAGS * cols, cols), jnp.float32),
                            pltpu.VMEM((LAGS * cols, STEP), jnp.bfloat16)],
        ),
        out_shape=result,
        compiler_params=PARAMS,
        cost_estimate=pl.CostEstimate(flops=0, bytes_accessed=0, transcendentals=0),
        name="late_near",
    )(switch, *own, coeffs, *parts)


def local(spectra, quality):
    count = lax.axis_size("chan")
    half = count // 2
    me = lax.axis_index("chan")
    freq_count, _, window_count, cols = spectra.shape
    block = spectra.reshape(-1, cols)

    first_far, second_far = [], []
    for p in range(half):
        if p in (0, half - 1):
            first_far.append((p + half, p))
        elif p % 2 == 0 and p >= half // 2:
            first_far.append((p, p + half))
        elif p in (1, 3):
            second_far.append((p, p + half))
        else:
            second_far.append((p + half, p))
    late_near = [(2, 1), (4, 3)]
    first_pairs = first_far + [(0, 1), (half - 1, half - 2)]
    second_pairs = second_far + late_near
    near_pairs = [(d + 1, d) for d in range(1, count - 1) if d not in (1, 3, half - 2, half - 1)]
    near_pairs += [(0, half - 1), (half - 1, 0)]
    receivers = {t for _, t in first_far}
    later_pairs = [pair for pair in near_pairs if receivers.intersection(pair)]
    early_pairs = [pair for pair in near_pairs if not receivers.intersection(pair)]
    back_pairs = [(t, s) for s, t in first_far + second_far] + [(1, 0)]
    side_pairs = [(0, half - 1), (half - 1, count - 1)]

    def among(devices):
        return functools.reduce(jnp.logical_or, [me == d for d in devices])

    def switch(on, other, *weights):
        flags = jnp.stack([jnp.asarray(on), jnp.asarray(other)]).astype(jnp.int32)
        return jnp.concatenate([flags, *weights])

    near_in = lax.ppermute(block, "chan", early_pairs)
    first_in = lax.ppermute(block, "chan", first_pairs)
    near_alt = lax.ppermute(block, "chan", later_pairs)
    coeffs = lag_rows(freq_count, window_count)
    own = turn(block, switch(True, False), "turn_own")
    parts = split(quality[0], block)
    first_flags = lax.ppermute(quality, "chan", first_pairs)[0]
    near_flags = lax.ppermute(quality, "chan", near_pairs)[0]
    special = among([0, half - 1])
    near_later = among([t for _, t in later_pairs])
    first_switch = jnp.concatenate(
        [jnp.stack([me == 0, special, near_later]).astype(jnp.int32), quality[0], near_flags, first_flags]
    )
    second_switch = switch(among([t for _, t in second_far]), False, quality[0])
    late_switch = switch(among([t for _, t in late_near]), False, quality[0])

    near_in, first_in, near_alt, parts, own, coeffs, first_switch = lax.optimization_barrier(
        (near_in, first_in, near_alt, parts, own, coeffs, first_switch)
    )
    second_in = [lax.ppermute(part, "chan", second_pairs) for part in parts]
    alt = turn(first_in, switch(special, False), "turn_first", common=False)
    near, far, back = first_sums(first_switch, own, alt, coeffs, near_in, near_alt, first_in, block)
    side_returned = lax.ppermute(near, "chan", side_pairs)
    second_switch, near = lax.optimization_barrier((second_switch, near))
    total, = second_sums(second_switch, own, coeffs, second_in[0], 0)
    far, back = second_sums(second_switch, own, coeffs, second_in[1], parts[0].shape[0], [total, far, back])
    returned = lax.ppermute(back, "chan", back_pairs)
    late_switch, far = lax.optimization_barrier((late_switch, far))
    late = late_sums(late_switch, own, coeffs, second_in)

    near = jnp.where(among([half - 1, count - 1]), side_returned, near)
    near = jnp.where(me == half - 2, far, near)
    near = jnp.where(among([t for _, t in late_near]), late, near)
    near = jnp.where(me == 0, returned, near)
    far = jnp.where(among([s for s, _ in first_far + second_far]), returned, far)
    return near[None], far[None]


def solution(mesh):
    return jax.shard_map(
        local,
        mesh=mesh,
        in_specs=(P(None, None, None, ("grp", "chan")), P(("grp", "chan"), None)),
        out_specs=(P(("grp", "chan"), None, None, None), P(("grp", "chan"), None, None, None)),
        check_vma=False,
    )
```

```python
import functools
import math

import jax
import jax.numpy as jnp
from jax import lax
from jax.experimental import pallas as pl
from jax.experimental.pallas import tpu as pltpu
from jax.sharding import PartitionSpec as P

HL = 4
LAGS = 2 * HL + 1
STEP = 1024
PARTS = (3, 8)
PARAMS = pltpu.CompilerParams(vmem_limit_bytes=16 * 1024 * 1024)


def lag_rows(freq_count, window_count):
    per_bin = 2 * window_count
    row = jnp.arange(freq_count * per_bin, dtype=jnp.int32)
    freq_values = (row // per_bin).astype(jnp.float32)
    sign = jnp.where(row % per_bin < window_count, 1.0, -1.0)
    lag_values = jnp.arange(HL + 1, dtype=jnp.float32)
    phases = jnp.pi / freq_count * lag_values[:, None] * freq_values[None, :]
    factor = 1.0 / math.sqrt(window_count * freq_count)
    cos_part = jnp.cos(phases) * factor
    sin_part = -jnp.sin(phases[1:]) * factor * sign[None, :]
    return jnp.concatenate([cos_part, sin_part], axis=0).astype(jnp.bfloat16)


def split_kernel(middle, x_ref, first_ref, last_ref):
    step = pl.program_id(0)

    @pl.when(step < middle)
    def _():
        first_ref[...] = x_ref[...]

    @pl.when(step >= middle)
    def _():
        last_ref[...] = x_ref[...]


def split(x):
    rows, cols = x.shape
    steps = rows // STEP
    middle = steps * PARTS[0] // PARTS[1]
    return pl.pallas_call(
        functools.partial(split_kernel, middle),
        grid=(steps,),
        in_specs=[pl.BlockSpec((STEP, cols), lambda s: (s, 0))],
        out_specs=[
            pl.BlockSpec((STEP, cols), lambda s: (jnp.minimum(s, middle - 1), 0)),
            pl.BlockSpec((STEP, cols), lambda s: (jnp.maximum(s - middle, 0), 0)),
        ],
        out_shape=[jax.ShapeDtypeStruct((n * STEP, cols), x.dtype) for n in (middle, steps - middle)],
        compiler_params=PARAMS,
        cost_estimate=pl.CostEstimate(flops=0, bytes_accessed=4 * rows * cols, transcendentals=0),
        name="split",
    )(x)


def turn_kernel(active_ref, x_ref, plain_ref, swapped_ref):
    @pl.when(active_ref[0] != 0)
    def _():
        rows, cols = x_ref.shape
        same = lax.broadcasted_iota(jnp.int32, (cols, cols), 0) == lax.broadcasted_iota(jnp.int32, (cols, cols), 1)
        eye = jnp.where(same, 1.0, 0.0).astype(jnp.bfloat16)
        source = lax.broadcasted_iota(jnp.int32, (2 * cols, 2 * cols), 0)
        target = lax.broadcasted_iota(jnp.int32, (2 * cols, 2 * cols), 1)
        exchange = jnp.where((source ^ 4) == target, 1.0, 0.0).astype(jnp.bfloat16)
        plain = lax.dot_general(eye, x_ref[...], (((1,), (1,)), ((), ())), preferred_element_type=jnp.float32)
        plain = plain.astype(jnp.bfloat16)
        plain_ref[...] = plain
        for t in range(0, rows, 2 * cols):
            swapped = jnp.dot(plain[:, t:t + 2 * cols], exchange, preferred_element_type=jnp.float32)
            swapped_ref[:, t:t + 2 * cols] = swapped.astype(jnp.bfloat16)


def turn(x, switch, name, common=True):
    rows, cols = x.shape
    out = jax.ShapeDtypeStruct((cols, rows), jnp.bfloat16)
    return pl.pallas_call(
        turn_kernel,
        grid_spec=pltpu.PrefetchScalarGridSpec(
            num_scalar_prefetch=1,
            grid=(rows // STEP,),
            in_specs=[pl.BlockSpec((STEP, cols), lambda s, on: (s * on[0], 0))],
            out_specs=[pl.BlockSpec((cols, STEP), lambda s, on: (0, s * on[0]))] * 2,
        ),
        out_shape=[out, out],
        compiler_params=PARAMS,
        cost_estimate=pl.CostEstimate(flops=0, bytes_accessed=6 * rows * cols if common else 0, transcendentals=0),
        name=name,
    )(switch, x)


def write_lags(out, acc, at, cols, mirrored):
    for lag in range(LAGS):
        k = abs(lag - HL)
        value = acc[k * cols:(k + 1) * cols, at]
        if k:
            odd = acc[(HL + k) * cols:(HL + k + 1) * cols, at]
            value = value + odd if lag > HL else value - odd
        value = value.astype(jnp.bfloat16)
        if mirrored:
            out[LAGS - 1 - lag] = value.T
        else:
            out[lag] = value


def scale(scaled, plain, swapped, coeff_ref):
    cols = plain.shape[0]
    for k in range(LAGS):
        part = plain if k <= HL else swapped
        scaled[k * cols:(k + 1) * cols, :] = part * coeff_ref[k:k + 1, :]


def weigh(x, window_weights):
    rows, cols = x.shape
    window = lax.broadcasted_iota(jnp.int32, (16, cols), 0) % len(window_weights)
    weights = jnp.zeros((16, cols), jnp.float32)
    for w, weight in enumerate(window_weights):
        weights = jnp.where(window == w, weight.astype(jnp.float32), weights)
    weights = jnp.broadcast_to(weights.astype(jnp.bfloat16)[None], (rows // 16, 16, cols))
    return x * weights.reshape(rows, cols)


def first_kernel(windows, switch_ref, plain_ref, swapped_ref, plain_alt, swapped_alt, coeff_ref, near_ref, first_ref,
                 own_ref, near_out, far_out, back_out, acc, scaled):
    step = pl.program_id(0)
    cols = plain_ref.shape[0]
    near_mirrored, special = switch_ref[0], switch_ref[1]

    @pl.when(step == 0)
    def _():
        acc[...] = jnp.zeros_like(acc)

    plain = jnp.where(special != 0, plain_alt[...], plain_ref[...])
    swapped = jnp.where(special != 0, swapped_alt[...], swapped_ref[...])
    scale(scaled, plain, swapped, coeff_ref)
    flags = [[switch_ref[2 + part * windows + w] for w in range(windows)] for part in range(3)]
    near_weights = [jnp.where(special != 0, first, own) * near for own, near, first in zip(*flags)]
    near = weigh(near_ref[...], near_weights)
    far = weigh(jnp.where(special != 0, own_ref[...], first_ref[...]), [own * first for own, _, first in zip(*flags)])
    acc[...] += jnp.dot(scaled[...], jnp.concatenate([near, far], axis=1), preferred_element_type=jnp.float32)

    @pl.when(step == pl.num_programs(0) - 1)
    def _():
        near_at, far_at = slice(0, cols), slice(cols, 2 * cols)

        @pl.when(special == 0)
        def _():
            write_lags(back_out, acc, far_at, cols, True)
            write_lags(far_out, acc, far_at, cols, False)

        @pl.when(special != 0)
        def _():
            write_lags(back_out, acc, far_at, cols, False)
            write_lags(far_out, acc, far_at, cols, True)

        pl.when(near_mirrored == 0)(lambda: write_lags(near_out, acc, near_at, cols, False))
        pl.when(near_mirrored != 0)(lambda: write_lags(near_out, acc, near_at, cols, True))


def first_sums(switch, own, alt, coeffs, near_in, first_in, block):
    rows, cols = block.shape
    windows = (switch.shape[0] - 2) // 3
    result = jax.ShapeDtypeStruct((LAGS, cols, cols), jnp.bfloat16)
    left = pl.BlockSpec((cols, STEP), lambda s, on: (0, s * (1 - on[1])))
    left_alt = pl.BlockSpec((cols, STEP), lambda s, on: (0, s * on[1]))
    right = pl.BlockSpec((STEP, cols), lambda s, on: (s, 0))
    right_usual = pl.BlockSpec((STEP, cols), lambda s, on: (s * (1 - on[1]), 0))
    right_special = pl.BlockSpec((STEP, cols), lambda s, on: (s * on[1], 0))
    return pl.pallas_call(
        functools.partial(first_kernel, windows),
        grid_spec=pltpu.PrefetchScalarGridSpec(
            num_scalar_prefetch=1,
            grid=(rows // STEP,),
            in_specs=[left, left, left_alt, left_alt, pl.BlockSpec((LAGS, STEP), lambda s, on: (0, s)),
                      right, right_usual, right_special],
            out_specs=[pl.BlockSpec(result.shape, lambda s, on: (0, 0, 0))] * 3,
            scratch_shapes=[pltpu.VMEM((LAGS * cols, 2 * cols), jnp.float32),
                            pltpu.VMEM((LAGS * cols, STEP), jnp.bfloat16)],
        ),
        out_shape=[result] * 3,
        compiler_params=PARAMS,
        cost_estimate=pl.CostEstimate(
            flops=4 * LAGS * cols * cols * rows, bytes_accessed=8 * rows * cols, transcendentals=0
        ),
        name="first_sums",
    )(switch, *own, *alt, coeffs, near_in, first_in, block)


def second_kernel(windows, first, switch_ref, plain_ref, swapped_ref, coeff_ref, partner_ref, *rest):
    step = pl.program_id(0)
    cols = plain_ref.shape[0]
    if first:
        acc, scaled = rest
    else:
        acc_in, far_in, back_in, far_out, back_out, acc, scaled = rest

    @pl.when(switch_ref[0] != 0)
    def _():
        @pl.when(step == 0)
        def _():
            acc[...] = jnp.zeros_like(acc) if first else acc_in[...]

        scale(scaled, plain_ref[...], swapped_ref[...], coeff_ref)
        partner = weigh(partner_ref[...], [switch_ref[2 + w] for w in range(windows)])
        acc[...] += jnp.dot(scaled[...], partner, preferred_element_type=jnp.float32)

    if not first:
        @pl.when(step == pl.num_programs(0) - 1)
        def _():
            here = slice(0, cols)

            @pl.when(switch_ref[0] != 0)
            def _():
                write_lags(back_out, acc, here, cols, True)
                write_lags(far_out, acc, here, cols, False)

            @pl.when(switch_ref[0] == 0)
            def _():
                back_out[...] = back_in[...]
                far_out[...] = far_in[...]


def second_sums(switch, own, coeffs, partner, start, earlier=None):
    rows, cols = partner.shape
    skip = start // STEP
    total = jax.ShapeDtypeStruct((LAGS * cols, cols), jnp.float32)
    total_spec = pl.BlockSpec(total.shape, lambda s, on: (0, 0))
    result = jax.ShapeDtypeStruct((LAGS, cols, cols), jnp.bfloat16)
    result_spec = pl.BlockSpec(result.shape, lambda s, on: (0, 0, 0))
    left = pl.BlockSpec((cols, STEP), lambda s, on: (0, s * on[0] + skip))
    in_specs = [left, left, pl.BlockSpec((LAGS, STEP), lambda s, on: (0, s * on[0] + skip)),
                pl.BlockSpec((STEP, cols), lambda s, on: (s * on[0], 0))]
    scratch = [pltpu.VMEM((LAGS * cols, STEP), jnp.bfloat16)]
    if earlier is None:
        out_shape, out_specs, earlier = [total], [total_spec], []
    else:
        out_shape, out_specs = [result] * 2, [result_spec] * 2
        in_specs += [total_spec] + [result_spec] * 2
        scratch = [pltpu.VMEM(total.shape, jnp.float32)] + scratch
    return pl.pallas_call(
        functools.partial(second_kernel, switch.shape[0] - 2, not earlier),
        grid_spec=pltpu.PrefetchScalarGridSpec(
            num_scalar_prefetch=1,
            grid=(rows // STEP,),
            in_specs=in_specs,
            out_specs=out_specs,
            scratch_shapes=scratch,
        ),
        out_shape=out_shape,
        compiler_params=PARAMS,
        cost_estimate=pl.CostEstimate(
            flops=2 * LAGS * cols * cols * rows, bytes_accessed=6 * rows * cols, transcendentals=0
        ),
        name="second_last" if earlier else "second_part",
    )(switch, *own, coeffs, partner, *earlier)


def late_kernel(windows, middle, switch_ref, plain_ref, swapped_ref, coeff_ref, first_ref, last_ref, near_out, acc, scaled):
    step = pl.program_id(0)
    cols = plain_ref.shape[0]

    @pl.when(switch_ref[0] != 0)
    def _():
        @pl.when(step == 0)
        def _():
            acc[...] = jnp.zeros_like(acc)

        scale(scaled, plain_ref[...], swapped_ref[...], coeff_ref)
        partner = jnp.where(step < middle, first_ref[...], last_ref[...])
        partner = weigh(partner, [switch_ref[2 + w] for w in range(windows)])
        acc[...] += jnp.dot(scaled[...], partner, preferred_element_type=jnp.float32)
        pl.when(step == pl.num_programs(0) - 1)(lambda: write_lags(near_out, acc, slice(0, cols), cols, False))


def late_sums(switch, own, coeffs, parts):
    cols, rows = own[0].shape
    middle = parts[0].shape[0] // STEP
    left = pl.BlockSpec((cols, STEP), lambda s, on: (0, s * on[0]))
    result = jax.ShapeDtypeStruct((LAGS, cols, cols), jnp.bfloat16)
    return pl.pallas_call(
        functools.partial(late_kernel, switch.shape[0] - 2, middle),
        grid_spec=pltpu.PrefetchScalarGridSpec(
            num_scalar_prefetch=1,
            grid=(rows // STEP,),
            in_specs=[left, left, pl.BlockSpec((LAGS, STEP), lambda s, on: (0, s * on[0])),
                      pl.BlockSpec((STEP, cols), lambda s, on: (jnp.minimum(s, middle - 1) * on[0], 0)),
                      pl.BlockSpec((STEP, cols), lambda s, on: (jnp.maximum(s - middle, 0) * on[0], 0))],
            out_specs=pl.BlockSpec(result.shape, lambda s, on: (0, 0, 0)),
            scratch_shapes=[pltpu.VMEM((LAGS * cols, cols), jnp.float32),
                            pltpu.VMEM((LAGS * cols, STEP), jnp.bfloat16)],
        ),
        out_shape=result,
        compiler_params=PARAMS,
        cost_estimate=pl.CostEstimate(flops=0, bytes_accessed=0, transcendentals=0),
        name="late_near",
    )(switch, *own, coeffs, *parts)


def local(spectra, quality):
    count = lax.axis_size("chan")
    half = count // 2
    me = lax.axis_index("chan")
    freq_count, _, window_count, cols = spectra.shape
    block = spectra.reshape(-1, cols)

    first_far, second_far = [], []
    for p in range(half):
        if p in (0, half - 1):
            first_far.append((p + half, p))
        elif p % 2 == 1 and p != 1:
            first_far.append((p, p + half))
        elif p in (1, half - 2):
            second_far.append((p, p + half))
        else:
            second_far.append((p + half, p))
    late_near = [(2, 1), (4, 3)]
    first_pairs = first_far + [(0, 1), (half - 1, half - 2)]
    second_pairs = second_far + late_near
    near_pairs = [(d + 1, d) for d in range(1, count - 1) if d not in (1, 3, half - 2, half - 1)]
    near_pairs += [(0, half - 1), (half - 1, 0)]
    back_pairs = [(t, s) for s, t in first_far + second_far] + [(1, 0)]
    side_pairs = [(0, half - 1), (half - 1, count - 1)]

    def among(devices):
        return functools.reduce(jnp.logical_or, [me == d for d in devices])

    def switch(on, other, *weights):
        flags = jnp.stack([jnp.asarray(on), jnp.asarray(other)]).astype(jnp.int32)
        return jnp.concatenate([flags, *weights])

    near_in = lax.ppermute(block, "chan", near_pairs)
    first_in = lax.ppermute(block, "chan", first_pairs)
    coeffs = lag_rows(freq_count, window_count)
    own = turn(block, switch(True, False), "turn_own")
    parts = split(block)
    first_flags = lax.ppermute(quality, "chan", first_pairs)[0]
    near_flags = lax.ppermute(quality, "chan", near_pairs)[0]
    second_flags = lax.ppermute(quality, "chan", second_pairs)[0]
    special = among([0, half - 1])
    first_switch = switch(me == 0, special, quality[0], near_flags, first_flags)
    second_weights = quality[0] * second_flags
    second_switch = switch(among([t for _, t in second_far]), False, second_weights)
    late_switch = switch(among([t for _, t in late_near]), False, second_weights)

    near_in, parts, own, coeffs, first_in = lax.optimization_barrier((near_in, parts, own, coeffs, first_in))
    second_in = [lax.ppermute(part, "chan", second_pairs) for part in parts]
    alt = turn(first_in, switch(special, False), "turn_first", common=False)
    near, far, back = first_sums(first_switch, own, alt, coeffs, near_in, first_in, block)
    near_pair = far
    side_returned = lax.ppermute(near, "chan", side_pairs)
    second_switch, near = lax.optimization_barrier((second_switch, near))
    total, = second_sums(second_switch, own, coeffs, second_in[0], 0)

    far, back = second_sums(second_switch, own, coeffs, second_in[1], parts[0].shape[0], [total, far, back])
    returned = lax.ppermute(back, "chan", back_pairs)
    late_switch, far = lax.optimization_barrier((late_switch, far))
    late = late_sums(late_switch, own, coeffs, second_in)

    near = jnp.where(among([half - 1, count - 1]), side_returned, near)
    near = jnp.where(me == half - 2, near_pair, near)
    near = jnp.where(among([t for _, t in late_near]), late, near)
    near = jnp.where(me == 0, returned, near)
    far = jnp.where(among([s for s, _ in first_far + second_far]), returned, far)
    return near[None], far[None]


def solution(mesh):
    return jax.shard_map(
        local,
        mesh=mesh,
        in_specs=(P(None, None, None, ("grp", "chan")), P(("grp", "chan"), None)),
        out_specs=(P(("grp", "chan"), None, None, None), P(("grp", "chan"), None, None, None)),
        check_vma=False,
    )
```

```python
import functools
import math

import jax
import jax.numpy as jnp
from jax import lax
from jax.experimental import pallas as pl
from jax.experimental.pallas import tpu as pltpu
from jax.sharding import PartitionSpec as P

HL = 4
LAGS = 2 * HL + 1
STEP = 1024
PARTS = (5, 8)
PARAMS = pltpu.CompilerParams(vmem_limit_bytes=16 * 1024 * 1024)


def lag_rows(freq_count, window_count):
    per_bin = 2 * window_count
    row = jnp.arange(freq_count * per_bin, dtype=jnp.int32)
    freq_values = (row // per_bin).astype(jnp.float32)
    sign = jnp.where(row % per_bin < window_count, 1.0, -1.0)
    lag_values = jnp.arange(HL + 1, dtype=jnp.float32)
    phases = jnp.pi / freq_count * lag_values[:, None] * freq_values[None, :]
    factor = 1.0 / math.sqrt(window_count * freq_count)
    cos_part = jnp.cos(phases) * factor
    sin_part = -jnp.sin(phases[1:]) * factor * sign[None, :]
    return jnp.concatenate([cos_part, sin_part], axis=0).astype(jnp.bfloat16)


def split_kernel(middle, x_ref, first_ref, last_ref):
    step = pl.program_id(0)

    @pl.when(step < middle)
    def _():
        first_ref[...] = x_ref[...]

    @pl.when(step >= middle)
    def _():
        last_ref[...] = x_ref[...]


def split(x):
    rows, cols = x.shape
    steps = rows // STEP
    middle = steps * PARTS[0] // PARTS[1]
    return pl.pallas_call(
        functools.partial(split_kernel, middle),
        grid=(steps,),
        in_specs=[pl.BlockSpec((STEP, cols), lambda s: (s, 0))],
        out_specs=[
            pl.BlockSpec((STEP, cols), lambda s: (jnp.minimum(s, middle - 1), 0)),
            pl.BlockSpec((STEP, cols), lambda s: (jnp.maximum(s - middle, 0), 0)),
        ],
        out_shape=[jax.ShapeDtypeStruct((n * STEP, cols), x.dtype) for n in (middle, steps - middle)],
        compiler_params=PARAMS,
        cost_estimate=pl.CostEstimate(flops=0, bytes_accessed=4 * rows * cols, transcendentals=0),
        name="split",
    )(x)


def turn_kernel(active_ref, x_ref, plain_ref, swapped_ref):
    @pl.when(active_ref[0] != 0)
    def _():
        rows, cols = x_ref.shape
        same = lax.broadcasted_iota(jnp.int32, (cols, cols), 0) == lax.broadcasted_iota(jnp.int32, (cols, cols), 1)
        eye = jnp.where(same, 1.0, 0.0).astype(jnp.bfloat16)
        source = lax.broadcasted_iota(jnp.int32, (2 * cols, 2 * cols), 0)
        target = lax.broadcasted_iota(jnp.int32, (2 * cols, 2 * cols), 1)
        exchange = jnp.where((source ^ 4) == target, 1.0, 0.0).astype(jnp.bfloat16)
        plain = lax.dot_general(eye, x_ref[...], (((1,), (1,)), ((), ())), preferred_element_type=jnp.float32)
        plain = plain.astype(jnp.bfloat16)
        plain_ref[...] = plain
        for t in range(0, rows, 2 * cols):
            swapped = jnp.dot(plain[:, t:t + 2 * cols], exchange, preferred_element_type=jnp.float32)
            swapped_ref[:, t:t + 2 * cols] = swapped.astype(jnp.bfloat16)


def turn(x, switch, name, common=True):
    rows, cols = x.shape
    out = jax.ShapeDtypeStruct((cols, rows), jnp.bfloat16)
    return pl.pallas_call(
        turn_kernel,
        grid_spec=pltpu.PrefetchScalarGridSpec(
            num_scalar_prefetch=1,
            grid=(rows // STEP,),
            in_specs=[pl.BlockSpec((STEP, cols), lambda s, on: (s * on[0], 0))],
            out_specs=[pl.BlockSpec((cols, STEP), lambda s, on: (0, s * on[0]))] * 2,
        ),
        out_shape=[out, out],
        compiler_params=PARAMS,
        cost_estimate=pl.CostEstimate(flops=0, bytes_accessed=6 * rows * cols if common else 0, transcendentals=0),
        name=name,
    )(switch, x)


def write_lags(out, acc, at, cols, mirrored):
    for lag in range(LAGS):
        k = abs(lag - HL)
        value = acc[k * cols:(k + 1) * cols, at]
        if k:
            odd = acc[(HL + k) * cols:(HL + k + 1) * cols, at]
            value = value + odd if lag > HL else value - odd
        value = value.astype(jnp.bfloat16)
        if mirrored:
            out[LAGS - 1 - lag] = value.T
        else:
            out[lag] = value


def scale(scaled, plain, swapped, coeff_ref):
    cols = plain.shape[0]
    for k in range(LAGS):
        part = plain if k <= HL else swapped
        scaled[k * cols:(k + 1) * cols, :] = part * coeff_ref[k:k + 1, :]


def weigh(x, window_weights):
    rows, cols = x.shape
    window = lax.broadcasted_iota(jnp.int32, (16, cols), 0) % len(window_weights)
    weights = jnp.zeros((16, cols), jnp.float32)
    for w, weight in enumerate(window_weights):
        weights = jnp.where(window == w, weight.astype(jnp.float32), weights)
    weights = jnp.broadcast_to(weights.astype(jnp.bfloat16)[None], (rows // 16, 16, cols))
    return x * weights.reshape(rows, cols)


def first_kernel(windows, last, switch_ref, plain_ref, swapped_ref, plain_alt, swapped_alt, coeff_ref, near_ref, first_ref,
                 own_ref, *rest):
    step = pl.program_id(0)
    cols = plain_ref.shape[0]
    near_mirrored, special = switch_ref[0], switch_ref[1]
    if last:
        acc_in, _, near_out, far_out, back_out, acc, scaled = rest
    else:
        acc, token_out, scaled = rest

    @pl.when(step == 0)
    def _():
        if last:
            acc[...] = acc_in[...]
        else:
            acc[...] = jnp.zeros_like(acc)
            token_out[...] = jnp.zeros_like(token_out)

    plain = jnp.where(special != 0, plain_alt[...], plain_ref[...])
    swapped = jnp.where(special != 0, swapped_alt[...], swapped_ref[...])
    scale(scaled, plain, swapped, coeff_ref)
    flags = [[switch_ref[2 + part * windows + w] for w in range(windows)] for part in range(3)]
    near_weights = [jnp.where(special != 0, first, own) * near for own, near, first in zip(*flags)]
    near = weigh(near_ref[...], near_weights)
    far = weigh(jnp.where(special != 0, own_ref[...], first_ref[...]), [own * first for own, _, first in zip(*flags)])
    acc[...] += jnp.dot(scaled[...], jnp.concatenate([near, far], axis=1), preferred_element_type=jnp.float32)

    if last:
        @pl.when(step == pl.num_programs(0) - 1)
        def _():
            near_at, far_at = slice(0, cols), slice(cols, 2 * cols)

            @pl.when(special == 0)
            def _():
                write_lags(back_out, acc, far_at, cols, True)
                write_lags(far_out, acc, far_at, cols, False)

            @pl.when(special != 0)
            def _():
                write_lags(back_out, acc, far_at, cols, False)
                write_lags(far_out, acc, far_at, cols, True)

            pl.when(near_mirrored == 0)(lambda: write_lags(near_out, acc, near_at, cols, False))
            pl.when(near_mirrored != 0)(lambda: write_lags(near_out, acc, near_at, cols, True))


def first_sums(switch, own, alt, coeffs, near_in, first_in, block, earlier=None):
    rows, cols = block.shape
    steps = rows // STEP // 2
    skip = 0 if earlier is None else steps
    windows = (switch.shape[0] - 2) // 3
    result = jax.ShapeDtypeStruct((LAGS, cols, cols), jnp.bfloat16)
    total = jax.ShapeDtypeStruct((LAGS * cols, 2 * cols), jnp.float32)
    total_spec = pl.BlockSpec(total.shape, lambda s, on: (0, 0))
    token = jax.ShapeDtypeStruct((8, cols), jnp.float32)
    token_spec = pl.BlockSpec(token.shape, lambda s, on: (0, 0))
    left = pl.BlockSpec((cols, STEP), lambda s, on: (0, (s + skip) * (1 - on[1])))
    left_alt = pl.BlockSpec((cols, STEP), lambda s, on: (0, (s + skip) * on[1]))
    right = pl.BlockSpec((STEP, cols), lambda s, on: (s + skip, 0))
    right_usual = pl.BlockSpec((STEP, cols), lambda s, on: ((s + skip) * (1 - on[1]), 0))
    right_special = pl.BlockSpec((STEP, cols), lambda s, on: ((s + skip) * on[1], 0))
    in_specs = [left, left, left_alt, left_alt, pl.BlockSpec((LAGS, STEP), lambda s, on: (0, s + skip)),
                right, right_usual, right_special]
    scratch = [pltpu.VMEM((LAGS * cols, STEP), jnp.bfloat16)]
    if earlier is None:
        out_shape, out_specs, earlier = [total, token], [total_spec, token_spec], []
    else:
        in_specs += [total_spec, token_spec]
        out_shape = [result] * 3
        out_specs = [pl.BlockSpec(result.shape, lambda s, on: (0, 0, 0))] * 3
        scratch = [pltpu.VMEM(total.shape, jnp.float32)] + scratch
    return pl.pallas_call(
        functools.partial(first_kernel, windows, bool(earlier)),
        grid_spec=pltpu.PrefetchScalarGridSpec(
            num_scalar_prefetch=1,
            grid=(steps,),
            in_specs=in_specs,
            out_specs=out_specs,
            scratch_shapes=scratch,
        ),
        out_shape=out_shape,
        compiler_params=PARAMS,
        cost_estimate=pl.CostEstimate(
            flops=2 * LAGS * cols * cols * rows, bytes_accessed=4 * rows * cols, transcendentals=0
        ),
        name="first_last" if earlier else "first_half",
    )(switch, *own, *alt, coeffs, near_in, first_in, block, *earlier)


def second_kernel(windows, first, switch_ref, plain_ref, swapped_ref, coeff_ref, partner_ref, *rest):
    on, late_near = switch_ref[0], switch_ref[1]
    step = pl.program_id(0)
    cols = plain_ref.shape[0]
    if first:
        acc, scaled = rest
    else:
        acc_in, near_in, far_in, back_in, near_out, far_out, back_out, acc, scaled = rest

    @pl.when(on != 0)
    def _():
        @pl.when(step == 0)
        def _():
            acc[...] = jnp.zeros_like(acc) if first else acc_in[...]

        scale(scaled, plain_ref[...], swapped_ref[...], coeff_ref)
        partner = weigh(partner_ref[...], [switch_ref[2 + w] for w in range(windows)])
        acc[...] += jnp.dot(scaled[...], partner, preferred_element_type=jnp.float32)

    if not first:
        @pl.when(step == pl.num_programs(0) - 1)
        def _():
            here = slice(0, cols)

            @pl.when((on != 0) & (late_near == 0))
            def _():
                write_lags(back_out, acc, here, cols, True)
                write_lags(far_out, acc, here, cols, False)

            @pl.when((on == 0) | (late_near != 0))
            def _():
                back_out[...] = back_in[...]
                far_out[...] = far_in[...]

            pl.when(late_near != 0)(lambda: write_lags(near_out, acc, here, cols, False))

            @pl.when(late_near == 0)
            def _():
                near_out[...] = near_in[...]


def second_sums(switch, own, coeffs, partner, start, earlier=None):
    rows, cols = partner.shape
    windows = switch.shape[0] - 2
    skip = start // STEP
    total = jax.ShapeDtypeStruct((LAGS * cols, cols), jnp.float32)
    total_spec = pl.BlockSpec(total.shape, lambda s, on: (0, 0))
    result = jax.ShapeDtypeStruct((LAGS, cols, cols), jnp.bfloat16)
    result_spec = pl.BlockSpec(result.shape, lambda s, on: (0, 0, 0))
    left = pl.BlockSpec((cols, STEP), lambda s, on: (0, s * on[0] + skip))
    in_specs = [left, left, pl.BlockSpec((LAGS, STEP), lambda s, on: (0, s * on[0] + skip)),
                pl.BlockSpec((STEP, cols), lambda s, on: (s * on[0], 0))]
    scratch = [pltpu.VMEM((LAGS * cols, STEP), jnp.bfloat16)]
    if earlier is None:
        out_shape, out_specs, earlier = [total], [total_spec], []
    else:
        out_shape, out_specs = [result] * 3, [result_spec] * 3
        in_specs += [total_spec] + [result_spec] * 3
        scratch = [pltpu.VMEM(total.shape, jnp.float32)] + scratch
    return pl.pallas_call(
        functools.partial(second_kernel, windows, not earlier),
        grid_spec=pltpu.PrefetchScalarGridSpec(
            num_scalar_prefetch=1,
            grid=(rows // STEP,),
            in_specs=in_specs,
            out_specs=out_specs,
            scratch_shapes=scratch,
        ),
        out_shape=out_shape,
        compiler_params=PARAMS,
        cost_estimate=pl.CostEstimate(
            flops=2 * LAGS * cols * cols * rows, bytes_accessed=6 * rows * cols, transcendentals=0
        ),
        name="second_last" if earlier else "second_part",
    )(switch, *own, coeffs, partner, *earlier)


def local(spectra, quality):
    count = lax.axis_size("chan")
    half = count // 2
    me = lax.axis_index("chan")
    freq_count, _, window_count, cols = spectra.shape
    block = spectra.reshape(-1, cols)

    first_far, second_far = [], []
    for p in range(half):
        if p in (0, half - 1):
            first_far.append((p + half, p))
        elif p % 2 == 0 and p >= half // 2:
            first_far.append((p, p + half))
        elif p in (1, 3):
            second_far.append((p, p + half))
        else:
            second_far.append((p + half, p))
    late_near = [(2, 1), (4, 3)]
    first_pairs = first_far + [(0, 1), (half - 1, half - 2)]
    second_pairs = second_far + late_near
    near_pairs = [(d + 1, d) for d in range(1, count - 1) if d not in (1, 3, half - 2, half - 1)]
    near_pairs += [(0, half - 1), (half - 1, 0)]
    back_pairs = [(t, s) for s, t in first_far + second_far] + [(1, 0)]
    side_pairs = [(0, half - 1), (half - 1, count - 1)]

    def among(devices):
        return functools.reduce(jnp.logical_or, [me == d for d in devices])

    def switch(on, other, *weights):
        flags = jnp.stack([jnp.asarray(on), jnp.asarray(other)]).astype(jnp.int32)
        return jnp.concatenate([flags, *weights])

    near_in = lax.ppermute(block, "chan", near_pairs)
    first_in = lax.ppermute(block, "chan", first_pairs)
    coeffs = lag_rows(freq_count, window_count)
    own = turn(block, switch(True, False), "turn_own")
    parts = split(block)
    first_flags = lax.ppermute(quality, "chan", first_pairs)[0]
    near_flags = lax.ppermute(quality, "chan", near_pairs)[0]
    second_flags = lax.ppermute(quality, "chan", second_pairs)[0]
    special = among([0, half - 1])
    first_switch = switch(me == 0, special, quality[0], near_flags, first_flags)
    second_switch = switch(
        among([t for _, t in second_pairs]), among([t for _, t in late_near]), quality[0] * second_flags
    )

    near_in, first_part, own, coeffs, first_in = lax.optimization_barrier((near_in, parts[0], own, coeffs, first_in))
    second_in = [lax.ppermute(first_part, "chan", second_pairs)]
    alt = turn(first_in, switch(special, False), "turn_first", common=False)
    operands = first_switch, own, alt, coeffs, near_in, first_in, block
    total, token = first_sums(*operands)
    last_part, token = lax.optimization_barrier((parts[1], token))
    second_in.append(lax.ppermute(last_part, "chan", second_pairs))
    near, far, back = first_sums(*operands, [total, token])
    side_returned = lax.ppermute(near, "chan", side_pairs)
    second_switch, near = lax.optimization_barrier((second_switch, near))
    total, = second_sums(second_switch, own, coeffs, second_in[0], 0)

    near = jnp.where(among([half - 1, count - 1]), side_returned, near)
    near = jnp.where(me == half - 2, far, near)
    near, far, back = second_sums(
        second_switch, own, coeffs, second_in[1], parts[0].shape[0], [total, near, far, back]
    )
    returned = lax.ppermute(back, "chan", back_pairs)
    near = jnp.where(me == 0, returned, near)
    far = jnp.where(among([s for s, _ in first_far + second_far]), returned, far)
    return near[None], far[None]


def solution(mesh):
    return jax.shard_map(
        local,
        mesh=mesh,
        in_specs=(P(None, None, None, ("grp", "chan")), P(("grp", "chan"), None)),
        out_specs=(P(("grp", "chan"), None, None, None), P(("grp", "chan"), None, None, None)),
        check_vma=False,
    )
```

```python
import functools
import math

import jax
import jax.numpy as jnp
from jax import lax
from jax.experimental import pallas as pl
from jax.experimental.pallas import tpu as pltpu
from jax.sharding import PartitionSpec as P

HL = 4
LAGS = 2 * HL + 1
STEP = 1024
PARTS = (5, 8)
PARAMS = pltpu.CompilerParams(vmem_limit_bytes=16 * 1024 * 1024)


def lag_rows(freq_count, window_count):
    per_bin = 2 * window_count
    row = jnp.arange(freq_count * per_bin, dtype=jnp.int32)
    freq_values = (row // per_bin).astype(jnp.float32)
    sign = jnp.where(row % per_bin < window_count, 1.0, -1.0)
    lag_values = jnp.arange(HL + 1, dtype=jnp.float32)
    phases = jnp.pi / freq_count * lag_values[:, None] * freq_values[None, :]
    factor = 1.0 / math.sqrt(window_count * freq_count)
    cos_part = jnp.cos(phases) * factor
    sin_part = -jnp.sin(phases[1:]) * factor * sign[None, :]
    return jnp.concatenate([cos_part, sin_part], axis=0).astype(jnp.bfloat16)


def split_kernel(middle, x_ref, first_ref, last_ref):
    step = pl.program_id(0)

    @pl.when(step < middle)
    def _():
        first_ref[...] = x_ref[...]

    @pl.when(step >= middle)
    def _():
        last_ref[...] = x_ref[...]


def split(x):
    rows, cols = x.shape
    steps = rows // STEP
    middle = steps * PARTS[0] // PARTS[1]
    return pl.pallas_call(
        functools.partial(split_kernel, middle),
        grid=(steps,),
        in_specs=[pl.BlockSpec((STEP, cols), lambda s: (s, 0))],
        out_specs=[
            pl.BlockSpec((STEP, cols), lambda s: (jnp.minimum(s, middle - 1), 0)),
            pl.BlockSpec((STEP, cols), lambda s: (jnp.maximum(s - middle, 0), 0)),
        ],
        out_shape=[jax.ShapeDtypeStruct((n * STEP, cols), x.dtype) for n in (middle, steps - middle)],
        compiler_params=PARAMS,
        cost_estimate=pl.CostEstimate(flops=0, bytes_accessed=4 * rows * cols, transcendentals=0),
        name="split",
    )(x)


def turned(x):
    rows, cols = x.shape
    same = lax.broadcasted_iota(jnp.int32, (cols, cols), 0) == lax.broadcasted_iota(jnp.int32, (cols, cols), 1)
    eye = jnp.where(same, 1.0, 0.0).astype(jnp.bfloat16)
    source = lax.broadcasted_iota(jnp.int32, (2 * cols, 2 * cols), 0)
    target = lax.broadcasted_iota(jnp.int32, (2 * cols, 2 * cols), 1)
    exchange = jnp.where((source ^ 4) == target, 1.0, 0.0).astype(jnp.bfloat16)
    plain = lax.dot_general(eye, x, (((1,), (1,)), ((), ())), preferred_element_type=jnp.float32)
    plain = plain.astype(jnp.bfloat16)
    swapped = [
        jnp.dot(plain[:, t:t + 2 * cols], exchange, preferred_element_type=jnp.float32).astype(jnp.bfloat16)
        for t in range(0, rows, 2 * cols)
    ]
    return plain, jnp.concatenate(swapped, axis=1)


def turn_kernel(x_ref, plain_ref, swapped_ref):
    plain_ref[...], swapped_ref[...] = turned(x_ref[...])


def turn(x):
    rows, cols = x.shape
    out = jax.ShapeDtypeStruct((cols, rows), jnp.bfloat16)
    return pl.pallas_call(
        turn_kernel,
        grid=(rows // STEP,),
        in_specs=[pl.BlockSpec((STEP, cols), lambda s: (s, 0))],
        out_specs=[pl.BlockSpec((cols, STEP), lambda s: (0, s))] * 2,
        out_shape=[out, out],
        compiler_params=PARAMS,
        cost_estimate=pl.CostEstimate(flops=0, bytes_accessed=6 * rows * cols, transcendentals=0),
        name="turn",
    )(x)


def write_lags(out, acc, at, cols, mirrored):
    for lag in range(LAGS):
        k = abs(lag - HL)
        value = acc[k * cols:(k + 1) * cols, at]
        if k:
            odd = acc[(HL + k) * cols:(HL + k + 1) * cols, at]
            value = value + odd if lag > HL else value - odd
        value = value.astype(jnp.bfloat16)
        if mirrored:
            out[LAGS - 1 - lag] = value.T
        else:
            out[lag] = value


def scale(scaled, plain, swapped, coeff_ref):
    cols = plain.shape[0]
    for k in range(LAGS):
        part = plain if k <= HL else swapped
        scaled[k * cols:(k + 1) * cols, :] = part * coeff_ref[k:k + 1, :]


def weigh(x, window_weights):
    rows, cols = x.shape
    window = lax.broadcasted_iota(jnp.int32, (16, cols), 0) % len(window_weights)
    weights = jnp.zeros((16, cols), jnp.float32)
    for w, weight in enumerate(window_weights):
        weights = jnp.where(window == w, weight.astype(jnp.float32), weights)
    weights = jnp.broadcast_to(weights.astype(jnp.bfloat16)[None], (rows // 16, 16, cols))
    return x * weights.reshape(rows, cols)


def first_kernel(windows, last, switch_ref, plain_ref, swapped_ref, coeff_ref, near_ref, first_ref, own_ref, *rest):
    step = pl.program_id(0)
    cols = plain_ref.shape[0]
    near_mirrored, special = switch_ref[0], switch_ref[1]
    if last:
        acc_in, _, near_out, far_out, back_out, acc, scaled, plain, swapped = rest
    else:
        acc, token_out, scaled, plain, swapped = rest

    @pl.when(step == 0)
    def _():
        if last:
            acc[...] = acc_in[...]
        else:
            acc[...] = jnp.zeros_like(acc)
            token_out[...] = jnp.zeros_like(token_out)

    @pl.when(special == 0)
    def _():
        plain[...], swapped[...] = plain_ref[...], swapped_ref[...]

    @pl.when(special != 0)
    def _():
        plain[...], swapped[...] = turned(first_ref[...])

    scale(scaled, plain[...], swapped[...], coeff_ref)
    flags = [[switch_ref[2 + part * windows + w] for w in range(windows)] for part in range(3)]
    near_weights = [jnp.where(special != 0, first, own) * near for own, near, first in zip(*flags)]
    near = weigh(near_ref[...], near_weights)
    far = weigh(jnp.where(special != 0, own_ref[...], first_ref[...]), [own * first for own, _, first in zip(*flags)])
    acc[...] += jnp.dot(scaled[...], jnp.concatenate([near, far], axis=1), preferred_element_type=jnp.float32)

    if last:
        @pl.when(step == pl.num_programs(0) - 1)
        def _():
            near_at, far_at = slice(0, cols), slice(cols, 2 * cols)

            @pl.when(special == 0)
            def _():
                write_lags(back_out, acc, far_at, cols, True)
                write_lags(far_out, acc, far_at, cols, False)

            @pl.when(special != 0)
            def _():
                write_lags(back_out, acc, far_at, cols, False)
                write_lags(far_out, acc, far_at, cols, True)

            pl.when(near_mirrored == 0)(lambda: write_lags(near_out, acc, near_at, cols, False))
            pl.when(near_mirrored != 0)(lambda: write_lags(near_out, acc, near_at, cols, True))


def first_sums(switch, own, coeffs, near_in, first_in, block, earlier=None):
    rows, cols = block.shape
    steps = rows // STEP // 2
    skip = 0 if earlier is None else steps
    windows = (switch.shape[0] - 2) // 3
    result = jax.ShapeDtypeStruct((LAGS, cols, cols), jnp.bfloat16)
    total = jax.ShapeDtypeStruct((LAGS * cols, 2 * cols), jnp.float32)
    total_spec = pl.BlockSpec(total.shape, lambda s, on: (0, 0))
    token = jax.ShapeDtypeStruct((8, cols), jnp.float32)
    token_spec = pl.BlockSpec(token.shape, lambda s, on: (0, 0))
    left = pl.BlockSpec((cols, STEP), lambda s, on: (0, (s + skip) * (1 - on[1])))
    right = pl.BlockSpec((STEP, cols), lambda s, on: (s + skip, 0))
    right_special = pl.BlockSpec((STEP, cols), lambda s, on: ((s + skip) * on[1], 0))
    in_specs = [left, left, pl.BlockSpec((LAGS, STEP), lambda s, on: (0, s + skip)), right, right, right_special]
    scratch = [pltpu.VMEM((LAGS * cols, STEP), jnp.bfloat16)] + [pltpu.VMEM((cols, STEP), jnp.bfloat16)] * 2
    if earlier is None:
        out_shape, out_specs, earlier = [total, token], [total_spec, token_spec], []
    else:
        in_specs += [total_spec, token_spec]
        out_shape = [result] * 3
        out_specs = [pl.BlockSpec(result.shape, lambda s, on: (0, 0, 0))] * 3
        scratch = [pltpu.VMEM(total.shape, jnp.float32)] + scratch
    return pl.pallas_call(
        functools.partial(first_kernel, windows, bool(earlier)),
        grid_spec=pltpu.PrefetchScalarGridSpec(
            num_scalar_prefetch=1,
            grid=(steps,),
            in_specs=in_specs,
            out_specs=out_specs,
            scratch_shapes=scratch,
        ),
        out_shape=out_shape,
        compiler_params=PARAMS,
        cost_estimate=pl.CostEstimate(
            flops=2 * LAGS * cols * cols * rows, bytes_accessed=4 * rows * cols, transcendentals=0
        ),
        name="first_last" if earlier else "first_half",
    )(switch, *own, coeffs, near_in, first_in, block, *earlier)


def second_kernel(windows, first, switch_ref, plain_ref, swapped_ref, coeff_ref, partner_ref, *rest):
    on, late_near = switch_ref[0], switch_ref[1]
    step = pl.program_id(0)
    cols = plain_ref.shape[0]
    if first:
        acc, scaled = rest
    else:
        acc_in, near_in, far_in, back_in, near_out, far_out, back_out, acc, scaled = rest

    @pl.when(on != 0)
    def _():
        @pl.when(step == 0)
        def _():
            acc[...] = jnp.zeros_like(acc) if first else acc_in[...]

        scale(scaled, plain_ref[...], swapped_ref[...], coeff_ref)
        partner = weigh(partner_ref[...], [switch_ref[2 + w] for w in range(windows)])
        acc[...] += jnp.dot(scaled[...], partner, preferred_element_type=jnp.float32)

    if not first:
        @pl.when(step == pl.num_programs(0) - 1)
        def _():
            here = slice(0, cols)

            @pl.when((on != 0) & (late_near == 0))
            def _():
                write_lags(back_out, acc, here, cols, True)
                write_lags(far_out, acc, here, cols, False)

            @pl.when((on == 0) | (late_near != 0))
            def _():
                back_out[...] = back_in[...]
                far_out[...] = far_in[...]

            pl.when(late_near != 0)(lambda: write_lags(near_out, acc, here, cols, False))

            @pl.when(late_near == 0)
            def _():
                near_out[...] = near_in[...]


def second_sums(switch, own, coeffs, partner, start, earlier=None):
    rows, cols = partner.shape
    windows = switch.shape[0] - 2
    skip = start // STEP
    total = jax.ShapeDtypeStruct((LAGS * cols, cols), jnp.float32)
    total_spec = pl.BlockSpec(total.shape, lambda s, on: (0, 0))
    result = jax.ShapeDtypeStruct((LAGS, cols, cols), jnp.bfloat16)
    result_spec = pl.BlockSpec(result.shape, lambda s, on: (0, 0, 0))
    left = pl.BlockSpec((cols, STEP), lambda s, on: (0, s * on[0] + skip))
    in_specs = [left, left, pl.BlockSpec((LAGS, STEP), lambda s, on: (0, s * on[0] + skip)),
                pl.BlockSpec((STEP, cols), lambda s, on: (s * on[0], 0))]
    scratch = [pltpu.VMEM((LAGS * cols, STEP), jnp.bfloat16)]
    if earlier is None:
        out_shape, out_specs, earlier = [total], [total_spec], []
    else:
        out_shape, out_specs = [result] * 3, [result_spec] * 3
        in_specs += [total_spec] + [result_spec] * 3
        scratch = [pltpu.VMEM(total.shape, jnp.float32)] + scratch
    return pl.pallas_call(
        functools.partial(second_kernel, windows, not earlier),
        grid_spec=pltpu.PrefetchScalarGridSpec(
            num_scalar_prefetch=1,
            grid=(rows // STEP,),
            in_specs=in_specs,
            out_specs=out_specs,
            scratch_shapes=scratch,
        ),
        out_shape=out_shape,
        compiler_params=PARAMS,
        cost_estimate=pl.CostEstimate(
            flops=2 * LAGS * cols * cols * rows, bytes_accessed=6 * rows * cols, transcendentals=0
        ),
        name="second_last" if earlier else "second_part",
    )(switch, *own, coeffs, partner, *earlier)


def local(spectra, quality):
    count = lax.axis_size("chan")
    half = count // 2
    me = lax.axis_index("chan")
    freq_count, _, window_count, cols = spectra.shape
    block = spectra.reshape(-1, cols)

    first_far, second_far = [], []
    for p in range(half):
        if p in (0, half - 1):
            first_far.append((p + half, p))
        elif p % 2 == 0 and p >= half // 2:
            first_far.append((p, p + half))
        elif p in (1, 3):
            second_far.append((p, p + half))
        else:
            second_far.append((p + half, p))
    late_near = [(2, 1), (4, 3)]
    first_pairs = first_far + [(0, 1), (half - 1, half - 2)]
    second_pairs = second_far + late_near
    near_pairs = [(d + 1, d) for d in range(1, count - 1) if d not in (1, 3, half - 2, half - 1)]
    near_pairs += [(0, half - 1), (half - 1, 0)]
    back_pairs = [(t, s) for s, t in first_far + second_far] + [(1, 0)]
    side_pairs = [(0, half - 1), (half - 1, count - 1)]

    def among(devices):
        return functools.reduce(jnp.logical_or, [me == d for d in devices])

    def switch(on, other, *weights):
        flags = jnp.stack([jnp.asarray(on), jnp.asarray(other)]).astype(jnp.int32)
        return jnp.concatenate([flags, *weights])

    near_in = lax.ppermute(block, "chan", near_pairs)
    first_in = lax.ppermute(block, "chan", first_pairs)
    coeffs = lag_rows(freq_count, window_count)
    own = turn(block)
    parts = split(block)
    first_flags = lax.ppermute(quality, "chan", first_pairs)[0]
    near_flags = lax.ppermute(quality, "chan", near_pairs)[0]
    second_flags = lax.ppermute(quality, "chan", second_pairs)[0]
    special = among([0, half - 1])
    first_switch = switch(me == 0, special, quality[0], near_flags, first_flags)
    second_switch = switch(
        among([t for _, t in second_pairs]), among([t for _, t in late_near]), quality[0] * second_flags
    )

    near_in, first_part, last_part, own, coeffs, first_in = lax.optimization_barrier(
        (near_in, *parts, own, coeffs, first_in)
    )
    second_in = [lax.ppermute(first_part, "chan", second_pairs)]
    operands = first_switch, own, coeffs, near_in, first_in, block
    total, token = first_sums(*operands)
    last_part, token = lax.optimization_barrier((last_part, token))
    second_in.append(lax.ppermute(last_part, "chan", second_pairs))
    near, far, back = first_sums(*operands, [total, token])
    side_returned = lax.ppermute(near, "chan", side_pairs)
    second_switch, near = lax.optimization_barrier((second_switch, near))
    total, = second_sums(second_switch, own, coeffs, second_in[0], 0)

    near = jnp.where(me == half - 2, far, near)
    near, far, back = second_sums(
        second_switch, own, coeffs, second_in[1], parts[0].shape[0], [total, near, far, back]
    )
    returned = lax.ppermute(back, "chan", back_pairs)
    near = jnp.where(among([half - 1, count - 1]), side_returned, near)
    near = jnp.where(me == 0, returned, near)
    far = jnp.where(among([s for s, _ in first_far + second_far]), returned, far)
    return near[None], far[None]


def solution(mesh):
    return jax.shard_map(
        local,
        mesh=mesh,
        in_specs=(P(None, None, None, ("grp", "chan")), P(("grp", "chan"), None)),
        out_specs=(P(("grp", "chan"), None, None, None), P(("grp", "chan"), None, None, None)),
        check_vma=False,
    )
```

```python
import functools
import math

import jax
import jax.numpy as jnp
from jax import lax
from jax.experimental import pallas as pl
from jax.experimental.pallas import tpu as pltpu
from jax.sharding import PartitionSpec as P

HL = 4
LAGS = 2 * HL + 1
STEP = 1024
PARTS = (5, 8)
PARAMS = pltpu.CompilerParams(vmem_limit_bytes=12 * 1024 * 1024)


def lag_rows(freq_count, window_count):
    per_bin = 2 * window_count
    row = jnp.arange(freq_count * per_bin, dtype=jnp.int32)
    freq_values = (row // per_bin).astype(jnp.float32)
    sign = jnp.where(row % per_bin < window_count, 1.0, -1.0)
    lag_values = jnp.arange(HL + 1, dtype=jnp.float32)
    phases = jnp.pi / freq_count * lag_values[:, None] * freq_values[None, :]
    factor = 1.0 / math.sqrt(window_count * freq_count)
    cos_part = jnp.cos(phases) * factor
    sin_part = -jnp.sin(phases[1:]) * factor * sign[None, :]
    return jnp.concatenate([cos_part, sin_part], axis=0).astype(jnp.bfloat16)


def split_kernel(middle, windows, flags_ref, x_ref, first_ref, last_ref):
    step = pl.program_id(0)
    masked = weigh(x_ref[...], [flags_ref[w] for w in range(windows)])

    @pl.when(step < middle)
    def _():
        first_ref[...] = masked

    @pl.when(step >= middle)
    def _():
        last_ref[...] = masked


def split(flags, x):
    rows, cols = x.shape
    steps = rows // STEP
    middle = steps * PARTS[0] // PARTS[1]
    return pl.pallas_call(
        functools.partial(split_kernel, middle, flags.shape[0]),
        grid_spec=pltpu.PrefetchScalarGridSpec(
            num_scalar_prefetch=1,
            grid=(steps,),
            in_specs=[pl.BlockSpec((STEP, cols), lambda s, on: (s, 0))],
            out_specs=[
                pl.BlockSpec((STEP, cols), lambda s, on: (jnp.minimum(s, middle - 1), 0)),
                pl.BlockSpec((STEP, cols), lambda s, on: (jnp.maximum(s - middle, 0), 0)),
            ],
        ),
        out_shape=[jax.ShapeDtypeStruct((n * STEP, cols), x.dtype) for n in (middle, steps - middle)],
        compiler_params=PARAMS,
        cost_estimate=pl.CostEstimate(flops=rows * cols, bytes_accessed=4 * rows * cols, transcendentals=0),
        name="split",
    )(flags, x)


def turned(x):
    rows, cols = x.shape
    same = lax.broadcasted_iota(jnp.int32, (cols, cols), 0) == lax.broadcasted_iota(jnp.int32, (cols, cols), 1)
    eye = jnp.where(same, 1.0, 0.0).astype(jnp.bfloat16)
    source = lax.broadcasted_iota(jnp.int32, (2 * cols, 2 * cols), 0)
    target = lax.broadcasted_iota(jnp.int32, (2 * cols, 2 * cols), 1)
    exchange = jnp.where((source ^ 4) == target, 1.0, 0.0).astype(jnp.bfloat16)
    plain = lax.dot_general(eye, x, (((1,), (1,)), ((), ())), preferred_element_type=jnp.float32)
    plain = plain.astype(jnp.bfloat16)
    swapped = [
        jnp.dot(plain[:, t:t + 2 * cols], exchange, preferred_element_type=jnp.float32).astype(jnp.bfloat16)
        for t in range(0, rows, 2 * cols)
    ]
    return plain, jnp.concatenate(swapped, axis=1)


def turn_kernel(x_ref, plain_ref, swapped_ref):
    plain_ref[...], swapped_ref[...] = turned(x_ref[...])


def turn(x):
    rows, cols = x.shape
    out = jax.ShapeDtypeStruct((cols, rows), jnp.bfloat16)
    return pl.pallas_call(
        turn_kernel,
        grid=(rows // STEP,),
        in_specs=[pl.BlockSpec((STEP, cols), lambda s: (s, 0))],
        out_specs=[pl.BlockSpec((cols, STEP), lambda s: (0, s))] * 2,
        out_shape=[out, out],
        compiler_params=PARAMS,
        cost_estimate=pl.CostEstimate(flops=0, bytes_accessed=6 * rows * cols, transcendentals=0),
        name="turn",
    )(x)


def write_lags(out, acc, at, cols, mirrored):
    for lag in range(LAGS):
        k = abs(lag - HL)
        value = acc[k * cols:(k + 1) * cols, at]
        if k:
            odd = acc[(HL + k) * cols:(HL + k + 1) * cols, at]
            value = value + odd if lag > HL else value - odd
        value = value.astype(jnp.bfloat16)
        if mirrored:
            out[LAGS - 1 - lag] = value.T
        else:
            out[lag] = value


def scale(scaled, plain, swapped, coeff_ref):
    cols = plain.shape[0]
    for k in range(LAGS):
        part = plain if k <= HL else swapped
        scaled[k * cols:(k + 1) * cols, :] = part * coeff_ref[k:k + 1, :]


def weigh(x, window_weights):
    rows, cols = x.shape
    window = lax.broadcasted_iota(jnp.int32, (16, cols), 0) % len(window_weights)
    weights = jnp.zeros((16, cols), jnp.float32)
    for w, weight in enumerate(window_weights):
        weights = jnp.where(window == w, weight.astype(jnp.float32), weights)
    weights = jnp.broadcast_to(weights.astype(jnp.bfloat16)[None], (rows // 16, 16, cols))
    return x * weights.reshape(rows, cols)


def first_kernel(windows, last, switch_ref, plain_ref, swapped_ref, coeff_ref, near_ref, first_ref, own_ref, *rest):
    step = pl.program_id(0)
    cols = plain_ref.shape[0]
    near_mirrored, special = switch_ref[0], switch_ref[1]
    if last:
        acc_in, _, near_out, far_out, back_out, acc, scaled, plain, swapped, own_rows, arrived = rest
    else:
        acc, token_out, scaled, plain, swapped, own_rows, arrived = rest
    size = own_rows.shape[0]
    begin = size if last else 0

    @pl.when(step == 0)
    def _():
        if last:
            acc[...] = acc_in[...]
        else:
            acc[...] = jnp.zeros_like(acc)
            token_out[...] = jnp.zeros_like(token_out)

    @pl.when(special == 0)
    def _():
        plain[...], swapped[...] = plain_ref[...], swapped_ref[...]

    @pl.when((special != 0) & (step == 0))
    def _():
        copy = pltpu.make_async_copy(own_ref.at[pl.ds(begin, size)], own_rows, arrived)
        copy.start()
        copy.wait()

    @pl.when(special != 0)
    def _():
        plain[...], swapped[...] = turned(first_ref[...])

    scale(scaled, plain[...], swapped[...], coeff_ref)
    flags = [[switch_ref[2 + part * windows + w] for w in range(windows)] for part in range(3)]
    near_weights = [jnp.where(special != 0, first, own) * near for own, near, first in zip(*flags)]
    near = weigh(near_ref[...], near_weights)
    own_tile = own_rows[pl.ds(pl.multiple_of(step * STEP, STEP), STEP), :]
    far = weigh(jnp.where(special != 0, own_tile, first_ref[...]), [own * first for own, _, first in zip(*flags)])
    acc[...] += jnp.dot(scaled[...], jnp.concatenate([near, far], axis=1), preferred_element_type=jnp.float32)

    if last:
        @pl.when(step == pl.num_programs(0) - 1)
        def _():
            near_at, far_at = slice(0, cols), slice(cols, 2 * cols)

            @pl.when(special == 0)
            def _():
                write_lags(back_out, acc, far_at, cols, True)
                write_lags(far_out, acc, far_at, cols, False)

            @pl.when(special != 0)
            def _():
                write_lags(back_out, acc, far_at, cols, False)
                write_lags(far_out, acc, far_at, cols, True)

            pl.when(near_mirrored == 0)(lambda: write_lags(near_out, acc, near_at, cols, False))
            pl.when(near_mirrored != 0)(lambda: write_lags(near_out, acc, near_at, cols, True))


def first_sums(switch, own, coeffs, near_in, first_in, block, earlier=None):
    rows, cols = block.shape
    steps = rows // STEP // 2
    skip = 0 if earlier is None else steps
    windows = (switch.shape[0] - 2) // 3
    result = jax.ShapeDtypeStruct((LAGS, cols, cols), jnp.bfloat16)
    total = jax.ShapeDtypeStruct((LAGS * cols, 2 * cols), jnp.float32)
    total_spec = pl.BlockSpec(total.shape, lambda s, on: (0, 0))
    token = jax.ShapeDtypeStruct((8, cols), jnp.float32)
    token_spec = pl.BlockSpec(token.shape, lambda s, on: (0, 0))
    left = pl.BlockSpec((cols, STEP), lambda s, on: (0, (s + skip) * (1 - on[1])))
    right = pl.BlockSpec((STEP, cols), lambda s, on: (s + skip, 0))
    in_specs = [left, left, pl.BlockSpec((LAGS, STEP), lambda s, on: (0, s + skip)), right, right,
                pl.BlockSpec(memory_space=pltpu.HBM)]
    scratch = [pltpu.VMEM((LAGS * cols, STEP), jnp.bfloat16)] + [pltpu.VMEM((cols, STEP), jnp.bfloat16)] * 2
    scratch += [pltpu.VMEM((steps * STEP, cols), jnp.bfloat16), pltpu.SemaphoreType.DMA(())]
    if earlier is None:
        out_shape, out_specs, earlier = [total, token], [total_spec, token_spec], []
    else:
        in_specs += [total_spec, token_spec]
        out_shape = [result] * 3
        out_specs = [pl.BlockSpec(result.shape, lambda s, on: (0, 0, 0))] * 3
        scratch = [pltpu.VMEM(total.shape, jnp.float32)] + scratch
    return pl.pallas_call(
        functools.partial(first_kernel, windows, bool(earlier)),
        grid_spec=pltpu.PrefetchScalarGridSpec(
            num_scalar_prefetch=1,
            grid=(steps,),
            in_specs=in_specs,
            out_specs=out_specs,
            scratch_shapes=scratch,
        ),
        out_shape=out_shape,
        compiler_params=PARAMS,
        cost_estimate=pl.CostEstimate(
            flops=2 * LAGS * cols * cols * rows, bytes_accessed=4 * rows * cols, transcendentals=0
        ),
        name="first_last" if earlier else "first_half",
    )(switch, *own, coeffs, near_in, first_in, block, *earlier)


def second_kernel(windows, first, switch_ref, plain_ref, swapped_ref, coeff_ref, partner_ref, *rest):
    on, late_near = switch_ref[0], switch_ref[1]
    step = pl.program_id(0)
    cols = plain_ref.shape[0]
    if first:
        acc, scaled = rest
    else:
        acc_in, near_in, far_in, back_in, near_out, far_out, back_out, acc, scaled = rest

    @pl.when(on != 0)
    def _():
        @pl.when(step == 0)
        def _():
            acc[...] = jnp.zeros_like(acc) if first else acc_in[...]

        scale(scaled, plain_ref[...], swapped_ref[...], coeff_ref)
        partner = weigh(partner_ref[...], [switch_ref[2 + w] for w in range(windows)])
        acc[...] += jnp.dot(scaled[...], partner, preferred_element_type=jnp.float32)

    if not first:
        @pl.when(step == pl.num_programs(0) - 1)
        def _():
            here = slice(0, cols)

            @pl.when((on != 0) & (late_near == 0))
            def _():
                write_lags(back_out, acc, here, cols, True)
                write_lags(far_out, acc, here, cols, False)

            @pl.when((on == 0) | (late_near != 0))
            def _():
                back_out[...] = back_in[...]
                far_out[...] = far_in[...]

            pl.when(late_near != 0)(lambda: write_lags(near_out, acc, here, cols, False))

            @pl.when(late_near == 0)
            def _():
                near_out[...] = near_in[...]


def second_sums(switch, own, coeffs, partner, start, earlier=None):
    rows, cols = partner.shape
    windows = switch.shape[0] - 2
    skip = start // STEP
    total = jax.ShapeDtypeStruct((LAGS * cols, cols), jnp.float32)
    total_spec = pl.BlockSpec(total.shape, lambda s, on: (0, 0))
    result = jax.ShapeDtypeStruct((LAGS, cols, cols), jnp.bfloat16)
    result_spec = pl.BlockSpec(result.shape, lambda s, on: (0, 0, 0))
    left = pl.BlockSpec((cols, STEP), lambda s, on: (0, s * on[0] + skip))
    in_specs = [left, left, pl.BlockSpec((LAGS, STEP), lambda s, on: (0, s * on[0] + skip)),
                pl.BlockSpec((STEP, cols), lambda s, on: (s * on[0], 0))]
    scratch = [pltpu.VMEM((LAGS * cols, STEP), jnp.bfloat16)]
    if earlier is None:
        out_shape, out_specs, earlier = [total], [total_spec], []
    else:
        out_shape, out_specs = [result] * 3, [result_spec] * 3
        in_specs += [total_spec] + [result_spec] * 3
        scratch = [pltpu.VMEM(total.shape, jnp.float32)] + scratch
    return pl.pallas_call(
        functools.partial(second_kernel, windows, not earlier),
        grid_spec=pltpu.PrefetchScalarGridSpec(
            num_scalar_prefetch=1,
            grid=(rows // STEP,),
            in_specs=in_specs,
            out_specs=out_specs,
            scratch_shapes=scratch,
        ),
        out_shape=out_shape,
        compiler_params=PARAMS,
        cost_estimate=pl.CostEstimate(
            flops=2 * LAGS * cols * cols * rows, bytes_accessed=6 * rows * cols, transcendentals=0
        ),
        name="second_last" if earlier else "second_part",
    )(switch, *own, coeffs, partner, *earlier)


def local(spectra, quality):
    count = lax.axis_size("chan")
    half = count // 2
    me = lax.axis_index("chan")
    freq_count, _, window_count, cols = spectra.shape
    block = spectra.reshape(-1, cols)

    first_far, second_far = [], []
    for p in range(half):
        if p in (0, half - 1):
            first_far.append((p + half, p))
        elif p % 2 == 0 and p >= half // 2:
            first_far.append((p, p + half))
        elif p in (1, 3):
            second_far.append((p, p + half))
        else:
            second_far.append((p + half, p))
    late_near = [(2, 1), (4, 3)]
    first_pairs = first_far + [(0, 1), (half - 1, half - 2)]
    second_pairs = second_far + late_near
    near_pairs = [(d + 1, d) for d in range(1, count - 1) if d not in (1, 3, half - 2, half - 1)]
    near_pairs += [(0, half - 1), (half - 1, 0)]
    first_back = [(t, s) for s, t in first_far]
    second_back = [(t, s) for s, t in second_far] + [(1, 0)]
    side_pairs = [(0, half - 1), (half - 1, count - 1)]

    def among(devices):
        return functools.reduce(jnp.logical_or, [me == d for d in devices])

    def switch(on, other, *weights):
        flags = jnp.stack([jnp.asarray(on), jnp.asarray(other)]).astype(jnp.int32)
        return jnp.concatenate([flags, *weights])

    near_in = lax.ppermute(block, "chan", near_pairs)
    first_in = lax.ppermute(block, "chan", first_pairs)
    coeffs = lag_rows(freq_count, window_count)
    own = turn(block)
    parts = split(quality[0], block)
    first_flags = lax.ppermute(quality, "chan", first_pairs)[0]
    near_flags = lax.ppermute(quality, "chan", near_pairs)[0]
    special = among([0, half - 1])
    second_switch = switch(
        among([t for _, t in second_pairs]), among([t for _, t in late_near]), quality[0]
    )

    near_in, first_part, last_part, own, coeffs, first_in, near_flags, first_flags = lax.optimization_barrier(
        (near_in, *parts, own, coeffs, first_in, near_flags, first_flags)
    )
    second_in = [lax.ppermute(first_part, "chan", second_pairs)]
    first_switch = switch(me == 0, special, quality[0], near_flags, first_flags)
    operands = first_switch, own, coeffs, near_in, first_in, block
    total, token = first_sums(*operands)
    last_part, token = lax.optimization_barrier((last_part, token))
    second_in.append(lax.ppermute(last_part, "chan", second_pairs))
    near, far, back = first_sums(*operands, [total, token])
    side_returned = lax.ppermute(near, "chan", side_pairs)
    second_switch, near = lax.optimization_barrier((second_switch, near))
    total, = second_sums(second_switch, own, coeffs, second_in[0], 0)
    total, back = lax.optimization_barrier((total, back))
    first_returned = lax.ppermute(back, "chan", first_back)

    near = jnp.where(among([half - 1, count - 1]), side_returned, near)
    near = jnp.where(me == half - 2, far, near)
    far = jnp.where(among([s for s, _ in first_far]), first_returned, far)
    near, far, back = second_sums(
        second_switch, own, coeffs, second_in[1], parts[0].shape[0], [total, near, far, back]
    )
    second_returned = lax.ppermute(back, "chan", second_back)
    near = jnp.where(me == 0, second_returned, near)
    far = jnp.where(among([s for s, _ in second_far]), second_returned, far)
    return near[None], far[None]


def solution(mesh):
    return jax.shard_map(
        local,
        mesh=mesh,
        in_specs=(P(None, None, None, ("grp", "chan")), P(("grp", "chan"), None)),
        out_specs=(P(("grp", "chan"), None, None, None), P(("grp", "chan"), None, None, None)),
        check_vma=False,
    )
```

```python
import functools
import math

import jax
import jax.numpy as jnp
from jax import lax
from jax.experimental import pallas as pl
from jax.experimental.pallas import tpu as pltpu
from jax.sharding import PartitionSpec as P

HL = 4
LAGS = 2 * HL + 1
STEP = 1024
PARTS = (5, 8)
PARAMS = pltpu.CompilerParams(vmem_limit_bytes=16 * 1024 * 1024)


def lag_rows(freq_count, window_count):
    per_bin = 2 * window_count
    row = jnp.arange(freq_count * per_bin, dtype=jnp.int32)
    freq_values = (row // per_bin).astype(jnp.float32)
    sign = jnp.where(row % per_bin < window_count, 1.0, -1.0)
    lag_values = jnp.arange(HL + 1, dtype=jnp.float32)
    phases = jnp.pi / freq_count * lag_values[:, None] * freq_values[None, :]
    factor = 1.0 / math.sqrt(window_count * freq_count)
    cos_part = jnp.cos(phases) * factor
    sin_part = -jnp.sin(phases[1:]) * factor * sign[None, :]
    return jnp.concatenate([cos_part, sin_part], axis=0).astype(jnp.bfloat16)


def split_kernel(middle, windows, flags_ref, x_ref, first_ref, last_ref):
    step = pl.program_id(0)
    masked = weigh(x_ref[...], [flags_ref[w] for w in range(windows)])

    @pl.when(step < middle)
    def _():
        first_ref[...] = masked

    @pl.when(step >= middle)
    def _():
        last_ref[...] = masked


def split(flags, x):
    rows, cols = x.shape
    steps = rows // STEP
    middle = steps * PARTS[0] // PARTS[1]
    return pl.pallas_call(
        functools.partial(split_kernel, middle, flags.shape[0]),
        grid_spec=pltpu.PrefetchScalarGridSpec(
            num_scalar_prefetch=1,
            grid=(steps,),
            in_specs=[pl.BlockSpec((STEP, cols), lambda s, on: (s, 0))],
            out_specs=[
                pl.BlockSpec((STEP, cols), lambda s, on: (jnp.minimum(s, middle - 1), 0)),
                pl.BlockSpec((STEP, cols), lambda s, on: (jnp.maximum(s - middle, 0), 0)),
            ],
        ),
        out_shape=[jax.ShapeDtypeStruct((n * STEP, cols), x.dtype) for n in (middle, steps - middle)],
        compiler_params=PARAMS,
        cost_estimate=pl.CostEstimate(flops=rows * cols, bytes_accessed=4 * rows * cols, transcendentals=0),
        name="split",
    )(flags, x)


def turned(x):
    rows, cols = x.shape
    same = lax.broadcasted_iota(jnp.int32, (cols, cols), 0) == lax.broadcasted_iota(jnp.int32, (cols, cols), 1)
    eye = jnp.where(same, 1.0, 0.0).astype(jnp.bfloat16)
    source = lax.broadcasted_iota(jnp.int32, (2 * cols, 2 * cols), 0)
    target = lax.broadcasted_iota(jnp.int32, (2 * cols, 2 * cols), 1)
    exchange = jnp.where((source ^ 4) == target, 1.0, 0.0).astype(jnp.bfloat16)
    plain = lax.dot_general(eye, x, (((1,), (1,)), ((), ())), preferred_element_type=jnp.float32)
    plain = plain.astype(jnp.bfloat16)
    swapped = [
        jnp.dot(plain[:, t:t + 2 * cols], exchange, preferred_element_type=jnp.float32).astype(jnp.bfloat16)
        for t in range(0, rows, 2 * cols)
    ]
    return plain, jnp.concatenate(swapped, axis=1)


def turn_kernel(x_ref, plain_ref, swapped_ref, token_ref):
    plain_ref[...], swapped_ref[...] = turned(x_ref[...])
    token_ref[...] = x_ref[:16, :]


def turn(x):
    rows, cols = x.shape
    out = jax.ShapeDtypeStruct((cols, rows), jnp.bfloat16)
    return pl.pallas_call(
        turn_kernel,
        grid=(rows // STEP,),
        in_specs=[pl.BlockSpec((STEP, cols), lambda s: (s, 0))],
        out_specs=[pl.BlockSpec((cols, STEP), lambda s: (0, s))] * 2 + [pl.BlockSpec((16, cols), lambda s: (0, 0))],
        out_shape=[out, out, jax.ShapeDtypeStruct((16, cols), jnp.bfloat16)],
        compiler_params=PARAMS,
        cost_estimate=pl.CostEstimate(flops=0, bytes_accessed=6 * rows * cols, transcendentals=0),
        name="turn",
    )(x)


def write_lags(out, acc, at, cols, mirrored):
    for lag in range(LAGS):
        k = abs(lag - HL)
        value = acc[k * cols:(k + 1) * cols, at]
        if k:
            odd = acc[(HL + k) * cols:(HL + k + 1) * cols, at]
            value = value + odd if lag > HL else value - odd
        value = value.astype(jnp.bfloat16)
        if mirrored:
            out[LAGS - 1 - lag] = value.T
        else:
            out[lag] = value


def scale(scaled, plain, swapped, coeff_ref):
    cols = plain.shape[0]
    for k in range(LAGS):
        part = plain if k <= HL else swapped
        scaled[k * cols:(k + 1) * cols, :] = part * coeff_ref[k:k + 1, :]


def weigh(x, window_weights):
    rows, cols = x.shape
    window = lax.broadcasted_iota(jnp.int32, (16, cols), 0) % len(window_weights)
    weights = jnp.zeros((16, cols), jnp.float32)
    for w, weight in enumerate(window_weights):
        weights = jnp.where(window == w, weight.astype(jnp.float32), weights)
    weights = jnp.broadcast_to(weights.astype(jnp.bfloat16)[None], (rows // 16, 16, cols))
    return x * weights.reshape(rows, cols)


def first_kernel(windows, last, switch_ref, plain_ref, swapped_ref, coeff_ref, near_ref, first_ref, own_ref, *rest):
    step = pl.program_id(0)
    cols = plain_ref.shape[0]
    near_mirrored, special = switch_ref[0], switch_ref[1]
    if last:
        acc_in, _, near_out, far_out, back_out, acc, scaled, plain, swapped, own_rows, arrived = rest
    else:
        _, _, _, acc, token_out, scaled, plain, swapped, own_rows, arrived = rest
    size = own_rows.shape[0]
    begin = size if last else 0

    @pl.when(step == 0)
    def _():
        if last:
            acc[...] = acc_in[...]
        else:
            acc[...] = jnp.zeros_like(acc)
            token_out[...] = jnp.zeros_like(token_out)

    @pl.when(special == 0)
    def _():
        plain[...], swapped[...] = plain_ref[...], swapped_ref[...]

    @pl.when((special != 0) & (step == 0))
    def _():
        copy = pltpu.make_async_copy(own_ref.at[pl.ds(begin, size)], own_rows, arrived)
        copy.start()
        copy.wait()

    @pl.when(special != 0)
    def _():
        plain[...], swapped[...] = turned(first_ref[...])

    scale(scaled, plain[...], swapped[...], coeff_ref)
    flags = [[switch_ref[2 + part * windows + w] for w in range(windows)] for part in range(3)]
    near_weights = [jnp.where(special != 0, first, own) * near for own, near, first in zip(*flags)]
    near = weigh(near_ref[...], near_weights)
    own_tile = own_rows[pl.ds(pl.multiple_of(step * STEP, STEP), STEP), :]
    far = weigh(jnp.where(special != 0, own_tile, first_ref[...]), [own * first for own, _, first in zip(*flags)])
    acc[...] += jnp.dot(scaled[...], jnp.concatenate([near, far], axis=1), preferred_element_type=jnp.float32)

    if last:
        @pl.when(step == pl.num_programs(0) - 1)
        def _():
            near_at, far_at = slice(0, cols), slice(cols, 2 * cols)

            @pl.when(special == 0)
            def _():
                write_lags(back_out, acc, far_at, cols, True)
                write_lags(far_out, acc, far_at, cols, False)

            @pl.when(special != 0)
            def _():
                write_lags(back_out, acc, far_at, cols, False)
                write_lags(far_out, acc, far_at, cols, True)

            pl.when(near_mirrored == 0)(lambda: write_lags(near_out, acc, near_at, cols, False))
            pl.when(near_mirrored != 0)(lambda: write_lags(near_out, acc, near_at, cols, True))


def first_sums(switch, own, coeffs, near_in, first_in, block, earlier, last):
    rows, cols = block.shape
    steps = rows // STEP // 2
    skip = steps if last else 0
    windows = (switch.shape[0] - 2) // 3
    result = jax.ShapeDtypeStruct((LAGS, cols, cols), jnp.bfloat16)
    total = jax.ShapeDtypeStruct((LAGS * cols, 2 * cols), jnp.float32)
    total_spec = pl.BlockSpec(total.shape, lambda s, on: (0, 0))
    token = jax.ShapeDtypeStruct((8, cols), jnp.float32)
    token_spec = pl.BlockSpec(token.shape, lambda s, on: (0, 0))
    left = pl.BlockSpec((cols, STEP), lambda s, on: (0, (s + skip) * (1 - on[1])))
    right = pl.BlockSpec((STEP, cols), lambda s, on: (s + skip, 0))
    in_specs = [left, left, pl.BlockSpec((LAGS, STEP), lambda s, on: (0, s + skip)), right, right,
                pl.BlockSpec(memory_space=pltpu.HBM)]
    scratch = [pltpu.VMEM((LAGS * cols, STEP), jnp.bfloat16)] + [pltpu.VMEM((cols, STEP), jnp.bfloat16)] * 2
    scratch += [pltpu.VMEM((steps * STEP, cols), jnp.bfloat16), pltpu.SemaphoreType.DMA(())]
    if not last:
        in_specs += [pl.BlockSpec((16, cols), lambda s, on: (0, 0))] * 3
        out_shape, out_specs = [total, token], [total_spec, token_spec]
    else:
        in_specs += [total_spec, token_spec]
        out_shape = [result] * 3
        out_specs = [pl.BlockSpec(result.shape, lambda s, on: (0, 0, 0))] * 3
        scratch = [pltpu.VMEM(total.shape, jnp.float32)] + scratch
    return pl.pallas_call(
        functools.partial(first_kernel, windows, last),
        grid_spec=pltpu.PrefetchScalarGridSpec(
            num_scalar_prefetch=1,
            grid=(steps,),
            in_specs=in_specs,
            out_specs=out_specs,
            scratch_shapes=scratch,
        ),
        out_shape=out_shape,
        compiler_params=PARAMS,
        cost_estimate=pl.CostEstimate(
            flops=2 * LAGS * cols * cols * rows, bytes_accessed=4 * rows * cols, transcendentals=0
        ),
        name="first_last" if last else "first_half",
    )(switch, *own, coeffs, near_in, first_in, block, *earlier)


def second_kernel(windows, first, switch_ref, plain_ref, swapped_ref, coeff_ref, partner_ref, *rest):
    on, late_near = switch_ref[0], switch_ref[1]
    step = pl.program_id(0)
    cols = plain_ref.shape[0]
    if first:
        acc, scaled = rest
    else:
        acc_in, near_in, far_in, back_in, near_out, far_out, back_out, acc, scaled = rest

    @pl.when(on != 0)
    def _():
        @pl.when(step == 0)
        def _():
            acc[...] = jnp.zeros_like(acc) if first else acc_in[...]

        scale(scaled, plain_ref[...], swapped_ref[...], coeff_ref)
        partner = weigh(partner_ref[...], [switch_ref[2 + w] for w in range(windows)])
        acc[...] += jnp.dot(scaled[...], partner, preferred_element_type=jnp.float32)

    if not first:
        @pl.when(step == pl.num_programs(0) - 1)
        def _():
            here = slice(0, cols)

            @pl.when((on != 0) & (late_near == 0))
            def _():
                write_lags(back_out, acc, here, cols, True)
                write_lags(far_out, acc, here, cols, False)

            @pl.when((on == 0) | (late_near != 0))
            def _():
                back_out[...] = back_in[...]
                far_out[...] = far_in[...]

            pl.when(late_near != 0)(lambda: write_lags(near_out, acc, here, cols, False))

            @pl.when(late_near == 0)
            def _():
                near_out[...] = near_in[...]


def second_sums(switch, own, coeffs, partner, start, earlier=None):
    rows, cols = partner.shape
    windows = switch.shape[0] - 2
    skip = start // STEP
    total = jax.ShapeDtypeStruct((LAGS * cols, cols), jnp.float32)
    total_spec = pl.BlockSpec(total.shape, lambda s, on: (0, 0))
    result = jax.ShapeDtypeStruct((LAGS, cols, cols), jnp.bfloat16)
    result_spec = pl.BlockSpec(result.shape, lambda s, on: (0, 0, 0))
    left = pl.BlockSpec((cols, STEP), lambda s, on: (0, s * on[0] + skip))
    in_specs = [left, left, pl.BlockSpec((LAGS, STEP), lambda s, on: (0, s * on[0] + skip)),
                pl.BlockSpec((STEP, cols), lambda s, on: (s * on[0], 0))]
    scratch = [pltpu.VMEM((LAGS * cols, STEP), jnp.bfloat16)]
    if earlier is None:
        out_shape, out_specs, earlier = [total], [total_spec], []
    else:
        out_shape, out_specs = [result] * 3, [result_spec] * 3
        in_specs += [total_spec] + [result_spec] * 3
        scratch = [pltpu.VMEM(total.shape, jnp.float32)] + scratch
    return pl.pallas_call(
        functools.partial(second_kernel, windows, not earlier),
        grid_spec=pltpu.PrefetchScalarGridSpec(
            num_scalar_prefetch=1,
            grid=(rows // STEP,),
            in_specs=in_specs,
            out_specs=out_specs,
            scratch_shapes=scratch,
        ),
        out_shape=out_shape,
        compiler_params=PARAMS,
        cost_estimate=pl.CostEstimate(
            flops=2 * LAGS * cols * cols * rows, bytes_accessed=6 * rows * cols, transcendentals=0
        ),
        name="second_last" if earlier else "second_part",
    )(switch, *own, coeffs, partner, *earlier)


def local(spectra, quality):
    count = lax.axis_size("chan")
    half = count // 2
    me = lax.axis_index("chan")
    freq_count, _, window_count, cols = spectra.shape
    block = spectra.reshape(-1, cols)

    first_far, second_far = [], []
    for p in range(half):
        if p in (0, half - 1):
            first_far.append((p + half, p))
        elif p % 2 == 0 and p >= half // 2:
            first_far.append((p, p + half))
        elif p in (1, 3):
            second_far.append((p, p + half))
        else:
            second_far.append((p + half, p))
    late_near = [(2, 1), (4, 3)]
    first_pairs = first_far + [(0, 1), (half - 1, half - 2)]
    second_pairs = second_far + late_near
    near_pairs = [(d + 1, d) for d in range(1, count - 1) if d not in (1, 3, half - 2, half - 1)]
    near_pairs += [(0, half - 1), (half - 1, 0)]
    first_back = [(t, s) for s, t in first_far]
    second_back = [(t, s) for s, t in second_far] + [(1, 0)]
    side_pairs = [(0, half - 1), (half - 1, count - 1)]

    def among(devices):
        return functools.reduce(jnp.logical_or, [me == d for d in devices])

    def switch(on, other, *weights):
        flags = jnp.stack([jnp.asarray(on), jnp.asarray(other)]).astype(jnp.int32)
        return jnp.concatenate([flags, *weights])

    near_in = lax.ppermute(block, "chan", near_pairs)
    first_in = lax.ppermute(block, "chan", first_pairs)
    coeffs = lag_rows(freq_count, window_count)
    *own, token = turn(block)
    parts = split(quality[0], block)
    first_flags = lax.ppermute(quality, "chan", first_pairs)[0]
    near_flags = lax.ppermute(quality, "chan", near_pairs)[0]
    special = among([0, half - 1])
    second_switch = switch(
        among([t for _, t in second_pairs]), among([t for _, t in late_near]), quality[0]
    )

    first_part, coeffs, near_flags, first_flags, *tokens = lax.optimization_barrier(
        (parts[0], coeffs, near_flags, first_flags, near_in[:16], first_in[:16], token)
    )
    second_in = [lax.ppermute(first_part, "chan", second_pairs)]
    first_switch = switch(me == 0, special, quality[0], near_flags, first_flags)
    operands = first_switch, own, coeffs, near_in, first_in, block
    total, token = first_sums(*operands, tokens, False)
    last_part, token = lax.optimization_barrier((parts[1], token))
    second_in.append(lax.ppermute(last_part, "chan", second_pairs))
    near, far, back = first_sums(*operands, [total, token], True)
    side_returned = lax.ppermute(near, "chan", side_pairs)
    second_switch, near = lax.optimization_barrier((second_switch, near))
    total, = second_sums(second_switch, own, coeffs, second_in[0], 0)
    total, back = lax.optimization_barrier((total, back))
    first_returned = lax.ppermute(back, "chan", first_back)

    near = jnp.where(among([half - 1, count - 1]), side_returned, near)
    near = jnp.where(me == half - 2, far, near)
    far = jnp.where(among([s for s, _ in first_far]), first_returned, far)
    near, far, back = second_sums(
        second_switch, own, coeffs, second_in[1], parts[0].shape[0], [total, near, far, back]
    )
    second_returned = lax.ppermute(back, "chan", second_back)
    near = jnp.where(me == 0, second_returned, near)
    far = jnp.where(among([s for s, _ in second_far]), second_returned, far)
    return near[None], far[None]


def solution(mesh):
    return jax.shard_map(
        local,
        mesh=mesh,
        in_specs=(P(None, None, None, ("grp", "chan")), P(("grp", "chan"), None)),
        out_specs=(P(("grp", "chan"), None, None, None), P(("grp", "chan"), None, None, None)),
        check_vma=False,
    )
```

```python
import functools
import math

import jax
import jax.numpy as jnp
from jax import lax
from jax.experimental import pallas as pl
from jax.experimental.pallas import tpu as pltpu
from jax.sharding import PartitionSpec as P

HL = 4
LAGS = 2 * HL + 1
STEP = 1024
PARTS = (5, 8)
PARAMS = pltpu.CompilerParams(vmem_limit_bytes=16 * 1024 * 1024)


def lag_rows(freq_count, window_count):
    per_bin = 2 * window_count
    row = jnp.arange(freq_count * per_bin, dtype=jnp.int32)
    freq_values = (row // per_bin).astype(jnp.float32)
    sign = jnp.where(row % per_bin < window_count, 1.0, -1.0)
    lag_values = jnp.arange(HL + 1, dtype=jnp.float32)
    phases = jnp.pi / freq_count * lag_values[:, None] * freq_values[None, :]
    factor = 1.0 / math.sqrt(window_count * freq_count)
    cos_part = jnp.cos(phases) * factor
    sin_part = -jnp.sin(phases[1:]) * factor * sign[None, :]
    return jnp.concatenate([cos_part, sin_part], axis=0).astype(jnp.bfloat16)


def split_kernel(middle, windows, flags_ref, x_ref, first_ref, last_ref):
    step = pl.program_id(0)
    masked = weigh(x_ref[...], [flags_ref[w] for w in range(windows)])

    @pl.when(step < middle)
    def _():
        first_ref[...] = masked

    @pl.when(step >= middle)
    def _():
        last_ref[...] = masked


def split(flags, x):
    rows, cols = x.shape
    steps = rows // STEP
    middle = steps * PARTS[0] // PARTS[1]
    return pl.pallas_call(
        functools.partial(split_kernel, middle, flags.shape[0]),
        grid_spec=pltpu.PrefetchScalarGridSpec(
            num_scalar_prefetch=1,
            grid=(steps,),
            in_specs=[pl.BlockSpec((STEP, cols), lambda s, on: (s, 0))],
            out_specs=[
                pl.BlockSpec((STEP, cols), lambda s, on: (jnp.minimum(s, middle - 1), 0)),
                pl.BlockSpec((STEP, cols), lambda s, on: (jnp.maximum(s - middle, 0), 0)),
            ],
        ),
        out_shape=[jax.ShapeDtypeStruct((n * STEP, cols), x.dtype) for n in (middle, steps - middle)],
        compiler_params=PARAMS,
        cost_estimate=pl.CostEstimate(flops=rows * cols, bytes_accessed=4 * rows * cols, transcendentals=0),
        name="split",
    )(flags, x)


def turned(x):
    rows, cols = x.shape
    same = lax.broadcasted_iota(jnp.int32, (cols, cols), 0) == lax.broadcasted_iota(jnp.int32, (cols, cols), 1)
    eye = jnp.where(same, 1.0, 0.0).astype(jnp.bfloat16)
    source = lax.broadcasted_iota(jnp.int32, (2 * cols, 2 * cols), 0)
    target = lax.broadcasted_iota(jnp.int32, (2 * cols, 2 * cols), 1)
    exchange = jnp.where((source ^ 4) == target, 1.0, 0.0).astype(jnp.bfloat16)
    plain = lax.dot_general(eye, x, (((1,), (1,)), ((), ())), preferred_element_type=jnp.float32)
    plain = plain.astype(jnp.bfloat16)
    swapped = [
        jnp.dot(plain[:, t:t + 2 * cols], exchange, preferred_element_type=jnp.float32).astype(jnp.bfloat16)
        for t in range(0, rows, 2 * cols)
    ]
    return plain, jnp.concatenate(swapped, axis=1)


def turn_kernel(x_ref, plain_ref, swapped_ref):
    plain_ref[...], swapped_ref[...] = turned(x_ref[...])


def turn(x):
    rows, cols = x.shape
    out = jax.ShapeDtypeStruct((cols, rows), jnp.bfloat16)
    return pl.pallas_call(
        turn_kernel,
        grid=(rows // STEP,),
        in_specs=[pl.BlockSpec((STEP, cols), lambda s: (s, 0))],
        out_specs=[pl.BlockSpec((cols, STEP), lambda s: (0, s))] * 2,
        out_shape=[out, out],
        compiler_params=PARAMS,
        cost_estimate=pl.CostEstimate(flops=0, bytes_accessed=6 * rows * cols, transcendentals=0),
        name="turn",
    )(x)


def write_lags(out, acc, at, cols, mirrored):
    for lag in range(LAGS):
        k = abs(lag - HL)
        value = acc[k * cols:(k + 1) * cols, at]
        if k:
            odd = acc[(HL + k) * cols:(HL + k + 1) * cols, at]
            value = value + odd if lag > HL else value - odd
        value = value.astype(jnp.bfloat16)
        if mirrored:
            out[LAGS - 1 - lag] = value.T
        else:
            out[lag] = value


def scale(scaled, plain, swapped, coeff_ref):
    cols = plain.shape[0]
    for k in range(LAGS):
        part = plain if k <= HL else swapped
        scaled[k * cols:(k + 1) * cols, :] = part * coeff_ref[k:k + 1, :]


def weigh(x, window_weights):
    rows, cols = x.shape
    window = lax.broadcasted_iota(jnp.int32, (16, cols), 0) % len(window_weights)
    weights = jnp.zeros((16, cols), jnp.float32)
    for w, weight in enumerate(window_weights):
        weights = jnp.where(window == w, weight.astype(jnp.float32), weights)
    weights = jnp.broadcast_to(weights.astype(jnp.bfloat16)[None], (rows // 16, 16, cols))
    return x * weights.reshape(rows, cols)


def first_kernel(windows, last, switch_ref, plain_ref, swapped_ref, coeff_ref, near_ref, first_ref, own_ref, *rest):
    step = pl.program_id(0)
    cols = plain_ref.shape[0]
    near_mirrored, special = switch_ref[0], switch_ref[1]
    if last:
        acc_in, _, near_out, far_out, back_out, acc, scaled, plain, swapped = rest
    else:
        acc, token_out, scaled, plain, swapped = rest

    @pl.when(step == 0)
    def _():
        if last:
            acc[...] = acc_in[...]
        else:
            acc[...] = jnp.zeros_like(acc)
            token_out[...] = jnp.zeros_like(token_out)

    @pl.when(special == 0)
    def _():
        plain[...], swapped[...] = plain_ref[...], swapped_ref[...]

    @pl.when(special != 0)
    def _():
        plain[...], swapped[...] = turned(first_ref[...])

    scale(scaled, plain[...], swapped[...], coeff_ref)
    flags = [[switch_ref[2 + part * windows + w] for w in range(windows)] for part in range(3)]
    near_weights = [jnp.where(special != 0, first, own) * near for own, near, first in zip(*flags)]
    near = weigh(near_ref[...], near_weights)
    far = weigh(jnp.where(special != 0, own_ref[...], first_ref[...]), [own * first for own, _, first in zip(*flags)])
    acc[...] += jnp.dot(scaled[...], jnp.concatenate([near, far], axis=1), preferred_element_type=jnp.float32)

    if last:
        @pl.when(step == pl.num_programs(0) - 1)
        def _():
            near_at, far_at = slice(0, cols), slice(cols, 2 * cols)

            @pl.when(special == 0)
            def _():
                write_lags(back_out, acc, far_at, cols, True)
                write_lags(far_out, acc, far_at, cols, False)

            @pl.when(special != 0)
            def _():
                write_lags(back_out, acc, far_at, cols, False)
                write_lags(far_out, acc, far_at, cols, True)

            pl.when(near_mirrored == 0)(lambda: write_lags(near_out, acc, near_at, cols, False))
            pl.when(near_mirrored != 0)(lambda: write_lags(near_out, acc, near_at, cols, True))


def first_sums(switch, own, coeffs, near_in, first_in, block, earlier=None):
    rows, cols = block.shape
    steps = rows // STEP // 2
    skip = 0 if earlier is None else steps
    windows = (switch.shape[0] - 2) // 3
    result = jax.ShapeDtypeStruct((LAGS, cols, cols), jnp.bfloat16)
    total = jax.ShapeDtypeStruct((LAGS * cols, 2 * cols), jnp.float32)
    total_spec = pl.BlockSpec(total.shape, lambda s, on: (0, 0))
    token = jax.ShapeDtypeStruct((8, cols), jnp.float32)
    token_spec = pl.BlockSpec(token.shape, lambda s, on: (0, 0))
    left = pl.BlockSpec((cols, STEP), lambda s, on: (0, (s + skip) * (1 - on[1])))
    right = pl.BlockSpec((STEP, cols), lambda s, on: (s + skip, 0))
    right_special = pl.BlockSpec((STEP, cols), lambda s, on: ((s + skip) * on[1], 0))
    in_specs = [left, left, pl.BlockSpec((LAGS, STEP), lambda s, on: (0, s + skip)), right, right, right_special]
    scratch = [pltpu.VMEM((LAGS * cols, STEP), jnp.bfloat16)] + [pltpu.VMEM((cols, STEP), jnp.bfloat16)] * 2
    if earlier is None:
        out_shape, out_specs, earlier = [total, token], [total_spec, token_spec], []
    else:
        in_specs += [total_spec, token_spec]
        out_shape = [result] * 3
        out_specs = [pl.BlockSpec(result.shape, lambda s, on: (0, 0, 0))] * 3
        scratch = [pltpu.VMEM(total.shape, jnp.float32)] + scratch
    return pl.pallas_call(
        functools.partial(first_kernel, windows, bool(earlier)),
        grid_spec=pltpu.PrefetchScalarGridSpec(
            num_scalar_prefetch=1,
            grid=(steps,),
            in_specs=in_specs,
            out_specs=out_specs,
            scratch_shapes=scratch,
        ),
        out_shape=out_shape,
        compiler_params=PARAMS,
        cost_estimate=pl.CostEstimate(
            flops=2 * LAGS * cols * cols * rows, bytes_accessed=4 * rows * cols, transcendentals=0
        ),
        name="first_last" if earlier else "first_half",
    )(switch, *own, coeffs, near_in, first_in, block, *earlier)


def second_kernel(windows, first, switch_ref, plain_ref, swapped_ref, coeff_ref, partner_ref, *rest):
    on, late_near = switch_ref[0], switch_ref[1]
    step = pl.program_id(0)
    cols = plain_ref.shape[0]
    if first:
        acc, scaled = rest
    else:
        acc_in, near_in, far_in, back_in, near_out, far_out, back_out, acc, scaled = rest

    @pl.when(on != 0)
    def _():
        @pl.when(step == 0)
        def _():
            acc[...] = jnp.zeros_like(acc) if first else acc_in[...]

        scale(scaled, plain_ref[...], swapped_ref[...], coeff_ref)
        partner = weigh(partner_ref[...], [switch_ref[2 + w] for w in range(windows)])
        acc[...] += jnp.dot(scaled[...], partner, preferred_element_type=jnp.float32)

    if not first:
        @pl.when(step == pl.num_programs(0) - 1)
        def _():
            here = slice(0, cols)

            @pl.when((on != 0) & (late_near == 0))
            def _():
                write_lags(back_out, acc, here, cols, True)
                write_lags(far_out, acc, here, cols, False)

            @pl.when((on == 0) | (late_near != 0))
            def _():
                back_out[...] = back_in[...]
                far_out[...] = far_in[...]

            pl.when(late_near != 0)(lambda: write_lags(near_out, acc, here, cols, False))

            @pl.when(late_near == 0)
            def _():
                near_out[...] = near_in[...]


def second_sums(switch, own, coeffs, partner, start, earlier=None):
    rows, cols = partner.shape
    windows = switch.shape[0] - 2
    skip = start // STEP
    total = jax.ShapeDtypeStruct((LAGS * cols, cols), jnp.float32)
    total_spec = pl.BlockSpec(total.shape, lambda s, on: (0, 0))
    result = jax.ShapeDtypeStruct((LAGS, cols, cols), jnp.bfloat16)
    result_spec = pl.BlockSpec(result.shape, lambda s, on: (0, 0, 0))
    left = pl.BlockSpec((cols, STEP), lambda s, on: (0, s * on[0] + skip))
    in_specs = [left, left, pl.BlockSpec((LAGS, STEP), lambda s, on: (0, s * on[0] + skip)),
                pl.BlockSpec((STEP, cols), lambda s, on: (s * on[0], 0))]
    scratch = [pltpu.VMEM((LAGS * cols, STEP), jnp.bfloat16)]
    if earlier is None:
        out_shape, out_specs, earlier = [total], [total_spec], []
    else:
        out_shape, out_specs = [result] * 3, [result_spec] * 3
        in_specs += [total_spec] + [result_spec] * 3
        scratch = [pltpu.VMEM(total.shape, jnp.float32)] + scratch
    return pl.pallas_call(
        functools.partial(second_kernel, windows, not earlier),
        grid_spec=pltpu.PrefetchScalarGridSpec(
            num_scalar_prefetch=1,
            grid=(rows // STEP,),
            in_specs=in_specs,
            out_specs=out_specs,
            scratch_shapes=scratch,
        ),
        out_shape=out_shape,
        compiler_params=PARAMS,
        cost_estimate=pl.CostEstimate(
            flops=2 * LAGS * cols * cols * rows, bytes_accessed=6 * rows * cols, transcendentals=0
        ),
        name="second_last" if earlier else "second_part",
    )(switch, *own, coeffs, partner, *earlier)


def local(spectra, quality):
    count = lax.axis_size("chan")
    half = count // 2
    me = lax.axis_index("chan")
    freq_count, _, window_count, cols = spectra.shape
    block = spectra.reshape(-1, cols)

    first_far, second_far = [], []
    for p in range(half):
        if p in (0, half - 1):
            first_far.append((p + half, p))
        elif p % 2 == 0 and p >= half // 2:
            first_far.append((p, p + half))
        elif p in (1, 3):
            second_far.append((p, p + half))
        else:
            second_far.append((p + half, p))
    late_near = [(2, 1), (4, 3)]
    first_pairs = first_far + [(0, 1), (half - 1, half - 2)]
    second_pairs = second_far + late_near
    near_pairs = [(d + 1, d) for d in range(1, count - 1) if d not in (1, 3, half - 2, half - 1)]
    near_pairs += [(0, half - 1), (half - 1, 0)]
    first_back = [(t, s) for s, t in first_far]
    second_back = [(t, s) for s, t in second_far] + [(1, 0)]
    side_pairs = [(0, half - 1), (half - 1, count - 1)]

    def among(devices):
        return functools.reduce(jnp.logical_or, [me == d for d in devices])

    def switch(on, other, *weights):
        flags = jnp.stack([jnp.asarray(on), jnp.asarray(other)]).astype(jnp.int32)
        return jnp.concatenate([flags, *weights])

    near_in = lax.ppermute(block, "chan", near_pairs)
    first_in = lax.ppermute(block, "chan", first_pairs)
    coeffs = lag_rows(freq_count, window_count)
    own = turn(block)
    parts = split(quality[0], block)
    first_flags = lax.ppermute(quality, "chan", first_pairs)[0]
    near_flags = lax.ppermute(quality, "chan", near_pairs)[0]
    special = among([0, half - 1])
    second_switch = switch(
        among([t for _, t in second_pairs]), among([t for _, t in late_near]), quality[0]
    )

    near_in, first_part, last_part, own, coeffs, first_in, near_flags, first_flags = lax.optimization_barrier(
        (near_in, *parts, own, coeffs, first_in, near_flags, first_flags)
    )
    second_in = [lax.ppermute(first_part, "chan", second_pairs)]
    first_switch = switch(me == 0, special, quality[0], near_flags, first_flags)
    operands = first_switch, own, coeffs, near_in, first_in, block
    total, token = first_sums(*operands)
    last_part, token = lax.optimization_barrier((last_part, token))
    second_in.append(lax.ppermute(last_part, "chan", second_pairs))
    near, far, back = first_sums(*operands, [total, token])
    side_returned = lax.ppermute(near, "chan", side_pairs)
    second_switch, near = lax.optimization_barrier((second_switch, near))
    total, = second_sums(second_switch, own, coeffs, second_in[0], 0)
    total, back = lax.optimization_barrier((total, back))
    first_returned = lax.ppermute(back, "chan", first_back)

    near = jnp.where(among([half - 1, count - 1]), side_returned, near)
    near = jnp.where(me == half - 2, far, near)
    far = jnp.where(among([s for s, _ in first_far]), first_returned, far)
    near, far, back = second_sums(
        second_switch, own, coeffs, second_in[1], parts[0].shape[0], [total, near, far, back]
    )
    second_returned = lax.ppermute(back, "chan", second_back)
    near = jnp.where(me == 0, second_returned, near)
    far = jnp.where(among([s for s, _ in second_far]), second_returned, far)
    return near[None], far[None]


def solution(mesh):
    return jax.shard_map(
        local,
        mesh=mesh,
        in_specs=(P(None, None, None, ("grp", "chan")), P(("grp", "chan"), None)),
        out_specs=(P(("grp", "chan"), None, None, None), P(("grp", "chan"), None, None, None)),
        check_vma=False,
    )
```

```python
import functools
import math

import jax
import jax.numpy as jnp
from jax import lax
from jax.experimental import pallas as pl
from jax.experimental.pallas import tpu as pltpu
from jax.sharding import PartitionSpec as P

HL = 4
LAGS = 2 * HL + 1
STEP = 1024
PARTS = (5, 8)
PARAMS = pltpu.CompilerParams(vmem_limit_bytes=16 * 1024 * 1024)


def lag_rows(freq_count, window_count):
    per_bin = 2 * window_count
    row = jnp.arange(freq_count * per_bin, dtype=jnp.int32)
    freq_values = (row // per_bin).astype(jnp.float32)
    sign = jnp.where(row % per_bin < window_count, 1.0, -1.0)
    lag_values = jnp.arange(HL + 1, dtype=jnp.float32)
    phases = jnp.pi / freq_count * lag_values[:, None] * freq_values[None, :]
    factor = 1.0 / math.sqrt(window_count * freq_count)
    cos_part = jnp.cos(phases) * factor
    sin_part = -jnp.sin(phases[1:]) * factor * sign[None, :]
    return jnp.concatenate([cos_part, sin_part], axis=0).astype(jnp.bfloat16)


def split_kernel(middle, x_ref, first_ref, last_ref):
    step = pl.program_id(0)

    @pl.when(step < middle)
    def _():
        first_ref[...] = x_ref[...]

    @pl.when(step >= middle)
    def _():
        last_ref[...] = x_ref[...]


def split(x):
    rows, cols = x.shape
    steps = rows // STEP
    middle = steps * PARTS[0] // PARTS[1]
    return pl.pallas_call(
        functools.partial(split_kernel, middle),
        grid=(steps,),
        in_specs=[pl.BlockSpec((STEP, cols), lambda s: (s, 0))],
        out_specs=[
            pl.BlockSpec((STEP, cols), lambda s: (jnp.minimum(s, middle - 1), 0)),
            pl.BlockSpec((STEP, cols), lambda s: (jnp.maximum(s - middle, 0), 0)),
        ],
        out_shape=[jax.ShapeDtypeStruct((n * STEP, cols), x.dtype) for n in (middle, steps - middle)],
        compiler_params=PARAMS,
        cost_estimate=pl.CostEstimate(flops=0, bytes_accessed=4 * rows * cols, transcendentals=0),
        name="split",
    )(x)


def turned(x):
    rows, cols = x.shape
    same = lax.broadcasted_iota(jnp.int32, (cols, cols), 0) == lax.broadcasted_iota(jnp.int32, (cols, cols), 1)
    eye = jnp.where(same, 1.0, 0.0).astype(jnp.bfloat16)
    source = lax.broadcasted_iota(jnp.int32, (2 * cols, 2 * cols), 0)
    target = lax.broadcasted_iota(jnp.int32, (2 * cols, 2 * cols), 1)
    exchange = jnp.where((source ^ 4) == target, 1.0, 0.0).astype(jnp.bfloat16)
    plain = lax.dot_general(eye, x, (((1,), (1,)), ((), ())), preferred_element_type=jnp.float32)
    plain = plain.astype(jnp.bfloat16)
    swapped = [
        jnp.dot(plain[:, t:t + 2 * cols], exchange, preferred_element_type=jnp.float32).astype(jnp.bfloat16)
        for t in range(0, rows, 2 * cols)
    ]
    return plain, jnp.concatenate(swapped, axis=1)


def turn_kernel(x_ref, plain_ref, swapped_ref):
    plain_ref[...], swapped_ref[...] = turned(x_ref[...])


def turn(x):
    rows, cols = x.shape
    out = jax.ShapeDtypeStruct((cols, rows), jnp.bfloat16)
    return pl.pallas_call(
        turn_kernel,
        grid=(rows // STEP,),
        in_specs=[pl.BlockSpec((STEP, cols), lambda s: (s, 0))],
        out_specs=[pl.BlockSpec((cols, STEP), lambda s: (0, s))] * 2,
        out_shape=[out, out],
        compiler_params=PARAMS,
        cost_estimate=pl.CostEstimate(flops=0, bytes_accessed=6 * rows * cols, transcendentals=0),
        name="turn",
    )(x)


def write_lags(out, acc, at, cols, mirrored):
    for lag in range(LAGS):
        k = abs(lag - HL)
        value = acc[k * cols:(k + 1) * cols, at]
        if k:
            odd = acc[(HL + k) * cols:(HL + k + 1) * cols, at]
            value = value + odd if lag > HL else value - odd
        value = value.astype(jnp.bfloat16)
        if mirrored:
            out[LAGS - 1 - lag] = value.T
        else:
            out[lag] = value


def scale(scaled, plain, swapped, coeff_ref):
    cols = plain.shape[0]
    for k in range(LAGS):
        part = plain if k <= HL else swapped
        scaled[k * cols:(k + 1) * cols, :] = part * coeff_ref[k:k + 1, :]


def weigh(x, window_weights):
    rows, cols = x.shape
    window = lax.broadcasted_iota(jnp.int32, (16, cols), 0) % len(window_weights)
    weights = jnp.zeros((16, cols), jnp.float32)
    for w, weight in enumerate(window_weights):
        weights = jnp.where(window == w, weight.astype(jnp.float32), weights)
    weights = jnp.broadcast_to(weights.astype(jnp.bfloat16)[None], (rows // 16, 16, cols))
    return x * weights.reshape(rows, cols)


def first_kernel(windows, last, switch_ref, plain_ref, swapped_ref, coeff_ref, near_ref, first_ref, own_ref, *rest):
    step = pl.program_id(0)
    cols = plain_ref.shape[0]
    near_mirrored, special = switch_ref[0], switch_ref[1]
    if last:
        acc_in, _, near_out, far_out, back_out, acc, scaled, plain, swapped = rest
    else:
        acc, token_out, scaled, plain, swapped = rest

    @pl.when(step == 0)
    def _():
        if last:
            acc[...] = acc_in[...]
        else:
            acc[...] = jnp.zeros_like(acc)
            token_out[...] = jnp.zeros_like(token_out)

    @pl.when(special == 0)
    def _():
        plain[...], swapped[...] = plain_ref[...], swapped_ref[...]

    @pl.when(special != 0)
    def _():
        plain[...], swapped[...] = turned(first_ref[...])

    scale(scaled, plain[...], swapped[...], coeff_ref)
    flags = [[switch_ref[2 + part * windows + w] for w in range(windows)] for part in range(3)]
    near_weights = [jnp.where(special != 0, first, own) * near for own, near, first in zip(*flags)]
    near = weigh(near_ref[...], near_weights)
    far = weigh(jnp.where(special != 0, own_ref[...], first_ref[...]), [own * first for own, _, first in zip(*flags)])
    acc[...] += jnp.dot(scaled[...], jnp.concatenate([near, far], axis=1), preferred_element_type=jnp.float32)

    if last:
        @pl.when(step == pl.num_programs(0) - 1)
        def _():
            near_at, far_at = slice(0, cols), slice(cols, 2 * cols)

            @pl.when(special == 0)
            def _():
                write_lags(back_out, acc, far_at, cols, True)
                write_lags(far_out, acc, far_at, cols, False)

            @pl.when(special != 0)
            def _():
                write_lags(back_out, acc, far_at, cols, False)
                write_lags(far_out, acc, far_at, cols, True)

            pl.when(near_mirrored == 0)(lambda: write_lags(near_out, acc, near_at, cols, False))
            pl.when(near_mirrored != 0)(lambda: write_lags(near_out, acc, near_at, cols, True))


def first_sums(switch, own, coeffs, near_in, first_in, block, earlier=None):
    rows, cols = block.shape
    steps = rows // STEP // 2
    skip = 0 if earlier is None else steps
    windows = (switch.shape[0] - 2) // 3
    result = jax.ShapeDtypeStruct((LAGS, cols, cols), jnp.bfloat16)
    total = jax.ShapeDtypeStruct((LAGS * cols, 2 * cols), jnp.float32)
    total_spec = pl.BlockSpec(total.shape, lambda s, on: (0, 0))
    token = jax.ShapeDtypeStruct((8, cols), jnp.float32)
    token_spec = pl.BlockSpec(token.shape, lambda s, on: (0, 0))
    left = pl.BlockSpec((cols, STEP), lambda s, on: (0, (s + skip) * (1 - on[1])))
    right = pl.BlockSpec((STEP, cols), lambda s, on: (s + skip, 0))
    right_special = pl.BlockSpec((STEP, cols), lambda s, on: ((s + skip) * on[1], 0))
    in_specs = [left, left, pl.BlockSpec((LAGS, STEP), lambda s, on: (0, s + skip)), right, right, right_special]
    scratch = [pltpu.VMEM((LAGS * cols, STEP), jnp.bfloat16)] + [pltpu.VMEM((cols, STEP), jnp.bfloat16)] * 2
    if earlier is None:
        out_shape, out_specs, earlier = [total, token], [total_spec, token_spec], []
    else:
        in_specs += [total_spec, token_spec]
        out_shape = [result] * 3
        out_specs = [pl.BlockSpec(result.shape, lambda s, on: (0, 0, 0))] * 3
        scratch = [pltpu.VMEM(total.shape, jnp.float32)] + scratch
    return pl.pallas_call(
        functools.partial(first_kernel, windows, bool(earlier)),
        grid_spec=pltpu.PrefetchScalarGridSpec(
            num_scalar_prefetch=1,
            grid=(steps,),
            in_specs=in_specs,
            out_specs=out_specs,
            scratch_shapes=scratch,
        ),
        out_shape=out_shape,
        compiler_params=PARAMS,
        cost_estimate=pl.CostEstimate(
            flops=2 * LAGS * cols * cols * rows, bytes_accessed=4 * rows * cols, transcendentals=0
        ),
        name="first_last" if earlier else "first_half",
    )(switch, *own, coeffs, near_in, first_in, block, *earlier)


def second_kernel(windows, first, switch_ref, plain_ref, swapped_ref, coeff_ref, partner_ref, *rest):
    on, late_near = switch_ref[0], switch_ref[1]
    step = pl.program_id(0)
    cols = plain_ref.shape[0]
    if first:
        acc, scaled = rest
    else:
        acc_in, near_in, far_in, back_in, near_out, far_out, back_out, acc, scaled = rest

    @pl.when(on != 0)
    def _():
        @pl.when(step == 0)
        def _():
            acc[...] = jnp.zeros_like(acc) if first else acc_in[...]

        scale(scaled, plain_ref[...], swapped_ref[...], coeff_ref)
        partner = weigh(partner_ref[...], [switch_ref[2 + w] for w in range(windows)])
        acc[...] += jnp.dot(scaled[...], partner, preferred_element_type=jnp.float32)

    if not first:
        @pl.when(step == pl.num_programs(0) - 1)
        def _():
            here = slice(0, cols)

            @pl.when((on != 0) & (late_near == 0))
            def _():
                write_lags(back_out, acc, here, cols, True)
                write_lags(far_out, acc, here, cols, False)

            @pl.when((on == 0) | (late_near != 0))
            def _():
                back_out[...] = back_in[...]
                far_out[...] = far_in[...]

            pl.when(late_near != 0)(lambda: write_lags(near_out, acc, here, cols, False))

            @pl.when(late_near == 0)
            def _():
                near_out[...] = near_in[...]


def second_sums(switch, own, coeffs, partner, start, earlier=None):
    rows, cols = partner.shape
    windows = switch.shape[0] - 2
    skip = start // STEP
    total = jax.ShapeDtypeStruct((LAGS * cols, cols), jnp.float32)
    total_spec = pl.BlockSpec(total.shape, lambda s, on: (0, 0))
    result = jax.ShapeDtypeStruct((LAGS, cols, cols), jnp.bfloat16)
    result_spec = pl.BlockSpec(result.shape, lambda s, on: (0, 0, 0))
    left = pl.BlockSpec((cols, STEP), lambda s, on: (0, s * on[0] + skip))
    in_specs = [left, left, pl.BlockSpec((LAGS, STEP), lambda s, on: (0, s * on[0] + skip)),
                pl.BlockSpec((STEP, cols), lambda s, on: (s * on[0], 0))]
    scratch = [pltpu.VMEM((LAGS * cols, STEP), jnp.bfloat16)]
    if earlier is None:
        out_shape, out_specs, earlier = [total], [total_spec], []
    else:
        out_shape, out_specs = [result] * 3, [result_spec] * 3
        in_specs += [total_spec] + [result_spec] * 3
        scratch = [pltpu.VMEM(total.shape, jnp.float32)] + scratch
    return pl.pallas_call(
        functools.partial(second_kernel, windows, not earlier),
        grid_spec=pltpu.PrefetchScalarGridSpec(
            num_scalar_prefetch=1,
            grid=(rows // STEP,),
            in_specs=in_specs,
            out_specs=out_specs,
            scratch_shapes=scratch,
        ),
        out_shape=out_shape,
        compiler_params=PARAMS,
        cost_estimate=pl.CostEstimate(
            flops=2 * LAGS * cols * cols * rows, bytes_accessed=6 * rows * cols, transcendentals=0
        ),
        name="second_last" if earlier else "second_part",
    )(switch, *own, coeffs, partner, *earlier)


def local(spectra, quality):
    count = lax.axis_size("chan")
    half = count // 2
    me = lax.axis_index("chan")
    freq_count, _, window_count, cols = spectra.shape
    block = spectra.reshape(-1, cols)

    first_far, second_far = [], []
    for p in range(half):
        if p in (0, half - 1):
            first_far.append((p + half, p))
        elif p > half // 2:
            first_far.append((p, p + half))
        elif p % 2 == 1:
            second_far.append((p, p + half))
        else:
            second_far.append((p + half, p))
    late_near = [(2, 1), (4, 3)]
    first_pairs = first_far + [(0, 1), (half - 1, half - 2)]
    second_pairs = second_far + late_near
    near_pairs = [(d + 1, d) for d in range(1, count - 1) if d not in (1, 3, half - 2, half - 1)]
    near_pairs += [(0, half - 1), (half - 1, 0)]
    back_pairs = [(t, s) for s, t in first_far + second_far] + [(1, 0)]
    side_pairs = [(0, half - 1), (half - 1, count - 1)]

    def among(devices):
        return functools.reduce(jnp.logical_or, [me == d for d in devices])

    def switch(on, other, *weights):
        flags = jnp.stack([jnp.asarray(on), jnp.asarray(other)]).astype(jnp.int32)
        return jnp.concatenate([flags, *weights])

    near_in = lax.ppermute(block, "chan", near_pairs)
    first_in = lax.ppermute(block, "chan", first_pairs)
    coeffs = lag_rows(freq_count, window_count)
    own = turn(block)
    parts = split(block)
    first_flags = lax.ppermute(quality, "chan", first_pairs)[0]
    near_flags = lax.ppermute(quality, "chan", near_pairs)[0]
    second_flags = lax.ppermute(quality, "chan", second_pairs)[0]
    special = among([0, half - 1])
    first_switch = switch(me == 0, special, quality[0], near_flags, first_flags)
    second_switch = switch(
        among([t for _, t in second_pairs]), among([t for _, t in late_near]), quality[0] * second_flags
    )

    near_in, first_part, last_part, own, coeffs, first_in = lax.optimization_barrier(
        (near_in, *parts, own, coeffs, first_in)
    )
    second_in = [lax.ppermute(first_part, "chan", second_pairs)]
    operands = first_switch, own, coeffs, near_in, first_in, block
    total, token = first_sums(*operands)
    last_part, token = lax.optimization_barrier((last_part, token))
    second_in.append(lax.ppermute(last_part, "chan", second_pairs))
    near, far, back = first_sums(*operands, [total, token])
    side_returned = lax.ppermute(near, "chan", side_pairs)
    second_switch, near = lax.optimization_barrier((second_switch, near))
    total, = second_sums(second_switch, own, coeffs, second_in[0], 0)

    near = jnp.where(me == half - 2, far, near)
    near, far, back = second_sums(
        second_switch, own, coeffs, second_in[1], parts[0].shape[0], [total, near, far, back]
    )
    returned = lax.ppermute(back, "chan", back_pairs)
    near = jnp.where(among([half - 1, count - 1]), side_returned, near)
    near = jnp.where(me == 0, returned, near)
    far = jnp.where(among([s for s, _ in first_far + second_far]), returned, far)
    return near[None], far[None]


def solution(mesh):
    return jax.shard_map(
        local,
        mesh=mesh,
        in_specs=(P(None, None, None, ("grp", "chan")), P(("grp", "chan"), None)),
        out_specs=(P(("grp", "chan"), None, None, None), P(("grp", "chan"), None, None, None)),
        check_vma=False,
    )
```

```python
import functools
import math

import jax
import jax.numpy as jnp
from jax import lax
from jax.experimental import pallas as pl
from jax.experimental.pallas import tpu as pltpu
from jax.sharding import PartitionSpec as P

HL = 4
LAGS = 2 * HL + 1
STEP = 1024
PARTS = (5, 8)
PARAMS = pltpu.CompilerParams(vmem_limit_bytes=16 * 1024 * 1024)


def lag_rows(freq_count, window_count):
    per_bin = 2 * window_count
    row = jnp.arange(freq_count * per_bin, dtype=jnp.int32)
    freq_values = (row // per_bin).astype(jnp.float32)
    sign = jnp.where(row % per_bin < window_count, 1.0, -1.0)
    lag_values = jnp.arange(HL + 1, dtype=jnp.float32)
    phases = jnp.pi / freq_count * lag_values[:, None] * freq_values[None, :]
    factor = 1.0 / math.sqrt(window_count * freq_count)
    cos_part = jnp.cos(phases) * factor
    sin_part = -jnp.sin(phases[1:]) * factor * sign[None, :]
    return jnp.concatenate([cos_part, sin_part], axis=0).astype(jnp.bfloat16)


def split_kernel(middle, x_ref, first_ref, last_ref):
    step = pl.program_id(0)

    @pl.when(step < middle)
    def _():
        first_ref[...] = x_ref[...]

    @pl.when(step >= middle)
    def _():
        last_ref[...] = x_ref[...]


def split(x):
    rows, cols = x.shape
    steps = rows // STEP
    middle = steps * PARTS[0] // PARTS[1]
    return pl.pallas_call(
        functools.partial(split_kernel, middle),
        grid=(steps,),
        in_specs=[pl.BlockSpec((STEP, cols), lambda s: (s, 0))],
        out_specs=[
            pl.BlockSpec((STEP, cols), lambda s: (jnp.minimum(s, middle - 1), 0)),
            pl.BlockSpec((STEP, cols), lambda s: (jnp.maximum(s - middle, 0), 0)),
        ],
        out_shape=[jax.ShapeDtypeStruct((n * STEP, cols), x.dtype) for n in (middle, steps - middle)],
        compiler_params=PARAMS,
        cost_estimate=pl.CostEstimate(flops=0, bytes_accessed=4 * rows * cols, transcendentals=0),
        name="split",
    )(x)


def turned(x):
    rows, cols = x.shape
    same = lax.broadcasted_iota(jnp.int32, (cols, cols), 0) == lax.broadcasted_iota(jnp.int32, (cols, cols), 1)
    eye = jnp.where(same, 1.0, 0.0).astype(jnp.bfloat16)
    source = lax.broadcasted_iota(jnp.int32, (2 * cols, 2 * cols), 0)
    target = lax.broadcasted_iota(jnp.int32, (2 * cols, 2 * cols), 1)
    exchange = jnp.where((source ^ 4) == target, 1.0, 0.0).astype(jnp.bfloat16)
    plain = lax.dot_general(eye, x, (((1,), (1,)), ((), ())), preferred_element_type=jnp.float32)
    plain = plain.astype(jnp.bfloat16)
    swapped = [
        jnp.dot(plain[:, t:t + 2 * cols], exchange, preferred_element_type=jnp.float32).astype(jnp.bfloat16)
        for t in range(0, rows, 2 * cols)
    ]
    return plain, jnp.concatenate(swapped, axis=1)


def turn_kernel(x_ref, plain_ref, swapped_ref):
    plain_ref[...], swapped_ref[...] = turned(x_ref[...])


def turn(x):
    rows, cols = x.shape
    out = jax.ShapeDtypeStruct((cols, rows), jnp.bfloat16)
    return pl.pallas_call(
        turn_kernel,
        grid=(rows // STEP,),
        in_specs=[pl.BlockSpec((STEP, cols), lambda s: (s, 0))],
        out_specs=[pl.BlockSpec((cols, STEP), lambda s: (0, s))] * 2,
        out_shape=[out, out],
        compiler_params=PARAMS,
        cost_estimate=pl.CostEstimate(flops=0, bytes_accessed=6 * rows * cols, transcendentals=0),
        name="turn",
    )(x)


def write_lags(out, acc, at, cols, mirrored):
    for lag in range(LAGS):
        k = abs(lag - HL)
        value = acc[k * cols:(k + 1) * cols, at]
        if k:
            odd = acc[(HL + k) * cols:(HL + k + 1) * cols, at]
            value = value + odd if lag > HL else value - odd
        value = value.astype(jnp.bfloat16)
        if mirrored:
            out[LAGS - 1 - lag] = value.T
        else:
            out[lag] = value


def scale(scaled, plain, swapped, coeff_ref):
    cols = plain.shape[0]
    for k in range(LAGS):
        part = plain if k <= HL else swapped
        scaled[k * cols:(k + 1) * cols, :] = part * coeff_ref[k:k + 1, :]


def weigh(x, window_weights):
    rows, cols = x.shape
    window = lax.broadcasted_iota(jnp.int32, (16, cols), 0) % len(window_weights)
    weights = jnp.zeros((16, cols), jnp.float32)
    for w, weight in enumerate(window_weights):
        weights = jnp.where(window == w, weight.astype(jnp.float32), weights)
    weights = jnp.broadcast_to(weights.astype(jnp.bfloat16)[None], (rows // 16, 16, cols))
    return x * weights.reshape(rows, cols)


def first_kernel(windows, last, switch_ref, plain_ref, swapped_ref, coeff_ref, near_ref, first_ref, own_ref, *rest):
    step = pl.program_id(0)
    cols = plain_ref.shape[0]
    near_mirrored, special = switch_ref[0], switch_ref[1]
    if last:
        acc_in, _, near_out, far_out, back_out, acc, scaled, plain, swapped, own_rows, arrived = rest
    else:
        acc, token_out, scaled, plain, swapped, own_rows, arrived = rest
    size = own_rows.shape[0]
    begin = size if last else 0

    @pl.when(step == 0)
    def _():
        if last:
            acc[...] = acc_in[...]
        else:
            acc[...] = jnp.zeros_like(acc)
            token_out[...] = jnp.zeros_like(token_out)

    @pl.when(special == 0)
    def _():
        plain[...], swapped[...] = plain_ref[...], swapped_ref[...]

    @pl.when((special != 0) & (step == 0))
    def _():
        copy = pltpu.make_async_copy(own_ref.at[pl.ds(begin, size)], own_rows, arrived)
        copy.start()
        copy.wait()

    @pl.when(special != 0)
    def _():
        plain[...], swapped[...] = turned(first_ref[...])

    scale(scaled, plain[...], swapped[...], coeff_ref)
    flags = [[switch_ref[2 + part * windows + w] for w in range(windows)] for part in range(3)]
    near_weights = [jnp.where(special != 0, first, own) * near for own, near, first in zip(*flags)]
    near = weigh(near_ref[...], near_weights)
    own_tile = own_rows[pl.ds(pl.multiple_of(step * STEP, STEP), STEP), :]
    far = weigh(jnp.where(special != 0, own_tile, first_ref[...]), [own * first for own, _, first in zip(*flags)])
    acc[...] += jnp.dot(scaled[...], jnp.concatenate([near, far], axis=1), preferred_element_type=jnp.float32)

    if last:
        @pl.when(step == pl.num_programs(0) - 1)
        def _():
            near_at, far_at = slice(0, cols), slice(cols, 2 * cols)

            @pl.when(special == 0)
            def _():
                write_lags(back_out, acc, far_at, cols, True)
                write_lags(far_out, acc, far_at, cols, False)

            @pl.when(special != 0)
            def _():
                write_lags(back_out, acc, far_at, cols, False)
                write_lags(far_out, acc, far_at, cols, True)

            pl.when(near_mirrored == 0)(lambda: write_lags(near_out, acc, near_at, cols, False))
            pl.when(near_mirrored != 0)(lambda: write_lags(near_out, acc, near_at, cols, True))


def first_sums(switch, own, coeffs, near_in, first_in, block, earlier=None):
    rows, cols = block.shape
    steps = rows // STEP // 2
    skip = 0 if earlier is None else steps
    windows = (switch.shape[0] - 2) // 3
    result = jax.ShapeDtypeStruct((LAGS, cols, cols), jnp.bfloat16)
    total = jax.ShapeDtypeStruct((LAGS * cols, 2 * cols), jnp.float32)
    total_spec = pl.BlockSpec(total.shape, lambda s, on: (0, 0))
    token = jax.ShapeDtypeStruct((8, cols), jnp.float32)
    token_spec = pl.BlockSpec(token.shape, lambda s, on: (0, 0))
    left = pl.BlockSpec((cols, STEP), lambda s, on: (0, (s + skip) * (1 - on[1])))
    right = pl.BlockSpec((STEP, cols), lambda s, on: (s + skip, 0))
    in_specs = [left, left, pl.BlockSpec((LAGS, STEP), lambda s, on: (0, s + skip)), right, right,
                pl.BlockSpec(memory_space=pltpu.HBM)]
    scratch = [pltpu.VMEM((LAGS * cols, STEP), jnp.bfloat16)] + [pltpu.VMEM((cols, STEP), jnp.bfloat16)] * 2
    scratch += [pltpu.VMEM((steps * STEP, cols), jnp.bfloat16), pltpu.SemaphoreType.DMA(())]
    if earlier is None:
        out_shape, out_specs, earlier = [total, token], [total_spec, token_spec], []
    else:
        in_specs += [total_spec, token_spec]
        out_shape = [result] * 3
        out_specs = [pl.BlockSpec(result.shape, lambda s, on: (0, 0, 0))] * 3
        scratch = [pltpu.VMEM(total.shape, jnp.float32)] + scratch
    return pl.pallas_call(
        functools.partial(first_kernel, windows, bool(earlier)),
        grid_spec=pltpu.PrefetchScalarGridSpec(
            num_scalar_prefetch=1,
            grid=(steps,),
            in_specs=in_specs,
            out_specs=out_specs,
            scratch_shapes=scratch,
        ),
        out_shape=out_shape,
        compiler_params=PARAMS,
        cost_estimate=pl.CostEstimate(
            flops=2 * LAGS * cols * cols * rows, bytes_accessed=4 * rows * cols, transcendentals=0
        ),
        name="first_last" if earlier else "first_half",
    )(switch, *own, coeffs, near_in, first_in, block, *earlier)


def second_kernel(windows, first, switch_ref, plain_ref, swapped_ref, coeff_ref, partner_ref, *rest):
    on, late_near = switch_ref[0], switch_ref[1]
    step = pl.program_id(0)
    cols = plain_ref.shape[0]
    if first:
        acc, scaled = rest
    else:
        acc_in, near_in, far_in, back_in, near_out, far_out, back_out, acc, scaled = rest

    @pl.when(on != 0)
    def _():
        @pl.when(step == 0)
        def _():
            acc[...] = jnp.zeros_like(acc) if first else acc_in[...]

        scale(scaled, plain_ref[...], swapped_ref[...], coeff_ref)
        partner = weigh(partner_ref[...], [switch_ref[2 + w] for w in range(windows)])
        acc[...] += jnp.dot(scaled[...], partner, preferred_element_type=jnp.float32)

    if not first:
        @pl.when(step == pl.num_programs(0) - 1)
        def _():
            here = slice(0, cols)

            @pl.when((on != 0) & (late_near == 0))
            def _():
                write_lags(back_out, acc, here, cols, True)
                write_lags(far_out, acc, here, cols, False)

            @pl.when((on == 0) | (late_near != 0))
            def _():
                back_out[...] = back_in[...]
                far_out[...] = far_in[...]

            pl.when(late_near != 0)(lambda: write_lags(near_out, acc, here, cols, False))

            @pl.when(late_near == 0)
            def _():
                near_out[...] = near_in[...]


def second_sums(switch, own, coeffs, partner, start, earlier=None):
    rows, cols = partner.shape
    windows = switch.shape[0] - 2
    skip = start // STEP
    total = jax.ShapeDtypeStruct((LAGS * cols, cols), jnp.float32)
    total_spec = pl.BlockSpec(total.shape, lambda s, on: (0, 0))
    result = jax.ShapeDtypeStruct((LAGS, cols, cols), jnp.bfloat16)
    result_spec = pl.BlockSpec(result.shape, lambda s, on: (0, 0, 0))
    left = pl.BlockSpec((cols, STEP), lambda s, on: (0, s * on[0] + skip))
    in_specs = [left, left, pl.BlockSpec((LAGS, STEP), lambda s, on: (0, s * on[0] + skip)),
                pl.BlockSpec((STEP, cols), lambda s, on: (s * on[0], 0))]
    scratch = [pltpu.VMEM((LAGS * cols, STEP), jnp.bfloat16)]
    if earlier is None:
        out_shape, out_specs, earlier = [total], [total_spec], []
    else:
        out_shape, out_specs = [result] * 3, [result_spec] * 3
        in_specs += [total_spec] + [result_spec] * 3
        scratch = [pltpu.VMEM(total.shape, jnp.float32)] + scratch
    return pl.pallas_call(
        functools.partial(second_kernel, windows, not earlier),
        grid_spec=pltpu.PrefetchScalarGridSpec(
            num_scalar_prefetch=1,
            grid=(rows // STEP,),
            in_specs=in_specs,
            out_specs=out_specs,
            scratch_shapes=scratch,
        ),
        out_shape=out_shape,
        compiler_params=PARAMS,
        cost_estimate=pl.CostEstimate(
            flops=2 * LAGS * cols * cols * rows, bytes_accessed=6 * rows * cols, transcendentals=0
        ),
        name="second_last" if earlier else "second_part",
    )(switch, *own, coeffs, partner, *earlier)


def local(spectra, quality):
    count = lax.axis_size("chan")
    half = count // 2
    me = lax.axis_index("chan")
    freq_count, _, window_count, cols = spectra.shape
    block = spectra.reshape(-1, cols)

    first_far, second_far = [], []
    for p in range(half):
        if p in (0, half - 1):
            first_far.append((p + half, p))
        elif p > half // 2:
            first_far.append((p, p + half))
        elif p % 2 == 1:
            second_far.append((p, p + half))
        else:
            second_far.append((p + half, p))
    late_near = [(2, 1), (4, 3)]
    first_pairs = first_far + [(0, 1), (half - 1, half - 2)]
    second_pairs = second_far + late_near
    near_pairs = [(d + 1, d) for d in range(1, count - 1) if d not in (1, 3, half - 2, half - 1)]
    near_pairs += [(0, half - 1), (half - 1, 0)]
    back_pairs = [(t, s) for s, t in first_far + second_far] + [(1, 0)]
    side_pairs = [(0, half - 1), (half - 1, count - 1)]

    def among(devices):
        return functools.reduce(jnp.logical_or, [me == d for d in devices])

    def switch(on, other, *weights):
        flags = jnp.stack([jnp.asarray(on), jnp.asarray(other)]).astype(jnp.int32)
        return jnp.concatenate([flags, *weights])

    near_in = lax.ppermute(block, "chan", near_pairs)
    first_in = lax.ppermute(block, "chan", first_pairs)
    coeffs = lag_rows(freq_count, window_count)
    own = turn(block)
    parts = split(block)
    first_flags = lax.ppermute(quality, "chan", first_pairs)[0]
    near_flags = lax.ppermute(quality, "chan", near_pairs)[0]
    second_flags = lax.ppermute(quality, "chan", second_pairs)[0]
    special = among([0, half - 1])
    first_switch = switch(me == 0, special, quality[0], near_flags, first_flags)
    second_switch = switch(
        among([t for _, t in second_pairs]), among([t for _, t in late_near]), quality[0] * second_flags
    )

    near_in, first_part, last_part, own, coeffs, first_in = lax.optimization_barrier(
        (near_in, *parts, own, coeffs, first_in)
    )
    second_in = [lax.ppermute(first_part, "chan", second_pairs)]
    operands = first_switch, own, coeffs, near_in, first_in, block
    total, token = first_sums(*operands)
    last_part, token = lax.optimization_barrier((last_part, token))
    second_in.append(lax.ppermute(last_part, "chan", second_pairs))
    near, far, back = first_sums(*operands, [total, token])
    side_returned = lax.ppermute(near, "chan", side_pairs)
    second_switch, near = lax.optimization_barrier((second_switch, near))
    total, = second_sums(second_switch, own, coeffs, second_in[0], 0)

    near = jnp.where(me == half - 2, far, near)
    near, far, back = second_sums(
        second_switch, own, coeffs, second_in[1], parts[0].shape[0], [total, near, far, back]
    )
    returned = lax.ppermute(back, "chan", back_pairs)
    near = jnp.where(among([half - 1, count - 1]), side_returned, near)
    near = jnp.where(me == 0, returned, near)
    far = jnp.where(among([s for s, _ in first_far + second_far]), returned, far)
    return near[None], far[None]


def solution(mesh):
    return jax.shard_map(
        local,
        mesh=mesh,
        in_specs=(P(None, None, None, ("grp", "chan")), P(("grp", "chan"), None)),
        out_specs=(P(("grp", "chan"), None, None, None), P(("grp", "chan"), None, None, None)),
        check_vma=False,
    )
```

```python
import functools
import math

import jax
import jax.numpy as jnp
from jax import lax
from jax.experimental import pallas as pl
from jax.experimental.pallas import tpu as pltpu
from jax.sharding import PartitionSpec as P

HL = 4
LAGS = 2 * HL + 1
STEP = 1024
PARTS = (5, 8)
PARAMS = pltpu.CompilerParams(vmem_limit_bytes=16 * 1024 * 1024)


def lag_rows(freq_count, window_count):
    per_bin = 2 * window_count
    row = jnp.arange(freq_count * per_bin, dtype=jnp.int32)
    freq_values = (row // per_bin).astype(jnp.float32)
    sign = jnp.where(row % per_bin < window_count, 1.0, -1.0)
    lag_values = jnp.arange(HL + 1, dtype=jnp.float32)
    phases = jnp.pi / freq_count * lag_values[:, None] * freq_values[None, :]
    factor = 1.0 / math.sqrt(window_count * freq_count)
    cos_part = jnp.cos(phases) * factor
    sin_part = -jnp.sin(phases[1:]) * factor * sign[None, :]
    return jnp.concatenate([cos_part, sin_part], axis=0).astype(jnp.bfloat16)


def split_kernel(middle, x_ref, first_ref, last_ref):
    step = pl.program_id(0)

    @pl.when(step < middle)
    def _():
        first_ref[...] = x_ref[...]

    @pl.when(step >= middle)
    def _():
        last_ref[...] = x_ref[...]


def split(x):
    rows, cols = x.shape
    steps = rows // STEP
    middle = steps * PARTS[0] // PARTS[1]
    return pl.pallas_call(
        functools.partial(split_kernel, middle),
        grid=(steps,),
        in_specs=[pl.BlockSpec((STEP, cols), lambda s: (s, 0))],
        out_specs=[
            pl.BlockSpec((STEP, cols), lambda s: (jnp.minimum(s, middle - 1), 0)),
            pl.BlockSpec((STEP, cols), lambda s: (jnp.maximum(s - middle, 0), 0)),
        ],
        out_shape=[jax.ShapeDtypeStruct((n * STEP, cols), x.dtype) for n in (middle, steps - middle)],
        compiler_params=PARAMS,
        cost_estimate=pl.CostEstimate(flops=0, bytes_accessed=4 * rows * cols, transcendentals=0),
        name="split",
    )(x)


def turned(x):
    rows, cols = x.shape
    same = lax.broadcasted_iota(jnp.int32, (cols, cols), 0) == lax.broadcasted_iota(jnp.int32, (cols, cols), 1)
    eye = jnp.where(same, 1.0, 0.0).astype(jnp.bfloat16)
    source = lax.broadcasted_iota(jnp.int32, (2 * cols, 2 * cols), 0)
    target = lax.broadcasted_iota(jnp.int32, (2 * cols, 2 * cols), 1)
    exchange = jnp.where((source ^ 4) == target, 1.0, 0.0).astype(jnp.bfloat16)
    plain = lax.dot_general(eye, x, (((1,), (1,)), ((), ())), preferred_element_type=jnp.float32)
    plain = plain.astype(jnp.bfloat16)
    swapped = [
        jnp.dot(plain[:, t:t + 2 * cols], exchange, preferred_element_type=jnp.float32).astype(jnp.bfloat16)
        for t in range(0, rows, 2 * cols)
    ]
    return plain, jnp.concatenate(swapped, axis=1)


def turn_kernel(x_ref, plain_ref, swapped_ref):
    plain_ref[...], swapped_ref[...] = turned(x_ref[...])


def turn(x):
    rows, cols = x.shape
    out = jax.ShapeDtypeStruct((cols, rows), jnp.bfloat16)
    return pl.pallas_call(
        turn_kernel,
        grid=(rows // STEP,),
        in_specs=[pl.BlockSpec((STEP, cols), lambda s: (s, 0))],
        out_specs=[pl.BlockSpec((cols, STEP), lambda s: (0, s))] * 2,
        out_shape=[out, out],
        compiler_params=PARAMS,
        cost_estimate=pl.CostEstimate(flops=0, bytes_accessed=6 * rows * cols, transcendentals=0),
        name="turn",
    )(x)


def write_lags(out, acc, at, cols, mirrored):
    for lag in range(LAGS):
        k = abs(lag - HL)
        value = acc[k * cols:(k + 1) * cols, at]
        if k:
            odd = acc[(HL + k) * cols:(HL + k + 1) * cols, at]
            value = value + odd if lag > HL else value - odd
        value = value.astype(jnp.bfloat16)
        if mirrored:
            out[LAGS - 1 - lag] = value.T
        else:
            out[lag] = value


def scale(scaled, plain, swapped, coeff_ref):
    cols = plain.shape[0]
    for k in range(LAGS):
        part = plain if k <= HL else swapped
        scaled[k * cols:(k + 1) * cols, :] = part * coeff_ref[k:k + 1, :]


def weigh(x, window_weights):
    rows, cols = x.shape
    window = lax.broadcasted_iota(jnp.int32, (16, cols), 0) % len(window_weights)
    weights = jnp.zeros((16, cols), jnp.float32)
    for w, weight in enumerate(window_weights):
        weights = jnp.where(window == w, weight.astype(jnp.float32), weights)
    weights = jnp.broadcast_to(weights.astype(jnp.bfloat16)[None], (rows // 16, 16, cols))
    return x * weights.reshape(rows, cols)


def first_kernel(windows, last, switch_ref, plain_ref, swapped_ref, coeff_ref, near_ref, first_ref, *rest):
    step = pl.program_id(0)
    cols = plain_ref.shape[0]
    near_mirrored, special = switch_ref[0], switch_ref[1]
    if last:
        acc_in, _, near_out, far_out, back_out, acc, scaled, plain, swapped, right = rest
    else:
        acc, token_out, scaled, plain, swapped, right = rest

    @pl.when(step == 0)
    def _():
        if last:
            acc[...] = acc_in[...]
        else:
            acc[...] = jnp.zeros_like(acc)
            token_out[...] = jnp.zeros_like(token_out)

    @pl.when(special == 0)
    def _():
        plain[...], swapped[...] = plain_ref[...], swapped_ref[...]
        right[...] = first_ref[...]

    @pl.when(special != 0)
    def _():
        plain[...], swapped[...] = turned(first_ref[...])
        for t in range(0, STEP, cols):
            right[t:t + cols, :] = plain_ref[:, t:t + cols].T

    scale(scaled, plain[...], swapped[...], coeff_ref)
    flags = [[switch_ref[2 + part * windows + w] for w in range(windows)] for part in range(3)]
    near_weights = [jnp.where(special != 0, first, own) * near for own, near, first in zip(*flags)]
    near = weigh(near_ref[...], near_weights)
    far = weigh(right[...], [own * first for own, _, first in zip(*flags)])
    acc[...] += jnp.dot(scaled[...], jnp.concatenate([near, far], axis=1), preferred_element_type=jnp.float32)

    if last:
        @pl.when(step == pl.num_programs(0) - 1)
        def _():
            near_at, far_at = slice(0, cols), slice(cols, 2 * cols)

            @pl.when(special == 0)
            def _():
                write_lags(back_out, acc, far_at, cols, True)
                write_lags(far_out, acc, far_at, cols, False)

            @pl.when(special != 0)
            def _():
                write_lags(back_out, acc, far_at, cols, False)
                write_lags(far_out, acc, far_at, cols, True)

            pl.when(near_mirrored == 0)(lambda: write_lags(near_out, acc, near_at, cols, False))
            pl.when(near_mirrored != 0)(lambda: write_lags(near_out, acc, near_at, cols, True))


def first_sums(switch, own, coeffs, near_in, first_in, earlier=None):
    rows, cols = near_in.shape
    steps = rows // STEP // 2
    skip = 0 if earlier is None else steps
    windows = (switch.shape[0] - 2) // 3
    result = jax.ShapeDtypeStruct((LAGS, cols, cols), jnp.bfloat16)
    total = jax.ShapeDtypeStruct((LAGS * cols, 2 * cols), jnp.float32)
    total_spec = pl.BlockSpec(total.shape, lambda s, on: (0, 0))
    token = jax.ShapeDtypeStruct((8, cols), jnp.float32)
    token_spec = pl.BlockSpec(token.shape, lambda s, on: (0, 0))
    left = pl.BlockSpec((cols, STEP), lambda s, on: (0, s + skip))
    right = pl.BlockSpec((STEP, cols), lambda s, on: (s + skip, 0))
    in_specs = [left, left, pl.BlockSpec((LAGS, STEP), lambda s, on: (0, s + skip)), right, right]
    scratch = [pltpu.VMEM((LAGS * cols, STEP), jnp.bfloat16)] + [pltpu.VMEM((cols, STEP), jnp.bfloat16)] * 2
    scratch += [pltpu.VMEM((STEP, cols), jnp.bfloat16)]
    if earlier is None:
        out_shape, out_specs, earlier = [total, token], [total_spec, token_spec], []
    else:
        in_specs += [total_spec, token_spec]
        out_shape = [result] * 3
        out_specs = [pl.BlockSpec(result.shape, lambda s, on: (0, 0, 0))] * 3
        scratch = [pltpu.VMEM(total.shape, jnp.float32)] + scratch
    return pl.pallas_call(
        functools.partial(first_kernel, windows, bool(earlier)),
        grid_spec=pltpu.PrefetchScalarGridSpec(
            num_scalar_prefetch=1,
            grid=(steps,),
            in_specs=in_specs,
            out_specs=out_specs,
            scratch_shapes=scratch,
        ),
        out_shape=out_shape,
        compiler_params=PARAMS,
        cost_estimate=pl.CostEstimate(
            flops=2 * LAGS * cols * cols * rows, bytes_accessed=4 * rows * cols, transcendentals=0
        ),
        name="first_last" if earlier else "first_half",
    )(switch, *own, coeffs, near_in, first_in, *earlier)


def second_kernel(windows, first, switch_ref, plain_ref, swapped_ref, coeff_ref, partner_ref, *rest):
    on, late_near = switch_ref[0], switch_ref[1]
    step = pl.program_id(0)
    cols = plain_ref.shape[0]
    if first:
        acc, scaled = rest
    else:
        acc_in, near_in, far_in, back_in, near_out, far_out, back_out, acc, scaled = rest

    @pl.when(on != 0)
    def _():
        @pl.when(step == 0)
        def _():
            acc[...] = jnp.zeros_like(acc) if first else acc_in[...]

        scale(scaled, plain_ref[...], swapped_ref[...], coeff_ref)
        partner = weigh(partner_ref[...], [switch_ref[2 + w] for w in range(windows)])
        acc[...] += jnp.dot(scaled[...], partner, preferred_element_type=jnp.float32)

    if not first:
        @pl.when(step == pl.num_programs(0) - 1)
        def _():
            here = slice(0, cols)

            @pl.when((on != 0) & (late_near == 0))
            def _():
                write_lags(back_out, acc, here, cols, True)
                write_lags(far_out, acc, here, cols, False)

            @pl.when((on == 0) | (late_near != 0))
            def _():
                back_out[...] = back_in[...]
                far_out[...] = far_in[...]

            pl.when(late_near != 0)(lambda: write_lags(near_out, acc, here, cols, False))

            @pl.when(late_near == 0)
            def _():
                near_out[...] = near_in[...]


def second_sums(switch, own, coeffs, partner, start, earlier=None):
    rows, cols = partner.shape
    windows = switch.shape[0] - 2
    skip = start // STEP
    total = jax.ShapeDtypeStruct((LAGS * cols, cols), jnp.float32)
    total_spec = pl.BlockSpec(total.shape, lambda s, on: (0, 0))
    result = jax.ShapeDtypeStruct((LAGS, cols, cols), jnp.bfloat16)
    result_spec = pl.BlockSpec(result.shape, lambda s, on: (0, 0, 0))
    left = pl.BlockSpec((cols, STEP), lambda s, on: (0, s * on[0] + skip))
    in_specs = [left, left, pl.BlockSpec((LAGS, STEP), lambda s, on: (0, s * on[0] + skip)),
                pl.BlockSpec((STEP, cols), lambda s, on: (s * on[0], 0))]
    scratch = [pltpu.VMEM((LAGS * cols, STEP), jnp.bfloat16)]
    if earlier is None:
        out_shape, out_specs, earlier = [total], [total_spec], []
    else:
        out_shape, out_specs = [result] * 3, [result_spec] * 3
        in_specs += [total_spec] + [result_spec] * 3
        scratch = [pltpu.VMEM(total.shape, jnp.float32)] + scratch
    return pl.pallas_call(
        functools.partial(second_kernel, windows, not earlier),
        grid_spec=pltpu.PrefetchScalarGridSpec(
            num_scalar_prefetch=1,
            grid=(rows // STEP,),
            in_specs=in_specs,
            out_specs=out_specs,
            scratch_shapes=scratch,
        ),
        out_shape=out_shape,
        compiler_params=PARAMS,
        cost_estimate=pl.CostEstimate(
            flops=2 * LAGS * cols * cols * rows, bytes_accessed=6 * rows * cols, transcendentals=0
        ),
        name="second_last" if earlier else "second_part",
    )(switch, *own, coeffs, partner, *earlier)


def local(spectra, quality):
    count = lax.axis_size("chan")
    half = count // 2
    me = lax.axis_index("chan")
    freq_count, _, window_count, cols = spectra.shape
    block = spectra.reshape(-1, cols)

    first_far, second_far = [], []
    for p in range(half):
        if p in (0, half - 1):
            first_far.append((p + half, p))
        elif p > half // 2:
            first_far.append((p, p + half))
        elif p % 2 == 1:
            second_far.append((p, p + half))
        else:
            second_far.append((p + half, p))
    late_near = [(2, 1), (4, 3)]
    first_pairs = first_far + [(0, 1), (half - 1, half - 2)]
    second_pairs = second_far + late_near
    near_pairs = [(d + 1, d) for d in range(1, count - 1) if d not in (1, 3, half - 2, half - 1)]
    near_pairs += [(0, half - 1), (half - 1, 0)]
    back_pairs = [(t, s) for s, t in first_far + second_far] + [(1, 0)]
    side_pairs = [(0, half - 1), (half - 1, count - 1)]

    def among(devices):
        return functools.reduce(jnp.logical_or, [me == d for d in devices])

    def switch(on, other, *weights):
        flags = jnp.stack([jnp.asarray(on), jnp.asarray(other)]).astype(jnp.int32)
        return jnp.concatenate([flags, *weights])

    near_in = lax.ppermute(block, "chan", near_pairs)
    first_in = lax.ppermute(block, "chan", first_pairs)
    coeffs = lag_rows(freq_count, window_count)
    own = turn(block)
    parts = split(block)
    first_flags = lax.ppermute(quality, "chan", first_pairs)[0]
    near_flags = lax.ppermute(quality, "chan", near_pairs)[0]
    second_flags = lax.ppermute(quality, "chan", second_pairs)[0]
    special = among([0, half - 1])
    second_switch = switch(
        among([t for _, t in second_pairs]), among([t for _, t in late_near]), quality[0] * second_flags
    )

    near_in, first_part, last_part, own, coeffs, first_in, near_flags, first_flags, second_flags = lax.optimization_barrier(
        (near_in, *parts, own, coeffs, first_in, near_flags, first_flags, second_flags)
    )
    second_in = [lax.ppermute(first_part, "chan", second_pairs)]
    first_switch = switch(me == 0, special, quality[0], near_flags, first_flags)
    operands = first_switch, own, coeffs, near_in, first_in
    total, token = first_sums(*operands)
    last_part, token = lax.optimization_barrier((last_part, token))
    second_in.append(lax.ppermute(last_part, "chan", second_pairs))
    near, far, back = first_sums(*operands, [total, token])
    side_returned = lax.ppermute(near, "chan", side_pairs)
    second_switch, near = lax.optimization_barrier((second_switch, near))
    total, = second_sums(second_switch, own, coeffs, second_in[0], 0)

    near = jnp.where(me == half - 2, far, near)
    near, far, back = second_sums(
        second_switch, own, coeffs, second_in[1], parts[0].shape[0], [total, near, far, back]
    )
    returned = lax.ppermute(back, "chan", back_pairs)
    near = jnp.where(among([half - 1, count - 1]), side_returned, near)
    near = jnp.where(me == 0, returned, near)
    far = jnp.where(among([s for s, _ in first_far + second_far]), returned, far)
    return near[None], far[None]


def solution(mesh):
    return jax.shard_map(
        local,
        mesh=mesh,
        in_specs=(P(None, None, None, ("grp", "chan")), P(("grp", "chan"), None)),
        out_specs=(P(("grp", "chan"), None, None, None), P(("grp", "chan"), None, None, None)),
        check_vma=False,
    )
```

```python
import functools
import math

import jax
import jax.numpy as jnp
from jax import lax
from jax.experimental import pallas as pl
from jax.experimental.pallas import tpu as pltpu
from jax.sharding import PartitionSpec as P

HL = 4
LAGS = 2 * HL + 1
STEP = 1024
PARTS = (5, 8)
PARAMS = pltpu.CompilerParams(vmem_limit_bytes=16 * 1024 * 1024)


def lag_rows(freq_count, window_count):
    per_bin = 2 * window_count
    row = jnp.arange(freq_count * per_bin, dtype=jnp.int32)
    freq_values = (row // per_bin).astype(jnp.float32)
    sign = jnp.where(row % per_bin < window_count, 1.0, -1.0)
    lag_values = jnp.arange(HL + 1, dtype=jnp.float32)
    phases = jnp.pi / freq_count * lag_values[:, None] * freq_values[None, :]
    factor = 1.0 / math.sqrt(window_count * freq_count)
    cos_part = jnp.cos(phases) * factor
    sin_part = -jnp.sin(phases[1:]) * factor * sign[None, :]
    return jnp.concatenate([cos_part, sin_part], axis=0).astype(jnp.bfloat16)


def split_kernel(middle, x_ref, first_ref, last_ref):
    step = pl.program_id(0)

    @pl.when(step < middle)
    def _():
        first_ref[...] = x_ref[...]

    @pl.when(step >= middle)
    def _():
        last_ref[...] = x_ref[...]


def split(x):
    rows, cols = x.shape
    steps = rows // STEP
    middle = steps * PARTS[0] // PARTS[1]
    return pl.pallas_call(
        functools.partial(split_kernel, middle),
        grid=(steps,),
        in_specs=[pl.BlockSpec((STEP, cols), lambda s: (s, 0))],
        out_specs=[
            pl.BlockSpec((STEP, cols), lambda s: (jnp.minimum(s, middle - 1), 0)),
            pl.BlockSpec((STEP, cols), lambda s: (jnp.maximum(s - middle, 0), 0)),
        ],
        out_shape=[jax.ShapeDtypeStruct((n * STEP, cols), x.dtype) for n in (middle, steps - middle)],
        compiler_params=PARAMS,
        cost_estimate=pl.CostEstimate(flops=0, bytes_accessed=4 * rows * cols, transcendentals=0),
        name="split",
    )(x)


def turned(x):
    rows, cols = x.shape
    same = lax.broadcasted_iota(jnp.int32, (cols, cols), 0) == lax.broadcasted_iota(jnp.int32, (cols, cols), 1)
    eye = jnp.where(same, 1.0, 0.0).astype(jnp.bfloat16)
    source = lax.broadcasted_iota(jnp.int32, (2 * cols, 2 * cols), 0)
    target = lax.broadcasted_iota(jnp.int32, (2 * cols, 2 * cols), 1)
    exchange = jnp.where((source ^ 4) == target, 1.0, 0.0).astype(jnp.bfloat16)
    plain = lax.dot_general(eye, x, (((1,), (1,)), ((), ())), preferred_element_type=jnp.float32)
    plain = plain.astype(jnp.bfloat16)
    swapped = [
        jnp.dot(plain[:, t:t + 2 * cols], exchange, preferred_element_type=jnp.float32).astype(jnp.bfloat16)
        for t in range(0, rows, 2 * cols)
    ]
    return plain, jnp.concatenate(swapped, axis=1)


def turn_kernel(x_ref, plain_ref, swapped_ref):
    plain_ref[...], swapped_ref[...] = turned(x_ref[...])


def turn(x):
    rows, cols = x.shape
    out = jax.ShapeDtypeStruct((cols, rows), jnp.bfloat16)
    return pl.pallas_call(
        turn_kernel,
        grid=(rows // STEP,),
        in_specs=[pl.BlockSpec((STEP, cols), lambda s: (s, 0))],
        out_specs=[pl.BlockSpec((cols, STEP), lambda s: (0, s))] * 2,
        out_shape=[out, out],
        compiler_params=PARAMS,
        cost_estimate=pl.CostEstimate(flops=0, bytes_accessed=6 * rows * cols, transcendentals=0),
        name="turn",
    )(x)


def write_lags(out, acc, at, cols, mirrored):
    for lag in range(LAGS):
        k = abs(lag - HL)
        value = acc[k * cols:(k + 1) * cols, at]
        if k:
            odd = acc[(HL + k) * cols:(HL + k + 1) * cols, at]
            value = value + odd if lag > HL else value - odd
        value = value.astype(jnp.bfloat16)
        if mirrored:
            out[LAGS - 1 - lag] = value.T
        else:
            out[lag] = value


def scale(scaled, plain, swapped, coeff_ref):
    cols = plain.shape[0]
    for k in range(LAGS):
        part = plain if k <= HL else swapped
        scaled[k * cols:(k + 1) * cols, :] = part * coeff_ref[k:k + 1, :]


def weigh(x, window_weights):
    rows, cols = x.shape
    window = lax.broadcasted_iota(jnp.int32, (16, cols), 0) % len(window_weights)
    weights = jnp.zeros((16, cols), jnp.float32)
    for w, weight in enumerate(window_weights):
        weights = jnp.where(window == w, weight.astype(jnp.float32), weights)
    weights = jnp.broadcast_to(weights.astype(jnp.bfloat16)[None], (rows // 16, 16, cols))
    return x * weights.reshape(rows, cols)


def first_kernel(windows, last, switch_ref, plain_ref, swapped_ref, coeff_ref, near_ref, first_ref, *rest):
    step = pl.program_id(0)
    cols = plain_ref.shape[0]
    near_mirrored, special = switch_ref[0], switch_ref[1]
    if last:
        acc_in, _, near_out, far_out, back_out, acc, scaled, plain, swapped, right = rest
    else:
        acc, token_out, scaled, plain, swapped, right = rest

    @pl.when(step == 0)
    def _():
        if last:
            acc[...] = acc_in[...]
        else:
            acc[...] = jnp.zeros_like(acc)
            token_out[...] = jnp.zeros_like(token_out)

    @pl.when(special == 0)
    def _():
        plain[...], swapped[...] = plain_ref[...], swapped_ref[...]
        right[...] = first_ref[...]

    @pl.when(special != 0)
    def _():
        plain[...], swapped[...] = turned(first_ref[...])
        for t in range(0, STEP, cols):
            right[t:t + cols, :] = plain_ref[:, t:t + cols].T

    scale(scaled, plain[...], swapped[...], coeff_ref)
    flags = [[switch_ref[2 + part * windows + w] for w in range(windows)] for part in range(3)]
    near_weights = [jnp.where(special != 0, first, own) * near for own, near, first in zip(*flags)]
    near = weigh(near_ref[...], near_weights)
    far = weigh(right[...], [own * first for own, _, first in zip(*flags)])
    acc[...] += jnp.dot(scaled[...], jnp.concatenate([near, far], axis=1), preferred_element_type=jnp.float32)

    if last:
        @pl.when(step == pl.num_programs(0) - 1)
        def _():
            near_at, far_at = slice(0, cols), slice(cols, 2 * cols)

            @pl.when(special == 0)
            def _():
                write_lags(back_out, acc, far_at, cols, True)
                write_lags(far_out, acc, far_at, cols, False)

            @pl.when(special != 0)
            def _():
                write_lags(back_out, acc, far_at, cols, False)
                write_lags(far_out, acc, far_at, cols, True)

            pl.when(near_mirrored == 0)(lambda: write_lags(near_out, acc, near_at, cols, False))
            pl.when(near_mirrored != 0)(lambda: write_lags(near_out, acc, near_at, cols, True))


def first_sums(switch, own, coeffs, near_in, first_in, earlier=None):
    rows, cols = near_in.shape
    steps = rows // STEP // 2
    skip = 0 if earlier is None else steps
    windows = (switch.shape[0] - 2) // 3
    result = jax.ShapeDtypeStruct((LAGS, cols, cols), jnp.bfloat16)
    total = jax.ShapeDtypeStruct((LAGS * cols, 2 * cols), jnp.float32)
    total_spec = pl.BlockSpec(total.shape, lambda s, on: (0, 0))
    token = jax.ShapeDtypeStruct((8, cols), jnp.float32)
    token_spec = pl.BlockSpec(token.shape, lambda s, on: (0, 0))
    left = pl.BlockSpec((cols, STEP), lambda s, on: (0, s + skip))
    right = pl.BlockSpec((STEP, cols), lambda s, on: (s + skip, 0))
    in_specs = [left, left, pl.BlockSpec((LAGS, STEP), lambda s, on: (0, s + skip)), right, right]
    scratch = [pltpu.VMEM((LAGS * cols, STEP), jnp.bfloat16)] + [pltpu.VMEM((cols, STEP), jnp.bfloat16)] * 2
    scratch += [pltpu.VMEM((STEP, cols), jnp.bfloat16)]
    if earlier is None:
        out_shape, out_specs, earlier = [total, token], [total_spec, token_spec], []
    else:
        in_specs += [total_spec, token_spec]
        out_shape = [result] * 3
        out_specs = [pl.BlockSpec(result.shape, lambda s, on: (0, 0, 0))] * 3
        scratch = [pltpu.VMEM(total.shape, jnp.float32)] + scratch
    return pl.pallas_call(
        functools.partial(first_kernel, windows, bool(earlier)),
        grid_spec=pltpu.PrefetchScalarGridSpec(
            num_scalar_prefetch=1,
            grid=(steps,),
            in_specs=in_specs,
            out_specs=out_specs,
            scratch_shapes=scratch,
        ),
        out_shape=out_shape,
        compiler_params=PARAMS,
        cost_estimate=pl.CostEstimate(
            flops=2 * LAGS * cols * cols * rows, bytes_accessed=4 * rows * cols, transcendentals=0
        ),
        name="first_last" if earlier else "first_half",
    )(switch, *own, coeffs, near_in, first_in, *earlier)


def second_kernel(windows, first, switch_ref, plain_ref, swapped_ref, coeff_ref, partner_ref, *rest):
    on, late_near = switch_ref[0], switch_ref[1]
    step = pl.program_id(0)
    cols = plain_ref.shape[0]
    if first:
        acc, scaled = rest
    else:
        acc_in, near_in, far_in, back_in, near_out, far_out, back_out, acc, scaled = rest

    @pl.when(on != 0)
    def _():
        @pl.when(step == 0)
        def _():
            acc[...] = jnp.zeros_like(acc) if first else acc_in[...]

        scale(scaled, plain_ref[...], swapped_ref[...], coeff_ref)
        partner = weigh(partner_ref[...], [switch_ref[2 + w] for w in range(windows)])
        acc[...] += jnp.dot(scaled[...], partner, preferred_element_type=jnp.float32)

    if not first:
        @pl.when(step == pl.num_programs(0) - 1)
        def _():
            here = slice(0, cols)

            @pl.when((on != 0) & (late_near == 0))
            def _():
                write_lags(back_out, acc, here, cols, True)
                write_lags(far_out, acc, here, cols, False)

            @pl.when((on == 0) | (late_near != 0))
            def _():
                back_out[...] = back_in[...]
                far_out[...] = far_in[...]

            pl.when(late_near != 0)(lambda: write_lags(near_out, acc, here, cols, False))

            @pl.when(late_near == 0)
            def _():
                near_out[...] = near_in[...]


def second_sums(switch, own, coeffs, partner, start, earlier=None):
    rows, cols = partner.shape
    windows = switch.shape[0] - 2
    skip = start // STEP
    total = jax.ShapeDtypeStruct((LAGS * cols, cols), jnp.float32)
    total_spec = pl.BlockSpec(total.shape, lambda s, on: (0, 0))
    result = jax.ShapeDtypeStruct((LAGS, cols, cols), jnp.bfloat16)
    result_spec = pl.BlockSpec(result.shape, lambda s, on: (0, 0, 0))
    left = pl.BlockSpec((cols, STEP), lambda s, on: (0, s * on[0] + skip))
    in_specs = [left, left, pl.BlockSpec((LAGS, STEP), lambda s, on: (0, s * on[0] + skip)),
                pl.BlockSpec((STEP, cols), lambda s, on: (s * on[0], 0))]
    scratch = [pltpu.VMEM((LAGS * cols, STEP), jnp.bfloat16)]
    if earlier is None:
        out_shape, out_specs, earlier = [total], [total_spec], []
    else:
        out_shape, out_specs = [result] * 3, [result_spec] * 3
        in_specs += [total_spec] + [result_spec] * 3
        scratch = [pltpu.VMEM(total.shape, jnp.float32)] + scratch
    return pl.pallas_call(
        functools.partial(second_kernel, windows, not earlier),
        grid_spec=pltpu.PrefetchScalarGridSpec(
            num_scalar_prefetch=1,
            grid=(rows // STEP,),
            in_specs=in_specs,
            out_specs=out_specs,
            scratch_shapes=scratch,
        ),
        out_shape=out_shape,
        compiler_params=PARAMS,
        cost_estimate=pl.CostEstimate(
            flops=2 * LAGS * cols * cols * rows, bytes_accessed=6 * rows * cols, transcendentals=0
        ),
        name="second_last" if earlier else "second_part",
    )(switch, *own, coeffs, partner, *earlier)


def local(spectra, quality):
    count = lax.axis_size("chan")
    half = count // 2
    me = lax.axis_index("chan")
    freq_count, _, window_count, cols = spectra.shape
    block = spectra.reshape(-1, cols)

    first_far, second_far = [], []
    for p in range(half):
        if p in (0, half - 1):
            first_far.append((p + half, p))
        elif p > half // 2:
            first_far.append((p, p + half))
        elif p % 2 == 1:
            second_far.append((p, p + half))
        else:
            second_far.append((p + half, p))
    late_near = [(2, 1), (4, 3)]
    first_pairs = first_far + [(0, 1), (half - 1, half - 2)]
    second_pairs = second_far + late_near
    near_pairs = [(d + 1, d) for d in range(1, count - 1) if d not in (1, 3, half - 2, half - 1)]
    near_pairs += [(0, half - 1), (half - 1, 0)]
    back_pairs = [(t, s) for s, t in first_far + second_far] + [(1, 0)]
    side_pairs = [(0, half - 1), (half - 1, count - 1)]

    def among(devices):
        return functools.reduce(jnp.logical_or, [me == d for d in devices])

    def switch(on, other, *weights):
        flags = jnp.stack([jnp.asarray(on), jnp.asarray(other)]).astype(jnp.int32)
        return jnp.concatenate([flags, *weights])

    first_in = lax.ppermute(block, "chan", first_pairs)
    near_in = lax.ppermute(block, "chan", near_pairs)
    coeffs = lag_rows(freq_count, window_count)
    own = turn(block)
    parts = split(block)
    first_flags = lax.ppermute(quality, "chan", first_pairs)[0]
    near_flags = lax.ppermute(quality, "chan", near_pairs)[0]
    second_flags = lax.ppermute(quality, "chan", second_pairs)[0]
    special = among([0, half - 1])
    second_switch = switch(
        among([t for _, t in second_pairs]), among([t for _, t in late_near]), quality[0] * second_flags
    )

    first_in, near_in, first_part, last_part, own, coeffs, first_flags, near_flags, second_flags = lax.optimization_barrier(
        (first_in, near_in, *parts, own, coeffs, first_flags, near_flags, second_flags)
    )
    second_in = [lax.ppermute(first_part, "chan", second_pairs)]
    first_switch = switch(me == 0, special, quality[0], near_flags, first_flags)
    operands = first_switch, own, coeffs, near_in, first_in
    total, token = first_sums(*operands)
    last_part, token = lax.optimization_barrier((last_part, token))
    second_in.append(lax.ppermute(last_part, "chan", second_pairs))
    near, far, back = first_sums(*operands, [total, token])
    side_returned = lax.ppermute(near, "chan", side_pairs)
    second_switch, near = lax.optimization_barrier((second_switch, near))
    total, = second_sums(second_switch, own, coeffs, second_in[0], 0)

    near = jnp.where(me == half - 2, far, near)
    near, far, back = second_sums(
        second_switch, own, coeffs, second_in[1], parts[0].shape[0], [total, near, far, back]
    )
    returned = lax.ppermute(back, "chan", back_pairs)
    near = jnp.where(among([half - 1, count - 1]), side_returned, near)
    near = jnp.where(me == 0, returned, near)
    far = jnp.where(among([s for s, _ in first_far + second_far]), returned, far)
    return near[None], far[None]


def solution(mesh):
    return jax.shard_map(
        local,
        mesh=mesh,
        in_specs=(P(None, None, None, ("grp", "chan")), P(("grp", "chan"), None)),
        out_specs=(P(("grp", "chan"), None, None, None), P(("grp", "chan"), None, None, None)),
        check_vma=False,
    )
```

```python
import functools
import math

import jax
import jax.numpy as jnp
from jax import lax
from jax.experimental import pallas as pl
from jax.experimental.pallas import tpu as pltpu
from jax.sharding import PartitionSpec as P

HL = 4
LAGS = 2 * HL + 1
STEP = 1024
PARTS = (5, 8)
PARAMS = pltpu.CompilerParams(vmem_limit_bytes=16 * 1024 * 1024)


def lag_rows(freq_count, window_count):
    per_bin = 2 * window_count
    row = jnp.arange(freq_count * per_bin, dtype=jnp.int32)
    freq_values = (row // per_bin).astype(jnp.float32)
    sign = jnp.where(row % per_bin < window_count, 1.0, -1.0)
    lag_values = jnp.arange(HL + 1, dtype=jnp.float32)
    phases = jnp.pi / freq_count * lag_values[:, None] * freq_values[None, :]
    factor = 1.0 / math.sqrt(window_count * freq_count)
    cos_part = jnp.cos(phases) * factor
    sin_part = -jnp.sin(phases[1:]) * factor * sign[None, :]
    return jnp.concatenate([cos_part, sin_part], axis=0).astype(jnp.bfloat16)


def split_kernel(middle, x_ref, first_ref, last_ref):
    step = pl.program_id(0)

    @pl.when(step < middle)
    def _():
        first_ref[...] = x_ref[...]

    @pl.when(step >= middle)
    def _():
        last_ref[...] = x_ref[...]


def split(x):
    rows, cols = x.shape
    steps = rows // STEP
    middle = steps * PARTS[0] // PARTS[1]
    return pl.pallas_call(
        functools.partial(split_kernel, middle),
        grid=(steps,),
        in_specs=[pl.BlockSpec((STEP, cols), lambda s: (s, 0))],
        out_specs=[
            pl.BlockSpec((STEP, cols), lambda s: (jnp.minimum(s, middle - 1), 0)),
            pl.BlockSpec((STEP, cols), lambda s: (jnp.maximum(s - middle, 0), 0)),
        ],
        out_shape=[jax.ShapeDtypeStruct((n * STEP, cols), x.dtype) for n in (middle, steps - middle)],
        compiler_params=PARAMS,
        cost_estimate=pl.CostEstimate(flops=0, bytes_accessed=4 * rows * cols, transcendentals=0),
        name="split",
    )(x)


def turned(x):
    rows, cols = x.shape
    same = lax.broadcasted_iota(jnp.int32, (cols, cols), 0) == lax.broadcasted_iota(jnp.int32, (cols, cols), 1)
    eye = jnp.where(same, 1.0, 0.0).astype(jnp.bfloat16)
    source = lax.broadcasted_iota(jnp.int32, (2 * cols, 2 * cols), 0)
    target = lax.broadcasted_iota(jnp.int32, (2 * cols, 2 * cols), 1)
    exchange = jnp.where((source ^ 4) == target, 1.0, 0.0).astype(jnp.bfloat16)
    plain = lax.dot_general(eye, x, (((1,), (1,)), ((), ())), preferred_element_type=jnp.float32)
    plain = plain.astype(jnp.bfloat16)
    swapped = [
        jnp.dot(plain[:, t:t + 2 * cols], exchange, preferred_element_type=jnp.float32).astype(jnp.bfloat16)
        for t in range(0, rows, 2 * cols)
    ]
    return plain, jnp.concatenate(swapped, axis=1)


def turn_kernel(x_ref, plain_ref, swapped_ref):
    plain_ref[...], swapped_ref[...] = turned(x_ref[...])


def turn(x):
    rows, cols = x.shape
    out = jax.ShapeDtypeStruct((cols, rows), jnp.bfloat16)
    return pl.pallas_call(
        turn_kernel,
        grid=(rows // STEP,),
        in_specs=[pl.BlockSpec((STEP, cols), lambda s: (s, 0))],
        out_specs=[pl.BlockSpec((cols, STEP), lambda s: (0, s))] * 2,
        out_shape=[out, out],
        compiler_params=PARAMS,
        cost_estimate=pl.CostEstimate(flops=0, bytes_accessed=6 * rows * cols, transcendentals=0),
        name="turn",
    )(x)


def write_lags(out, acc, at, cols, mirrored):
    for lag in range(LAGS):
        k = abs(lag - HL)
        value = acc[k * cols:(k + 1) * cols, at]
        if k:
            odd = acc[(HL + k) * cols:(HL + k + 1) * cols, at]
            value = value + odd if lag > HL else value - odd
        value = value.astype(jnp.bfloat16)
        if mirrored:
            out[LAGS - 1 - lag] = value.T
        else:
            out[lag] = value


def scale(scaled, plain, swapped, coeff_ref):
    cols = plain.shape[0]
    for k in range(LAGS):
        part = plain if k <= HL else swapped
        scaled[k * cols:(k + 1) * cols, :] = part * coeff_ref[k:k + 1, :]


def weigh(x, window_weights):
    rows, cols = x.shape
    window = lax.broadcasted_iota(jnp.int32, (16, cols), 0) % len(window_weights)
    weights = jnp.zeros((16, cols), jnp.float32)
    for w, weight in enumerate(window_weights):
        weights = jnp.where(window == w, weight.astype(jnp.float32), weights)
    weights = jnp.broadcast_to(weights.astype(jnp.bfloat16)[None], (rows // 16, 16, cols))
    return x * weights.reshape(rows, cols)


def first_kernel(windows, last, switch_ref, plain_ref, swapped_ref, coeff_ref, near_ref, first_ref, *rest):
    step = pl.program_id(0)
    cols = plain_ref.shape[0]
    near_mirrored, special = switch_ref[0], switch_ref[1]
    if last:
        acc_in, _, near_out, far_out, back_out, acc, scaled, plain, swapped, right = rest
    else:
        acc, token_out, scaled, plain, swapped, right = rest

    @pl.when(step == 0)
    def _():
        if last:
            acc[...] = acc_in[...]
        else:
            acc[...] = jnp.zeros_like(acc)
            token_out[...] = jnp.zeros_like(token_out)

    @pl.when(special == 0)
    def _():
        plain[...], swapped[...] = plain_ref[...], swapped_ref[...]
        right[...] = first_ref[...]

    @pl.when(special != 0)
    def _():
        plain[...], swapped[...] = turned(first_ref[...])
        for t in range(0, STEP, cols):
            right[t:t + cols, :] = plain_ref[:, t:t + cols].T

    scale(scaled, plain[...], swapped[...], coeff_ref)
    flags = [[switch_ref[2 + part * windows + w] for w in range(windows)] for part in range(3)]
    near_weights = [jnp.where(special != 0, first, own) * near for own, near, first in zip(*flags)]
    near = weigh(near_ref[...], near_weights)
    far = weigh(right[...], [own * first for own, _, first in zip(*flags)])
    acc[...] += jnp.dot(scaled[...], jnp.concatenate([near, far], axis=1), preferred_element_type=jnp.float32)

    if last:
        @pl.when(step == pl.num_programs(0) - 1)
        def _():
            near_at, far_at = slice(0, cols), slice(cols, 2 * cols)

            @pl.when(special == 0)
            def _():
                write_lags(back_out, acc, far_at, cols, True)
                write_lags(far_out, acc, far_at, cols, False)

            @pl.when(special != 0)
            def _():
                write_lags(back_out, acc, far_at, cols, False)
                write_lags(far_out, acc, far_at, cols, True)

            pl.when(near_mirrored == 0)(lambda: write_lags(near_out, acc, near_at, cols, False))
            pl.when(near_mirrored != 0)(lambda: write_lags(near_out, acc, near_at, cols, True))


def first_sums(switch, own, coeffs, near_in, first_in, earlier=None):
    rows, cols = near_in.shape
    steps = rows // STEP // 2
    skip = 0 if earlier is None else steps
    windows = (switch.shape[0] - 2) // 3
    result = jax.ShapeDtypeStruct((LAGS, cols, cols), jnp.bfloat16)
    total = jax.ShapeDtypeStruct((LAGS * cols, 2 * cols), jnp.float32)
    total_spec = pl.BlockSpec(total.shape, lambda s, on: (0, 0))
    token = jax.ShapeDtypeStruct((8, cols), jnp.float32)
    token_spec = pl.BlockSpec(token.shape, lambda s, on: (0, 0))
    left = pl.BlockSpec((cols, STEP), lambda s, on: (0, s + skip))
    right = pl.BlockSpec((STEP, cols), lambda s, on: (s + skip, 0))
    in_specs = [left, left, pl.BlockSpec((LAGS, STEP), lambda s, on: (0, s + skip)), right, right]
    scratch = [pltpu.VMEM((LAGS * cols, STEP), jnp.bfloat16)] + [pltpu.VMEM((cols, STEP), jnp.bfloat16)] * 2
    scratch += [pltpu.VMEM((STEP, cols), jnp.bfloat16)]
    if earlier is None:
        out_shape, out_specs, earlier = [total, token], [total_spec, token_spec], []
    else:
        in_specs += [total_spec, token_spec]
        out_shape = [result] * 3
        out_specs = [pl.BlockSpec(result.shape, lambda s, on: (0, 0, 0))] * 3
        scratch = [pltpu.VMEM(total.shape, jnp.float32)] + scratch
    return pl.pallas_call(
        functools.partial(first_kernel, windows, bool(earlier)),
        grid_spec=pltpu.PrefetchScalarGridSpec(
            num_scalar_prefetch=1,
            grid=(steps,),
            in_specs=in_specs,
            out_specs=out_specs,
            scratch_shapes=scratch,
        ),
        out_shape=out_shape,
        compiler_params=PARAMS,
        cost_estimate=pl.CostEstimate(
            flops=2 * LAGS * cols * cols * rows, bytes_accessed=4 * rows * cols, transcendentals=0
        ),
        name="first_last" if earlier else "first_half",
    )(switch, *own, coeffs, near_in, first_in, *earlier)


def second_kernel(windows, first, switch_ref, plain_ref, swapped_ref, coeff_ref, partner_ref, *rest):
    on, late_near = switch_ref[0], switch_ref[1]
    step = pl.program_id(0)
    cols = plain_ref.shape[0]
    if first:
        acc, scaled = rest
    else:
        acc_in, near_in, far_in, back_in, near_out, far_out, back_out, acc, scaled = rest

    @pl.when(on != 0)
    def _():
        @pl.when(step == 0)
        def _():
            acc[...] = jnp.zeros_like(acc) if first else acc_in[...]

        scale(scaled, plain_ref[...], swapped_ref[...], coeff_ref)
        partner = weigh(partner_ref[...], [switch_ref[2 + w] for w in range(windows)])
        acc[...] += jnp.dot(scaled[...], partner, preferred_element_type=jnp.float32)

    if not first:
        @pl.when(step == pl.num_programs(0) - 1)
        def _():
            here = slice(0, cols)

            @pl.when((on != 0) & (late_near == 0))
            def _():
                write_lags(back_out, acc, here, cols, True)
                write_lags(far_out, acc, here, cols, False)

            @pl.when((on == 0) | (late_near != 0))
            def _():
                back_out[...] = back_in[...]
                far_out[...] = far_in[...]

            pl.when(late_near != 0)(lambda: write_lags(near_out, acc, here, cols, False))

            @pl.when(late_near == 0)
            def _():
                near_out[...] = near_in[...]


def second_sums(switch, own, coeffs, partner, start, earlier=None):
    rows, cols = partner.shape
    windows = switch.shape[0] - 2
    skip = start // STEP
    total = jax.ShapeDtypeStruct((LAGS * cols, cols), jnp.float32)
    total_spec = pl.BlockSpec(total.shape, lambda s, on: (0, 0))
    result = jax.ShapeDtypeStruct((LAGS, cols, cols), jnp.bfloat16)
    result_spec = pl.BlockSpec(result.shape, lambda s, on: (0, 0, 0))
    left = pl.BlockSpec((cols, STEP), lambda s, on: (0, s * on[0] + skip))
    in_specs = [left, left, pl.BlockSpec((LAGS, STEP), lambda s, on: (0, s * on[0] + skip)),
                pl.BlockSpec((STEP, cols), lambda s, on: (s * on[0], 0))]
    scratch = [pltpu.VMEM((LAGS * cols, STEP), jnp.bfloat16)]
    if earlier is None:
        out_shape, out_specs, earlier = [total], [total_spec], []
    else:
        out_shape, out_specs = [result] * 3, [result_spec] * 3
        in_specs += [total_spec] + [result_spec] * 3
        scratch = [pltpu.VMEM(total.shape, jnp.float32)] + scratch
    return pl.pallas_call(
        functools.partial(second_kernel, windows, not earlier),
        grid_spec=pltpu.PrefetchScalarGridSpec(
            num_scalar_prefetch=1,
            grid=(rows // STEP,),
            in_specs=in_specs,
            out_specs=out_specs,
            scratch_shapes=scratch,
        ),
        out_shape=out_shape,
        compiler_params=PARAMS,
        cost_estimate=pl.CostEstimate(
            flops=2 * LAGS * cols * cols * rows, bytes_accessed=6 * rows * cols, transcendentals=0
        ),
        name="second_last" if earlier else "second_part",
    )(switch, *own, coeffs, partner, *earlier)


def local(spectra, quality):
    count = lax.axis_size("chan")
    half = count // 2
    me = lax.axis_index("chan")
    freq_count, _, window_count, cols = spectra.shape
    block = spectra.reshape(-1, cols)

    first_far, second_far = [], []
    for p in range(half):
        if p in (0, half - 1):
            first_far.append((p + half, p))
        elif p > half // 2:
            first_far.append((p, p + half))
        elif p % 2 == 1:
            second_far.append((p, p + half))
        else:
            second_far.append((p + half, p))
    late_near = [(2, 1), (4, 3)]
    first_pairs = first_far + [(0, 1), (half - 1, half - 2)]
    second_pairs = second_far + late_near
    near_pairs = [(d + 1, d) for d in range(1, count - 1) if d not in (1, 3, half - 2, half - 1)]
    near_pairs += [(0, half - 1), (half - 1, 0)]
    back_pairs = [(t, s) for s, t in first_far + second_far] + [(1, 0)]
    side_pairs = [(0, half - 1), (half - 1, count - 1)]

    def among(devices):
        return functools.reduce(jnp.logical_or, [me == d for d in devices])

    def switch(on, other, *weights):
        flags = jnp.stack([jnp.asarray(on), jnp.asarray(other)]).astype(jnp.int32)
        return jnp.concatenate([flags, *weights])

    near_in = lax.ppermute(block, "chan", near_pairs)
    first_in = lax.ppermute(block, "chan", first_pairs)
    coeffs = lag_rows(freq_count, window_count)
    own = turn(block)
    parts = split(block)
    first_flags = lax.ppermute(quality, "chan", first_pairs)[0]
    near_flags = lax.ppermute(quality, "chan", near_pairs)[0]
    second_flags = lax.ppermute(quality, "chan", second_pairs)[0]
    special = among([0, half - 1])
    second_switch = switch(
        among([t for _, t in second_pairs]), among([t for _, t in late_near]), quality[0] * second_flags
    )

    near_in, first_part, last_part, own, coeffs, first_in, near_flags, first_flags, second_flags = lax.optimization_barrier(
        (near_in, *parts, own, coeffs, first_in, near_flags, first_flags, second_flags)
    )
    second_in = [lax.ppermute(first_part, "chan", second_pairs)]
    first_switch = switch(me == 0, special, quality[0], near_flags, first_flags)
    operands = first_switch, own, coeffs, near_in, first_in
    total, token = first_sums(*operands)
    last_part, token = lax.optimization_barrier((last_part, token))
    second_in.append(lax.ppermute(last_part, "chan", second_pairs))
    near, far, back = first_sums(*operands, [total, token])
    second_switch, near = lax.optimization_barrier((second_switch, near))
    total, = second_sums(second_switch, own, coeffs, second_in[0], 0)

    near = jnp.where(me == half - 2, far, near)
    near, far, back = second_sums(
        second_switch, own, coeffs, second_in[1], parts[0].shape[0], [total, near, far, back]
    )
    returned = lax.ppermute(back, "chan", back_pairs)
    side_returned = lax.ppermute(near, "chan", side_pairs)
    near = jnp.where(among([half - 1, count - 1]), side_returned, near)
    near = jnp.where(me == 0, returned, near)
    far = jnp.where(among([s for s, _ in first_far + second_far]), returned, far)
    return near[None], far[None]


def solution(mesh):
    return jax.shard_map(
        local,
        mesh=mesh,
        in_specs=(P(None, None, None, ("grp", "chan")), P(("grp", "chan"), None)),
        out_specs=(P(("grp", "chan"), None, None, None), P(("grp", "chan"), None, None, None)),
        check_vma=False,
    )
```

```python
import functools
import math

import jax
import jax.numpy as jnp
from jax import lax
from jax.experimental import pallas as pl
from jax.experimental.pallas import tpu as pltpu
from jax.sharding import PartitionSpec as P

HL = 4
LAGS = 2 * HL + 1
STEP = 1024
ENDS = (4, 6, 8)
PARAMS = pltpu.CompilerParams(vmem_limit_bytes=16 * 1024 * 1024)


def lag_rows(freq_count, window_count):
    per_bin = 2 * window_count
    row = jnp.arange(freq_count * per_bin, dtype=jnp.int32)
    freq_values = (row // per_bin).astype(jnp.float32)
    sign = jnp.where(row % per_bin < window_count, 1.0, -1.0)
    lag_values = jnp.arange(HL + 1, dtype=jnp.float32)
    phases = jnp.pi / freq_count * lag_values[:, None] * freq_values[None, :]
    factor = 1.0 / math.sqrt(window_count * freq_count)
    cos_part = jnp.cos(phases) * factor
    sin_part = -jnp.sin(phases[1:]) * factor * sign[None, :]
    return jnp.concatenate([cos_part, sin_part], axis=0).astype(jnp.bfloat16)


def split_kernel(ends, x_ref, *part_refs):
    step = pl.program_id(0)
    for begin, end, part_ref in zip((0, *ends), ends, part_refs):
        @pl.when((step >= begin) & (step < end))
        def _():
            part_ref[...] = x_ref[...]


def split(x):
    rows, cols = x.shape
    steps = rows // STEP
    ends = [steps * e // ENDS[-1] for e in ENDS]
    sizes = [e - b for b, e in zip([0] + ends, ends)]

    def place(end, size):
        return lambda s: (jnp.clip(s - end + size, 0, size - 1), 0)

    return pl.pallas_call(
        functools.partial(split_kernel, ends),
        grid=(steps,),
        in_specs=[pl.BlockSpec((STEP, cols), lambda s: (s, 0))],
        out_specs=[pl.BlockSpec((STEP, cols), place(e, n)) for e, n in zip(ends, sizes)],
        out_shape=[jax.ShapeDtypeStruct((n * STEP, cols), x.dtype) for n in sizes],
        compiler_params=PARAMS,
        cost_estimate=pl.CostEstimate(flops=0, bytes_accessed=4 * rows * cols, transcendentals=0),
        name="split",
    )(x)


def turned(x):
    rows, cols = x.shape
    same = lax.broadcasted_iota(jnp.int32, (cols, cols), 0) == lax.broadcasted_iota(jnp.int32, (cols, cols), 1)
    eye = jnp.where(same, 1.0, 0.0).astype(jnp.bfloat16)
    source = lax.broadcasted_iota(jnp.int32, (2 * cols, 2 * cols), 0)
    target = lax.broadcasted_iota(jnp.int32, (2 * cols, 2 * cols), 1)
    exchange = jnp.where((source ^ 4) == target, 1.0, 0.0).astype(jnp.bfloat16)
    plain = lax.dot_general(eye, x, (((1,), (1,)), ((), ())), preferred_element_type=jnp.float32)
    plain = plain.astype(jnp.bfloat16)
    swapped = [
        jnp.dot(plain[:, t:t + 2 * cols], exchange, preferred_element_type=jnp.float32).astype(jnp.bfloat16)
        for t in range(0, rows, 2 * cols)
    ]
    return plain, jnp.concatenate(swapped, axis=1)


def turn_kernel(x_ref, plain_ref, swapped_ref):
    plain_ref[...], swapped_ref[...] = turned(x_ref[...])


def turn(x):
    rows, cols = x.shape
    out = jax.ShapeDtypeStruct((cols, rows), jnp.bfloat16)
    return pl.pallas_call(
        turn_kernel,
        grid=(rows // STEP,),
        in_specs=[pl.BlockSpec((STEP, cols), lambda s: (s, 0))],
        out_specs=[pl.BlockSpec((cols, STEP), lambda s: (0, s))] * 2,
        out_shape=[out, out],
        compiler_params=PARAMS,
        cost_estimate=pl.CostEstimate(flops=0, bytes_accessed=6 * rows * cols, transcendentals=0),
        name="turn",
    )(x)


def write_lags(out, acc, at, cols, mirrored):
    for lag in range(LAGS):
        k = abs(lag - HL)
        value = acc[k * cols:(k + 1) * cols, at]
        if k:
            odd = acc[(HL + k) * cols:(HL + k + 1) * cols, at]
            value = value + odd if lag > HL else value - odd
        value = value.astype(jnp.bfloat16)
        if mirrored:
            out[LAGS - 1 - lag] = value.T
        else:
            out[lag] = value


def scale(scaled, plain, swapped, coeff_ref):
    cols = plain.shape[0]
    for k in range(LAGS):
        part = plain if k <= HL else swapped
        scaled[k * cols:(k + 1) * cols, :] = part * coeff_ref[k:k + 1, :]


def weigh(x, window_weights):
    rows, cols = x.shape
    window = lax.broadcasted_iota(jnp.int32, (16, cols), 0) % len(window_weights)
    weights = jnp.zeros((16, cols), jnp.float32)
    for w, weight in enumerate(window_weights):
        weights = jnp.where(window == w, weight.astype(jnp.float32), weights)
    weights = jnp.broadcast_to(weights.astype(jnp.bfloat16)[None], (rows // 16, 16, cols))
    return x * weights.reshape(rows, cols)


def first_kernel(windows, last, switch_ref, plain_ref, swapped_ref, coeff_ref, near_ref, first_ref, *rest):
    step = pl.program_id(0)
    cols = plain_ref.shape[0]
    near_mirrored, special = switch_ref[0], switch_ref[1]
    if last:
        acc_in, _, near_out, far_out, back_out, acc, scaled, plain, swapped, right = rest
    else:
        acc, token_out, scaled, plain, swapped, right = rest

    @pl.when(step == 0)
    def _():
        if last:
            acc[...] = acc_in[...]
        else:
            acc[...] = jnp.zeros_like(acc)
            token_out[...] = jnp.zeros_like(token_out)

    @pl.when(special == 0)
    def _():
        plain[...], swapped[...] = plain_ref[...], swapped_ref[...]
        right[...] = first_ref[...]

    @pl.when(special != 0)
    def _():
        plain[...], swapped[...] = turned(first_ref[...])
        for t in range(0, STEP, cols):
            right[t:t + cols, :] = plain_ref[:, t:t + cols].T

    scale(scaled, plain[...], swapped[...], coeff_ref)
    flags = [[switch_ref[2 + part * windows + w] for w in range(windows)] for part in range(3)]
    near_weights = [jnp.where(special != 0, first, own) * near for own, near, first in zip(*flags)]
    near = weigh(near_ref[...], near_weights)
    far = weigh(right[...], [own * first for own, _, first in zip(*flags)])
    acc[...] += jnp.dot(scaled[...], jnp.concatenate([near, far], axis=1), preferred_element_type=jnp.float32)

    if last:
        @pl.when(step == pl.num_programs(0) - 1)
        def _():
            near_at, far_at = slice(0, cols), slice(cols, 2 * cols)

            @pl.when(special == 0)
            def _():
                write_lags(back_out, acc, far_at, cols, True)
                write_lags(far_out, acc, far_at, cols, False)

            @pl.when(special != 0)
            def _():
                write_lags(back_out, acc, far_at, cols, False)
                write_lags(far_out, acc, far_at, cols, True)

            pl.when(near_mirrored == 0)(lambda: write_lags(near_out, acc, near_at, cols, False))
            pl.when(near_mirrored != 0)(lambda: write_lags(near_out, acc, near_at, cols, True))


def first_sums(switch, own, coeffs, near_in, first_in, earlier=None):
    rows, cols = near_in.shape
    steps = rows // STEP // 2
    skip = 0 if earlier is None else steps
    windows = (switch.shape[0] - 2) // 3
    result = jax.ShapeDtypeStruct((LAGS, cols, cols), jnp.bfloat16)
    total = jax.ShapeDtypeStruct((LAGS * cols, 2 * cols), jnp.float32)
    total_spec = pl.BlockSpec(total.shape, lambda s, on: (0, 0))
    token = jax.ShapeDtypeStruct((8, cols), jnp.float32)
    token_spec = pl.BlockSpec(token.shape, lambda s, on: (0, 0))
    left = pl.BlockSpec((cols, STEP), lambda s, on: (0, s + skip))
    right = pl.BlockSpec((STEP, cols), lambda s, on: (s + skip, 0))
    in_specs = [left, left, pl.BlockSpec((LAGS, STEP), lambda s, on: (0, s + skip)), right, right]
    scratch = [pltpu.VMEM((LAGS * cols, STEP), jnp.bfloat16)] + [pltpu.VMEM((cols, STEP), jnp.bfloat16)] * 2
    scratch += [pltpu.VMEM((STEP, cols), jnp.bfloat16)]
    if earlier is None:
        out_shape, out_specs, earlier = [total, token], [total_spec, token_spec], []
    else:
        in_specs += [total_spec, token_spec]
        out_shape = [result] * 3
        out_specs = [pl.BlockSpec(result.shape, lambda s, on: (0, 0, 0))] * 3
        scratch = [pltpu.VMEM(total.shape, jnp.float32)] + scratch
    return pl.pallas_call(
        functools.partial(first_kernel, windows, bool(earlier)),
        grid_spec=pltpu.PrefetchScalarGridSpec(
            num_scalar_prefetch=1,
            grid=(steps,),
            in_specs=in_specs,
            out_specs=out_specs,
            scratch_shapes=scratch,
        ),
        out_shape=out_shape,
        compiler_params=PARAMS,
        cost_estimate=pl.CostEstimate(
            flops=2 * LAGS * cols * cols * rows, bytes_accessed=4 * rows * cols, transcendentals=0
        ),
        name="first_last" if earlier else "first_half",
    )(switch, *own, coeffs, near_in, first_in, *earlier)


def second_kernel(windows, first, last, switch_ref, plain_ref, swapped_ref, coeff_ref, partner_ref, *rest):
    on, late_near = switch_ref[0], switch_ref[1]
    step = pl.program_id(0)
    cols = plain_ref.shape[0]
    if first:
        acc, scaled = rest
    elif not last:
        acc_in, acc, scaled = rest
    else:
        acc_in, near_in, far_in, back_in, near_out, far_out, back_out, acc, scaled = rest

    @pl.when(on != 0)
    def _():
        @pl.when(step == 0)
        def _():
            acc[...] = jnp.zeros_like(acc) if first else acc_in[...]

        scale(scaled, plain_ref[...], swapped_ref[...], coeff_ref)
        partner = weigh(partner_ref[...], [switch_ref[2 + w] for w in range(windows)])
        acc[...] += jnp.dot(scaled[...], partner, preferred_element_type=jnp.float32)

    if last:
        @pl.when(step == pl.num_programs(0) - 1)
        def _():
            here = slice(0, cols)

            @pl.when((on != 0) & (late_near == 0))
            def _():
                write_lags(back_out, acc, here, cols, True)
                write_lags(far_out, acc, here, cols, False)

            @pl.when((on == 0) | (late_near != 0))
            def _():
                back_out[...] = back_in[...]
                far_out[...] = far_in[...]

            pl.when(late_near != 0)(lambda: write_lags(near_out, acc, here, cols, False))

            @pl.when(late_near == 0)
            def _():
                near_out[...] = near_in[...]


def second_sums(switch, own, coeffs, partner, start, earlier=()):
    rows, cols = partner.shape
    windows = switch.shape[0] - 2
    skip = start // STEP
    total = jax.ShapeDtypeStruct((LAGS * cols, cols), jnp.float32)
    total_spec = pl.BlockSpec(total.shape, lambda s, on: (0, 0))
    result = jax.ShapeDtypeStruct((LAGS, cols, cols), jnp.bfloat16)
    result_spec = pl.BlockSpec(result.shape, lambda s, on: (0, 0, 0))
    left = pl.BlockSpec((cols, STEP), lambda s, on: (0, s * on[0] + skip))
    in_specs = [left, left, pl.BlockSpec((LAGS, STEP), lambda s, on: (0, s * on[0] + skip)),
                pl.BlockSpec((STEP, cols), lambda s, on: (s * on[0], 0))]
    scratch = [pltpu.VMEM((LAGS * cols, STEP), jnp.bfloat16)]
    last = len(earlier) > 1
    in_specs += [total_spec, result_spec, result_spec, result_spec][:len(earlier)]
    if not last:
        out_shape, out_specs = [total], [total_spec]
    else:
        out_shape, out_specs = [result] * 3, [result_spec] * 3
        scratch = [pltpu.VMEM(total.shape, jnp.float32)] + scratch
    return pl.pallas_call(
        functools.partial(second_kernel, windows, not earlier, last),
        grid_spec=pltpu.PrefetchScalarGridSpec(
            num_scalar_prefetch=1,
            grid=(rows // STEP,),
            in_specs=in_specs,
            out_specs=out_specs,
            scratch_shapes=scratch,
        ),
        out_shape=out_shape,
        compiler_params=PARAMS,
        cost_estimate=pl.CostEstimate(
            flops=2 * LAGS * cols * cols * rows, bytes_accessed=6 * rows * cols, transcendentals=0
        ),
        name="second_last" if last else "second_part",
    )(switch, *own, coeffs, partner, *earlier)


def local(spectra, quality):
    count = lax.axis_size("chan")
    half = count // 2
    me = lax.axis_index("chan")
    freq_count, _, window_count, cols = spectra.shape
    block = spectra.reshape(-1, cols)

    first_far, second_far = [], []
    for p in range(half):
        if p in (0, half - 1):
            first_far.append((p + half, p))
        elif p > half // 2:
            first_far.append((p, p + half))
        elif p % 2 == 1:
            second_far.append((p, p + half))
        else:
            second_far.append((p + half, p))
    late_near = [(2, 1), (4, 3)]
    first_pairs = first_far + [(0, 1), (half - 1, half - 2)]
    second_pairs = second_far + late_near
    near_pairs = [(d + 1, d) for d in range(1, count - 1) if d not in (1, 3, half - 2, half - 1)]
    near_pairs += [(0, half - 1), (half - 1, 0)]
    back_pairs = [(t, s) for s, t in first_far + second_far] + [(1, 0)]
    side_pairs = [(0, half - 1), (half - 1, count - 1)]

    def among(devices):
        return functools.reduce(jnp.logical_or, [me == d for d in devices])

    def switch(on, other, *weights):
        flags = jnp.stack([jnp.asarray(on), jnp.asarray(other)]).astype(jnp.int32)
        return jnp.concatenate([flags, *weights])

    near_in = lax.ppermute(block, "chan", near_pairs)
    first_in = lax.ppermute(block, "chan", first_pairs)
    coeffs = lag_rows(freq_count, window_count)
    own = turn(block)
    parts = split(block)
    first_flags = lax.ppermute(quality, "chan", first_pairs)[0]
    near_flags = lax.ppermute(quality, "chan", near_pairs)[0]
    second_flags = lax.ppermute(quality, "chan", second_pairs)[0]
    special = among([0, half - 1])
    second_switch = switch(
        among([t for _, t in second_pairs]), among([t for _, t in late_near]), quality[0] * second_flags
    )

    near_in, *parts, own, coeffs, first_in, near_flags, first_flags, second_flags = lax.optimization_barrier(
        (near_in, *parts, own, coeffs, first_in, near_flags, first_flags, second_flags)
    )
    second_in = [lax.ppermute(parts[0], "chan", second_pairs)]
    first_switch = switch(me == 0, special, quality[0], near_flags, first_flags)
    operands = first_switch, own, coeffs, near_in, first_in
    total, token = first_sums(*operands)
    part, token = lax.optimization_barrier((parts[1], token))
    second_in.append(lax.ppermute(part, "chan", second_pairs))
    near, far, back = first_sums(*operands, [total, token])
    second_switch, near, part = lax.optimization_barrier((second_switch, near, parts[2]))
    second_in.append(lax.ppermute(part, "chan", second_pairs))
    starts = [0, parts[0].shape[0], parts[0].shape[0] + parts[1].shape[0]]
    total = second_sums(second_switch, own, coeffs, second_in[0], starts[0])
    total, = second_sums(second_switch, own, coeffs, second_in[1], starts[1], total)

    near = jnp.where(me == half - 2, far, near)
    near, far, back = second_sums(
        second_switch, own, coeffs, second_in[2], starts[2], [total, near, far, back]
    )
    returned = lax.ppermute(back, "chan", back_pairs)
    side_returned = lax.ppermute(near, "chan", side_pairs)
    near = jnp.where(among([half - 1, count - 1]), side_returned, near)
    near = jnp.where(me == 0, returned, near)
    far = jnp.where(among([s for s, _ in first_far + second_far]), returned, far)
    return near[None], far[None]


def solution(mesh):
    return jax.shard_map(
        local,
        mesh=mesh,
        in_specs=(P(None, None, None, ("grp", "chan")), P(("grp", "chan"), None)),
        out_specs=(P(("grp", "chan"), None, None, None), P(("grp", "chan"), None, None, None)),
        check_vma=False,
    )
```

```python
import functools
import math

import jax
import jax.numpy as jnp
from jax import lax
from jax.experimental import pallas as pl
from jax.experimental.pallas import tpu as pltpu
from jax.sharding import PartitionSpec as P

HL = 4
LAGS = 2 * HL + 1
STEP = 1024
PARTS = (5, 8)
PARAMS = pltpu.CompilerParams(vmem_limit_bytes=16 * 1024 * 1024)


def lag_rows(freq_count, window_count):
    per_bin = 2 * window_count
    row = jnp.arange(freq_count * per_bin, dtype=jnp.int32)
    freq_values = (row // per_bin).astype(jnp.float32)
    sign = jnp.where(row % per_bin < window_count, 1.0, -1.0)
    lag_values = jnp.arange(HL + 1, dtype=jnp.float32)
    phases = jnp.pi / freq_count * lag_values[:, None] * freq_values[None, :]
    factor = 1.0 / math.sqrt(window_count * freq_count)
    cos_part = jnp.cos(phases) * factor
    sin_part = -jnp.sin(phases[1:]) * factor * sign[None, :]
    return jnp.concatenate([cos_part, sin_part], axis=0).astype(jnp.bfloat16)


def split_kernel(middle, x_ref, first_ref, last_ref):
    step = pl.program_id(0)

    @pl.when(step < middle)
    def _():
        first_ref[...] = x_ref[...]

    @pl.when(step >= middle)
    def _():
        last_ref[...] = x_ref[...]


def split(x):
    rows, cols = x.shape
    steps = rows // STEP
    middle = steps * PARTS[0] // PARTS[1]
    return pl.pallas_call(
        functools.partial(split_kernel, middle),
        grid=(steps,),
        in_specs=[pl.BlockSpec((STEP, cols), lambda s: (s, 0))],
        out_specs=[
            pl.BlockSpec((STEP, cols), lambda s: (jnp.minimum(s, middle - 1), 0)),
            pl.BlockSpec((STEP, cols), lambda s: (jnp.maximum(s - middle, 0), 0)),
        ],
        out_shape=[jax.ShapeDtypeStruct((n * STEP, cols), x.dtype) for n in (middle, steps - middle)],
        compiler_params=PARAMS,
        cost_estimate=pl.CostEstimate(flops=0, bytes_accessed=4 * rows * cols, transcendentals=0),
        name="split",
    )(x)


def turned(x):
    rows, cols = x.shape
    same = lax.broadcasted_iota(jnp.int32, (cols, cols), 0) == lax.broadcasted_iota(jnp.int32, (cols, cols), 1)
    eye = jnp.where(same, 1.0, 0.0).astype(jnp.bfloat16)
    source = lax.broadcasted_iota(jnp.int32, (2 * cols, 2 * cols), 0)
    target = lax.broadcasted_iota(jnp.int32, (2 * cols, 2 * cols), 1)
    exchange = jnp.where((source ^ 4) == target, 1.0, 0.0).astype(jnp.bfloat16)
    plain = lax.dot_general(eye, x, (((1,), (1,)), ((), ())), preferred_element_type=jnp.float32)
    plain = plain.astype(jnp.bfloat16)
    swapped = [
        jnp.dot(plain[:, t:t + 2 * cols], exchange, preferred_element_type=jnp.float32).astype(jnp.bfloat16)
        for t in range(0, rows, 2 * cols)
    ]
    return plain, jnp.concatenate(swapped, axis=1)


def turn_kernel(x_ref, plain_ref, swapped_ref):
    plain_ref[...], swapped_ref[...] = turned(x_ref[...])


def turn(x):
    rows, cols = x.shape
    out = jax.ShapeDtypeStruct((cols, rows), jnp.bfloat16)
    return pl.pallas_call(
        turn_kernel,
        grid=(rows // STEP,),
        in_specs=[pl.BlockSpec((STEP, cols), lambda s: (s, 0))],
        out_specs=[pl.BlockSpec((cols, STEP), lambda s: (0, s))] * 2,
        out_shape=[out, out],
        compiler_params=PARAMS,
        cost_estimate=pl.CostEstimate(flops=0, bytes_accessed=6 * rows * cols, transcendentals=0),
        name="turn",
    )(x)


def write_lags(out, acc, at, cols, mirrored):
    for lag in range(LAGS):
        k = abs(lag - HL)
        value = acc[k * cols:(k + 1) * cols, at]
        if k:
            odd = acc[(HL + k) * cols:(HL + k + 1) * cols, at]
            value = value + odd if lag > HL else value - odd
        value = value.astype(jnp.bfloat16)
        if mirrored:
            out[LAGS - 1 - lag] = value.T
        else:
            out[lag] = value


def scale(scaled, plain, swapped, coeff_ref):
    cols = plain.shape[0]
    for k in range(LAGS):
        part = plain if k <= HL else swapped
        scaled[k * cols:(k + 1) * cols, :] = part * coeff_ref[k:k + 1, :]


def weigh(x, window_weights):
    rows, cols = x.shape
    window = lax.broadcasted_iota(jnp.int32, (16, cols), 0) % len(window_weights)
    weights = jnp.zeros((16, cols), jnp.float32)
    for w, weight in enumerate(window_weights):
        weights = jnp.where(window == w, weight.astype(jnp.float32), weights)
    weights = jnp.broadcast_to(weights.astype(jnp.bfloat16)[None], (rows // 16, 16, cols))
    return x * weights.reshape(rows, cols)


def first_kernel(windows, last, switch_ref, plain_ref, swapped_ref, coeff_ref, near_ref, first_ref, *rest):
    step = pl.program_id(0)
    cols = plain_ref.shape[0]
    near_mirrored, special = switch_ref[0], switch_ref[1]
    if last:
        acc_in, _, near_out, far_out, back_out, acc, scaled, plain, swapped, right = rest
    else:
        acc, token_out, scaled, plain, swapped, right = rest

    @pl.when(step == 0)
    def _():
        if last:
            acc[...] = acc_in[...]
        else:
            acc[...] = jnp.zeros_like(acc)
            token_out[...] = jnp.zeros_like(token_out)

    @pl.when(special == 0)
    def _():
        plain[...], swapped[...] = plain_ref[...], swapped_ref[...]
        right[...] = first_ref[...]

    @pl.when(special != 0)
    def _():
        plain[...], swapped[...] = turned(first_ref[...])
        for t in range(0, STEP, cols):
            right[t:t + cols, :] = plain_ref[:, t:t + cols].T

    scale(scaled, plain[...], swapped[...], coeff_ref)
    flags = [[switch_ref[2 + part * windows + w] for w in range(windows)] for part in range(3)]
    near_weights = [jnp.where(special != 0, first, own) * near for own, near, first in zip(*flags)]
    near = weigh(near_ref[...], near_weights)
    far = weigh(right[...], [own * first for own, _, first in zip(*flags)])
    acc[...] += jnp.dot(scaled[...], jnp.concatenate([near, far], axis=1), preferred_element_type=jnp.float32)

    if last:
        @pl.when(step == pl.num_programs(0) - 1)
        def _():
            near_at, far_at = slice(0, cols), slice(cols, 2 * cols)

            @pl.when(special == 0)
            def _():
                write_lags(back_out, acc, far_at, cols, True)
                write_lags(far_out, acc, far_at, cols, False)

            @pl.when(special != 0)
            def _():
                write_lags(back_out, acc, far_at, cols, False)
                write_lags(far_out, acc, far_at, cols, True)

            pl.when(near_mirrored == 0)(lambda: write_lags(near_out, acc, near_at, cols, False))
            pl.when(near_mirrored != 0)(lambda: write_lags(near_out, acc, near_at, cols, True))


def first_sums(switch, own, coeffs, near_in, first_in, earlier=None):
    rows, cols = near_in.shape
    steps = rows // STEP // 2
    skip = 0 if earlier is None else steps
    windows = (switch.shape[0] - 2) // 3
    result = jax.ShapeDtypeStruct((LAGS, cols, cols), jnp.bfloat16)
    total = jax.ShapeDtypeStruct((LAGS * cols, 2 * cols), jnp.float32)
    total_spec = pl.BlockSpec(total.shape, lambda s, on: (0, 0))
    token = jax.ShapeDtypeStruct((8, cols), jnp.float32)
    token_spec = pl.BlockSpec(token.shape, lambda s, on: (0, 0))
    left = pl.BlockSpec((cols, STEP), lambda s, on: (0, s + skip))
    right = pl.BlockSpec((STEP, cols), lambda s, on: (s + skip, 0))
    in_specs = [left, left, pl.BlockSpec((LAGS, STEP), lambda s, on: (0, s + skip)), right, right]
    scratch = [pltpu.VMEM((LAGS * cols, STEP), jnp.bfloat16)] + [pltpu.VMEM((cols, STEP), jnp.bfloat16)] * 2
    scratch += [pltpu.VMEM((STEP, cols), jnp.bfloat16)]
    if earlier is None:
        out_shape, out_specs, earlier = [total, token], [total_spec, token_spec], []
    else:
        in_specs += [total_spec, token_spec]
        out_shape = [result] * 3
        out_specs = [pl.BlockSpec(result.shape, lambda s, on: (0, 0, 0))] * 3
        scratch = [pltpu.VMEM(total.shape, jnp.float32)] + scratch
    return pl.pallas_call(
        functools.partial(first_kernel, windows, bool(earlier)),
        grid_spec=pltpu.PrefetchScalarGridSpec(
            num_scalar_prefetch=1,
            grid=(steps,),
            in_specs=in_specs,
            out_specs=out_specs,
            scratch_shapes=scratch,
        ),
        out_shape=out_shape,
        compiler_params=PARAMS,
        cost_estimate=pl.CostEstimate(
            flops=2 * LAGS * cols * cols * rows, bytes_accessed=4 * rows * cols, transcendentals=0
        ),
        name="first_last" if earlier else "first_half",
    )(switch, *own, coeffs, near_in, first_in, *earlier)


def second_kernel(windows, first, switch_ref, plain_ref, swapped_ref, coeff_ref, partner_ref, *rest):
    on, late_near = switch_ref[0], switch_ref[1]
    step = pl.program_id(0)
    cols = plain_ref.shape[0]
    if first:
        acc, scaled = rest
    else:
        acc_in, near_in, far_in, back_in, near_out, far_out, back_out, acc, scaled = rest

    @pl.when(on != 0)
    def _():
        @pl.when(step == 0)
        def _():
            acc[...] = jnp.zeros_like(acc) if first else acc_in[...]

        scale(scaled, plain_ref[...], swapped_ref[...], coeff_ref)
        partner = weigh(partner_ref[...], [switch_ref[2 + w] for w in range(windows)])
        acc[...] += jnp.dot(scaled[...], partner, preferred_element_type=jnp.float32)

    if not first:
        @pl.when(step == pl.num_programs(0) - 1)
        def _():
            here = slice(0, cols)

            @pl.when((on != 0) & (late_near == 0))
            def _():
                write_lags(back_out, acc, here, cols, True)
                write_lags(far_out, acc, here, cols, False)

            @pl.when((on == 0) | (late_near != 0))
            def _():
                back_out[...] = back_in[...]
                far_out[...] = far_in[...]

            pl.when(late_near != 0)(lambda: write_lags(near_out, acc, here, cols, False))

            @pl.when(late_near == 0)
            def _():
                near_out[...] = near_in[...]


def second_sums(switch, own, coeffs, partner, start, earlier=None):
    rows, cols = partner.shape
    windows = switch.shape[0] - 2
    skip = start // STEP
    total = jax.ShapeDtypeStruct((LAGS * cols, cols), jnp.float32)
    total_spec = pl.BlockSpec(total.shape, lambda s, on: (0, 0))
    result = jax.ShapeDtypeStruct((LAGS, cols, cols), jnp.bfloat16)
    result_spec = pl.BlockSpec(result.shape, lambda s, on: (0, 0, 0))
    left = pl.BlockSpec((cols, STEP), lambda s, on: (0, s * on[0] + skip))
    in_specs = [left, left, pl.BlockSpec((LAGS, STEP), lambda s, on: (0, s * on[0] + skip)),
                pl.BlockSpec((STEP, cols), lambda s, on: (s * on[0], 0))]
    scratch = [pltpu.VMEM((LAGS * cols, STEP), jnp.bfloat16)]
    if earlier is None:
        out_shape, out_specs, earlier = [total], [total_spec], []
    else:
        out_shape, out_specs = [result] * 3, [result_spec] * 3
        in_specs += [total_spec] + [result_spec] * 3
        scratch = [pltpu.VMEM(total.shape, jnp.float32)] + scratch
    return pl.pallas_call(
        functools.partial(second_kernel, windows, not earlier),
        grid_spec=pltpu.PrefetchScalarGridSpec(
            num_scalar_prefetch=1,
            grid=(rows // STEP,),
            in_specs=in_specs,
            out_specs=out_specs,
            scratch_shapes=scratch,
        ),
        out_shape=out_shape,
        compiler_params=PARAMS,
        cost_estimate=pl.CostEstimate(
            flops=2 * LAGS * cols * cols * rows, bytes_accessed=6 * rows * cols, transcendentals=0
        ),
        name="second_last" if earlier else "second_part",
    )(switch, *own, coeffs, partner, *earlier)


def local(spectra, quality):
    count = lax.axis_size("chan")
    half = count // 2
    me = lax.axis_index("chan")
    freq_count, _, window_count, cols = spectra.shape
    block = spectra.reshape(-1, cols)

    first_far, second_far = [], []
    for p in range(half):
        if p in (0, half - 1):
            first_far.append((p + half, p))
        elif p == 2 or p % 2 == 1 and p > 3:
            first_far.append((p, p + half))
        elif p % 2 == 1:
            second_far.append((p, p + half))
        else:
            second_far.append((p + half, p))
    late_near = [(2, 1), (4, 3)]
    first_pairs = first_far + [(0, 1), (half - 1, half - 2)]
    second_pairs = second_far + late_near
    near_pairs = [(d + 1, d) for d in range(1, count - 1) if d not in (1, 3, half - 2, half - 1)]
    near_pairs += [(0, half - 1), (half - 1, 0)]
    back_pairs = [(t, s) for s, t in first_far + second_far] + [(1, 0)]
    side_pairs = [(0, half - 1), (half - 1, count - 1)]

    def among(devices):
        return functools.reduce(jnp.logical_or, [me == d for d in devices])

    def switch(on, other, *weights):
        flags = jnp.stack([jnp.asarray(on), jnp.asarray(other)]).astype(jnp.int32)
        return jnp.concatenate([flags, *weights])

    near_in = lax.ppermute(block, "chan", near_pairs)
    first_in = lax.ppermute(block, "chan", first_pairs)
    coeffs = lag_rows(freq_count, window_count)
    own = turn(block)
    parts = split(block)
    first_flags = lax.ppermute(quality, "chan", first_pairs)[0]
    near_flags = lax.ppermute(quality, "chan", near_pairs)[0]
    second_flags = lax.ppermute(quality, "chan", second_pairs)[0]
    special = among([0, half - 1])
    second_switch = switch(
        among([t for _, t in second_pairs]), among([t for _, t in late_near]), quality[0] * second_flags
    )

    near_in, first_part, last_part, own, coeffs, first_in, near_flags, first_flags, second_flags = lax.optimization_barrier(
        (near_in, *parts, own, coeffs, first_in, near_flags, first_flags, second_flags)
    )
    second_in = [lax.ppermute(first_part, "chan", second_pairs)]
    first_switch = switch(me == 0, special, quality[0], near_flags, first_flags)
    operands = first_switch, own, coeffs, near_in, first_in
    total, token = first_sums(*operands)
    last_part, token = lax.optimization_barrier((last_part, token))
    second_in.append(lax.ppermute(last_part, "chan", second_pairs))
    near, far, back = first_sums(*operands, [total, token])
    second_switch, near = lax.optimization_barrier((second_switch, near))
    total, = second_sums(second_switch, own, coeffs, second_in[0], 0)

    near = jnp.where(me == half - 2, far, near)
    near, far, back = second_sums(
        second_switch, own, coeffs, second_in[1], parts[0].shape[0], [total, near, far, back]
    )
    returned = lax.ppermute(back, "chan", back_pairs)
    side_returned = lax.ppermute(near, "chan", side_pairs)
    near = jnp.where(among([half - 1, count - 1]), side_returned, near)
    near = jnp.where(me == 0, returned, near)
    far = jnp.where(among([s for s, _ in first_far + second_far]), returned, far)
    return near[None], far[None]


def solution(mesh):
    return jax.shard_map(
        local,
        mesh=mesh,
        in_specs=(P(None, None, None, ("grp", "chan")), P(("grp", "chan"), None)),
        out_specs=(P(("grp", "chan"), None, None, None), P(("grp", "chan"), None, None, None)),
        check_vma=False,
    )
```

```python
import functools
import math

import jax
import jax.numpy as jnp
from jax import lax
from jax.experimental import pallas as pl
from jax.experimental.pallas import tpu as pltpu
from jax.sharding import PartitionSpec as P

HL = 4
LAGS = 2 * HL + 1
STEP = 1024
PARTS = (5, 8)
PARAMS = pltpu.CompilerParams(vmem_limit_bytes=28 * 1024 * 1024)


def lag_rows(freq_count, window_count):
    per_bin = 2 * window_count
    row = jnp.arange(freq_count * per_bin, dtype=jnp.int32)
    freq_values = (row // per_bin).astype(jnp.float32)
    sign = jnp.where(row % per_bin < window_count, 1.0, -1.0)
    lag_values = jnp.arange(HL + 1, dtype=jnp.float32)
    phases = jnp.pi / freq_count * lag_values[:, None] * freq_values[None, :]
    factor = 1.0 / math.sqrt(window_count * freq_count)
    cos_part = jnp.cos(phases) * factor
    sin_part = -jnp.sin(phases[1:]) * factor * sign[None, :]
    return jnp.concatenate([cos_part, sin_part], axis=0).astype(jnp.bfloat16)


def split_kernel(middle, x_ref, first_ref, last_ref):
    step = pl.program_id(0)

    @pl.when(step < middle)
    def _():
        first_ref[...] = x_ref[...]

    @pl.when(step >= middle)
    def _():
        last_ref[...] = x_ref[...]


def split(x):
    rows, cols = x.shape
    steps = rows // STEP
    middle = steps * PARTS[0] // PARTS[1]
    return pl.pallas_call(
        functools.partial(split_kernel, middle),
        grid=(steps,),
        in_specs=[pl.BlockSpec((STEP, cols), lambda s: (s, 0))],
        out_specs=[
            pl.BlockSpec((STEP, cols), lambda s: (jnp.minimum(s, middle - 1), 0)),
            pl.BlockSpec((STEP, cols), lambda s: (jnp.maximum(s - middle, 0), 0)),
        ],
        out_shape=[jax.ShapeDtypeStruct((n * STEP, cols), x.dtype) for n in (middle, steps - middle)],
        compiler_params=PARAMS,
        cost_estimate=pl.CostEstimate(flops=0, bytes_accessed=4 * rows * cols, transcendentals=0),
        name="split",
    )(x)


def turned(x):
    rows, cols = x.shape
    same = lax.broadcasted_iota(jnp.int32, (cols, cols), 0) == lax.broadcasted_iota(jnp.int32, (cols, cols), 1)
    eye = jnp.where(same, 1.0, 0.0).astype(jnp.bfloat16)
    source = lax.broadcasted_iota(jnp.int32, (2 * cols, 2 * cols), 0)
    target = lax.broadcasted_iota(jnp.int32, (2 * cols, 2 * cols), 1)
    exchange = jnp.where((source ^ 4) == target, 1.0, 0.0).astype(jnp.bfloat16)
    plain = lax.dot_general(eye, x, (((1,), (1,)), ((), ())), preferred_element_type=jnp.float32)
    plain = plain.astype(jnp.bfloat16)
    swapped = [
        jnp.dot(plain[:, t:t + 2 * cols], exchange, preferred_element_type=jnp.float32).astype(jnp.bfloat16)
        for t in range(0, rows, 2 * cols)
    ]
    return plain, jnp.concatenate(swapped, axis=1)


def turn_kernel(x_ref, plain_ref, swapped_ref):
    plain_ref[...], swapped_ref[...] = turned(x_ref[...])


def turn(x):
    rows, cols = x.shape
    out = jax.ShapeDtypeStruct((cols, rows), jnp.bfloat16)
    return pl.pallas_call(
        turn_kernel,
        grid=(rows // STEP,),
        in_specs=[pl.BlockSpec((STEP, cols), lambda s: (s, 0))],
        out_specs=[pl.BlockSpec((cols, STEP), lambda s: (0, s))] * 2,
        out_shape=[out, out],
        compiler_params=PARAMS,
        cost_estimate=pl.CostEstimate(flops=0, bytes_accessed=6 * rows * cols, transcendentals=0),
        name="turn",
    )(x)


def write_lags(out, acc, at, cols, mirrored):
    for lag in range(LAGS):
        k = abs(lag - HL)
        value = acc[k * cols:(k + 1) * cols, at]
        if k:
            odd = acc[(HL + k) * cols:(HL + k + 1) * cols, at]
            value = value + odd if lag > HL else value - odd
        value = value.astype(jnp.bfloat16)
        if mirrored:
            out[LAGS - 1 - lag] = value.T
        else:
            out[lag] = value


def scale(scaled, plain, swapped, coeff_ref):
    cols = plain.shape[0]
    for k in range(LAGS):
        part = plain if k <= HL else swapped
        scaled[k * cols:(k + 1) * cols, :] = part * coeff_ref[k:k + 1, :]


def weigh(x, window_weights):
    rows, cols = x.shape
    window = lax.broadcasted_iota(jnp.int32, (16, cols), 0) % len(window_weights)
    weights = jnp.zeros((16, cols), jnp.float32)
    for w, weight in enumerate(window_weights):
        weights = jnp.where(window == w, weight.astype(jnp.float32), weights)
    weights = jnp.broadcast_to(weights.astype(jnp.bfloat16)[None], (rows // 16, 16, cols))
    return x * weights.reshape(rows, cols)


def first_kernel(windows, last, switch_ref, plain_ref, swapped_ref, coeff_ref, near_ref, first_ref, *rest):
    step = pl.program_id(0)
    cols = plain_ref.shape[0]
    near_mirrored, special = switch_ref[0], switch_ref[1]
    if last:
        acc_in, _, near_out, far_out, back_out, acc, scaled, plain, swapped, right = rest
    else:
        acc, token_out, scaled, plain, swapped, right = rest

    @pl.when(step == 0)
    def _():
        if last:
            acc[...] = acc_in[...]
        else:
            acc[...] = jnp.zeros_like(acc)
            token_out[...] = jnp.zeros_like(token_out)

    @pl.when(special == 0)
    def _():
        plain[...], swapped[...] = plain_ref[...], swapped_ref[...]
        right[...] = first_ref[...]

    @pl.when(special != 0)
    def _():
        plain[...], swapped[...] = turned(first_ref[...])
        for t in range(0, STEP, cols):
            right[t:t + cols, :] = plain_ref[:, t:t + cols].T

    scale(scaled, plain[...], swapped[...], coeff_ref)
    flags = [[switch_ref[2 + part * windows + w] for w in range(windows)] for part in range(3)]
    near_weights = [jnp.where(special != 0, first, own) * near for own, near, first in zip(*flags)]
    near = weigh(near_ref[...], near_weights)
    far = weigh(right[...], [own * first for own, _, first in zip(*flags)])
    acc[...] += jnp.dot(scaled[...], jnp.concatenate([near, far], axis=1), preferred_element_type=jnp.float32)

    if last:
        @pl.when(step == pl.num_programs(0) - 1)
        def _():
            near_at, far_at = slice(0, cols), slice(cols, 2 * cols)

            @pl.when(special == 0)
            def _():
                write_lags(back_out, acc, far_at, cols, True)
                write_lags(far_out, acc, far_at, cols, False)

            @pl.when(special != 0)
            def _():
                write_lags(back_out, acc, far_at, cols, False)
                write_lags(far_out, acc, far_at, cols, True)

            pl.when(near_mirrored == 0)(lambda: write_lags(near_out, acc, near_at, cols, False))
            pl.when(near_mirrored != 0)(lambda: write_lags(near_out, acc, near_at, cols, True))


def first_sums(switch, own, coeffs, near_in, first_in, earlier=None):
    rows, cols = near_in.shape
    steps = rows // STEP // 2
    skip = 0 if earlier is None else steps
    windows = (switch.shape[0] - 2) // 3
    result = jax.ShapeDtypeStruct((LAGS, cols, cols), jnp.bfloat16)
    total = jax.ShapeDtypeStruct((LAGS * cols, 2 * cols), jnp.float32)
    total_spec = pl.BlockSpec(total.shape, lambda s, on: (0, 0))
    token = jax.ShapeDtypeStruct((8, cols), jnp.float32)
    token_spec = pl.BlockSpec(token.shape, lambda s, on: (0, 0))
    left = pl.BlockSpec((cols, STEP), lambda s, on: (0, s + skip))
    right = pl.BlockSpec((STEP, cols), lambda s, on: (s + skip, 0))
    in_specs = [left, left, pl.BlockSpec((LAGS, STEP), lambda s, on: (0, s + skip)), right, right]
    scratch = [pltpu.VMEM((LAGS * cols, STEP), jnp.bfloat16)] + [pltpu.VMEM((cols, STEP), jnp.bfloat16)] * 2
    scratch += [pltpu.VMEM((STEP, cols), jnp.bfloat16)]
    if earlier is None:
        out_shape, out_specs, earlier = [total, token], [total_spec, token_spec], []
    else:
        in_specs += [total_spec, token_spec]
        out_shape = [result] * 3
        out_specs = [pl.BlockSpec(result.shape, lambda s, on: (0, 0, 0))] * 3
        scratch = [pltpu.VMEM(total.shape, jnp.float32)] + scratch
    return pl.pallas_call(
        functools.partial(first_kernel, windows, bool(earlier)),
        grid_spec=pltpu.PrefetchScalarGridSpec(
            num_scalar_prefetch=1,
            grid=(steps,),
            in_specs=in_specs,
            out_specs=out_specs,
            scratch_shapes=scratch,
        ),
        out_shape=out_shape,
        compiler_params=PARAMS,
        cost_estimate=pl.CostEstimate(
            flops=2 * LAGS * cols * cols * rows, bytes_accessed=4 * rows * cols, transcendentals=0
        ),
        name="first_last" if earlier else "first_half",
    )(switch, *own, coeffs, near_in, first_in, *earlier)


def second_kernel(windows, first, switch_ref, plain_ref, swapped_ref, coeff_ref, partner_ref, *rest):
    on, late_near = switch_ref[0], switch_ref[1]
    step = pl.program_id(0)
    cols = plain_ref.shape[0]
    if first:
        acc, scaled = rest
    else:
        acc_in, near_in, far_in, back_in, near_out, far_out, back_out, acc, scaled = rest

    @pl.when(on != 0)
    def _():
        @pl.when(step == 0)
        def _():
            acc[...] = jnp.zeros_like(acc) if first else acc_in[...]

        scale(scaled, plain_ref[...], swapped_ref[...], coeff_ref)
        partner = weigh(partner_ref[...], [switch_ref[2 + w] for w in range(windows)])
        acc[...] += jnp.dot(scaled[...], partner, preferred_element_type=jnp.float32)

    if not first:
        @pl.when(step == pl.num_programs(0) - 1)
        def _():
            here = slice(0, cols)

            @pl.when((on != 0) & (late_near == 0))
            def _():
                write_lags(back_out, acc, here, cols, True)
                write_lags(far_out, acc, here, cols, False)

            @pl.when((on == 0) | (late_near != 0))
            def _():
                back_out[...] = back_in[...]
                far_out[...] = far_in[...]

            pl.when(late_near != 0)(lambda: write_lags(near_out, acc, here, cols, False))

            @pl.when(late_near == 0)
            def _():
                near_out[...] = near_in[...]


def second_sums(switch, own, coeffs, partner, start, earlier=None):
    rows, cols = partner.shape
    windows = switch.shape[0] - 2
    skip = start // STEP
    total = jax.ShapeDtypeStruct((LAGS * cols, cols), jnp.float32)
    total_spec = pl.BlockSpec(total.shape, lambda s, on: (0, 0))
    result = jax.ShapeDtypeStruct((LAGS, cols, cols), jnp.bfloat16)
    result_spec = pl.BlockSpec(result.shape, lambda s, on: (0, 0, 0))
    left = pl.BlockSpec((cols, STEP), lambda s, on: (0, s * on[0] + skip))
    in_specs = [left, left, pl.BlockSpec((LAGS, STEP), lambda s, on: (0, s * on[0] + skip)),
                pl.BlockSpec((STEP, cols), lambda s, on: (s * on[0], 0))]
    scratch = [pltpu.VMEM((LAGS * cols, STEP), jnp.bfloat16)]
    if earlier is None:
        out_shape, out_specs, earlier = [total], [total_spec], []
    else:
        out_shape, out_specs = [result] * 3, [result_spec] * 3
        in_specs += [total_spec] + [result_spec] * 3
        scratch = [pltpu.VMEM(total.shape, jnp.float32)] + scratch
    return pl.pallas_call(
        functools.partial(second_kernel, windows, not earlier),
        grid_spec=pltpu.PrefetchScalarGridSpec(
            num_scalar_prefetch=1,
            grid=(rows // STEP,),
            in_specs=in_specs,
            out_specs=out_specs,
            scratch_shapes=scratch,
        ),
        out_shape=out_shape,
        compiler_params=PARAMS,
        cost_estimate=pl.CostEstimate(
            flops=2 * LAGS * cols * cols * rows, bytes_accessed=6 * rows * cols, transcendentals=0
        ),
        name="second_last" if earlier else "second_part",
    )(switch, *own, coeffs, partner, *earlier)


def local(spectra, quality):
    count = lax.axis_size("chan")
    half = count // 2
    me = lax.axis_index("chan")
    freq_count, _, window_count, cols = spectra.shape
    block = spectra.reshape(-1, cols)

    first_far, second_far = [], []
    for p in range(half):
        if p in (0, half - 1):
            first_far.append((p + half, p))
        elif p > half // 2:
            first_far.append((p, p + half))
        elif p % 2 == 1:
            second_far.append((p, p + half))
        else:
            second_far.append((p + half, p))
    late_near = [(2, 1), (4, 3)]
    first_pairs = first_far + [(0, 1), (half - 1, half - 2)]
    second_pairs = second_far + late_near
    near_pairs = [(d + 1, d) for d in range(1, count - 1) if d not in (1, 3, half - 2, half - 1)]
    near_pairs += [(0, half - 1), (half - 1, 0)]
    back_pairs = [(t, s) for s, t in first_far + second_far] + [(1, 0)]
    side_pairs = [(0, half - 1), (half - 1, count - 1)]

    def among(devices):
        return functools.reduce(jnp.logical_or, [me == d for d in devices])

    def switch(on, other, *weights):
        flags = jnp.stack([jnp.asarray(on), jnp.asarray(other)]).astype(jnp.int32)
        return jnp.concatenate([flags, *weights])

    near_in = lax.ppermute(block, "chan", near_pairs)
    first_in = lax.ppermute(block, "chan", first_pairs)
    coeffs = lag_rows(freq_count, window_count)
    own = turn(block)
    parts = split(block)
    first_flags = lax.ppermute(quality, "chan", first_pairs)[0]
    near_flags = lax.ppermute(quality, "chan", near_pairs)[0]
    second_flags = lax.ppermute(quality, "chan", second_pairs)[0]
    special = among([0, half - 1])
    second_switch = switch(
        among([t for _, t in second_pairs]), among([t for _, t in late_near]), quality[0] * second_flags
    )

    near_in, first_part, last_part, own, coeffs, first_in, near_flags, first_flags, second_flags = lax.optimization_barrier(
        (near_in, *parts, own, coeffs, first_in, near_flags, first_flags, second_flags)
    )
    second_in = [lax.ppermute(first_part, "chan", second_pairs)]
    first_switch = switch(me == 0, special, quality[0], near_flags, first_flags)
    operands = first_switch, own, coeffs, near_in, first_in
    total, token = first_sums(*operands)
    last_part, token = lax.optimization_barrier((last_part, token))
    second_in.append(lax.ppermute(last_part, "chan", second_pairs))
    near, far, back = first_sums(*operands, [total, token])
    second_switch, near = lax.optimization_barrier((second_switch, near))
    total, = second_sums(second_switch, own, coeffs, second_in[0], 0)

    near = jnp.where(me == half - 2, far, near)
    near, far, back = second_sums(
        second_switch, own, coeffs, second_in[1], parts[0].shape[0], [total, near, far, back]
    )
    returned = lax.ppermute(back, "chan", back_pairs)
    side_returned = lax.ppermute(near, "chan", side_pairs)
    near = jnp.where(among([half - 1, count - 1]), side_returned, near)
    near = jnp.where(me == 0, returned, near)
    far = jnp.where(among([s for s, _ in first_far + second_far]), returned, far)
    return near[None], far[None]


def solution(mesh):
    return jax.shard_map(
        local,
        mesh=mesh,
        in_specs=(P(None, None, None, ("grp", "chan")), P(("grp", "chan"), None)),
        out_specs=(P(("grp", "chan"), None, None, None), P(("grp", "chan"), None, None, None)),
        check_vma=False,
    )
```

```python
import functools
import math

import jax
import jax.numpy as jnp
from jax import lax
from jax.experimental import pallas as pl
from jax.experimental.pallas import tpu as pltpu
from jax.sharding import PartitionSpec as P

HL = 4
LAGS = 2 * HL + 1
STEP = 1024
PARTS = (5, 8)
PARAMS = pltpu.CompilerParams(vmem_limit_bytes=16 * 1024 * 1024)


def lag_rows(freq_count, window_count):
    per_bin = 2 * window_count
    row = jnp.arange(freq_count * per_bin, dtype=jnp.int32)
    freq_values = (row // per_bin).astype(jnp.float32)
    sign = jnp.where(row % per_bin < window_count, 1.0, -1.0)
    lag_values = jnp.arange(HL + 1, dtype=jnp.float32)
    phases = jnp.pi / freq_count * lag_values[:, None] * freq_values[None, :]
    factor = 1.0 / math.sqrt(window_count * freq_count)
    cos_part = jnp.cos(phases) * factor
    sin_part = -jnp.sin(phases[1:]) * factor * sign[None, :]
    return jnp.concatenate([cos_part, sin_part], axis=0).astype(jnp.bfloat16)


def split_kernel(middle, x_ref, first_ref, last_ref):
    step = pl.program_id(0)

    @pl.when(step < middle)
    def _():
        first_ref[...] = x_ref[...]

    @pl.when(step >= middle)
    def _():
        last_ref[...] = x_ref[...]


def split(x):
    rows, cols = x.shape
    steps = rows // STEP
    middle = steps * PARTS[0] // PARTS[1]
    return pl.pallas_call(
        functools.partial(split_kernel, middle),
        grid=(steps,),
        in_specs=[pl.BlockSpec((STEP, cols), lambda s: (s, 0))],
        out_specs=[
            pl.BlockSpec((STEP, cols), lambda s: (jnp.minimum(s, middle - 1), 0)),
            pl.BlockSpec((STEP, cols), lambda s: (jnp.maximum(s - middle, 0), 0)),
        ],
        out_shape=[jax.ShapeDtypeStruct((n * STEP, cols), x.dtype) for n in (middle, steps - middle)],
        compiler_params=PARAMS,
        cost_estimate=pl.CostEstimate(flops=0, bytes_accessed=4 * rows * cols, transcendentals=0),
        name="split",
    )(x)


def identity(size):
    same = lax.broadcasted_iota(jnp.int32, (size, size), 0) == lax.broadcasted_iota(jnp.int32, (size, size), 1)
    return jnp.where(same, 1.0, 0.0).astype(jnp.bfloat16)


def across(a, b):
    return lax.dot_general(a, b, (((1,), (1,)), ((), ())), preferred_element_type=jnp.float32)


def turned(x):
    rows, cols = x.shape
    source = lax.broadcasted_iota(jnp.int32, (2 * cols, 2 * cols), 0)
    target = lax.broadcasted_iota(jnp.int32, (2 * cols, 2 * cols), 1)
    exchange = jnp.where((source ^ 4) == target, 1.0, 0.0).astype(jnp.bfloat16)
    plain = across(identity(cols), x).astype(jnp.bfloat16)
    swapped = [
        jnp.dot(plain[:, t:t + 2 * cols], exchange, preferred_element_type=jnp.float32).astype(jnp.bfloat16)
        for t in range(0, rows, 2 * cols)
    ]
    return plain, jnp.concatenate(swapped, axis=1)


def turn_kernel(x_ref, plain_ref, swapped_ref):
    plain_ref[...], swapped_ref[...] = turned(x_ref[...])


def turn(x):
    rows, cols = x.shape
    out = jax.ShapeDtypeStruct((cols, rows), jnp.bfloat16)
    return pl.pallas_call(
        turn_kernel,
        grid=(rows // STEP,),
        in_specs=[pl.BlockSpec((STEP, cols), lambda s: (s, 0))],
        out_specs=[pl.BlockSpec((cols, STEP), lambda s: (0, s))] * 2,
        out_shape=[out, out],
        compiler_params=PARAMS,
        cost_estimate=pl.CostEstimate(flops=0, bytes_accessed=6 * rows * cols, transcendentals=0),
        name="turn",
    )(x)


def write_lags(out, acc, at, cols, mirrored):
    for lag in range(LAGS):
        k = abs(lag - HL)
        value = acc[k * cols:(k + 1) * cols, at]
        if k:
            odd = acc[(HL + k) * cols:(HL + k + 1) * cols, at]
            value = value + odd if lag > HL else value - odd
        value = value.astype(jnp.bfloat16)
        if mirrored:
            out[LAGS - 1 - lag] = value.T
        else:
            out[lag] = value


def scale(scaled, plain, swapped, coeff_ref):
    cols = plain.shape[0]
    for k in range(LAGS):
        part = plain if k <= HL else swapped
        scaled[k * cols:(k + 1) * cols, :] = part * coeff_ref[k:k + 1, :]


def weigh(x, window_weights):
    rows, cols = x.shape
    window = lax.broadcasted_iota(jnp.int32, (16, cols), 0) % len(window_weights)
    weights = jnp.zeros((16, cols), jnp.float32)
    for w, weight in enumerate(window_weights):
        weights = jnp.where(window == w, weight.astype(jnp.float32), weights)
    weights = jnp.broadcast_to(weights.astype(jnp.bfloat16)[None], (rows // 16, 16, cols))
    return x * weights.reshape(rows, cols)


def first_kernel(windows, last, switch_ref, plain_ref, swapped_ref, coeff_ref, near_ref, first_ref, *rest):
    step = pl.program_id(0)
    cols = plain_ref.shape[0]
    near_mirrored, special = switch_ref[0], switch_ref[1]
    if last:
        acc_in, _, near_out, far_out, back_out, acc, scaled, plain, swapped, right = rest
    else:
        acc, token_out, scaled, plain, swapped, right = rest

    @pl.when(step == 0)
    def _():
        if last:
            acc[...] = acc_in[...]
        else:
            acc[...] = jnp.zeros_like(acc)
            token_out[...] = jnp.zeros_like(token_out)

    @pl.when(special == 0)
    def _():
        plain[...], swapped[...] = plain_ref[...], swapped_ref[...]
        right[...] = first_ref[...]

    @pl.when(special != 0)
    def _():
        plain[...], swapped[...] = turned(first_ref[...])
        for t in range(0, STEP, cols):
            right[t:t + cols, :] = plain_ref[:, t:t + cols].T

    scale(scaled, plain[...], swapped[...], coeff_ref)
    flags = [[switch_ref[2 + part * windows + w] for w in range(windows)] for part in range(3)]
    near_weights = [jnp.where(special != 0, first, own) * near for own, near, first in zip(*flags)]
    near = weigh(near_ref[...], near_weights)
    far = weigh(right[...], [own * first for own, _, first in zip(*flags)])
    acc[...] += jnp.dot(scaled[...], jnp.concatenate([near, far], axis=1), preferred_element_type=jnp.float32)

    if last:
        @pl.when(step == pl.num_programs(0) - 1)
        def _():
            near_at, far_at = slice(0, cols), slice(cols, 2 * cols)

            @pl.when(special == 0)
            def _():
                write_lags(back_out, acc, far_at, cols, True)
                write_lags(far_out, acc, far_at, cols, False)

            @pl.when(special != 0)
            def _():
                write_lags(back_out, acc, far_at, cols, False)
                write_lags(far_out, acc, far_at, cols, True)

            pl.when(near_mirrored == 0)(lambda: write_lags(near_out, acc, near_at, cols, False))
            pl.when(near_mirrored != 0)(lambda: write_lags(near_out, acc, near_at, cols, True))


def first_sums(switch, own, coeffs, near_in, first_in, earlier=None):
    rows, cols = near_in.shape
    steps = rows // STEP // 2
    skip = 0 if earlier is None else steps
    windows = (switch.shape[0] - 2) // 3
    result = jax.ShapeDtypeStruct((LAGS, cols, cols), jnp.bfloat16)
    total = jax.ShapeDtypeStruct((LAGS * cols, 2 * cols), jnp.float32)
    total_spec = pl.BlockSpec(total.shape, lambda s, on: (0, 0))
    token = jax.ShapeDtypeStruct((8, cols), jnp.float32)
    token_spec = pl.BlockSpec(token.shape, lambda s, on: (0, 0))
    left = pl.BlockSpec((cols, STEP), lambda s, on: (0, s + skip))
    right = pl.BlockSpec((STEP, cols), lambda s, on: (s + skip, 0))
    in_specs = [left, left, pl.BlockSpec((LAGS, STEP), lambda s, on: (0, s + skip)), right, right]
    scratch = [pltpu.VMEM((LAGS * cols, STEP), jnp.bfloat16)] + [pltpu.VMEM((cols, STEP), jnp.bfloat16)] * 2
    scratch += [pltpu.VMEM((STEP, cols), jnp.bfloat16)]
    if earlier is None:
        out_shape, out_specs, earlier = [total, token], [total_spec, token_spec], []
    else:
        in_specs += [total_spec, token_spec]
        out_shape = [result] * 3
        out_specs = [pl.BlockSpec(result.shape, lambda s, on: (0, 0, 0))] * 3
        scratch = [pltpu.VMEM(total.shape, jnp.float32)] + scratch
    return pl.pallas_call(
        functools.partial(first_kernel, windows, bool(earlier)),
        grid_spec=pltpu.PrefetchScalarGridSpec(
            num_scalar_prefetch=1,
            grid=(steps,),
            in_specs=in_specs,
            out_specs=out_specs,
            scratch_shapes=scratch,
        ),
        out_shape=out_shape,
        compiler_params=PARAMS,
        cost_estimate=pl.CostEstimate(
            flops=2 * LAGS * cols * cols * rows, bytes_accessed=4 * rows * cols, transcendentals=0
        ),
        name="first_last" if earlier else "first_half",
    )(switch, *own, coeffs, near_in, first_in, *earlier)


def write_turned_lags(out, acc, cols, mirrored):
    for lag in range(LAGS):
        k = abs(lag - HL)
        value = acc[:, k * cols:(k + 1) * cols]
        if k:
            odd = acc[:, (HL + k) * cols:(HL + k + 1) * cols]
            value = value + odd if lag > HL else value - odd
        value = value.astype(jnp.bfloat16)
        if mirrored:
            out[LAGS - 1 - lag] = value
        else:
            out[lag] = value.T


def second_kernel(windows, first, switch_ref, plain_ref, swapped_ref, coeff_ref, partner_ref, *rest):
    on, late_near = switch_ref[0], switch_ref[1]
    step = pl.program_id(0)
    cols = plain_ref.shape[0]
    if first:
        acc, scaled = rest
    else:
        acc_in, near_in, far_in, back_in, near_out, far_out, back_out, acc, scaled = rest

    @pl.when(on != 0)
    def _():
        @pl.when(step == 0)
        def _():
            acc[...] = jnp.zeros_like(acc) if first else acc_in[...]

        scale(scaled, plain_ref[...], swapped_ref[...], coeff_ref)
        partner = weigh(partner_ref[...], [switch_ref[2 + w] for w in range(windows)])
        columns = across(identity(cols), partner).astype(jnp.bfloat16)
        acc[...] += across(columns, scaled[...])

    if not first:
        @pl.when(step == pl.num_programs(0) - 1)
        def _():
            @pl.when((on != 0) & (late_near == 0))
            def _():
                write_turned_lags(back_out, acc, cols, True)
                write_turned_lags(far_out, acc, cols, False)

            @pl.when((on == 0) | (late_near != 0))
            def _():
                back_out[...] = back_in[...]
                far_out[...] = far_in[...]

            pl.when(late_near != 0)(lambda: write_turned_lags(near_out, acc, cols, False))

            @pl.when(late_near == 0)
            def _():
                near_out[...] = near_in[...]


def second_sums(switch, own, coeffs, partner, start, earlier=None):
    rows, cols = partner.shape
    windows = switch.shape[0] - 2
    skip = start // STEP
    total = jax.ShapeDtypeStruct((cols, LAGS * cols), jnp.float32)
    total_spec = pl.BlockSpec(total.shape, lambda s, on: (0, 0))
    result = jax.ShapeDtypeStruct((LAGS, cols, cols), jnp.bfloat16)
    result_spec = pl.BlockSpec(result.shape, lambda s, on: (0, 0, 0))
    left = pl.BlockSpec((cols, STEP), lambda s, on: (0, s * on[0] + skip))
    in_specs = [left, left, pl.BlockSpec((LAGS, STEP), lambda s, on: (0, s * on[0] + skip)),
                pl.BlockSpec((STEP, cols), lambda s, on: (s * on[0], 0))]
    scratch = [pltpu.VMEM((LAGS * cols, STEP), jnp.bfloat16)]
    if earlier is None:
        out_shape, out_specs, earlier = [total], [total_spec], []
    else:
        out_shape, out_specs = [result] * 3, [result_spec] * 3
        in_specs += [total_spec] + [result_spec] * 3
        scratch = [pltpu.VMEM(total.shape, jnp.float32)] + scratch
    return pl.pallas_call(
        functools.partial(second_kernel, windows, not earlier),
        grid_spec=pltpu.PrefetchScalarGridSpec(
            num_scalar_prefetch=1,
            grid=(rows // STEP,),
            in_specs=in_specs,
            out_specs=out_specs,
            scratch_shapes=scratch,
        ),
        out_shape=out_shape,
        compiler_params=PARAMS,
        cost_estimate=pl.CostEstimate(
            flops=2 * LAGS * cols * cols * rows, bytes_accessed=6 * rows * cols, transcendentals=0
        ),
        name="second_last" if earlier else "second_part",
    )(switch, *own, coeffs, partner, *earlier)


def local(spectra, quality):
    count = lax.axis_size("chan")
    half = count // 2
    me = lax.axis_index("chan")
    freq_count, _, window_count, cols = spectra.shape
    block = spectra.reshape(-1, cols)

    first_far, second_far = [], []
    for p in range(half):
        if p in (0, half - 1):
            first_far.append((p + half, p))
        elif p > half // 2:
            first_far.append((p, p + half))
        elif p % 2 == 1:
            second_far.append((p, p + half))
        else:
            second_far.append((p + half, p))
    late_near = [(2, 1), (4, 3)]
    first_pairs = first_far + [(0, 1), (half - 1, half - 2)]
    second_pairs = second_far + late_near
    near_pairs = [(d + 1, d) for d in range(1, count - 1) if d not in (1, 3, half - 2, half - 1)]
    near_pairs += [(0, half - 1), (half - 1, 0)]
    back_pairs = [(t, s) for s, t in first_far + second_far] + [(1, 0)]
    side_pairs = [(0, half - 1), (half - 1, count - 1)]

    def among(devices):
        return functools.reduce(jnp.logical_or, [me == d for d in devices])

    def switch(on, other, *weights):
        flags = jnp.stack([jnp.asarray(on), jnp.asarray(other)]).astype(jnp.int32)
        return jnp.concatenate([flags, *weights])

    near_in = lax.ppermute(block, "chan", near_pairs)
    first_in = lax.ppermute(block, "chan", first_pairs)
    coeffs = lag_rows(freq_count, window_count)
    own = turn(block)
    parts = split(block)
    first_flags = lax.ppermute(quality, "chan", first_pairs)[0]
    near_flags = lax.ppermute(quality, "chan", near_pairs)[0]
    second_flags = lax.ppermute(quality, "chan", second_pairs)[0]
    special = among([0, half - 1])
    second_switch = switch(
        among([t for _, t in second_pairs]), among([t for _, t in late_near]), quality[0] * second_flags
    )

    near_in, first_part, last_part, own, coeffs, first_in, near_flags, first_flags, second_flags = lax.optimization_barrier(
        (near_in, *parts, own, coeffs, first_in, near_flags, first_flags, second_flags)
    )
    second_in = [lax.ppermute(first_part, "chan", second_pairs)]
    first_switch = switch(me == 0, special, quality[0], near_flags, first_flags)
    operands = first_switch, own, coeffs, near_in, first_in
    total, token = first_sums(*operands)
    last_part, token = lax.optimization_barrier((last_part, token))
    second_in.append(lax.ppermute(last_part, "chan", second_pairs))
    near, far, back = first_sums(*operands, [total, token])
    second_switch, near = lax.optimization_barrier((second_switch, near))
    total, = second_sums(second_switch, own, coeffs, second_in[0], 0)

    near = jnp.where(me == half - 2, far, near)
    near, far, back = second_sums(
        second_switch, own, coeffs, second_in[1], parts[0].shape[0], [total, near, far, back]
    )
    returned = lax.ppermute(back, "chan", back_pairs)
    side_returned = lax.ppermute(near, "chan", side_pairs)
    near = jnp.where(among([half - 1, count - 1]), side_returned, near)
    near = jnp.where(me == 0, returned, near)
    far = jnp.where(among([s for s, _ in first_far + second_far]), returned, far)
    return near[None], far[None]


def solution(mesh):
    return jax.shard_map(
        local,
        mesh=mesh,
        in_specs=(P(None, None, None, ("grp", "chan")), P(("grp", "chan"), None)),
        out_specs=(P(("grp", "chan"), None, None, None), P(("grp", "chan"), None, None, None)),
        check_vma=False,
    )
```

```python
import functools
import math

import jax
import jax.numpy as jnp
from jax import lax
from jax.experimental import pallas as pl
from jax.experimental.pallas import tpu as pltpu
from jax.sharding import PartitionSpec as P

HL = 4
LAGS = 2 * HL + 1
STEP = 1024
PARTS = (5, 8)
PARAMS = pltpu.CompilerParams(vmem_limit_bytes=16 * 1024 * 1024)


def lag_rows(freq_count, window_count):
    per_bin = 2 * window_count
    row = jnp.arange(freq_count * per_bin, dtype=jnp.int32)
    freq_values = (row // per_bin).astype(jnp.float32)
    sign = jnp.where(row % per_bin < window_count, 1.0, -1.0)
    lag_values = jnp.arange(HL + 1, dtype=jnp.float32)
    phases = jnp.pi / freq_count * lag_values[:, None] * freq_values[None, :]
    factor = 1.0 / math.sqrt(window_count * freq_count)
    cos_part = jnp.cos(phases) * factor
    sin_part = -jnp.sin(phases[1:]) * factor * sign[None, :]
    return jnp.concatenate([cos_part, sin_part], axis=0).astype(jnp.bfloat16)


def split_kernel(middle, x_ref, first_ref, last_ref):
    step = pl.program_id(0)

    @pl.when(step < middle)
    def _():
        first_ref[...] = x_ref[...]

    @pl.when(step >= middle)
    def _():
        last_ref[...] = x_ref[...]


def split(x):
    rows, cols = x.shape
    steps = rows // STEP
    middle = steps * PARTS[0] // PARTS[1]
    return pl.pallas_call(
        functools.partial(split_kernel, middle),
        grid=(steps,),
        in_specs=[pl.BlockSpec((STEP, cols), lambda s: (s, 0))],
        out_specs=[
            pl.BlockSpec((STEP, cols), lambda s: (jnp.minimum(s, middle - 1), 0)),
            pl.BlockSpec((STEP, cols), lambda s: (jnp.maximum(s - middle, 0), 0)),
        ],
        out_shape=[jax.ShapeDtypeStruct((n * STEP, cols), x.dtype) for n in (middle, steps - middle)],
        compiler_params=PARAMS,
        cost_estimate=pl.CostEstimate(flops=0, bytes_accessed=4 * rows * cols, transcendentals=0),
        name="split",
    )(x)


def turned(x):
    rows, cols = x.shape
    same = lax.broadcasted_iota(jnp.int32, (cols, cols), 0) == lax.broadcasted_iota(jnp.int32, (cols, cols), 1)
    eye = jnp.where(same, 1.0, 0.0).astype(jnp.bfloat16)
    source = lax.broadcasted_iota(jnp.int32, (2 * cols, 2 * cols), 0)
    target = lax.broadcasted_iota(jnp.int32, (2 * cols, 2 * cols), 1)
    exchange = jnp.where((source ^ 4) == target, 1.0, 0.0).astype(jnp.bfloat16)
    plain = lax.dot_general(eye, x, (((1,), (1,)), ((), ())), preferred_element_type=jnp.float32)
    plain = plain.astype(jnp.bfloat16)
    swapped = [
        jnp.dot(plain[:, t:t + 2 * cols], exchange, preferred_element_type=jnp.float32).astype(jnp.bfloat16)
        for t in range(0, rows, 2 * cols)
    ]
    return plain, jnp.concatenate(swapped, axis=1)


def turn_kernel(x_ref, plain_ref, swapped_ref):
    plain_ref[...], swapped_ref[...] = turned(x_ref[...])


def turn(x):
    rows, cols = x.shape
    out = jax.ShapeDtypeStruct((cols, rows), jnp.bfloat16)
    return pl.pallas_call(
        turn_kernel,
        grid=(rows // STEP,),
        in_specs=[pl.BlockSpec((STEP, cols), lambda s: (s, 0))],
        out_specs=[pl.BlockSpec((cols, STEP), lambda s: (0, s))] * 2,
        out_shape=[out, out],
        compiler_params=PARAMS,
        cost_estimate=pl.CostEstimate(flops=0, bytes_accessed=6 * rows * cols, transcendentals=0),
        name="turn",
    )(x)


def write_lags(out, acc, at, cols, mirrored):
    for lag in range(LAGS):
        k = abs(lag - HL)
        value = acc[k * cols:(k + 1) * cols, at]
        if k:
            odd = acc[(HL + k) * cols:(HL + k + 1) * cols, at]
            value = value + odd if lag > HL else value - odd
        value = value.astype(jnp.bfloat16)
        if mirrored:
            out[LAGS - 1 - lag] = value.T
        else:
            out[lag] = value


def scale(scaled, plain, swapped, coeff_ref):
    cols = plain.shape[0]
    for k in range(LAGS):
        part = plain if k <= HL else swapped
        scaled[k * cols:(k + 1) * cols, :] = part * coeff_ref[k:k + 1, :]


def weigh(x, window_weights):
    rows, cols = x.shape
    window = lax.broadcasted_iota(jnp.int32, (16, cols), 0) % len(window_weights)
    weights = jnp.zeros((16, cols), jnp.float32)
    for w, weight in enumerate(window_weights):
        weights = jnp.where(window == w, weight.astype(jnp.float32), weights)
    weights = jnp.broadcast_to(weights.astype(jnp.bfloat16)[None], (rows // 16, 16, cols))
    return x * weights.reshape(rows, cols)


def first_kernel(windows, last, switch_ref, plain_ref, swapped_ref, coeff_ref, near_ref, first_ref, *rest):
    step = pl.program_id(0)
    cols = plain_ref.shape[0]
    near_mirrored, special = switch_ref[0], switch_ref[1]
    if last:
        acc_in, _, near_out, far_out, back_out, acc, scaled, plain, swapped, right = rest
    else:
        acc, token_out, scaled, plain, swapped, right = rest

    @pl.when(step == 0)
    def _():
        if last:
            acc[...] = acc_in[...]
        else:
            acc[...] = jnp.zeros_like(acc)
            token_out[...] = jnp.zeros_like(token_out)

    @pl.when(special == 0)
    def _():
        plain[...], swapped[...] = plain_ref[...], swapped_ref[...]
        right[...] = first_ref[...]

    @pl.when(special != 0)
    def _():
        plain[...], swapped[...] = turned(first_ref[...])
        for t in range(0, STEP, cols):
            right[t:t + cols, :] = plain_ref[:, t:t + cols].T

    scale(scaled, plain[...], swapped[...], coeff_ref)
    flags = [[switch_ref[2 + part * windows + w] for w in range(windows)] for part in range(3)]
    near_weights = [jnp.where(special != 0, first, own) * near for own, near, first in zip(*flags)]
    near = weigh(near_ref[...], near_weights)
    far = weigh(right[...], [own * first for own, _, first in zip(*flags)])
    acc[...] += jnp.dot(scaled[...], jnp.concatenate([near, far], axis=1), preferred_element_type=jnp.float32)

    if last:
        @pl.when(step == pl.num_programs(0) - 1)
        def _():
            near_at, far_at = slice(0, cols), slice(cols, 2 * cols)

            @pl.when(special == 0)
            def _():
                write_lags(back_out, acc, far_at, cols, True)
                write_lags(far_out, acc, far_at, cols, False)

            @pl.when(special != 0)
            def _():
                write_lags(back_out, acc, far_at, cols, False)
                write_lags(far_out, acc, far_at, cols, True)

            pl.when(near_mirrored == 0)(lambda: write_lags(near_out, acc, near_at, cols, False))
            pl.when(near_mirrored != 0)(lambda: write_lags(near_out, acc, near_at, cols, True))


def first_sums(switch, own, coeffs, near_in, first_in, earlier=None):
    rows, cols = near_in.shape
    steps = rows // STEP // 2
    skip = 0 if earlier is None else steps
    windows = (switch.shape[0] - 2) // 3
    result = jax.ShapeDtypeStruct((LAGS, cols, cols), jnp.bfloat16)
    total = jax.ShapeDtypeStruct((LAGS * cols, 2 * cols), jnp.float32)
    total_spec = pl.BlockSpec(total.shape, lambda s, on: (0, 0))
    token = jax.ShapeDtypeStruct((8, cols), jnp.float32)
    token_spec = pl.BlockSpec(token.shape, lambda s, on: (0, 0))
    left = pl.BlockSpec((cols, STEP), lambda s, on: (0, s + skip))
    right = pl.BlockSpec((STEP, cols), lambda s, on: (s + skip, 0))
    in_specs = [left, left, pl.BlockSpec((LAGS, STEP), lambda s, on: (0, s + skip)), right, right]
    scratch = [pltpu.VMEM((LAGS * cols, STEP), jnp.bfloat16)] + [pltpu.VMEM((cols, STEP), jnp.bfloat16)] * 2
    scratch += [pltpu.VMEM((STEP, cols), jnp.bfloat16)]
    if earlier is None:
        out_shape, out_specs, earlier = [total, token], [total_spec, token_spec], []
    else:
        in_specs += [total_spec, token_spec]
        out_shape = [result] * 3
        out_specs = [pl.BlockSpec(result.shape, lambda s, on: (0, 0, 0))] * 3
        scratch = [pltpu.VMEM(total.shape, jnp.float32)] + scratch
    return pl.pallas_call(
        functools.partial(first_kernel, windows, bool(earlier)),
        grid_spec=pltpu.PrefetchScalarGridSpec(
            num_scalar_prefetch=1,
            grid=(steps,),
            in_specs=in_specs,
            out_specs=out_specs,
            scratch_shapes=scratch,
        ),
        out_shape=out_shape,
        compiler_params=PARAMS,
        cost_estimate=pl.CostEstimate(
            flops=2 * LAGS * cols * cols * rows, bytes_accessed=4 * rows * cols, transcendentals=0
        ),
        name="first_last" if earlier else "first_half",
    )(switch, *own, coeffs, near_in, first_in, *earlier)


def second_kernel(windows, first, switch_ref, plain_ref, swapped_ref, coeff_ref, partner_ref, *rest):
    on, late_near = switch_ref[0], switch_ref[1]
    step = pl.program_id(0)
    cols = plain_ref.shape[0]
    if first:
        acc, scaled = rest
    else:
        acc_in, near_in, far_in, back_in, near_out, far_out, back_out, acc, scaled = rest

    @pl.when(on != 0)
    def _():
        @pl.when(step == 0)
        def _():
            acc[...] = jnp.zeros_like(acc) if first else acc_in[...]

        scale(scaled, plain_ref[...], swapped_ref[...], coeff_ref)
        partner = weigh(partner_ref[...], [switch_ref[2 + w] for w in range(windows)])
        acc[...] += jnp.dot(scaled[...], partner, preferred_element_type=jnp.float32)

    if not first:
        @pl.when(step == pl.num_programs(0) - 1)
        def _():
            here = slice(0, cols)

            @pl.when((on != 0) & (late_near == 0))
            def _():
                write_lags(back_out, acc, here, cols, True)
                write_lags(far_out, acc, here, cols, False)

            @pl.when((on == 0) | (late_near != 0))
            def _():
                back_out[...] = back_in[...]
                far_out[...] = far_in[...]

            pl.when(late_near != 0)(lambda: write_lags(near_out, acc, here, cols, False))

            @pl.when(late_near == 0)
            def _():
                near_out[...] = near_in[...]


def second_sums(switch, own, coeffs, partner, start, earlier=None):
    rows, cols = partner.shape
    windows = switch.shape[0] - 2
    skip = start // STEP
    total = jax.ShapeDtypeStruct((LAGS * cols, cols), jnp.float32)
    total_spec = pl.BlockSpec(total.shape, lambda s, on: (0, 0))
    result = jax.ShapeDtypeStruct((LAGS, cols, cols), jnp.bfloat16)
    result_spec = pl.BlockSpec(result.shape, lambda s, on: (0, 0, 0))
    left = pl.BlockSpec((cols, STEP), lambda s, on: (0, s * on[0] + skip))
    in_specs = [left, left, pl.BlockSpec((LAGS, STEP), lambda s, on: (0, s * on[0] + skip)),
                pl.BlockSpec((STEP, cols), lambda s, on: (s * on[0], 0))]
    scratch = [pltpu.VMEM((LAGS * cols, STEP), jnp.bfloat16)]
    if earlier is None:
        out_shape, out_specs, earlier = [total], [total_spec], []
    else:
        out_shape, out_specs = [result] * 3, [result_spec] * 3
        in_specs += [total_spec] + [result_spec] * 3
        scratch = [pltpu.VMEM(total.shape, jnp.float32)] + scratch
    return pl.pallas_call(
        functools.partial(second_kernel, windows, not earlier),
        grid_spec=pltpu.PrefetchScalarGridSpec(
            num_scalar_prefetch=1,
            grid=(rows // STEP,),
            in_specs=in_specs,
            out_specs=out_specs,
            scratch_shapes=scratch,
        ),
        out_shape=out_shape,
        compiler_params=PARAMS,
        cost_estimate=pl.CostEstimate(
            flops=2 * LAGS * cols * cols * rows, bytes_accessed=6 * rows * cols, transcendentals=0
        ),
        name="second_last" if earlier else "second_part",
    )(switch, *own, coeffs, partner, *earlier)


def local(spectra, quality):
    count = lax.axis_size("chan")
    half = count // 2
    me = lax.axis_index("chan")
    freq_count, _, window_count, cols = spectra.shape
    block = spectra.reshape(-1, cols)

    first_far, second_far = [], []
    for p in range(half):
        if p in (0, half - 1):
            first_far.append((p + half, p))
        elif p > half // 2:
            first_far.append((p, p + half))
        elif p % 2 == 1:
            second_far.append((p, p + half))
        else:
            second_far.append((p + half, p))
    late_near = [(2, 1), (4, 3)]
    first_pairs = first_far + [(0, 1), (half - 1, half - 2)]
    second_pairs = second_far + late_near
    near_pairs = [(d + 1, d) for d in range(1, count - 1) if d not in (1, 3, half - 2, half - 1)]
    near_pairs += [(0, half - 1), (half - 1, 0)]
    back_pairs = [(t, s) for s, t in first_far + second_far] + [(1, 0)]
    side_pairs = [(0, half - 1), (half - 1, count - 1)]

    def among(devices):
        return functools.reduce(jnp.logical_or, [me == d for d in devices])

    def switch(on, other, *weights):
        flags = jnp.stack([jnp.asarray(on), jnp.asarray(other)]).astype(jnp.int32)
        return jnp.concatenate([flags, *weights])

    near_in = lax.ppermute(block, "chan", near_pairs)
    first_in = lax.ppermute(block, "chan", first_pairs)
    coeffs = lag_rows(freq_count, window_count)
    own = turn(block)
    parts = split(block)
    first_flags = lax.ppermute(quality, "chan", first_pairs)[0]
    near_flags = lax.ppermute(quality, "chan", near_pairs)[0]
    second_flags = lax.ppermute(quality, "chan", second_pairs)[0]
    special = among([0, half - 1])
    second_switch = switch(
        among([t for _, t in second_pairs]), among([t for _, t in late_near]), quality[0] * second_flags
    )

    near_in, first_part, last_part, own, coeffs, first_in, near_flags, first_flags, second_flags = lax.optimization_barrier(
        (near_in, *parts, own, coeffs, first_in, near_flags, first_flags, second_flags)
    )
    first_switch = switch(me == 0, special, quality[0], near_flags, first_flags)
    second_in = [lax.ppermute(part, "chan", second_pairs) for part in (first_part, last_part)]
    operands = first_switch, own, coeffs, near_in, first_in
    total, token = first_sums(*operands)
    near, far, back = first_sums(*operands, [total, token])
    second_switch, near = lax.optimization_barrier((second_switch, near))
    total, = second_sums(second_switch, own, coeffs, second_in[0], 0)

    near = jnp.where(me == half - 2, far, near)
    near, far, back = second_sums(
        second_switch, own, coeffs, second_in[1], parts[0].shape[0], [total, near, far, back]
    )
    returned = lax.ppermute(back, "chan", back_pairs)
    side_returned = lax.ppermute(near, "chan", side_pairs)
    near = jnp.where(among([half - 1, count - 1]), side_returned, near)
    near = jnp.where(me == 0, returned, near)
    far = jnp.where(among([s for s, _ in first_far + second_far]), returned, far)
    return near[None], far[None]


def solution(mesh):
    return jax.shard_map(
        local,
        mesh=mesh,
        in_specs=(P(None, None, None, ("grp", "chan")), P(("grp", "chan"), None)),
        out_specs=(P(("grp", "chan"), None, None, None), P(("grp", "chan"), None, None, None)),
        check_vma=False,
    )
```

```python
import functools
import math

import jax
import jax.numpy as jnp
from jax import lax
from jax.experimental import pallas as pl
from jax.experimental.pallas import tpu as pltpu
from jax.sharding import PartitionSpec as P

HL = 4
LAGS = 2 * HL + 1
STEP = 1024
ENDS = (4, 6, 8)
PARAMS = pltpu.CompilerParams(vmem_limit_bytes=16 * 1024 * 1024)


def lag_rows(freq_count, window_count):
    per_bin = 2 * window_count
    row = jnp.arange(freq_count * per_bin, dtype=jnp.int32)
    freq_values = (row // per_bin).astype(jnp.float32)
    sign = jnp.where(row % per_bin < window_count, 1.0, -1.0)
    lag_values = jnp.arange(HL + 1, dtype=jnp.float32)
    phases = jnp.pi / freq_count * lag_values[:, None] * freq_values[None, :]
    factor = 1.0 / math.sqrt(window_count * freq_count)
    cos_part = jnp.cos(phases) * factor
    sin_part = -jnp.sin(phases[1:]) * factor * sign[None, :]
    return jnp.concatenate([cos_part, sin_part], axis=0).astype(jnp.bfloat16)


def split_kernel(ends, x_ref, *part_refs):
    step = pl.program_id(0)
    for begin, end, part_ref in zip((0, *ends), ends, part_refs):
        @pl.when((step >= begin) & (step < end))
        def _():
            part_ref[...] = x_ref[...]


def split(x):
    rows, cols = x.shape
    steps = rows // STEP
    ends = [steps * e // ENDS[-1] for e in ENDS]
    sizes = [e - b for b, e in zip([0] + ends, ends)]

    def place(end, size):
        return lambda s: (jnp.clip(s - end + size, 0, size - 1), 0)

    return pl.pallas_call(
        functools.partial(split_kernel, ends),
        grid=(steps,),
        in_specs=[pl.BlockSpec((STEP, cols), lambda s: (s, 0))],
        out_specs=[pl.BlockSpec((STEP, cols), place(e, n)) for e, n in zip(ends, sizes)],
        out_shape=[jax.ShapeDtypeStruct((n * STEP, cols), x.dtype) for n in sizes],
        compiler_params=PARAMS,
        cost_estimate=pl.CostEstimate(flops=0, bytes_accessed=4 * rows * cols, transcendentals=0),
        name="split",
    )(x)


def turned(x):
    rows, cols = x.shape
    same = lax.broadcasted_iota(jnp.int32, (cols, cols), 0) == lax.broadcasted_iota(jnp.int32, (cols, cols), 1)
    eye = jnp.where(same, 1.0, 0.0).astype(jnp.bfloat16)
    source = lax.broadcasted_iota(jnp.int32, (2 * cols, 2 * cols), 0)
    target = lax.broadcasted_iota(jnp.int32, (2 * cols, 2 * cols), 1)
    exchange = jnp.where((source ^ 4) == target, 1.0, 0.0).astype(jnp.bfloat16)
    plain = lax.dot_general(eye, x, (((1,), (1,)), ((), ())), preferred_element_type=jnp.float32)
    plain = plain.astype(jnp.bfloat16)
    swapped = [
        jnp.dot(plain[:, t:t + 2 * cols], exchange, preferred_element_type=jnp.float32).astype(jnp.bfloat16)
        for t in range(0, rows, 2 * cols)
    ]
    return plain, jnp.concatenate(swapped, axis=1)


def turn_kernel(x_ref, plain_ref, swapped_ref):
    plain_ref[...], swapped_ref[...] = turned(x_ref[...])


def turn(x):
    rows, cols = x.shape
    out = jax.ShapeDtypeStruct((cols, rows), jnp.bfloat16)
    return pl.pallas_call(
        turn_kernel,
        grid=(rows // STEP,),
        in_specs=[pl.BlockSpec((STEP, cols), lambda s: (s, 0))],
        out_specs=[pl.BlockSpec((cols, STEP), lambda s: (0, s))] * 2,
        out_shape=[out, out],
        compiler_params=PARAMS,
        cost_estimate=pl.CostEstimate(flops=0, bytes_accessed=6 * rows * cols, transcendentals=0),
        name="turn",
    )(x)


def write_lags(out, acc, at, cols, mirrored):
    for lag in range(LAGS):
        k = abs(lag - HL)
        value = acc[k * cols:(k + 1) * cols, at]
        if k:
            odd = acc[(HL + k) * cols:(HL + k + 1) * cols, at]
            value = value + odd if lag > HL else value - odd
        value = value.astype(jnp.bfloat16)
        if mirrored:
            out[LAGS - 1 - lag] = value.T
        else:
            out[lag] = value


def scale(scaled, plain, swapped, coeff_ref):
    cols = plain.shape[0]
    for k in range(LAGS):
        part = plain if k <= HL else swapped
        scaled[k * cols:(k + 1) * cols, :] = part * coeff_ref[k:k + 1, :]


def weigh(x, window_weights):
    rows, cols = x.shape
    window = lax.broadcasted_iota(jnp.int32, (16, cols), 0) % len(window_weights)
    weights = jnp.zeros((16, cols), jnp.float32)
    for w, weight in enumerate(window_weights):
        weights = jnp.where(window == w, weight.astype(jnp.float32), weights)
    weights = jnp.broadcast_to(weights.astype(jnp.bfloat16)[None], (rows // 16, 16, cols))
    return x * weights.reshape(rows, cols)


def first_kernel(windows, last, switch_ref, plain_ref, swapped_ref, coeff_ref, near_ref, first_ref, *rest):
    step = pl.program_id(0)
    cols = plain_ref.shape[0]
    near_mirrored, special = switch_ref[0], switch_ref[1]
    if last:
        acc_in, _, near_out, far_out, back_out, acc, scaled, plain, swapped, right = rest
    else:
        acc, token_out, scaled, plain, swapped, right = rest

    @pl.when(step == 0)
    def _():
        if last:
            acc[...] = acc_in[...]
        else:
            acc[...] = jnp.zeros_like(acc)
            token_out[...] = jnp.zeros_like(token_out)

    @pl.when(special == 0)
    def _():
        plain[...], swapped[...] = plain_ref[...], swapped_ref[...]
        right[...] = first_ref[...]

    @pl.when(special != 0)
    def _():
        plain[...], swapped[...] = turned(first_ref[...])
        for t in range(0, STEP, cols):
            right[t:t + cols, :] = plain_ref[:, t:t + cols].T

    scale(scaled, plain[...], swapped[...], coeff_ref)
    flags = [[switch_ref[2 + part * windows + w] for w in range(windows)] for part in range(3)]
    near_weights = [jnp.where(special != 0, first, own) * near for own, near, first in zip(*flags)]
    near = weigh(near_ref[...], near_weights)
    far = weigh(right[...], [own * first for own, _, first in zip(*flags)])
    acc[...] += jnp.dot(scaled[...], jnp.concatenate([near, far], axis=1), preferred_element_type=jnp.float32)

    if last:
        @pl.when(step == pl.num_programs(0) - 1)
        def _():
            near_at, far_at = slice(0, cols), slice(cols, 2 * cols)

            @pl.when(special == 0)
            def _():
                write_lags(back_out, acc, far_at, cols, True)
                write_lags(far_out, acc, far_at, cols, False)

            @pl.when(special != 0)
            def _():
                write_lags(back_out, acc, far_at, cols, False)
                write_lags(far_out, acc, far_at, cols, True)

            pl.when(near_mirrored == 0)(lambda: write_lags(near_out, acc, near_at, cols, False))
            pl.when(near_mirrored != 0)(lambda: write_lags(near_out, acc, near_at, cols, True))


def first_sums(switch, own, coeffs, near_in, first_in, earlier=None):
    rows, cols = near_in.shape
    steps = rows // STEP // 2
    skip = 0 if earlier is None else steps
    windows = (switch.shape[0] - 2) // 3
    result = jax.ShapeDtypeStruct((LAGS, cols, cols), jnp.bfloat16)
    total = jax.ShapeDtypeStruct((LAGS * cols, 2 * cols), jnp.float32)
    total_spec = pl.BlockSpec(total.shape, lambda s, on: (0, 0))
    token = jax.ShapeDtypeStruct((8, cols), jnp.float32)
    token_spec = pl.BlockSpec(token.shape, lambda s, on: (0, 0))
    left = pl.BlockSpec((cols, STEP), lambda s, on: (0, s + skip))
    right = pl.BlockSpec((STEP, cols), lambda s, on: (s + skip, 0))
    in_specs = [left, left, pl.BlockSpec((LAGS, STEP), lambda s, on: (0, s + skip)), right, right]
    scratch = [pltpu.VMEM((LAGS * cols, STEP), jnp.bfloat16)] + [pltpu.VMEM((cols, STEP), jnp.bfloat16)] * 2
    scratch += [pltpu.VMEM((STEP, cols), jnp.bfloat16)]
    if earlier is None:
        out_shape, out_specs, earlier = [total, token], [total_spec, token_spec], []
    else:
        in_specs += [total_spec, token_spec]
        out_shape = [result] * 3
        out_specs = [pl.BlockSpec(result.shape, lambda s, on: (0, 0, 0))] * 3
        scratch = [pltpu.VMEM(total.shape, jnp.float32)] + scratch
    return pl.pallas_call(
        functools.partial(first_kernel, windows, bool(earlier)),
        grid_spec=pltpu.PrefetchScalarGridSpec(
            num_scalar_prefetch=1,
            grid=(steps,),
            in_specs=in_specs,
            out_specs=out_specs,
            scratch_shapes=scratch,
        ),
        out_shape=out_shape,
        compiler_params=PARAMS,
        cost_estimate=pl.CostEstimate(
            flops=2 * LAGS * cols * cols * rows, bytes_accessed=4 * rows * cols, transcendentals=0
        ),
        name="first_last" if earlier else "first_half",
    )(switch, *own, coeffs, near_in, first_in, *earlier)


def second_kernel(windows, first, last, switch_ref, plain_ref, swapped_ref, coeff_ref, partner_ref, *rest):
    on, late_near = switch_ref[0], switch_ref[1]
    step = pl.program_id(0)
    cols = plain_ref.shape[0]
    if first:
        acc, scaled = rest
    elif not last:
        acc_in, acc, scaled = rest
    else:
        acc_in, near_in, far_in, back_in, near_out, far_out, back_out, acc, scaled = rest

    @pl.when(on != 0)
    def _():
        @pl.when(step == 0)
        def _():
            acc[...] = jnp.zeros_like(acc) if first else acc_in[...]

        scale(scaled, plain_ref[...], swapped_ref[...], coeff_ref)
        partner = weigh(partner_ref[...], [switch_ref[2 + w] for w in range(windows)])
        acc[...] += jnp.dot(scaled[...], partner, preferred_element_type=jnp.float32)

    if last:
        @pl.when(step == pl.num_programs(0) - 1)
        def _():
            here = slice(0, cols)

            @pl.when((on != 0) & (late_near == 0))
            def _():
                write_lags(back_out, acc, here, cols, True)
                write_lags(far_out, acc, here, cols, False)

            @pl.when((on == 0) | (late_near != 0))
            def _():
                back_out[...] = back_in[...]
                far_out[...] = far_in[...]

            pl.when(late_near != 0)(lambda: write_lags(near_out, acc, here, cols, False))

            @pl.when(late_near == 0)
            def _():
                near_out[...] = near_in[...]


def second_sums(switch, own, coeffs, partner, start, earlier=()):
    rows, cols = partner.shape
    windows = switch.shape[0] - 2
    skip = start // STEP
    total = jax.ShapeDtypeStruct((LAGS * cols, cols), jnp.float32)
    total_spec = pl.BlockSpec(total.shape, lambda s, on: (0, 0))
    result = jax.ShapeDtypeStruct((LAGS, cols, cols), jnp.bfloat16)
    result_spec = pl.BlockSpec(result.shape, lambda s, on: (0, 0, 0))
    left = pl.BlockSpec((cols, STEP), lambda s, on: (0, s * on[0] + skip))
    in_specs = [left, left, pl.BlockSpec((LAGS, STEP), lambda s, on: (0, s * on[0] + skip)),
                pl.BlockSpec((STEP, cols), lambda s, on: (s * on[0], 0))]
    scratch = [pltpu.VMEM((LAGS * cols, STEP), jnp.bfloat16)]
    last = len(earlier) > 1
    in_specs += [total_spec, result_spec, result_spec, result_spec][:len(earlier)]
    if not last:
        out_shape, out_specs = [total], [total_spec]
    else:
        out_shape, out_specs = [result] * 3, [result_spec] * 3
        scratch = [pltpu.VMEM(total.shape, jnp.float32)] + scratch
    return pl.pallas_call(
        functools.partial(second_kernel, windows, not earlier, last),
        grid_spec=pltpu.PrefetchScalarGridSpec(
            num_scalar_prefetch=1,
            grid=(rows // STEP,),
            in_specs=in_specs,
            out_specs=out_specs,
            scratch_shapes=scratch,
        ),
        out_shape=out_shape,
        compiler_params=PARAMS,
        cost_estimate=pl.CostEstimate(
            flops=2 * LAGS * cols * cols * rows, bytes_accessed=6 * rows * cols, transcendentals=0
        ),
        name="second_last" if last else "second_part",
    )(switch, *own, coeffs, partner, *earlier)


def local(spectra, quality):
    count = lax.axis_size("chan")
    half = count // 2
    me = lax.axis_index("chan")
    freq_count, _, window_count, cols = spectra.shape
    block = spectra.reshape(-1, cols)

    first_far, second_far = [], []
    for p in range(half):
        if p in (0, half - 1):
            first_far.append((p + half, p))
        elif p > half // 2:
            first_far.append((p, p + half))
        elif p % 2 == 1:
            second_far.append((p, p + half))
        else:
            second_far.append((p + half, p))
    late_near = [(2, 1), (4, 3)]
    first_pairs = first_far + [(0, 1), (half - 1, half - 2)]
    second_pairs = second_far + late_near
    near_pairs = [(d + 1, d) for d in range(1, count - 1) if d not in (1, 3, half - 2, half - 1)]
    near_pairs += [(0, half - 1), (half - 1, 0)]
    back_pairs = [(t, s) for s, t in first_far + second_far] + [(1, 0)]
    side_pairs = [(0, half - 1), (half - 1, count - 1)]

    def among(devices):
        return functools.reduce(jnp.logical_or, [me == d for d in devices])

    def switch(on, other, *weights):
        flags = jnp.stack([jnp.asarray(on), jnp.asarray(other)]).astype(jnp.int32)
        return jnp.concatenate([flags, *weights])

    near_in = lax.ppermute(block, "chan", near_pairs)
    first_in = lax.ppermute(block, "chan", first_pairs)
    coeffs = lag_rows(freq_count, window_count)
    own = turn(block)
    parts = split(block)
    first_flags = lax.ppermute(quality, "chan", first_pairs)[0]
    near_flags = lax.ppermute(quality, "chan", near_pairs)[0]
    second_flags = lax.ppermute(quality, "chan", second_pairs)[0]
    special = among([0, half - 1])
    second_switch = switch(
        among([t for _, t in second_pairs]), among([t for _, t in late_near]), quality[0] * second_flags
    )

    near_in, *parts, own, coeffs, first_in, near_flags, first_flags, second_flags = lax.optimization_barrier(
        (near_in, *parts, own, coeffs, first_in, near_flags, first_flags, second_flags)
    )
    first_switch = switch(me == 0, special, quality[0], near_flags, first_flags)
    second_in = [lax.ppermute(part, "chan", second_pairs) for part in parts]
    operands = first_switch, own, coeffs, near_in, first_in
    total, token = first_sums(*operands)
    near, far, back = first_sums(*operands, [total, token])
    second_switch, near = lax.optimization_barrier((second_switch, near))
    starts = [0, parts[0].shape[0], parts[0].shape[0] + parts[1].shape[0]]
    total = second_sums(second_switch, own, coeffs, second_in[0], starts[0])
    total, = second_sums(second_switch, own, coeffs, second_in[1], starts[1], total)

    near = jnp.where(me == half - 2, far, near)
    near, far, back = second_sums(
        second_switch, own, coeffs, second_in[2], starts[2], [total, near, far, back]
    )
    returned = lax.ppermute(back, "chan", back_pairs)
    side_returned = lax.ppermute(near, "chan", side_pairs)
    near = jnp.where(among([half - 1, count - 1]), side_returned, near)
    near = jnp.where(me == 0, returned, near)
    far = jnp.where(among([s for s, _ in first_far + second_far]), returned, far)
    return near[None], far[None]


def solution(mesh):
    return jax.shard_map(
        local,
        mesh=mesh,
        in_specs=(P(None, None, None, ("grp", "chan")), P(("grp", "chan"), None)),
        out_specs=(P(("grp", "chan"), None, None, None), P(("grp", "chan"), None, None, None)),
        check_vma=False,
    )
```

```python
import functools
import math

import jax
import jax.numpy as jnp
from jax import lax
from jax.experimental import pallas as pl
from jax.experimental.pallas import tpu as pltpu
from jax.sharding import PartitionSpec as P

HL = 4
LAGS = 2 * HL + 1
STEP = 1024
ENDS = (4, 6, 8)
PARAMS = pltpu.CompilerParams(vmem_limit_bytes=16 * 1024 * 1024)


def lag_rows(freq_count, window_count):
    per_bin = 2 * window_count
    row = jnp.arange(freq_count * per_bin, dtype=jnp.int32)
    freq_values = (row // per_bin).astype(jnp.float32)
    sign = jnp.where(row % per_bin < window_count, 1.0, -1.0)
    lag_values = jnp.arange(HL + 1, dtype=jnp.float32)
    phases = jnp.pi / freq_count * lag_values[:, None] * freq_values[None, :]
    factor = 1.0 / math.sqrt(window_count * freq_count)
    cos_part = jnp.cos(phases) * factor
    sin_part = -jnp.sin(phases[1:]) * factor * sign[None, :]
    return jnp.concatenate([cos_part, sin_part], axis=0).astype(jnp.bfloat16)


def split_kernel(ends, x_ref, *part_refs):
    step = pl.program_id(0)
    for begin, end, part_ref in zip((0, *ends), ends, part_refs):
        @pl.when((step >= begin) & (step < end))
        def _():
            part_ref[...] = x_ref[...]


def split(x):
    rows, cols = x.shape
    steps = rows // STEP
    ends = [steps * e // ENDS[-1] for e in ENDS]
    sizes = [e - b for b, e in zip([0] + ends, ends)]

    def place(end, size):
        return lambda s: (jnp.clip(s - end + size, 0, size - 1), 0)

    return pl.pallas_call(
        functools.partial(split_kernel, ends),
        grid=(steps,),
        in_specs=[pl.BlockSpec((STEP, cols), lambda s: (s, 0))],
        out_specs=[pl.BlockSpec((STEP, cols), place(e, n)) for e, n in zip(ends, sizes)],
        out_shape=[jax.ShapeDtypeStruct((n * STEP, cols), x.dtype) for n in sizes],
        compiler_params=PARAMS,
        cost_estimate=pl.CostEstimate(flops=0, bytes_accessed=4 * rows * cols, transcendentals=0),
        name="split",
    )(x)


def turned(x):
    rows, cols = x.shape
    same = lax.broadcasted_iota(jnp.int32, (cols, cols), 0) == lax.broadcasted_iota(jnp.int32, (cols, cols), 1)
    eye = jnp.where(same, 1.0, 0.0).astype(jnp.bfloat16)
    source = lax.broadcasted_iota(jnp.int32, (2 * cols, 2 * cols), 0)
    target = lax.broadcasted_iota(jnp.int32, (2 * cols, 2 * cols), 1)
    exchange = jnp.where((source ^ 4) == target, 1.0, 0.0).astype(jnp.bfloat16)
    plain = lax.dot_general(eye, x, (((1,), (1,)), ((), ())), preferred_element_type=jnp.float32)
    plain = plain.astype(jnp.bfloat16)
    swapped = [
        jnp.dot(plain[:, t:t + 2 * cols], exchange, preferred_element_type=jnp.float32).astype(jnp.bfloat16)
        for t in range(0, rows, 2 * cols)
    ]
    return plain, jnp.concatenate(swapped, axis=1)


def turn_kernel(x_ref, plain_ref, swapped_ref):
    plain_ref[...], swapped_ref[...] = turned(x_ref[...])


def turn(x):
    rows, cols = x.shape
    out = jax.ShapeDtypeStruct((cols, rows), jnp.bfloat16)
    return pl.pallas_call(
        turn_kernel,
        grid=(rows // STEP,),
        in_specs=[pl.BlockSpec((STEP, cols), lambda s: (s, 0))],
        out_specs=[pl.BlockSpec((cols, STEP), lambda s: (0, s))] * 2,
        out_shape=[out, out],
        compiler_params=PARAMS,
        cost_estimate=pl.CostEstimate(flops=0, bytes_accessed=6 * rows * cols, transcendentals=0),
        name="turn",
    )(x)


def write_lags(out, acc, at, cols, mirrored):
    for lag in range(LAGS):
        k = abs(lag - HL)
        value = acc[k * cols:(k + 1) * cols, at]
        if k:
            odd = acc[(HL + k) * cols:(HL + k + 1) * cols, at]
            value = value + odd if lag > HL else value - odd
        value = value.astype(jnp.bfloat16)
        if mirrored:
            out[LAGS - 1 - lag] = value.T
        else:
            out[lag] = value


def scale(scaled, plain, swapped, coeff_ref):
    cols = plain.shape[0]
    for k in range(LAGS):
        part = plain if k <= HL else swapped
        scaled[k * cols:(k + 1) * cols, :] = part * coeff_ref[k:k + 1, :]


def weigh(x, window_weights):
    rows, cols = x.shape
    window = lax.broadcasted_iota(jnp.int32, (16, cols), 0) % len(window_weights)
    weights = jnp.zeros((16, cols), jnp.float32)
    for w, weight in enumerate(window_weights):
        weights = jnp.where(window == w, weight.astype(jnp.float32), weights)
    weights = jnp.broadcast_to(weights.astype(jnp.bfloat16)[None], (rows // 16, 16, cols))
    return x * weights.reshape(rows, cols)


def first_kernel(windows, switch_ref, plain_ref, swapped_ref, coeff_ref, near_ref, first_ref, *rest):
    step = pl.program_id(0)
    cols = plain_ref.shape[0]
    near_mirrored, special = switch_ref[0], switch_ref[1]
    near_out, far_out, back_out, acc, scaled, plain, swapped, right = rest

    @pl.when(step == 0)
    def _():
        acc[...] = jnp.zeros_like(acc)

    @pl.when(special == 0)
    def _():
        plain[...], swapped[...] = plain_ref[...], swapped_ref[...]
        right[...] = first_ref[...]

    @pl.when(special != 0)
    def _():
        plain[...], swapped[...] = turned(first_ref[...])
        for t in range(0, STEP, cols):
            right[t:t + cols, :] = plain_ref[:, t:t + cols].T

    scale(scaled, plain[...], swapped[...], coeff_ref)
    flags = [[switch_ref[2 + part * windows + w] for w in range(windows)] for part in range(3)]
    near_weights = [jnp.where(special != 0, first, own) * near for own, near, first in zip(*flags)]
    near = weigh(near_ref[...], near_weights)
    far = weigh(right[...], [own * first for own, _, first in zip(*flags)])
    acc[...] += jnp.dot(scaled[...], jnp.concatenate([near, far], axis=1), preferred_element_type=jnp.float32)

    @pl.when(step == pl.num_programs(0) - 1)
    def _():
        near_at, far_at = slice(0, cols), slice(cols, 2 * cols)

        @pl.when(special == 0)
        def _():
            write_lags(back_out, acc, far_at, cols, True)
            write_lags(far_out, acc, far_at, cols, False)

        @pl.when(special != 0)
        def _():
            write_lags(back_out, acc, far_at, cols, False)
            write_lags(far_out, acc, far_at, cols, True)

        pl.when(near_mirrored == 0)(lambda: write_lags(near_out, acc, near_at, cols, False))
        pl.when(near_mirrored != 0)(lambda: write_lags(near_out, acc, near_at, cols, True))


def first_sums(switch, own, coeffs, near_in, first_in):
    rows, cols = near_in.shape
    windows = (switch.shape[0] - 2) // 3
    result = jax.ShapeDtypeStruct((LAGS, cols, cols), jnp.bfloat16)
    left = pl.BlockSpec((cols, STEP), lambda s, on: (0, s))
    right = pl.BlockSpec((STEP, cols), lambda s, on: (s, 0))
    return pl.pallas_call(
        functools.partial(first_kernel, windows),
        grid_spec=pltpu.PrefetchScalarGridSpec(
            num_scalar_prefetch=1,
            grid=(rows // STEP,),
            in_specs=[left, left, pl.BlockSpec((LAGS, STEP), lambda s, on: (0, s)), right, right],
            out_specs=[pl.BlockSpec(result.shape, lambda s, on: (0, 0, 0))] * 3,
            scratch_shapes=[
                pltpu.VMEM((LAGS * cols, 2 * cols), jnp.float32),
                pltpu.VMEM((LAGS * cols, STEP), jnp.bfloat16),
                pltpu.VMEM((cols, STEP), jnp.bfloat16),
                pltpu.VMEM((cols, STEP), jnp.bfloat16),
                pltpu.VMEM((STEP, cols), jnp.bfloat16),
            ],
        ),
        out_shape=[result] * 3,
        compiler_params=PARAMS,
        cost_estimate=pl.CostEstimate(
            flops=4 * LAGS * cols * cols * rows, bytes_accessed=8 * rows * cols, transcendentals=0
        ),
        name="first_sums",
    )(switch, *own, coeffs, near_in, first_in)


def second_kernel(windows, first, last, switch_ref, plain_ref, swapped_ref, coeff_ref, partner_ref, *rest):
    on, late_near = switch_ref[0], switch_ref[1]
    step = pl.program_id(0)
    cols = plain_ref.shape[0]
    if first:
        acc, scaled = rest
    elif not last:
        acc_in, acc, scaled = rest
    else:
        acc_in, near_in, far_in, back_in, near_out, far_out, back_out, acc, scaled = rest

    @pl.when(on != 0)
    def _():
        @pl.when(step == 0)
        def _():
            acc[...] = jnp.zeros_like(acc) if first else acc_in[...]

        scale(scaled, plain_ref[...], swapped_ref[...], coeff_ref)
        partner = weigh(partner_ref[...], [switch_ref[2 + w] for w in range(windows)])
        acc[...] += jnp.dot(scaled[...], partner, preferred_element_type=jnp.float32)

    if last:
        @pl.when(step == pl.num_programs(0) - 1)
        def _():
            here = slice(0, cols)

            @pl.when((on != 0) & (late_near == 0))
            def _():
                write_lags(back_out, acc, here, cols, True)
                write_lags(far_out, acc, here, cols, False)

            @pl.when((on == 0) | (late_near != 0))
            def _():
                back_out[...] = back_in[...]
                far_out[...] = far_in[...]

            pl.when(late_near != 0)(lambda: write_lags(near_out, acc, here, cols, False))

            @pl.when(late_near == 0)
            def _():
                near_out[...] = near_in[...]


def second_sums(switch, own, coeffs, partner, start, earlier=()):
    rows, cols = partner.shape
    windows = switch.shape[0] - 2
    skip = start // STEP
    total = jax.ShapeDtypeStruct((LAGS * cols, cols), jnp.float32)
    total_spec = pl.BlockSpec(total.shape, lambda s, on: (0, 0))
    result = jax.ShapeDtypeStruct((LAGS, cols, cols), jnp.bfloat16)
    result_spec = pl.BlockSpec(result.shape, lambda s, on: (0, 0, 0))
    left = pl.BlockSpec((cols, STEP), lambda s, on: (0, s * on[0] + skip))
    in_specs = [left, left, pl.BlockSpec((LAGS, STEP), lambda s, on: (0, s * on[0] + skip)),
                pl.BlockSpec((STEP, cols), lambda s, on: (s * on[0], 0))]
    scratch = [pltpu.VMEM((LAGS * cols, STEP), jnp.bfloat16)]
    last = len(earlier) > 1
    in_specs += [total_spec, result_spec, result_spec, result_spec][:len(earlier)]
    if not last:
        out_shape, out_specs = [total], [total_spec]
    else:
        out_shape, out_specs = [result] * 3, [result_spec] * 3
        scratch = [pltpu.VMEM(total.shape, jnp.float32)] + scratch
    return pl.pallas_call(
        functools.partial(second_kernel, windows, not earlier, last),
        grid_spec=pltpu.PrefetchScalarGridSpec(
            num_scalar_prefetch=1,
            grid=(rows // STEP,),
            in_specs=in_specs,
            out_specs=out_specs,
            scratch_shapes=scratch,
        ),
        out_shape=out_shape,
        compiler_params=PARAMS,
        cost_estimate=pl.CostEstimate(
            flops=2 * LAGS * cols * cols * rows, bytes_accessed=6 * rows * cols, transcendentals=0
        ),
        name="second_last" if last else "second_part",
    )(switch, *own, coeffs, partner, *earlier)


def local(spectra, quality):
    count = lax.axis_size("chan")
    half = count // 2
    me = lax.axis_index("chan")
    freq_count, _, window_count, cols = spectra.shape
    block = spectra.reshape(-1, cols)

    first_far, second_far = [], []
    for p in range(half):
        if p in (0, half - 1):
            first_far.append((p + half, p))
        elif p > half // 2:
            first_far.append((p, p + half))
        elif p % 2 == 1:
            second_far.append((p, p + half))
        else:
            second_far.append((p + half, p))
    late_near = [(2, 1), (4, 3)]
    first_pairs = first_far + [(0, 1), (half - 1, half - 2)]
    second_pairs = second_far + late_near
    near_pairs = [(d + 1, d) for d in range(1, count - 1) if d not in (1, 3, half - 2, half - 1)]
    near_pairs += [(0, half - 1), (half - 1, 0)]
    back_pairs = [(t, s) for s, t in first_far + second_far] + [(1, 0)]
    side_pairs = [(0, half - 1), (half - 1, count - 1)]

    def among(devices):
        return functools.reduce(jnp.logical_or, [me == d for d in devices])

    def switch(on, other, *weights):
        flags = jnp.stack([jnp.asarray(on), jnp.asarray(other)]).astype(jnp.int32)
        return jnp.concatenate([flags, *weights])

    near_in = lax.ppermute(block, "chan", near_pairs)
    first_in = lax.ppermute(block, "chan", first_pairs)
    coeffs = lag_rows(freq_count, window_count)
    own = turn(block)
    parts = split(block)
    first_flags = lax.ppermute(quality, "chan", first_pairs)[0]
    near_flags = lax.ppermute(quality, "chan", near_pairs)[0]
    second_flags = lax.ppermute(quality, "chan", second_pairs)[0]
    special = among([0, half - 1])
    second_switch = switch(
        among([t for _, t in second_pairs]), among([t for _, t in late_near]), quality[0] * second_flags
    )

    near_in, *parts, own, coeffs, first_in, near_flags, first_flags, second_flags = lax.optimization_barrier(
        (near_in, *parts, own, coeffs, first_in, near_flags, first_flags, second_flags)
    )
    first_switch = switch(me == 0, special, quality[0], near_flags, first_flags)
    second_in = [lax.ppermute(part, "chan", second_pairs) for part in parts]
    near, far, back = first_sums(first_switch, own, coeffs, near_in, first_in)
    second_switch, near = lax.optimization_barrier((second_switch, near))
    starts = [0, parts[0].shape[0], parts[0].shape[0] + parts[1].shape[0]]
    total = second_sums(second_switch, own, coeffs, second_in[0], starts[0])
    total, = second_sums(second_switch, own, coeffs, second_in[1], starts[1], total)

    near = jnp.where(me == half - 2, far, near)
    near, far, back = second_sums(
        second_switch, own, coeffs, second_in[2], starts[2], [total, near, far, back]
    )
    returned = lax.ppermute(back, "chan", back_pairs)
    side_returned = lax.ppermute(near, "chan", side_pairs)
    near = jnp.where(among([half - 1, count - 1]), side_returned, near)
    near = jnp.where(me == 0, returned, near)
    far = jnp.where(among([s for s, _ in first_far + second_far]), returned, far)
    return near[None], far[None]


def solution(mesh):
    return jax.shard_map(
        local,
        mesh=mesh,
        in_specs=(P(None, None, None, ("grp", "chan")), P(("grp", "chan"), None)),
        out_specs=(P(("grp", "chan"), None, None, None), P(("grp", "chan"), None, None, None)),
        check_vma=False,
    )
```

```python
import functools
import math

import jax
import jax.numpy as jnp
from jax import lax
from jax.experimental import pallas as pl
from jax.experimental.pallas import tpu as pltpu
from jax.sharding import PartitionSpec as P

HL = 4
LAGS = 2 * HL + 1
STEP = 1024
ENDS = (5, 7, 8)
PARAMS = pltpu.CompilerParams(vmem_limit_bytes=16 * 1024 * 1024)


def lag_rows(freq_count, window_count):
    per_bin = 2 * window_count
    row = jnp.arange(freq_count * per_bin, dtype=jnp.int32)
    freq_values = (row // per_bin).astype(jnp.float32)
    sign = jnp.where(row % per_bin < window_count, 1.0, -1.0)
    lag_values = jnp.arange(HL + 1, dtype=jnp.float32)
    phases = jnp.pi / freq_count * lag_values[:, None] * freq_values[None, :]
    factor = 1.0 / math.sqrt(window_count * freq_count)
    cos_part = jnp.cos(phases) * factor
    sin_part = -jnp.sin(phases[1:]) * factor * sign[None, :]
    return jnp.concatenate([cos_part, sin_part], axis=0).astype(jnp.bfloat16)


def split_kernel(ends, x_ref, *part_refs):
    step = pl.program_id(0)
    for begin, end, part_ref in zip((0, *ends), ends, part_refs):
        @pl.when((step >= begin) & (step < end))
        def _():
            part_ref[...] = x_ref[...]


def split(x):
    rows, cols = x.shape
    steps = rows // STEP
    ends = [steps * e // ENDS[-1] for e in ENDS]
    sizes = [e - b for b, e in zip([0] + ends, ends)]

    def place(end, size):
        return lambda s: (jnp.clip(s - end + size, 0, size - 1), 0)

    return pl.pallas_call(
        functools.partial(split_kernel, ends),
        grid=(steps,),
        in_specs=[pl.BlockSpec((STEP, cols), lambda s: (s, 0))],
        out_specs=[pl.BlockSpec((STEP, cols), place(e, n)) for e, n in zip(ends, sizes)],
        out_shape=[jax.ShapeDtypeStruct((n * STEP, cols), x.dtype) for n in sizes],
        compiler_params=PARAMS,
        cost_estimate=pl.CostEstimate(flops=0, bytes_accessed=4 * rows * cols, transcendentals=0),
        name="split",
    )(x)


def turned(x):
    rows, cols = x.shape
    same = lax.broadcasted_iota(jnp.int32, (cols, cols), 0) == lax.broadcasted_iota(jnp.int32, (cols, cols), 1)
    eye = jnp.where(same, 1.0, 0.0).astype(jnp.bfloat16)
    source = lax.broadcasted_iota(jnp.int32, (2 * cols, 2 * cols), 0)
    target = lax.broadcasted_iota(jnp.int32, (2 * cols, 2 * cols), 1)
    exchange = jnp.where((source ^ 4) == target, 1.0, 0.0).astype(jnp.bfloat16)
    plain = lax.dot_general(eye, x, (((1,), (1,)), ((), ())), preferred_element_type=jnp.float32)
    plain = plain.astype(jnp.bfloat16)
    swapped = [
        jnp.dot(plain[:, t:t + 2 * cols], exchange, preferred_element_type=jnp.float32).astype(jnp.bfloat16)
        for t in range(0, rows, 2 * cols)
    ]
    return plain, jnp.concatenate(swapped, axis=1)


def turn_kernel(x_ref, plain_ref, swapped_ref):
    plain_ref[...], swapped_ref[...] = turned(x_ref[...])


def turn(x):
    rows, cols = x.shape
    out = jax.ShapeDtypeStruct((cols, rows), jnp.bfloat16)
    return pl.pallas_call(
        turn_kernel,
        grid=(rows // STEP,),
        in_specs=[pl.BlockSpec((STEP, cols), lambda s: (s, 0))],
        out_specs=[pl.BlockSpec((cols, STEP), lambda s: (0, s))] * 2,
        out_shape=[out, out],
        compiler_params=PARAMS,
        cost_estimate=pl.CostEstimate(flops=0, bytes_accessed=6 * rows * cols, transcendentals=0),
        name="turn",
    )(x)


def write_lags(out, acc, at, cols, mirrored):
    for lag in range(LAGS):
        k = abs(lag - HL)
        value = acc[k * cols:(k + 1) * cols, at]
        if k:
            odd = acc[(HL + k) * cols:(HL + k + 1) * cols, at]
            value = value + odd if lag > HL else value - odd
        value = value.astype(jnp.bfloat16)
        if mirrored:
            out[LAGS - 1 - lag] = value.T
        else:
            out[lag] = value


def scale(scaled, plain, swapped, coeff_ref):
    cols = plain.shape[0]
    for k in range(LAGS):
        part = plain if k <= HL else swapped
        scaled[k * cols:(k + 1) * cols, :] = part * coeff_ref[k:k + 1, :]


def weigh(x, window_weights):
    rows, cols = x.shape
    window = lax.broadcasted_iota(jnp.int32, (16, cols), 0) % len(window_weights)
    weights = jnp.zeros((16, cols), jnp.float32)
    for w, weight in enumerate(window_weights):
        weights = jnp.where(window == w, weight.astype(jnp.float32), weights)
    weights = jnp.broadcast_to(weights.astype(jnp.bfloat16)[None], (rows // 16, 16, cols))
    return x * weights.reshape(rows, cols)


def first_kernel(windows, switch_ref, plain_ref, swapped_ref, coeff_ref, near_ref, first_ref, *rest):
    step = pl.program_id(0)
    cols = plain_ref.shape[0]
    near_mirrored, special = switch_ref[0], switch_ref[1]
    near_out, far_out, back_out, acc, scaled, plain, swapped, right = rest

    @pl.when(step == 0)
    def _():
        acc[...] = jnp.zeros_like(acc)

    @pl.when(special == 0)
    def _():
        plain[...], swapped[...] = plain_ref[...], swapped_ref[...]
        right[...] = first_ref[...]

    @pl.when(special != 0)
    def _():
        plain[...], swapped[...] = turned(first_ref[...])
        for t in range(0, STEP, cols):
            right[t:t + cols, :] = plain_ref[:, t:t + cols].T

    scale(scaled, plain[...], swapped[...], coeff_ref)
    flags = [[switch_ref[2 + part * windows + w] for w in range(windows)] for part in range(3)]
    near_weights = [jnp.where(special != 0, first, own) * near for own, near, first in zip(*flags)]
    near = weigh(near_ref[...], near_weights)
    far = weigh(right[...], [own * first for own, _, first in zip(*flags)])
    acc[...] += jnp.dot(scaled[...], jnp.concatenate([near, far], axis=1), preferred_element_type=jnp.float32)

    @pl.when(step == pl.num_programs(0) - 1)
    def _():
        near_at, far_at = slice(0, cols), slice(cols, 2 * cols)

        @pl.when(special == 0)
        def _():
            write_lags(back_out, acc, far_at, cols, True)
            write_lags(far_out, acc, far_at, cols, False)

        @pl.when(special != 0)
        def _():
            write_lags(back_out, acc, far_at, cols, False)
            write_lags(far_out, acc, far_at, cols, True)

        pl.when(near_mirrored == 0)(lambda: write_lags(near_out, acc, near_at, cols, False))
        pl.when(near_mirrored != 0)(lambda: write_lags(near_out, acc, near_at, cols, True))


def first_sums(switch, own, coeffs, near_in, first_in):
    rows, cols = near_in.shape
    windows = (switch.shape[0] - 2) // 3
    result = jax.ShapeDtypeStruct((LAGS, cols, cols), jnp.bfloat16)
    left = pl.BlockSpec((cols, STEP), lambda s, on: (0, s))
    right = pl.BlockSpec((STEP, cols), lambda s, on: (s, 0))
    return pl.pallas_call(
        functools.partial(first_kernel, windows),
        grid_spec=pltpu.PrefetchScalarGridSpec(
            num_scalar_prefetch=1,
            grid=(rows // STEP,),
            in_specs=[left, left, pl.BlockSpec((LAGS, STEP), lambda s, on: (0, s)), right, right],
            out_specs=[pl.BlockSpec(result.shape, lambda s, on: (0, 0, 0))] * 3,
            scratch_shapes=[
                pltpu.VMEM((LAGS * cols, 2 * cols), jnp.float32),
                pltpu.VMEM((LAGS * cols, STEP), jnp.bfloat16),
                pltpu.VMEM((cols, STEP), jnp.bfloat16),
                pltpu.VMEM((cols, STEP), jnp.bfloat16),
                pltpu.VMEM((STEP, cols), jnp.bfloat16),
            ],
        ),
        out_shape=[result] * 3,
        compiler_params=PARAMS,
        cost_estimate=pl.CostEstimate(
            flops=4 * LAGS * cols * cols * rows, bytes_accessed=8 * rows * cols, transcendentals=0
        ),
        name="first_sums",
    )(switch, *own, coeffs, near_in, first_in)


def second_kernel(windows, first, last, switch_ref, plain_ref, swapped_ref, coeff_ref, partner_ref, *rest):
    on, late_near = switch_ref[0], switch_ref[1]
    step = pl.program_id(0)
    cols = plain_ref.shape[0]
    if first:
        acc, scaled = rest
    elif not last:
        acc_in, acc, scaled = rest
    else:
        acc_in, near_in, far_in, back_in, near_out, far_out, back_out, acc, scaled = rest

    @pl.when(on != 0)
    def _():
        @pl.when(step == 0)
        def _():
            acc[...] = jnp.zeros_like(acc) if first else acc_in[...]

        scale(scaled, plain_ref[...], swapped_ref[...], coeff_ref)
        partner = weigh(partner_ref[...], [switch_ref[2 + w] for w in range(windows)])
        acc[...] += jnp.dot(scaled[...], partner, preferred_element_type=jnp.float32)

    if last:
        @pl.when(step == pl.num_programs(0) - 1)
        def _():
            here = slice(0, cols)

            @pl.when((on != 0) & (late_near == 0))
            def _():
                write_lags(back_out, acc, here, cols, True)
                write_lags(far_out, acc, here, cols, False)

            @pl.when((on == 0) | (late_near != 0))
            def _():
                back_out[...] = back_in[...]
                far_out[...] = far_in[...]

            pl.when(late_near != 0)(lambda: write_lags(near_out, acc, here, cols, False))

            @pl.when(late_near == 0)
            def _():
                near_out[...] = near_in[...]


def second_sums(switch, own, coeffs, partner, start, earlier=()):
    rows, cols = partner.shape
    windows = switch.shape[0] - 2
    skip = start // STEP
    total = jax.ShapeDtypeStruct((LAGS * cols, cols), jnp.float32)
    total_spec = pl.BlockSpec(total.shape, lambda s, on: (0, 0))
    result = jax.ShapeDtypeStruct((LAGS, cols, cols), jnp.bfloat16)
    result_spec = pl.BlockSpec(result.shape, lambda s, on: (0, 0, 0))
    left = pl.BlockSpec((cols, STEP), lambda s, on: (0, s * on[0] + skip))
    in_specs = [left, left, pl.BlockSpec((LAGS, STEP), lambda s, on: (0, s * on[0] + skip)),
                pl.BlockSpec((STEP, cols), lambda s, on: (s * on[0], 0))]
    scratch = [pltpu.VMEM((LAGS * cols, STEP), jnp.bfloat16)]
    last = len(earlier) > 1
    in_specs += [total_spec, result_spec, result_spec, result_spec][:len(earlier)]
    if not last:
        out_shape, out_specs = [total], [total_spec]
    else:
        out_shape, out_specs = [result] * 3, [result_spec] * 3
        scratch = [pltpu.VMEM(total.shape, jnp.float32)] + scratch
    return pl.pallas_call(
        functools.partial(second_kernel, windows, not earlier, last),
        grid_spec=pltpu.PrefetchScalarGridSpec(
            num_scalar_prefetch=1,
            grid=(rows // STEP,),
            in_specs=in_specs,
            out_specs=out_specs,
            scratch_shapes=scratch,
        ),
        out_shape=out_shape,
        compiler_params=PARAMS,
        cost_estimate=pl.CostEstimate(
            flops=2 * LAGS * cols * cols * rows, bytes_accessed=6 * rows * cols, transcendentals=0
        ),
        name="second_last" if last else "second_part",
    )(switch, *own, coeffs, partner, *earlier)


def local(spectra, quality):
    count = lax.axis_size("chan")
    half = count // 2
    me = lax.axis_index("chan")
    freq_count, _, window_count, cols = spectra.shape
    block = spectra.reshape(-1, cols)

    first_far, second_far = [], []
    for p in range(half):
        if p in (0, half - 1):
            first_far.append((p + half, p))
        elif p > half // 2:
            first_far.append((p, p + half))
        elif p % 2 == 1:
            second_far.append((p, p + half))
        else:
            second_far.append((p + half, p))
    late_near = [(2, 1), (4, 3)]
    first_pairs = first_far + [(0, 1), (half - 1, half - 2)]
    second_pairs = second_far + late_near
    near_pairs = [(d + 1, d) for d in range(1, count - 1) if d not in (1, 3, half - 2, half - 1)]
    near_pairs += [(0, half - 1), (half - 1, 0)]
    back_pairs = [(t, s) for s, t in first_far + second_far] + [(1, 0)]
    side_pairs = [(0, half - 1), (half - 1, count - 1)]

    def among(devices):
        return functools.reduce(jnp.logical_or, [me == d for d in devices])

    def switch(on, other, *weights):
        flags = jnp.stack([jnp.asarray(on), jnp.asarray(other)]).astype(jnp.int32)
        return jnp.concatenate([flags, *weights])

    near_in = lax.ppermute(block, "chan", near_pairs)
    first_in = lax.ppermute(block, "chan", first_pairs)
    coeffs = lag_rows(freq_count, window_count)
    own = turn(block)
    parts = split(block)
    first_flags = lax.ppermute(quality, "chan", first_pairs)[0]
    near_flags = lax.ppermute(quality, "chan", near_pairs)[0]
    second_flags = lax.ppermute(quality, "chan", second_pairs)[0]
    special = among([0, half - 1])
    second_switch = switch(
        among([t for _, t in second_pairs]), among([t for _, t in late_near]), quality[0] * second_flags
    )

    near_in, *parts, own, coeffs, first_in, near_flags, first_flags, second_flags = lax.optimization_barrier(
        (near_in, *parts, own, coeffs, first_in, near_flags, first_flags, second_flags)
    )
    first_switch = switch(me == 0, special, quality[0], near_flags, first_flags)
    second_in = [lax.ppermute(part, "chan", second_pairs) for part in parts]
    near, far, back = first_sums(first_switch, own, coeffs, near_in, first_in)
    second_switch, near = lax.optimization_barrier((second_switch, near))
    starts = [0, parts[0].shape[0], parts[0].shape[0] + parts[1].shape[0]]
    total = second_sums(second_switch, own, coeffs, second_in[0], starts[0])
    total, = second_sums(second_switch, own, coeffs, second_in[1], starts[1], total)

    near = jnp.where(me == half - 2, far, near)
    near, far, back = second_sums(
        second_switch, own, coeffs, second_in[2], starts[2], [total, near, far, back]
    )
    returned = lax.ppermute(back, "chan", back_pairs)
    side_returned = lax.ppermute(near, "chan", side_pairs)
    near = jnp.where(among([half - 1, count - 1]), side_returned, near)
    near = jnp.where(me == 0, returned, near)
    far = jnp.where(among([s for s, _ in first_far + second_far]), returned, far)
    return near[None], far[None]


def solution(mesh):
    return jax.shard_map(
        local,
        mesh=mesh,
        in_specs=(P(None, None, None, ("grp", "chan")), P(("grp", "chan"), None)),
        out_specs=(P(("grp", "chan"), None, None, None), P(("grp", "chan"), None, None, None)),
        check_vma=False,
    )
```

```python
import functools
import math

import jax
import jax.numpy as jnp
from jax import lax
from jax.experimental import pallas as pl
from jax.experimental.pallas import tpu as pltpu
from jax.sharding import PartitionSpec as P

HL = 4
LAGS = 2 * HL + 1
STEP = 1024
ENDS = (4, 7, 8)
PARAMS = pltpu.CompilerParams(vmem_limit_bytes=16 * 1024 * 1024)


def lag_rows(freq_count, window_count):
    per_bin = 2 * window_count
    row = jnp.arange(freq_count * per_bin, dtype=jnp.int32)
    freq_values = (row // per_bin).astype(jnp.float32)
    sign = jnp.where(row % per_bin < window_count, 1.0, -1.0)
    lag_values = jnp.arange(HL + 1, dtype=jnp.float32)
    phases = jnp.pi / freq_count * lag_values[:, None] * freq_values[None, :]
    factor = 1.0 / math.sqrt(window_count * freq_count)
    cos_part = jnp.cos(phases) * factor
    sin_part = -jnp.sin(phases[1:]) * factor * sign[None, :]
    return jnp.concatenate([cos_part, sin_part], axis=0).astype(jnp.bfloat16)


def split_kernel(ends, x_ref, *part_refs):
    step = pl.program_id(0)
    for begin, end, part_ref in zip((0, *ends), ends, part_refs):
        @pl.when((step >= begin) & (step < end))
        def _():
            part_ref[...] = x_ref[...]


def split(x):
    rows, cols = x.shape
    steps = rows // STEP
    ends = [steps * e // ENDS[-1] for e in ENDS]
    sizes = [e - b for b, e in zip([0] + ends, ends)]

    def place(end, size):
        return lambda s: (jnp.clip(s - end + size, 0, size - 1), 0)

    return pl.pallas_call(
        functools.partial(split_kernel, ends),
        grid=(steps,),
        in_specs=[pl.BlockSpec((STEP, cols), lambda s: (s, 0))],
        out_specs=[pl.BlockSpec((STEP, cols), place(e, n)) for e, n in zip(ends, sizes)],
        out_shape=[jax.ShapeDtypeStruct((n * STEP, cols), x.dtype) for n in sizes],
        compiler_params=PARAMS,
        cost_estimate=pl.CostEstimate(flops=0, bytes_accessed=4 * rows * cols, transcendentals=0),
        name="split",
    )(x)


def turned(x):
    rows, cols = x.shape
    same = lax.broadcasted_iota(jnp.int32, (cols, cols), 0) == lax.broadcasted_iota(jnp.int32, (cols, cols), 1)
    eye = jnp.where(same, 1.0, 0.0).astype(jnp.bfloat16)
    source = lax.broadcasted_iota(jnp.int32, (2 * cols, 2 * cols), 0)
    target = lax.broadcasted_iota(jnp.int32, (2 * cols, 2 * cols), 1)
    exchange = jnp.where((source ^ 4) == target, 1.0, 0.0).astype(jnp.bfloat16)
    plain = lax.dot_general(eye, x, (((1,), (1,)), ((), ())), preferred_element_type=jnp.float32)
    plain = plain.astype(jnp.bfloat16)
    swapped = [
        jnp.dot(plain[:, t:t + 2 * cols], exchange, preferred_element_type=jnp.float32).astype(jnp.bfloat16)
        for t in range(0, rows, 2 * cols)
    ]
    return plain, jnp.concatenate(swapped, axis=1)


def turn_kernel(x_ref, plain_ref, swapped_ref):
    plain_ref[...], swapped_ref[...] = turned(x_ref[...])


def turn(x):
    rows, cols = x.shape
    out = jax.ShapeDtypeStruct((cols, rows), jnp.bfloat16)
    return pl.pallas_call(
        turn_kernel,
        grid=(rows // STEP,),
        in_specs=[pl.BlockSpec((STEP, cols), lambda s: (s, 0))],
        out_specs=[pl.BlockSpec((cols, STEP), lambda s: (0, s))] * 2,
        out_shape=[out, out],
        compiler_params=PARAMS,
        cost_estimate=pl.CostEstimate(flops=0, bytes_accessed=6 * rows * cols, transcendentals=0),
        name="turn",
    )(x)


def write_lags(out, acc, at, cols, mirrored):
    for lag in range(LAGS):
        k = abs(lag - HL)
        value = acc[k * cols:(k + 1) * cols, at]
        if k:
            odd = acc[(HL + k) * cols:(HL + k + 1) * cols, at]
            value = value + odd if lag > HL else value - odd
        value = value.astype(jnp.bfloat16)
        if mirrored:
            out[LAGS - 1 - lag] = value.T
        else:
            out[lag] = value


def scale(scaled, plain, swapped, coeff_ref):
    cols = plain.shape[0]
    for k in range(LAGS):
        part = plain if k <= HL else swapped
        scaled[k * cols:(k + 1) * cols, :] = part * coeff_ref[k:k + 1, :]


def weigh(x, window_weights):
    rows, cols = x.shape
    window = lax.broadcasted_iota(jnp.int32, (16, cols), 0) % len(window_weights)
    weights = jnp.zeros((16, cols), jnp.float32)
    for w, weight in enumerate(window_weights):
        weights = jnp.where(window == w, weight.astype(jnp.float32), weights)
    weights = jnp.broadcast_to(weights.astype(jnp.bfloat16)[None], (rows // 16, 16, cols))
    return x * weights.reshape(rows, cols)


def first_kernel(windows, switch_ref, plain_ref, swapped_ref, coeff_ref, near_ref, first_ref, *rest):
    step = pl.program_id(0)
    cols = plain_ref.shape[0]
    near_mirrored, special = switch_ref[0], switch_ref[1]
    near_out, far_out, back_out, acc, scaled, plain, swapped, right = rest

    @pl.when(step == 0)
    def _():
        acc[...] = jnp.zeros_like(acc)

    @pl.when(special == 0)
    def _():
        plain[...], swapped[...] = plain_ref[...], swapped_ref[...]
        right[...] = first_ref[...]

    @pl.when(special != 0)
    def _():
        plain[...], swapped[...] = turned(first_ref[...])
        for t in range(0, STEP, cols):
            right[t:t + cols, :] = plain_ref[:, t:t + cols].T

    scale(scaled, plain[...], swapped[...], coeff_ref)
    flags = [[switch_ref[2 + part * windows + w] for w in range(windows)] for part in range(3)]
    near_weights = [jnp.where(special != 0, first, own) * near for own, near, first in zip(*flags)]
    near = weigh(near_ref[...], near_weights)
    far = weigh(right[...], [own * first for own, _, first in zip(*flags)])
    acc[...] += jnp.dot(scaled[...], jnp.concatenate([near, far], axis=1), preferred_element_type=jnp.float32)

    @pl.when(step == pl.num_programs(0) - 1)
    def _():
        near_at, far_at = slice(0, cols), slice(cols, 2 * cols)

        @pl.when(special == 0)
        def _():
            write_lags(back_out, acc, far_at, cols, True)
            write_lags(far_out, acc, far_at, cols, False)

        @pl.when(special != 0)
        def _():
            write_lags(back_out, acc, far_at, cols, False)
            write_lags(far_out, acc, far_at, cols, True)

        pl.when(near_mirrored == 0)(lambda: write_lags(near_out, acc, near_at, cols, False))
        pl.when(near_mirrored != 0)(lambda: write_lags(near_out, acc, near_at, cols, True))


def first_sums(switch, own, coeffs, near_in, first_in):
    rows, cols = near_in.shape
    windows = (switch.shape[0] - 2) // 3
    result = jax.ShapeDtypeStruct((LAGS, cols, cols), jnp.bfloat16)
    left = pl.BlockSpec((cols, STEP), lambda s, on: (0, s))
    right = pl.BlockSpec((STEP, cols), lambda s, on: (s, 0))
    return pl.pallas_call(
        functools.partial(first_kernel, windows),
        grid_spec=pltpu.PrefetchScalarGridSpec(
            num_scalar_prefetch=1,
            grid=(rows // STEP,),
            in_specs=[left, left, pl.BlockSpec((LAGS, STEP), lambda s, on: (0, s)), right, right],
            out_specs=[pl.BlockSpec(result.shape, lambda s, on: (0, 0, 0))] * 3,
            scratch_shapes=[
                pltpu.VMEM((LAGS * cols, 2 * cols), jnp.float32),
                pltpu.VMEM((LAGS * cols, STEP), jnp.bfloat16),
                pltpu.VMEM((cols, STEP), jnp.bfloat16),
                pltpu.VMEM((cols, STEP), jnp.bfloat16),
                pltpu.VMEM((STEP, cols), jnp.bfloat16),
            ],
        ),
        out_shape=[result] * 3,
        compiler_params=PARAMS,
        cost_estimate=pl.CostEstimate(
            flops=4 * LAGS * cols * cols * rows, bytes_accessed=8 * rows * cols, transcendentals=0
        ),
        name="first_sums",
    )(switch, *own, coeffs, near_in, first_in)


def second_kernel(windows, first, last, switch_ref, plain_ref, swapped_ref, coeff_ref, partner_ref, *rest):
    on, late_near = switch_ref[0], switch_ref[1]
    step = pl.program_id(0)
    cols = plain_ref.shape[0]
    if first:
        acc, scaled = rest
    elif not last:
        acc_in, acc, scaled = rest
    else:
        acc_in, near_in, far_in, back_in, near_out, far_out, back_out, acc, scaled = rest

    @pl.when(on != 0)
    def _():
        @pl.when(step == 0)
        def _():
            acc[...] = jnp.zeros_like(acc) if first else acc_in[...]

        scale(scaled, plain_ref[...], swapped_ref[...], coeff_ref)
        partner = weigh(partner_ref[...], [switch_ref[2 + w] for w in range(windows)])
        acc[...] += jnp.dot(scaled[...], partner, preferred_element_type=jnp.float32)

    if last:
        @pl.when(step == pl.num_programs(0) - 1)
        def _():
            here = slice(0, cols)

            @pl.when((on != 0) & (late_near == 0))
            def _():
                write_lags(back_out, acc, here, cols, True)
                write_lags(far_out, acc, here, cols, False)

            @pl.when((on == 0) | (late_near != 0))
            def _():
                back_out[...] = back_in[...]
                far_out[...] = far_in[...]

            pl.when(late_near != 0)(lambda: write_lags(near_out, acc, here, cols, False))

            @pl.when(late_near == 0)
            def _():
                near_out[...] = near_in[...]


def second_sums(switch, own, coeffs, partner, start, earlier=()):
    rows, cols = partner.shape
    windows = switch.shape[0] - 2
    skip = start // STEP
    total = jax.ShapeDtypeStruct((LAGS * cols, cols), jnp.float32)
    total_spec = pl.BlockSpec(total.shape, lambda s, on: (0, 0))
    result = jax.ShapeDtypeStruct((LAGS, cols, cols), jnp.bfloat16)
    result_spec = pl.BlockSpec(result.shape, lambda s, on: (0, 0, 0))
    left = pl.BlockSpec((cols, STEP), lambda s, on: (0, s * on[0] + skip))
    in_specs = [left, left, pl.BlockSpec((LAGS, STEP), lambda s, on: (0, s * on[0] + skip)),
                pl.BlockSpec((STEP, cols), lambda s, on: (s * on[0], 0))]
    scratch = [pltpu.VMEM((LAGS * cols, STEP), jnp.bfloat16)]
    last = len(earlier) > 1
    in_specs += [total_spec, result_spec, result_spec, result_spec][:len(earlier)]
    if not last:
        out_shape, out_specs = [total], [total_spec]
    else:
        out_shape, out_specs = [result] * 3, [result_spec] * 3
        scratch = [pltpu.VMEM(total.shape, jnp.float32)] + scratch
    return pl.pallas_call(
        functools.partial(second_kernel, windows, not earlier, last),
        grid_spec=pltpu.PrefetchScalarGridSpec(
            num_scalar_prefetch=1,
            grid=(rows // STEP,),
            in_specs=in_specs,
            out_specs=out_specs,
            scratch_shapes=scratch,
        ),
        out_shape=out_shape,
        compiler_params=PARAMS,
        cost_estimate=pl.CostEstimate(
            flops=2 * LAGS * cols * cols * rows, bytes_accessed=6 * rows * cols, transcendentals=0
        ),
        name="second_last" if last else "second_part",
    )(switch, *own, coeffs, partner, *earlier)


def local(spectra, quality):
    count = lax.axis_size("chan")
    half = count // 2
    me = lax.axis_index("chan")
    freq_count, _, window_count, cols = spectra.shape
    block = spectra.reshape(-1, cols)

    first_far, second_far = [], []
    for p in range(half):
        if p in (0, half - 1):
            first_far.append((p + half, p))
        elif p > half // 2:
            first_far.append((p, p + half))
        elif p % 2 == 1:
            second_far.append((p, p + half))
        else:
            second_far.append((p + half, p))
    late_near = [(2, 1), (4, 3)]
    first_pairs = first_far + [(0, 1), (half - 1, half - 2)]
    second_pairs = second_far + late_near
    near_pairs = [(d + 1, d) for d in range(1, count - 1) if d not in (1, 3, half - 2, half - 1)]
    near_pairs += [(0, half - 1), (half - 1, 0)]
    back_pairs = [(t, s) for s, t in first_far + second_far] + [(1, 0)]
    side_pairs = [(0, half - 1), (half - 1, count - 1)]

    def among(devices):
        return functools.reduce(jnp.logical_or, [me == d for d in devices])

    def switch(on, other, *weights):
        flags = jnp.stack([jnp.asarray(on), jnp.asarray(other)]).astype(jnp.int32)
        return jnp.concatenate([flags, *weights])

    near_in = lax.ppermute(block, "chan", near_pairs)
    first_in = lax.ppermute(block, "chan", first_pairs)
    coeffs = lag_rows(freq_count, window_count)
    own = turn(block)
    parts = split(block)
    first_flags = lax.ppermute(quality, "chan", first_pairs)[0]
    near_flags = lax.ppermute(quality, "chan", near_pairs)[0]
    second_flags = lax.ppermute(quality, "chan", second_pairs)[0]
    special = among([0, half - 1])
    second_switch = switch(
        among([t for _, t in second_pairs]), among([t for _, t in late_near]), quality[0] * second_flags
    )

    near_in, *parts, own, coeffs, first_in, near_flags, first_flags, second_flags = lax.optimization_barrier(
        (near_in, *parts, own, coeffs, first_in, near_flags, first_flags, second_flags)
    )
    first_switch = switch(me == 0, special, quality[0], near_flags, first_flags)
    second_in = [lax.ppermute(part, "chan", second_pairs) for part in parts]
    near, far, back = first_sums(first_switch, own, coeffs, near_in, first_in)
    second_switch, near = lax.optimization_barrier((second_switch, near))
    starts = [0, parts[0].shape[0], parts[0].shape[0] + parts[1].shape[0]]
    total = second_sums(second_switch, own, coeffs, second_in[0], starts[0])
    total, = second_sums(second_switch, own, coeffs, second_in[1], starts[1], total)

    near = jnp.where(me == half - 2, far, near)
    near, far, back = second_sums(
        second_switch, own, coeffs, second_in[2], starts[2], [total, near, far, back]
    )
    returned = lax.ppermute(back, "chan", back_pairs)
    side_returned = lax.ppermute(near, "chan", side_pairs)
    near = jnp.where(among([half - 1, count - 1]), side_returned, near)
    near = jnp.where(me == 0, returned, near)
    far = jnp.where(among([s for s, _ in first_far + second_far]), returned, far)
    return near[None], far[None]


def solution(mesh):
    return jax.shard_map(
        local,
        mesh=mesh,
        in_specs=(P(None, None, None, ("grp", "chan")), P(("grp", "chan"), None)),
        out_specs=(P(("grp", "chan"), None, None, None), P(("grp", "chan"), None, None, None)),
        check_vma=False,
    )
```
